32 devices in a mesh: lat: 4 (over y, core), lon: 8 (over z, x).
Axes of the slice: x: 2, y: 2, z: 4, core: 2. Of those that a mesh axis runs over, the one named last changes fastest.
Arguments:
- depth: float32 [32, 8192], P('lat', 'lon'), may hold values from 0.5 to 4
- friction: float32 [32, 8192], P('lat', 'lon'), may hold values from 0.2 to 2
- ocean_mask: int32 [32, 8192], P('lat', 'lon'), may hold values 0 or 1
- forcing: float32 [16, 32, 8192], P(None, 'lat', 'lon'), may hold values from -24 to 24
- tile_route: int32 [512, 1], P(('lat', 'lon')), may hold values from 0 to 7; in each aligned block of 16 rows (0 to 15, 16 to 31, ...) at most 2 rows name the same one
- tile_block: int32 [512], P(('lat', 'lon')), may hold values from 0 to 63
- obs_cell: int32 [512, 128], P(('lat', 'lon')), may hold values from 0 to 127
- obs_time: float32 [512, 128], P(('lat', 'lon')), may hold values from 0 to 720
- obs_value: float32 [512, 128], P(('lat', 'lon')), may hold values from -6 to 6
- obs_weight: float32 [512, 128], P(('lat', 'lon')), may hold values from 0.5 to 4
Outputs:
- elevation: float32 [16, 32, 8192], P(None, 'lat', 'lon')
- residual: float32 [16, 32, 8192], P(None, 'lat', 'lon')
The draws below stay inside these ranges and needn't reach their ends.
Inputs may be any that keep to these rules, and one draw needn't show every extreme that they name: `tile_route`: among the 16 tiles of one device at most 2 name the same owner, and in some device exactly 2 do.
All inputs are finite; a program needn't handle non-finite values. No bound on the sum of `ocean_mask` on one device may be relied on, other than what follows from the above.
Results may differ from the reference program's by a relative error of at most 0.0007.
Values sent between devices are 32-bit elements; how exact they have to be, the bound alone decides.
A program may use at most 64 MiB of HBM per device.

```python
import math
import jax
import jax.numpy as jnp
import numpy as np
from jax import lax

NC = 8
CLAT = 8
CLON = 1024
TILES_DEV = 16
OBS_TILE = 128
BLOCK = 128
CAP = 2
ITERS = 3
OUTER = 2
CHANNELS = 16
NLAT = 32
NLON = 8192
OWNERS = 8
NTILES = 512
BLOCKS_DEV = 64
N_LON = 8


def draw_forcing(key, part):
    first_key, second_key = jax.random.split(jax.random.fold_in(key, 11))
    latitude = jnp.arange(NLAT, dtype=jnp.float32) / max(NLAT - 1, 1)
    jitter = jnp.exp(jax.random.uniform(second_key, (1, NLAT, 1), minval=-0.35, maxval=0.35))
    base = jnp.clip(jax.random.normal(first_key, (2 * NC, NLAT, NLON)), -5.0, 5.0)
    envelope = 3.0 ** latitude
    return (base * envelope[None, :, None] * jitter).astype(jnp.float32)


def place_ends(result, own_key, least, top_value):
    extent = result.shape
    place = [jax.random.randint(jax.random.fold_in(own_key, axis), (), 0, extent[axis]) for axis in range(len(extent))]
    result = result.at[tuple(place)].set(least)
    longest = extent.index(max(extent))
    place[longest] = (place[longest] + 1) % extent[longest]
    return result.at[tuple(place)].set(top_value)


def steps_of(own_key, extent, pieces, low, largest):
    level, own = 1.0, jax.random.fold_in(own_key, 6)
    for dim, blocks in pieces:
        steps = jnp.exp(jax.random.uniform(jax.random.fold_in(own, dim), (blocks,), jnp.float32, low / len(pieces), largest / len(pieces)))
        level = level * jnp.repeat(steps, extent[dim] // blocks).reshape([-1 if axis == dim else 1 for axis in range(len(extent))])
    return level


def assign_block(rng, own, number, rows, number_of, top, most, lean):
    order = jax.random.permutation(rng, number_of)
    packed, common = portions_of(number_of, rows * top, most, lean, True), portions_of(number_of, rows * top, most, lean, False)
    places = jnp.arange(number_of)

    def named(lengths, turn):
        used = int((lengths > 0).sum())
        fixed = max(1, used // 4)
        moved = fixed + (places - fixed + turn * (used - fixed)) % max(1, number_of - fixed)
        return jnp.zeros((number_of,), jnp.int32).at[order[jnp.where(places < fixed, places, moved)]].set(jnp.asarray(lengths, jnp.int32))

    lengths = jnp.where(number % 4 == 0, named(packed, number // 4), named(common, number - number // 4 - 1))
    mixed = jax.random.permutation(jax.random.fold_in(own, 3), number_of)
    source_of, sink = mixed[0:number_of // 2 * 2:2], mixed[1:number_of // 2 * 2:2]
    room = jnp.minimum(lengths[source_of] - 1, most - lengths[sink]) // 2
    room = jnp.where((source_of == order[0]) | (sink == order[0]) | (lengths[sink] == 0), 0, jnp.maximum(room, 0))
    moved = jax.random.randint(jax.random.fold_in(own, 4), (number_of // 2,), 0, 1 << 20) % (room + 1)
    lengths = lengths.at[source_of].add(-moved).at[sink].add(moved)
    items = jnp.searchsorted(jnp.cumsum(lengths), jnp.arange(rows * top), side="right").astype(jnp.int32)
    listing = items.reshape(top, rows).T
    listing = listing[jax.random.permutation(jax.random.fold_in(own, 1), rows)]
    turn = jax.random.randint(jax.random.fold_in(own, 2), (rows, 1), 0, top)
    return jnp.take_along_axis(listing, (jnp.arange(top)[None, :] + turn) % top, axis=1)


def portions_of(amount, total, reach, slope, full):
    loads = [(1 << 20) // math.isqrt(rank ** slope) + 1 for rank in range(1, amount + 1)]
    largest = reach if full else min(reach, max(-(-total // amount), total * loads[0] // sum(loads)))
    least = 1 if total - largest >= amount - 1 else 0
    holding, spare = [largest] + [least] * (amount - 1), total - largest - least * (amount - 1)
    while spare > 0:
        candidates = [i for i in range(1, amount) if holding[i] < largest] or [i for i in range(1, amount) if holding[i] < reach]
        pool, left = sum([loads[i] for i in candidates]), spare
        for i in candidates:
            addition = min(reach - holding[i], max(1, left * loads[i] // pool), spare)
            holding[i] = holding[i] + addition
            spare = spare - addition
    return np.array(holding)


def noise(key, shape, width, most, shards=(), kind=jnp.bfloat16):
    result = width * jax.random.normal(key, shape, jnp.float32)
    if shards:
        result = result * steps_of(key, shape, shards, -0.22, 0.18)
    return jnp.clip(result, -most, most).astype(kind)


def setup_inputs(seed: int = 0) -> dict:
    seeds = jax.random.split(jax.random.key(seed), 11)
    depth = jnp.clip(jnp.exp(math.log(4.0) - 2.0794415 * jax.random.uniform(seeds[0], (NLAT, NLON), jnp.float32) ** steps_of(seeds[0], (NLAT, NLON), ((0, 4), (1, 8)), -0.2, 0.2)), 0.5, 4.0)
    friction = jnp.clip(jnp.exp(math.log(2.0) - 2.3025851 * jax.random.uniform(seeds[1], (NLAT, NLON), jnp.float32) ** steps_of(seeds[1], (NLAT, NLON), ((0, 4), (1, 8)), -0.2, 0.2)), 0.2, 2.0)
    ocean_mask = place_ends((jax.random.randint(seeds[2], (NLAT, NLON), 0, 4) < 3).astype(jnp.int32), jax.random.fold_in(seeds[2], 1), 0, 1)
    forcing = draw_forcing(jax.random.fold_in(seeds[10], 71), 0)
    tile_route_keys = jax.random.split(jax.random.fold_in(seeds[4], 1), NTILES // TILES_DEV)
    tile_route_turns = jax.random.permutation(jax.random.fold_in(seeds[4], 3), NTILES // TILES_DEV)
    tile_route = jax.vmap(lambda own, number: assign_block(jax.random.fold_in(seeds[4], 2), own, number, TILES_DEV, OWNERS, 1, CAP, 2))(tile_route_keys, tile_route_turns).reshape((NTILES, 1))
    tile_block = place_ends(jax.random.randint(seeds[5], (NTILES,), 0, BLOCKS_DEV), jax.random.fold_in(seeds[5], 1), 0, BLOCKS_DEV - 1).astype(jnp.int32)
    obs_cell = place_ends(jax.random.randint(seeds[6], (NTILES, OBS_TILE), 0, BLOCK), jax.random.fold_in(seeds[6], 1), 0, BLOCK - 1).astype(jnp.int32)
    obs_time = jnp.clip(720.0 * jax.random.uniform(seeds[7], (NTILES, OBS_TILE), jnp.float32) ** steps_of(seeds[7], (NTILES, OBS_TILE), ((0, 32),), -0.2, 0.2), 0.0, 720.0)
    obs_value = noise(seeds[8], (NTILES, OBS_TILE), 1.0, 6.0, ((0, 32),), jnp.float32)
    obs_weight = jnp.clip(jnp.exp(math.log(4.0) - 2.0794415 * jax.random.uniform(seeds[9], (NTILES, OBS_TILE), jnp.float32) ** steps_of(seeds[9], (NTILES, OBS_TILE), ((0, 32),), -0.2, 0.2)), 0.5, 4.0)
    return {"depth": depth, "friction": friction, "ocean_mask": ocean_mask, "forcing": forcing, "tile_route": tile_route, "tile_block": tile_block, "obs_cell": obs_cell, "obs_time": obs_time, "obs_value": obs_value, "obs_weight": obs_weight}


OMEGA_DEGREES = (28.984104, 30.0, 28.43973, 30.082137, 15.041069, 13.943036, 14.958931, 13.398661)

def angular_rates():
    return jnp.array(OMEGA_DEGREES, dtype=jnp.float32) * (math.pi / 180.0)

def harmonic(first, second):
    return 2.0 * first * second / (first + second)

def neighbours(vector):
    east = jnp.roll(vector, -1, axis=2)
    west = jnp.roll(vector, 1, axis=2)
    north = jnp.concatenate([vector[:, 1:], jnp.zeros_like(vector[:, :1])], axis=1)
    south = jnp.concatenate([jnp.zeros_like(vector[:, :1]), vector[:, :-1]], axis=1)
    return (east, west, north, south)

def reference(depth, friction, ocean_mask, forcing, tile_route, tile_block, obs_cell, obs_time, obs_value, obs_weight):
    wet = ocean_mask.astype(jnp.float32)
    depth_east = jnp.roll(depth, -1, axis=1)
    wet_east = jnp.roll(wet, -1, axis=1)
    east_coef = wet * wet_east * harmonic(depth, depth_east)
    depth_north = jnp.concatenate([depth[1:], depth[:1]], axis=0)
    wet_north = jnp.concatenate([wet[1:], jnp.zeros_like(wet[:1])], axis=0)
    north_coef = wet * wet_north * harmonic(depth, depth_north)
    west_coef = jnp.roll(east_coef, 1, axis=1)
    south_coef = jnp.concatenate([jnp.zeros_like(north_coef[:1]), north_coef[:-1]], axis=0)
    rates = angular_rates()
    stiff_half = 0.2 * (rates / rates[0]) ** 2
    stiffness = jnp.concatenate([stiff_half, stiff_half])
    tile_ids = jnp.arange(NTILES, dtype=jnp.int32)
    lat_device = tile_ids // TILES_DEV // N_LON
    per_row = CLON // BLOCK
    row_index = lat_device * CLAT + tile_block // per_row
    col_index = tile_route[:, 0][:, None] * CLON + (tile_block % per_row)[:, None] * BLOCK + obs_cell
    rows_flat = jnp.broadcast_to(row_index[:, None], obs_cell.shape).reshape(-1).astype(jnp.int32)
    cols_flat = col_index.reshape(-1).astype(jnp.int32)
    flat_times = obs_time.reshape(-1)
    angles = rates[:, None] * flat_times[None, :]
    basis = jnp.concatenate([jnp.cos(angles), jnp.sin(angles)], axis=0)
    weights = obs_weight.reshape(-1)

    def spread(contrib):
        return jnp.zeros((CHANNELS, NLAT, NLON), jnp.float32).at[:, rows_flat, cols_flat].add(contrib)

    def observe(vector):
        projected = lax.optimization_barrier(jnp.sum(basis * vector[:, rows_flat, cols_flat], axis=0))
        return spread(weights * projected * basis)
    rhs = wet * forcing + spread(weights * obs_value.reshape(-1) * basis)

    def apply_with(vector, diagonal, sides):
        east, west, north, south = sides
        return diagonal * vector + east_coef * (vector - east) + west_coef * (vector - west) + north_coef * (vector - north) + south_coef * (vector - south) + observe(vector)

    def operate(vector, diagonal):
        return apply_with(vector, diagonal, neighbours(vector))
    elevation = jnp.zeros((CHANNELS, NLAT, NLON), jnp.float32)
    residual = rhs
    for outer_turn in range(OUTER):
        sides = neighbours(elevation)
        east, west, north, south = sides
        east_flux = east_coef * (east - elevation)
        north_flux = north_coef * (north - elevation)
        speed_sq = lax.optimization_barrier(jnp.sum(east_flux * east_flux + north_flux * north_flux, axis=0))
        drag = friction * jnp.sqrt(1.0 + speed_sq / (2 * NC))
        diagonal = wet * (stiffness[:, None, None] + drag) + (1.0 - wet)
        residual = rhs - apply_with(elevation, diagonal, sides)
        direction = residual
        norm_now = jnp.sum(residual * residual)
        for turn in range(ITERS):
            image = operate(direction, diagonal)
            step_size = norm_now / jnp.sum(direction * image)
            elevation = elevation + step_size * direction
            residual = residual - step_size * image
            norm_next = jnp.sum(residual * residual)
            direction = residual + norm_next / norm_now * direction
            norm_now = norm_next
    return (elevation, residual)
```

```python
import functools
import math

import jax
import jax.numpy as jnp
import numpy as np
from jax import lax
from jax.experimental import pallas as pl
from jax.experimental.pallas import tpu as pltpu
from jax.sharding import PartitionSpec as P

BLOCK = 128
CAP = 2
ITERS = 3
OUTER = 2
STEPS = ITERS * OUTER
MESH = pl.DeviceIdType.MESH
OMEGA_DEGREES = (28.984104, 30.0, 28.43973, 30.082137, 15.041069, 13.943036, 14.958931, 13.398661)
RATES = np.array(OMEGA_DEGREES, np.float32) * np.float32(math.pi / 180.0)
STIFF = np.float32(0.2) * (RATES / RATES[0]) ** 2


def sin_cos(angle):
    turn = jnp.floor(angle * (2.0 / math.pi) + 0.5)
    x = ((angle - turn * 1.5703125) - turn * 4.837512969970703125e-4) - turn * 7.54978995489188216e-8
    z = x * x
    s = ((-1.9515295891e-4 * z + 8.3321608736e-3) * z - 1.6666654611e-1) * z * x + x
    c = ((2.443315711809948e-5 * z - 1.388731625493765e-3) * z + 4.166664568298827e-2) * z * z - 0.5 * z + 1.0
    quarter = turn.astype(jnp.int32)
    odd = (quarter & 1) == 1
    sine = jnp.where(odd, c, s)
    cosine = jnp.where(odd, s, c)
    sine = jnp.where((quarter & 2) == 2, -sine, sine)
    cosine = jnp.where(((quarter + 1) & 2) == 2, -cosine, cosine)
    return sine, cosine


def kernel(
    nlat, nlon,
    route, tblk, *refs,
):
    sources, refs = refs[:8], refs[8:]
    landed = refs[-9:-1]
    work(nlat, nlon, sources, refs[-1], route, tblk, *landed, *refs[:-9])


def work(
    nlat, nlon, sources, load,
    route, tblk, depth, fric, mask, forc, ocell, otime, oval, oweight,
    x_out, r_out,
    dw, dwn, dws, dwe, dww, wetb, wetfric, coef, diag,
    payf, payi, outf, outi, inf, ini, plan, splan, mats, oslot,
    d, db, x, r, q, hd, hx, hr, hq, pk, sum_a, part_row, ready,
    hs, hrv, as_, ar, os_, orv, ds_, dr, loc,
):
    rows, cols = depth.shape
    nblk = cols // BLOCK
    slots = nlon * CAP
    tiles = otime.shape[0]
    me_lat = lax.axis_index("lat")
    me_lon = lax.axis_index("lon")
    north, south = lax.rem(me_lat + 1, nlat), lax.rem(me_lat + nlat - 1, nlat)
    east, west = lax.rem(me_lon + 1, nlon), lax.rem(me_lon + nlon - 1, nlon)

    loads = [
        pltpu.make_async_copy(src, dst, load.at[k])
        for k, (src, dst) in enumerate(zip(sources, (depth, fric, mask, forc, ocell, otime, oval, oweight)))
    ]
    for c in loads:
        c.start()
    barrier = pltpu.get_barrier_semaphore()
    for k in range(1, nlon):
        pl.semaphore_signal(barrier, inc=1, device_id={"lon": lax.rem(me_lon + k, nlon)}, device_id_type=MESH)
    for k in range(1, nlat):
        pl.semaphore_signal(barrier, inc=1, device_id={"lat": lax.rem(me_lat + k, nlat)}, device_id_type=MESH)

    def remote(src, dst, send, recv, where):
        return pltpu.make_async_remote_copy(
            src_ref=src, dst_ref=dst, send_sem=send, recv_sem=recv, device_id=where, device_id_type=MESH
        )

    lane = lax.broadcasted_iota(jnp.int32, (1, BLOCK), 1)
    lane8 = lax.broadcasted_iota(jnp.int32, (8, BLOCK), 1)
    sub8 = lax.broadcasted_iota(jnp.int32, (8, BLOCK), 0)

    for c in loads:
        c.wait()
    wet = mask[...].astype(jnp.float32)
    dw[...] = depth[...] * wet

    for t in range(tiles):
        payf[t, 0:1] = otime[t : t + 1]
        payf[t, 1:2] = oval[t : t + 1]
        payf[t, 2:3] = oweight[t : t + 1]
        payf[t, 3:4] = jnp.zeros((1, BLOCK), jnp.float32)
        payi[t] = jnp.broadcast_to(ocell[t : t + 1] + tblk[t] * BLOCK, (8, BLOCK))
    payf[tiles] = jnp.zeros((8, BLOCK), jnp.float32)
    payi[tiles] = jnp.zeros((8, BLOCK), jnp.int32)

    def pick(p, carry):
        first, second = jnp.int32(tiles), jnp.int32(tiles)
        for t in reversed(range(tiles)):
            hit = route[t] == p
            second = jnp.where(hit, first, second)
            first = jnp.where(hit, jnp.int32(t), first)
        one, two = payf[first], payf[second]
        outf[p] = jnp.concatenate([one[0:4], two[0:4]], axis=0)
        outi[p] = jnp.where(sub8 == 0, payi[first], payi[second])
        return carry

    lax.fori_loop(0, nlon, pick, 0)
    pl.semaphore_wait(barrier, nlon + nlat - 2)
    for k in range(1, nlat):
        pl.semaphore_signal(ready, inc=1, device_id={"lat": lax.rem(me_lat + k, nlat)}, device_id_type=MESH)

    first_copies = [
        remote(dw, dws, ds_.at[0], dr.at[0], {"lat": north}),
        remote(dw, dwn, ds_.at[1], dr.at[1], {"lat": south}),
        remote(dw.at[:, pl.ds(0, BLOCK)], dwe, ds_.at[2], dr.at[2], {"lon": west}),
        remote(dw.at[:, pl.ds(cols - BLOCK, BLOCK)], dww, ds_.at[3], dr.at[3], {"lon": east}),
    ]

    def obs_copy(k):
        peer = lax.rem(me_lon + k, nlon)
        return [
            remote(outf.at[peer], inf.at[me_lon], os_.at[0, peer], orv.at[0, me_lon], {"lon": peer}),
            remote(outi.at[peer], ini.at[me_lon], os_.at[1, peer], orv.at[1, me_lon], {"lon": peer}),
        ]

    def obs_wait(k):
        peer = lax.rem(me_lon + k, nlon)
        remote(outf.at[peer], inf.at[peer], os_.at[0, peer], orv.at[0, peer], {"lon": peer}).wait_recv()
        remote(outi.at[peer], ini.at[peer], os_.at[1, peer], orv.at[1, peer], {"lon": peer}).wait_recv()

    obs_sends = [c for k in range(1, nlon) for c in obs_copy(k)]
    for c in obs_sends:
        c.start()
    for c in first_copies:
        c.start()
    inf[me_lon] = outf[me_lon]
    ini[me_lon] = outi[me_lon]

    for cb in range(nblk):
        at = pl.ds(cb * BLOCK, BLOCK)
        for h in range(2):
            r[pl.ds(1, rows), h, :, at] = jnp.swapaxes(forc[h, :, :, at], 0, 1)
    x[...] = jnp.zeros_like(x)
    hx[...] = jnp.zeros_like(hx)
    oslot[slots] = jnp.zeros((2, 8, BLOCK), jnp.float32)

    for c in first_copies:
        c.wait_recv()
    a = dw[...]
    colid = lax.broadcasted_iota(jnp.int32, (rows, cols), 1)
    rowid = lax.broadcasted_iota(jnp.int32, (rows, cols), 0)
    keep_n = (me_lat < nlat - 1).astype(jnp.float32)
    keep_s = (me_lat > 0).astype(jnp.float32)

    def harmonic(first, second):
        return 2.0 * first * second / jnp.maximum(first + second, 0.5)

    side = harmonic(a, jnp.where(colid == cols - 1, dwe[:, 0:1], pltpu.roll(a, cols - 1, 1)))
    total = side
    for row in range(rows):
        coef[0, row] = jnp.broadcast_to(side[row : row + 1], (8, cols))
    side = harmonic(a, jnp.where(colid == 0, dww[:, BLOCK - 1 : BLOCK], pltpu.roll(a, 1, 1)))
    total = total + side
    for row in range(rows):
        coef[1, row] = jnp.broadcast_to(side[row : row + 1], (8, cols))
    side = harmonic(a, jnp.where(rowid == rows - 1, dwn[0:1, :] * keep_n, pltpu.roll(a, rows - 1, 0)))
    total = total + side
    for row in range(rows):
        coef[2, row] = jnp.broadcast_to(side[row : row + 1], (8, cols))
    side = harmonic(a, jnp.where(rowid == 0, dws[rows - 1 : rows, :] * keep_s, pltpu.roll(a, 1, 0)))
    total = total + side
    for row in range(rows):
        coef[3, row] = jnp.broadcast_to(side[row : row + 1], (8, cols))
    stiff = jnp.zeros((8, 1), jnp.float32)
    rate = jnp.zeros((8, BLOCK), jnp.float32)
    sub1 = lax.broadcasted_iota(jnp.int32, (8, 1), 0)
    for c in range(8):
        stiff = jnp.where(sub1 == c, float(STIFF[c]), stiff)
        rate = jnp.where(sub8 == c, float(RATES[c]), rate)
    drag = fric[...]
    total = total + wet * drag + (1.0 - wet)
    for row in range(rows):
        wide = jnp.broadcast_to(wet[row : row + 1], (8, cols))
        wetb[row] = wide
        wetfric[row] = wide * jnp.broadcast_to(drag[row : row + 1], (8, cols))
        diag[row] = wide * stiff + jnp.broadcast_to(total[row : row + 1], (8, cols))

    for k in range(1, nlon):
        obs_wait(k)
    rep = jnp.full((1, BLOCK), slots, jnp.int32)
    homes = jnp.full((1, BLOCK), -1, jnp.int32)
    for s in reversed(range(slots)):
        home = ini[s // CAP, pl.ds(s % CAP, 1), :] >> 7
        rep = jnp.where(home == lane, s, rep)
        homes = jnp.where(lane == s, home, homes)
    chain = jnp.full((1, BLOCK), slots, jnp.int32)
    for s in reversed(range(slots)):
        home = ini[s // CAP, pl.ds(s % CAP, 1), :] >> 7
        chain = jnp.where((home == homes) & (lane < s), s, chain)
    plan[...] = jnp.where(
        sub8 == 0,
        jnp.broadcast_to(homes, (8, BLOCK)),
        jnp.where(sub8 == 1, jnp.broadcast_to(chain, (8, BLOCK)), jnp.broadcast_to(rep, (8, BLOCK))),
    )
    to_scalars = pltpu.make_async_copy(plan, splan, loc.at[0])
    to_scalars.start()

    cells = lax.broadcasted_iota(jnp.int32, (BLOCK, BLOCK), 0)

    def build(o, carry):
        for k in range(CAP):
            times = inf[o, pl.ds(4 * k, 1), :]
            value = inf[o, pl.ds(4 * k + 1, 1), :]
            weight = inf[o, pl.ds(4 * k + 2, 1), :]
            cell = ini[o, pl.ds(k, 1), :] & (BLOCK - 1)
            sine, cosine = sin_cos(rate * times)
            basis = (cosine, sine)
            weighted = (weight * cosine, weight * sine)
            parts = []
            for h in range(2):
                for c in range(8):
                    one = weighted[h][c : c + 1]
                    parts.append(one * basis[0])
                    parts.append(one * basis[1])
            parts.append(weighted[0] * value)
            parts.append(weighted[1] * value)
            terms = jnp.concatenate(parts, axis=0)
            high = terms.astype(jnp.bfloat16)
            low = (terms - high.astype(jnp.float32)).astype(jnp.bfloat16)
            hot = (cells == cell).astype(jnp.float32).astype(jnp.bfloat16)
            mats[o * CAP + k] = lax.dot_general(
                jnp.concatenate([high, low], axis=1),
                jnp.concatenate([hot, hot], axis=1),
                (((1,), (1,)), ((), ())),
                preferred_element_type=jnp.float32,
            )
        return carry

    lax.fori_loop(0, nlon, build, 0)
    to_scalars.wait()

    def first_slots(i, carry):
        s = slots - 1 - i
        after = oslot[splan[1, s]]
        oslot[s] = mats[s, 256:272, :].reshape(2, 8, BLOCK) + after
        return carry

    lax.fori_loop(0, slots, first_slots, 0)

    def pack(row, col, value, packed):
        shift = row if col == 0 else row + 1
        moved = pltpu.roll(value, shift, 2)
        return jnp.where(lane8 == row, moved, packed)

    zero = jnp.zeros((2, 8, BLOCK), jnp.float32)

    def start_rhs(row, carry):
        lo, hi = carry
        for cb in range(nblk):
            at = pl.ds(cb * BLOCK, BLOCK)
            v = wetb[row, :, at] * r[row + 1, :, :, at] + oslot[splan[2, row * nblk + cb]]
            r[row + 1, :, :, at] = v
            q[STEPS, row + 1, :, :, at] = v
            db[(row + 1) * nblk + cb] = v
            if cb == 0:
                lo = pack(row, 0, v, lo)
            if cb == nblk - 1:
                hi = pack(row, 1, v, hi)
        return lo, hi

    lo, hi = lax.fori_loop(0, rows, start_rhs, (zero, zero))
    pk[STEPS, 0] = lo
    pk[STEPS, 1] = hi

    def halo(i):
        return [
            remote(q.at[i, 1], q.at[i, rows + 1], hs.at[i, 0], hrv.at[i, 0], {"lat": south}),
            remote(q.at[i, rows], q.at[i, 0], hs.at[i, 1], hrv.at[i, 1], {"lat": north}),
            remote(pk.at[i, 0], hq.at[i, 1], hs.at[i, 2], hrv.at[i, 2], {"lon": west}),
            remote(pk.at[i, 1], hq.at[i, 0], hs.at[i, 3], hrv.at[i, 3], {"lon": east}),
        ]

    def begin(i):
        for c in halo(i):
            c.start()
        d[pl.ds(1, rows)] = r[pl.ds(1, rows)]
        for c in halo(i):
            c.wait()
        for edge in (0, rows + 1):
            d[edge] = q[i, edge]
            r[edge] = q[i, edge]
        hd[...] = hq[i]
        hr[...] = hq[i]

    me = me_lat * nlon + me_lon
    count = nlat * nlon

    def sum_copy(i, k):
        peer = lax.rem(me + k, count)
        where = {"lat": peer // nlon, "lon": lax.rem(peer, nlon)}
        return remote(part_row.at[i], sum_a.at[i, pl.ds(me, 1)], as_.at[i], ar.at[i], where)

    def sum_wait(i):
        whole = sum_a.at[i, pl.ds(0, count - 1)]
        return remote(whole, whole, as_.at[i], ar.at[i], {"lat": south})

    def all_sum(i, part):
        part = part + pltpu.roll(part, 64, 1)
        part = part + pltpu.roll(part, 32, 1)
        row = jnp.sum(jnp.where(lane8 >> 5 == sub8, part, 0.0), axis=0, keepdims=True)
        part_row[i] = row
        sum_a[i, pl.ds(me, 1)] = row

        def send(k, carry):
            sum_copy(i, k).start()
            return carry

        lax.fori_loop(1, count, send, 0, unroll=True)
        sum_wait(i).wait_recv()
        total = jnp.sum(sum_a[i], axis=0, keepdims=True)
        return jnp.sum(jnp.where(lane8 >> 5 == sub8, total, 0.0), axis=1, keepdims=True)

    def sides(ref, halos, row):
        v = [ref[row + 1, :, :, pl.ds(cb * BLOCK, BLOCK)] for cb in range(nblk)]
        to_west = [pltpu.roll(b, BLOCK - 1, 2) for b in v]
        to_west.append(pltpu.roll(halos[1], BLOCK - 1 - row, 2))
        to_east = [pltpu.roll(halos[0], BLOCK - row, 2)] + [pltpu.roll(b, 1, 2) for b in v]
        e = [jnp.where(lane8 == BLOCK - 1, to_west[cb + 1], to_west[cb]) for cb in range(nblk)]
        w = [jnp.where(lane8 == 0, to_east[cb], to_east[cb + 1]) for cb in range(nblk)]
        return v, e, w

    def step(i, carry):
        def slot(j, carry):
            s = slots - 1 - j
            after = oslot[splan[1, s]]
            v = db[splan[0, s] + nblk]
            acc = [after, zero]
            for c in range(16):
                m = mats[s, 16 * c : 16 * c + 16, :].reshape(2, 8, BLOCK)
                acc[c % 2] = acc[c % 2] + m * v[c // 8, c % 8 : c % 8 + 1, :]
            oslot[s] = acc[0] + acc[1]
            return carry

        lax.fori_loop(0, slots, slot, 0)

        def line(row, carry):
            lo, hi, rr, rq, dq, qq = carry
            v, e, w = sides(d, hd, row)
            for cb in range(nblk):
                at = pl.ds(cb * BLOCK, BLOCK)
                image = (
                    diag[row, :, at] * v[cb]
                    - coef[0, row, :, at] * e[cb]
                    - coef[1, row, :, at] * w[cb]
                    - coef[2, row, :, at] * d[row + 2, :, :, at]
                    - coef[3, row, :, at] * d[row, :, :, at]
                    + oslot[splan[2, row * nblk + cb]]
                )
                q[i, row + 1, :, :, at] = image
                res = r[row + 1, :, :, at]
                rr = rr + res * res
                rq = rq + res * image
                dq = dq + v[cb] * image
                qq = qq + image * image
                if cb == 0:
                    lo = pack(row, 0, image, lo)
                if cb == nblk - 1:
                    hi = pack(row, 1, image, hi)
            return lo, hi, rr, rq, dq, qq

        lo, hi, *sums = lax.fori_loop(0, rows, line, (zero,) * 6)
        pk[i, 0] = lo
        pk[i, 1] = hi
        part = jnp.zeros((8, BLOCK), jnp.float32)
        for k, s in enumerate(sums):
            part = jnp.where(sub8 == k, jnp.sum(s[0] + s[1], axis=0, keepdims=True), part)
        more = lax.rem(i, ITERS) < ITERS - 1

        @pl.when(more)
        def _():
            for c in halo(i):
                c.start()

        whole = all_sum(i, part)
        rr, rq, dq, qq = (whole[k : k + 1] for k in range(4))
        size = rr / dq
        beta = (rr - 2.0 * size * rq + size * size * qq) / rr

        @pl.when(more)
        def _():
            for c in halo(i):
                c.wait()

        def update(row, carry):
            for cb in range(nblk):
                at = pl.ds(cb * BLOCK, BLOCK)
                old = d[row, :, :, at]
                x[row, :, :, at] = x[row, :, :, at] + size * old
                res = r[row, :, :, at] - size * q[i, row, :, :, at]
                r[row, :, :, at] = res
                new = res + beta * old
                d[row, :, :, at] = new
                db[row * nblk + cb] = new
            return carry

        lax.fori_loop(0, rows + 2, update, 0)
        hx[...] = hx[...] + size * hd[...]
        hr[...] = hr[...] - size * hq[i]
        hd[...] = hr[...] + beta * hd[...]
        sum_wait(i).wait_send()
        return carry

    begin(STEPS)
    pl.semaphore_wait(ready, nlat - 1)
    for c in obs_sends + first_copies:
        c.wait_send()
    lax.fori_loop(0, ITERS, step, 0)

    def friction(row, carry):
        lo, hi = carry
        v, e, _ = sides(x, hx, row)
        for cb in range(nblk):
            at = pl.ds(cb * BLOCK, BLOCK)
            flux_e = coef[0, row, :, at] * (e[cb] - v[cb])
            flux_n = coef[2, row, :, at] * (x[row + 2, :, :, at] - v[cb])
            square = flux_e * flux_e + flux_n * flux_n
            speed = jnp.sum(square[0] + square[1], axis=0, keepdims=True)
            extra = wetfric[row, :, at] * (jnp.sqrt(1.0 + speed / 16.0) - 1.0)
            diag[row, :, at] = diag[row, :, at] + extra
            res = r[row + 1, :, :, at] - extra * v[cb]
            r[row + 1, :, :, at] = res
            q[STEPS + 1, row + 1, :, :, at] = res
            db[(row + 1) * nblk + cb] = res
            if cb == 0:
                lo = pack(row, 0, res, lo)
            if cb == nblk - 1:
                hi = pack(row, 1, res, hi)
        return lo, hi

    lo, hi = lax.fori_loop(0, rows, friction, (zero, zero))
    pk[STEPS + 1, 0] = lo
    pk[STEPS + 1, 1] = hi
    begin(STEPS + 1)
    lax.fori_loop(ITERS, STEPS, step, 0)

    for cb in range(nblk):
        at = pl.ds(cb * BLOCK, BLOCK)
        for h in range(2):
            x_out[h, :, :, at] = jnp.swapaxes(x[pl.ds(1, rows), h, :, at], 0, 1)
            r_out[h, :, :, at] = jnp.swapaxes(r[pl.ds(1, rows), h, :, at], 0, 1)


def shards(nlat, nlon, depth, friction, ocean_mask, forcing, tile_route, tile_block, obs_cell, obs_time, obs_value, obs_weight):
    channels, rows, cols = forcing.shape
    slots = nlon * CAP
    nblk, tiles = cols // BLOCK, obs_time.shape[0]
    f32, i32 = jnp.float32, jnp.int32
    vmem = pl.BlockSpec(memory_space=pltpu.VMEM)
    smem = pl.BlockSpec(memory_space=pltpu.SMEM)
    field = (rows + 2, 2, 8, cols)
    dma = pltpu.SemaphoreType.DMA
    scratch = [
        pltpu.VMEM((rows, cols), f32),
        pltpu.VMEM((rows, cols), f32),
        pltpu.VMEM((rows, cols), f32),
        pltpu.VMEM((rows, BLOCK), f32),
        pltpu.VMEM((rows, BLOCK), f32),
        pltpu.VMEM((rows, 8, cols), f32),
        pltpu.VMEM((rows, 8, cols), f32),
        pltpu.VMEM((4, rows, 8, cols), f32),
        pltpu.VMEM((rows, 8, cols), f32),
        pltpu.VMEM((tiles + 1, 8, BLOCK), f32),
        pltpu.VMEM((tiles + 1, 8, BLOCK), i32),
        pltpu.VMEM((nlon, 8, BLOCK), f32),
        pltpu.VMEM((nlon, 8, BLOCK), i32),
        pltpu.VMEM((nlon, 8, BLOCK), f32),
        pltpu.VMEM((nlon, 8, BLOCK), i32),
        pltpu.VMEM((8, BLOCK), i32),
        pltpu.SMEM((8, BLOCK), i32),
        pltpu.VMEM((slots, 272, BLOCK), f32),
        pltpu.VMEM((slots + 1, 2, 8, BLOCK), f32),
        pltpu.VMEM(field, f32),
        pltpu.VMEM(((rows + 2) * nblk, 2, 8, BLOCK), f32),
        pltpu.VMEM(field, f32),
        pltpu.VMEM(field, f32),
        pltpu.VMEM((STEPS + 2,) + field, f32),
        pltpu.VMEM((2, 2, 8, BLOCK), f32),
        pltpu.VMEM((2, 2, 8, BLOCK), f32),
        pltpu.VMEM((2, 2, 8, BLOCK), f32),
        pltpu.VMEM((STEPS + 2, 2, 2, 8, BLOCK), f32),
        pltpu.VMEM((STEPS + 2, 2, 2, 8, BLOCK), f32),
        pltpu.VMEM((STEPS, nlat * nlon, BLOCK), f32),
        pltpu.VMEM((STEPS, 1, BLOCK), f32),
        pltpu.SemaphoreType.REGULAR,
        dma((STEPS + 2, 4)),
        dma((STEPS + 2, 4)),
        dma((STEPS,)),
        dma((STEPS,)),
        dma((2, nlon)),
        dma((2, nlon)),
        dma((4,)),
        dma((4,)),
        dma((1,)),
        pltpu.VMEM((rows, cols), f32),
        pltpu.VMEM((rows, cols), f32),
        pltpu.VMEM((rows, cols), i32),
        pltpu.VMEM((2, channels // 2, rows, cols), f32),
        pltpu.VMEM((tiles, BLOCK), i32),
        pltpu.VMEM((tiles, BLOCK), f32),
        pltpu.VMEM((tiles, BLOCK), f32),
        pltpu.VMEM((tiles, BLOCK), f32),
        dma((8,)),
    ]
    shape = jax.ShapeDtypeStruct((2, channels // 2, rows, cols), f32)
    x, r = pl.pallas_call(
        functools.partial(kernel, nlat, nlon),
        out_shape=(shape, shape),
        in_specs=[smem, smem] + [pl.BlockSpec(memory_space=pltpu.HBM)] * 8,
        out_specs=(vmem, vmem),
        scratch_shapes=scratch,
        compiler_params=pltpu.CompilerParams(
            collective_id=0, has_side_effects=True, vmem_limit_bytes=62 * 2**20
        ),
    )(
        tile_route.reshape(-1), tile_block, depth, friction, ocean_mask, forcing.reshape(2, channels // 2, rows, cols),
        obs_cell, obs_time, obs_value, obs_weight,
    )
    return x.reshape(forcing.shape), r.reshape(forcing.shape)


def solution(mesh):
    tile = P(("lat", "lon"), None)
    grid = P("lat", "lon")
    in_specs = (grid, grid, grid, P(None, "lat", "lon"), tile, P(("lat", "lon")), tile, tile, tile, tile)
    out_specs = (P(None, "lat", "lon"), P(None, "lat", "lon"))
    body = functools.partial(shards, mesh.shape["lat"], mesh.shape["lon"])
    return jax.shard_map(body, mesh=mesh, in_specs=in_specs, out_specs=out_specs, check_vma=False)
```

```python
import functools
import math

import jax
import jax.numpy as jnp
import numpy as np
from jax import lax
from jax.experimental import pallas as pl
from jax.experimental.pallas import tpu as pltpu
from jax.sharding import PartitionSpec as P

BLOCK = 128
CAP = 2
ITERS = 3
OUTER = 2
SUMS = ITERS * OUTER
MESH = pl.DeviceIdType.MESH
OMEGA_DEGREES = (28.984104, 30.0, 28.43973, 30.082137, 15.041069, 13.943036, 14.958931, 13.398661)
RATES = np.array(OMEGA_DEGREES, np.float32) * np.float32(math.pi / 180.0)
STIFF = np.float32(0.2) * (RATES / RATES[0]) ** 2


def sin_cos(angle):
    turn = jnp.floor(angle * (2.0 / math.pi) + 0.5)
    x = ((angle - turn * 1.5703125) - turn * 4.837512969970703125e-4) - turn * 7.54978995489188216e-8
    z = x * x
    s = ((-1.9515295891e-4 * z + 8.3321608736e-3) * z - 1.6666654611e-1) * z * x + x
    c = ((2.443315711809948e-5 * z - 1.388731625493765e-3) * z + 4.166664568298827e-2) * z * z - 0.5 * z + 1.0
    quarter = turn.astype(jnp.int32)
    odd = (quarter & 1) == 1
    sine = jnp.where(odd, c, s)
    cosine = jnp.where(odd, s, c)
    sine = jnp.where((quarter & 2) == 2, -sine, sine)
    cosine = jnp.where(((quarter + 1) & 2) == 2, -cosine, cosine)
    return sine, cosine


def kernel(
    nlat, nlon,
    route_in, tblk_in, depth_in, fric_in, mask_in, forc_in, ocell_in, otime_in, oval_in, oweight_in,
    x_out, p_out, r_out, q_out, size_out,
    route, tblk, depth, fric, mask, forc, ocell, otime, oval, oweight,
    dw, dwn, dws, dwe, dww, wetfric, coef, diag,
    pay, payi, outf, outi, inf, ini, plan, splan, waves, mats, oslot,
    field, seen, r1, p1, q1, z1, r2, p2, q2, x, turned,
    pk, hq, hq1, hx, hp, sum_a, part_row, ready,
    load, hs, hrv, as_, ar, os_, orv, ds_, dr, loc, out_sem,
):
    rows, cols = depth.shape
    nblk = cols // BLOCK
    slots = nlon * CAP
    tiles = otime.shape[0]
    me_lat = lax.axis_index("lat")
    me_lon = lax.axis_index("lon")
    north, south = lax.rem(me_lat + 1, nlat), lax.rem(me_lat + nlat - 1, nlat)
    east, west = lax.rem(me_lon + 1, nlon), lax.rem(me_lon + nlon - 1, nlon)
    me = me_lat * nlon + me_lon
    count = nlat * nlon

    barrier = pltpu.get_barrier_semaphore()
    for k in range(1, nlon):
        pl.semaphore_signal(barrier, inc=1, device_id={"lon": lax.rem(me_lon + k, nlon)}, device_id_type=MESH)
    for k in range(1, nlat):
        pl.semaphore_signal(barrier, inc=1, device_id={"lat": lax.rem(me_lat + k, nlat)}, device_id_type=MESH)
    pairs = [
        (route_in, route), (tblk_in, tblk), (ocell_in, ocell), (otime_in, otime), (oval_in, oval),
        (oweight_in, oweight), (depth_in, depth), (mask_in, mask), (fric_in, fric), (forc_in, forc),
    ]
    loads = [pltpu.make_async_copy(src, dst, load.at[k]) for k, (src, dst) in enumerate(pairs)]
    for c in loads:
        c.start()

    def remote(src, dst, send, recv, where):
        return pltpu.make_async_remote_copy(
            src_ref=src, dst_ref=dst, send_sem=send, recv_sem=recv, device_id=where, device_id_type=MESH
        )

    lane = lax.broadcasted_iota(jnp.int32, (1, BLOCK), 1)
    lane8 = lax.broadcasted_iota(jnp.int32, (8, BLOCK), 1)
    sub8 = lax.broadcasted_iota(jnp.int32, (8, BLOCK), 0)
    zero = jnp.zeros((2, 8, BLOCK), jnp.float32)

    for c in loads[:8]:
        c.wait()
    wet = mask[...].astype(jnp.float32)
    dw[...] = depth[...] * wet

    for t in range(tiles):
        pay[t] = jnp.concatenate([otime[t : t + 1], oval[t : t + 1], oweight[t : t + 1], oval[t : t + 1]] * 2, axis=0)
        payi[t] = jnp.broadcast_to(ocell[t : t + 1] + tblk[t] * BLOCK, (8, BLOCK))
    pay[tiles] = jnp.zeros((8, BLOCK), jnp.float32)
    payi[tiles] = jnp.zeros((8, BLOCK), jnp.int32)

    def pick(p, carry):
        first, second = jnp.int32(tiles), jnp.int32(tiles)
        for t in reversed(range(tiles)):
            hit = route[t] == p
            second = jnp.where(hit, first, second)
            first = jnp.where(hit, jnp.int32(t), first)
        outf[p] = jnp.where(sub8 < 4, pay[first], pay[second])
        outi[p] = jnp.where(sub8 == 0, payi[first], payi[second])
        return carry

    lax.fori_loop(0, nlon, pick, 0)
    pl.semaphore_wait(barrier, nlon + nlat - 2)

    def obs_copy(k):
        peer = lax.rem(me_lon + k, nlon)
        return [
            remote(outf.at[peer], inf.at[me_lon], os_.at[0, peer], orv.at[0, me_lon], {"lon": peer}),
            remote(outi.at[peer], ini.at[me_lon], os_.at[1, peer], orv.at[1, me_lon], {"lon": peer}),
        ]

    def obs_wait(k):
        peer = lax.rem(me_lon + k, nlon)
        remote(outf.at[peer], inf.at[peer], os_.at[0, peer], orv.at[0, peer], {"lon": peer}).wait_recv()
        remote(outi.at[peer], ini.at[peer], os_.at[1, peer], orv.at[1, peer], {"lon": peer}).wait_recv()

    obs_sends = [c for k in range(1, nlon) for c in obs_copy(k)]
    for c in obs_sends:
        c.start()
    first_copies = [
        remote(dw.at[:, pl.ds(0, BLOCK)], dwe, ds_.at[2], dr.at[2], {"lon": west}),
        remote(dw.at[:, pl.ds(cols - BLOCK, BLOCK)], dww, ds_.at[3], dr.at[3], {"lon": east}),
        remote(dw, dws, ds_.at[0], dr.at[0], {"lat": north}),
        remote(dw, dwn, ds_.at[1], dr.at[1], {"lat": south}),
    ]
    for c in first_copies:
        c.start()
    for k in range(1, nlat):
        pl.semaphore_signal(ready, inc=1, device_id={"lat": lax.rem(me_lat + k, nlat)}, device_id_type=MESH)
    inf[me_lon] = outf[me_lon]
    ini[me_lon] = outi[me_lon]
    for c in loads[8:]:
        c.wait()

    for cb in range(nblk):
        at = pl.ds(cb * BLOCK, BLOCK)
        for h in range(2):
            wetted = forc[h, :, :, at] * wet[None, :, cb * BLOCK : cb * BLOCK + BLOCK]
            field[0, pl.ds(1, rows), cb, h] = jnp.swapaxes(wetted, 0, 1)
    oslot[slots] = zero
    mats[slots] = jnp.zeros((256, BLOCK), jnp.float32)
    stiff = jnp.zeros((8, 1), jnp.float32)
    rate = jnp.zeros((8, BLOCK), jnp.float32)
    sub1 = lax.broadcasted_iota(jnp.int32, (8, 1), 0)
    for c in range(8):
        stiff = jnp.where(sub1 == c, float(STIFF[c]), stiff)
        rate = jnp.where(sub8 == c, float(RATES[c]), rate)
    cells = lax.broadcasted_iota(jnp.int32, (BLOCK, BLOCK), 0)

    for k in range(1, nlon):
        obs_wait(k)

    def where_is(s):
        return ini[s // CAP, pl.ds(s % CAP, 1), :]

    rep = jnp.full((1, BLOCK), slots, jnp.int32)
    homes = jnp.full((1, BLOCK), -1, jnp.int32)
    for s in reversed(range(slots)):
        home = where_is(s) >> 7
        rep = jnp.where(home == lane, s, rep)
        homes = jnp.where(lane == s, home, homes)
    chain = jnp.full((1, BLOCK), slots, jnp.int32)
    for s in reversed(range(slots)):
        home = where_is(s) >> 7
        chain = jnp.where((home == homes) & (lane < s), s, chain)
    plan[...] = jnp.where(
        sub8 == 0,
        jnp.broadcast_to(homes, (8, BLOCK)),
        jnp.where(sub8 == 1, jnp.broadcast_to(chain, (8, BLOCK)), jnp.broadcast_to(rep, (8, BLOCK))),
    )
    to_scalars = pltpu.make_async_copy(plan, splan, loc.at[0])
    to_scalars.start()

    def onto_cells(o, k, terms):
        cell = ini[o, pl.ds(k, 1), :] & (BLOCK - 1)
        high = terms.astype(jnp.bfloat16)
        low = (terms - high.astype(jnp.float32)).astype(jnp.bfloat16)
        hot = (cells == cell).astype(jnp.float32).astype(jnp.bfloat16)
        return lax.dot_general(
            jnp.concatenate([high, low], axis=1),
            jnp.concatenate([hot, hot], axis=1),
            (((1,), (1,)), ((), ())),
            preferred_element_type=jnp.float32,
        )

    def values(o, carry):
        for k in range(CAP):
            times = inf[o, pl.ds(4 * k, 1), :]
            scaled = inf[o, pl.ds(4 * k + 2, 1), :] * inf[o, pl.ds(4 * k + 1, 1), :]
            sine, cosine = sin_cos(rate * times)
            waves[o * CAP + k, 0] = cosine
            waves[o * CAP + k, 1] = sine
            terms = jnp.concatenate([cosine * scaled, sine * scaled], axis=0)
            oslot[o * CAP + k] = onto_cells(o, k, terms).reshape(2, 8, BLOCK)
        return carry

    lax.fori_loop(0, nlon, values, 0, unroll=4)
    to_scalars.wait()

    def join_values(i, carry):
        s = slots - 1 - i
        oslot[s] = oslot[s] + oslot[splan[1, s]]
        return carry

    lax.fori_loop(0, slots, join_values, 0)

    def pack(row, col, value, packed):
        shift = row if col == 0 else row + 1
        moved = pltpu.roll(value, shift, 2)
        return jnp.where(lane8 == row, moved, packed)

    def pack_ends(row, first, last, carry):
        return pack(row, 0, first, carry[0]), pack(row, 1, last, carry[1])

    def keep_ends(k, ends):
        pk[k, 0] = ends[0]
        pk[k, 1] = ends[1]

    def start_rhs(row, ends):
        v = []
        for cb in range(nblk):
            v.append(field[0, row + 1, cb] + oslot[splan[2, row * nblk + cb]])
            field[0, row + 1, cb] = v[cb]
            seen[row * nblk + cb] = v[cb]
        return pack_ends(row, v[0], v[-1], ends)

    keep_ends(0, lax.fori_loop(0, rows, start_rhs, (zero, zero)))

    def halo(k):
        return [
            remote(pk.at[k, 0], hq.at[k, 1], hs.at[k, 2], hrv.at[k, 2], {"lon": west}),
            remote(pk.at[k, 1], hq.at[k, 0], hs.at[k, 3], hrv.at[k, 3], {"lon": east}),
            remote(field.at[k, 1], field.at[k, rows + 1], hs.at[k, 0], hrv.at[k, 0], {"lat": south}),
            remote(field.at[k, rows], field.at[k, 0], hs.at[k, 1], hrv.at[k, 1], {"lat": north}),
        ]

    def send_halo(k):
        for c in halo(k):
            c.start()

    def wait_halo(k):
        for c in halo(k):
            c.wait_recv()

    send_halo(0)

    for c in first_copies:
        c.wait_recv()
    a = dw[...]
    colid = lax.broadcasted_iota(jnp.int32, (rows, cols), 1)
    rowid = lax.broadcasted_iota(jnp.int32, (rows, cols), 0)
    keep_n = (me_lat < nlat - 1).astype(jnp.float32)
    keep_s = (me_lat > 0).astype(jnp.float32)

    def harmonic(first, second):
        return 2.0 * first * second / jnp.maximum(first + second, 0.5)

    drag = fric[...]
    total = wet * drag + (1.0 - wet)
    around = (
        lambda: jnp.where(colid == cols - 1, dwe[:, 0:1], pltpu.roll(a, cols - 1, 1)),
        lambda: jnp.where(colid == 0, dww[:, BLOCK - 1 : BLOCK], pltpu.roll(a, 1, 1)),
        lambda: jnp.where(rowid == rows - 1, dwn[0:1, :] * keep_n, pltpu.roll(a, rows - 1, 0)),
        lambda: jnp.where(rowid == 0, dws[rows - 1 : rows, :] * keep_s, pltpu.roll(a, 1, 0)),
    )
    for k in range(4):
        side = harmonic(a, around[k]())
        total = total + side
        for row in range(rows):
            coef[k, row] = jnp.broadcast_to(side[row : row + 1], (8, cols))
    dragged = wet * drag
    for row in range(rows):
        wetfric[row] = jnp.broadcast_to(dragged[row : row + 1], (8, cols))
        wide = jnp.broadcast_to(wet[row : row + 1], (8, cols))
        diag[row] = wide * stiff + jnp.broadcast_to(total[row : row + 1], (8, cols))

    def build(o, carry):
        for k in range(CAP):
            weight = inf[o, pl.ds(4 * k + 2, 1), :]
            basis = (waves[o * CAP + k, 0], waves[o * CAP + k, 1])
            parts = []
            for h in range(2):
                for c in range(8):
                    one = weight * basis[h][c : c + 1]
                    parts.append(one * basis[0])
                    parts.append(one * basis[1])
            mats[o * CAP + k] = onto_cells(o, k, jnp.concatenate(parts, axis=0))
        return carry

    lax.fori_loop(0, nlon, build, 0)

    def join_mats(i, carry):
        s = slots - 1 - i
        mats[s] = mats[s] + mats[splan[1, s]]
        return carry

    lax.fori_loop(0, slots, join_mats, 0)

    def observe():
        def slot(s, carry):
            v = seen[splan[0, s]]
            acc = [zero, zero]
            for c in range(16):
                m = mats[s, 16 * c : 16 * c + 16, :].reshape(2, 8, BLOCK)
                acc[c % 2] = acc[c % 2] + m * v[c // 8, c % 8 : c % 8 + 1, :]
            oslot[s] = acc[0] + acc[1]
            return carry

        lax.fori_loop(0, slots, slot, 0, unroll=2)

    def eastward(v, beyond):
        moved = [pltpu.roll(b, BLOCK - 1, 2) for b in v] + [beyond]
        return [jnp.where(lane8 == BLOCK - 1, moved[cb + 1], moved[cb]) for cb in range(nblk)]

    def westward(v, beyond):
        moved = [beyond] + [pltpu.roll(b, 1, 2) for b in v]
        return [jnp.where(lane8 == 0, moved[cb], moved[cb + 1]) for cb in range(nblk)]

    def from_east(halos, row):
        return pltpu.roll(halos[1], BLOCK - 1 - row, 2)

    def from_west(halos, row):
        return pltpu.roll(halos[0], BLOCK - row, 2)

    def image_row(src, dst, row, east_side, west_side):
        v = [src[row + 1, cb] for cb in range(nblk)]
        e = eastward(v, east_side)
        w = westward(v, west_side)
        for cb in range(nblk):
            at = pl.ds(cb * BLOCK, BLOCK)
            dst[row + 1, cb] = (
                diag[row, :, at] * v[cb]
                - coef[0, row, :, at] * e[cb]
                - coef[1, row, :, at] * w[cb]
                - coef[2, row, :, at] * src[row + 2, cb]
                - coef[3, row, :, at] * src[row, cb]
                + oslot[splan[2, row * nblk + cb]]
            )

    def inside(src, dst):
        def line(row, carry):
            image_row(src, dst, row, zero, zero)
            return carry

        lax.fori_loop(1, rows - 1, line, 0)

    def edges(src, halos, dst):
        for row in (0, rows - 1):
            image_row(src, dst, row, from_east(halos, row), from_west(halos, row))

        def mend(row, carry):
            last = pl.ds(cols - BLOCK, BLOCK)
            dst[row + 1, 0] = dst[row + 1, 0] - coef[1, row, :, pl.ds(0, BLOCK)] * jnp.where(
                lane8 == 0, from_west(halos, row), 0.0
            )
            dst[row + 1, nblk - 1] = dst[row + 1, nblk - 1] - coef[0, row, :, last] * jnp.where(
                lane8 == BLOCK - 1, from_east(halos, row), 0.0
            )
            return carry

        lax.fori_loop(1, rows - 1, mend, 0)

    def sum_copy(i, k):
        peer = lax.rem(me + k, count)
        where = {"lat": peer // nlon, "lon": lax.rem(peer, nlon)}
        return remote(part_row.at[i], sum_a.at[i, pl.ds(me, 1)], as_.at[i], ar.at[i], where)

    def sum_wait(i):
        whole = sum_a.at[i, pl.ds(0, count - 1)]
        return remote(whole, whole, as_.at[i], ar.at[i], {"lat": south})

    def send_sums(i, sums):
        part = jnp.zeros((8, BLOCK), jnp.float32)
        for k, s in enumerate(sums):
            part = jnp.where(sub8 == k, jnp.sum(s[0] + s[1], axis=0, keepdims=True), part)
        part = part + pltpu.roll(part, 64, 1)
        part = part + pltpu.roll(part, 32, 1)
        row = jnp.sum(jnp.where(lane8 >> 5 == sub8, part, 0.0), axis=0, keepdims=True)
        part_row[i] = row
        sum_a[i, pl.ds(me, 1)] = row

        def send(k, carry):
            sum_copy(i, k).start()
            return carry

        lax.fori_loop(1, count, send, 0, unroll=True)

    def take_sums(i):
        sum_wait(i).wait_recv()
        total = jnp.sum(sum_a[i], axis=0, keepdims=True)
        whole = jnp.sum(jnp.where(lane8 >> 5 == sub8, total, 0.0), axis=1, keepdims=True)
        return [jnp.broadcast_to(whole[k : k + 1], (8, BLOCK)) for k in range(4)]

    def beta_of(size, rr, rq, qq):
        return (rr - 2.0 * size * rq + size * size * qq) / rr

    def outer(o):
        k0, kq, kz = 3 * o, 3 * o + 1, 3 * o + 2
        r0, q0, z0 = field.at[k0], field.at[kq], field.at[kz]
        observe()
        inside(r0, q0)
        wait_halo(k0)
        edges(r0, hq.at[k0], q0)

        def first_dots(row, carry):
            ends, rr, rq, qq = carry
            for cb in range(nblk):
                res, image = r0[row + 1, cb], q0[row + 1, cb]
                seen[row * nblk + cb] = image
                rr = rr + res * res
                rq = rq + res * image
                qq = qq + image * image
            return pack_ends(row, q0[row + 1, 0], q0[row + 1, nblk - 1], ends), rr, rq, qq

        ends, *sums = lax.fori_loop(0, rows, first_dots, ((zero, zero), zero, zero, zero))
        keep_ends(kq, ends)
        if o == 0:
            pl.semaphore_wait(ready, nlat - 1)
        send_sums(k0, sums)
        send_halo(kq)
        observe()
        inside(q0, z0)
        wait_halo(kq)
        edges(q0, hq.at[kq], z0)

        def pack_z(row, ends):
            return pack_ends(row, z0[row + 1, 0], z0[row + 1, nblk - 1], ends)

        keep_ends(kz, lax.fori_loop(0, rows, pack_z, (zero, zero)))
        send_halo(kz)
        rr, rq, qq, _ = take_sums(k0)
        size0 = rr / rq
        beta0 = beta_of(size0, rr, rq, qq)
        more = 1.0 + beta0

        def second(row, carry):
            rr, rq, dq, qq = carry
            for cb in range(nblk):
                r, q, z = r0[row + 1, cb], q0[row + 1, cb], z0[row + 1, cb]
                res = r - size0 * q
                way = res + beta0 * r
                image = more * q - size0 * z
                r1[row + 1, cb] = res
                p1[row + 1, cb] = way
                q1[row + 1, cb] = image
                seen[row * nblk + cb] = image
                rr = rr + res * res
                rq = rq + res * image
                dq = dq + way * image
                qq = qq + image * image
            return rr, rq, dq, qq

        send_sums(kq, lax.fori_loop(0, rows, second, (zero,) * 4))
        observe()
        inside(q1, z1)
        wait_halo(kz)
        for edge in (0, rows + 1):
            for cb in range(nblk):
                q1[edge, cb] = more * q0[edge, cb] - size0 * z0[edge, cb]
        hq1[...] = more * hq[kq] - size0 * hq[kz]
        edges(q1, hq1, z1)
        rr, rq, dq, qq = take_sums(kq)
        size1 = rr / dq
        beta1 = beta_of(size1, rr, rq, qq)

        def third(row, carry):
            rr, dq = carry
            for cb in range(nblk):
                q = q1[row + 1, cb]
                res = r1[row + 1, cb] - size1 * q
                way = res + beta1 * p1[row + 1, cb]
                image = ((q0[row + 1, cb] - size0 * z0[row + 1, cb]) - size1 * z1[row + 1, cb]) + beta1 * q
                r2[row + 1, cb] = res
                p2[row + 1, cb] = way
                q2[row + 1, cb] = image
                rr = rr + res * res
                dq = dq + way * image
            return rr, dq

        send_sums(kz, lax.fori_loop(0, rows, third, (zero,) * 2))
        return size0, beta0, size1, beta1

    size0, beta0, size1, beta1 = outer(0)
    for c in obs_sends + first_copies:
        c.wait_send()

    def advance(row, carry):
        for cb in range(nblk):
            x[row + 1, cb] = size0 * field[0, row + 1, cb] + size1 * p1[row + 1, cb]
        return carry

    lax.fori_loop(0, rows, advance, 0)

    def beyond(r, q, q_next):
        res = r - size0 * q
        way = res + beta0 * r
        return size0 * r + size1 * way, (res - size1 * q_next) + beta1 * way

    for cb in range(nblk):
        x[rows + 1, cb], p2[rows + 1, cb] = beyond(field[0, rows + 1, cb], field[1, rows + 1, cb], q1[rows + 1, cb])
    hx[...], hp[...] = beyond(hq[0], hq[1], hq1[...])
    rr, dq, _, _ = take_sums(2)
    size2 = rr / dq

    def finish(row, carry):
        for cb in range(nblk):
            x[row + 1, cb] = x[row + 1, cb] + size2 * p2[row + 1, cb]
        return carry

    lax.fori_loop(0, rows + 1, finish, 0)
    hx[...] = hx[...] + size2 * hp[...]

    def friction(row, ends):
        v = [x[row + 1, cb] for cb in range(nblk)]
        e = eastward(v, from_east(hx, row))
        new = []
        for cb in range(nblk):
            at = pl.ds(cb * BLOCK, BLOCK)
            flux_e = coef[0, row, :, at] * (e[cb] - v[cb])
            flux_n = coef[2, row, :, at] * (x[row + 2, cb] - v[cb])
            square = flux_e * flux_e + flux_n * flux_n
            speed = jnp.sum(square[0] + square[1], axis=0, keepdims=True)
            extra = wetfric[row, :, at] * (jnp.sqrt(1.0 + speed / 16.0) - 1.0)
            diag[row, :, at] = diag[row, :, at] + extra
            new.append((r2[row + 1, cb] - size2 * q2[row + 1, cb]) - extra * v[cb])
            field[3, row + 1, cb] = new[cb]
            seen[row * nblk + cb] = new[cb]
        return pack_ends(row, new[0], new[-1], ends)

    keep_ends(3, lax.fori_loop(0, rows, friction, (zero, zero)))
    send_halo(3)
    size0, beta0, size1, beta1 = outer(1)

    def advance_last(row, carry):
        for cb in range(nblk):
            x[row + 1, cb] = (x[row + 1, cb] + size0 * field[3, row + 1, cb]) + size1 * p1[row + 1, cb]
        return carry

    lax.fori_loop(0, rows, advance_last, 0)
    outs = []
    for n, (src, dst) in enumerate(((x, x_out), (p2, p_out), (r2, r_out), (q2, q_out))):
        for cb in range(nblk):
            for h in range(2):
                turned[n, h, :, :, pl.ds(cb * BLOCK, BLOCK)] = jnp.swapaxes(src[pl.ds(1, rows), cb, h], 0, 1)
        outs.append(pltpu.make_async_copy(turned.at[n], dst, out_sem.at[n]))
        outs[n].start()
    for k in range(SUMS):
        for c in halo(k):
            c.wait_send()
    rr, dq, _, _ = take_sums(SUMS - 1)
    size_out[...] = jnp.broadcast_to((rr / dq)[:, 0:1], (8, cols))
    for i in range(SUMS):
        sum_wait(i).wait_send()
    for c in outs:
        c.wait()


def shards(nlat, nlon, depth, friction, ocean_mask, forcing, tile_route, tile_block, obs_cell, obs_time, obs_value, obs_weight):
    channels, rows, cols = forcing.shape
    slots = nlon * CAP
    nblk, tiles = cols // BLOCK, obs_time.shape[0]
    f32, i32 = jnp.float32, jnp.int32
    vmem, smem = pltpu.VMEM, pltpu.SMEM
    hbm = pl.BlockSpec(memory_space=pltpu.HBM)
    field = (rows + 2, nblk, 2, 8, BLOCK)
    ends = (2, 2, 8, BLOCK)
    split = (2, channels // 2, rows, cols)
    dma = pltpu.SemaphoreType.DMA
    scratch = [
        smem((tiles,), i32),
        smem((tiles,), i32),
        vmem((rows, cols), f32),
        vmem((rows, cols), f32),
        vmem((rows, cols), i32),
        vmem(split, f32),
        vmem((tiles, BLOCK), i32),
        vmem((tiles, BLOCK), f32),
        vmem((tiles, BLOCK), f32),
        vmem((tiles, BLOCK), f32),
        vmem((rows, cols), f32),
        vmem((rows, cols), f32),
        vmem((rows, cols), f32),
        vmem((rows, BLOCK), f32),
        vmem((rows, BLOCK), f32),
        vmem((rows, 8, cols), f32),
        vmem((4, rows, 8, cols), f32),
        vmem((rows, 8, cols), f32),
        vmem((tiles + 1, 8, BLOCK), f32),
        vmem((tiles + 1, 8, BLOCK), i32),
        vmem((nlon, 8, BLOCK), f32),
        vmem((nlon, 8, BLOCK), i32),
        vmem((nlon, 8, BLOCK), f32),
        vmem((nlon, 8, BLOCK), i32),
        vmem((8, BLOCK), i32),
        smem((8, BLOCK), i32),
        vmem((slots, 2, 8, BLOCK), f32),
        vmem((slots + 1, 256, BLOCK), f32),
        vmem((slots + 1, 2, 8, BLOCK), f32),
        vmem((SUMS,) + field, f32),
        vmem((rows * nblk, 2, 8, BLOCK), f32),
        vmem(field, f32),
        vmem(field, f32),
        vmem(field, f32),
        vmem(field, f32),
        vmem(field, f32),
        vmem(field, f32),
        vmem(field, f32),
        vmem(field, f32),
        vmem((4,) + split, f32),
        vmem((SUMS,) + ends, f32),
        vmem((SUMS,) + ends, f32),
        vmem(ends, f32),
        vmem(ends, f32),
        vmem(ends, f32),
        vmem((SUMS, nlat * nlon, BLOCK), f32),
        vmem((SUMS, 1, BLOCK), f32),
        pltpu.SemaphoreType.REGULAR,
        dma((10,)),
        dma((SUMS, 4)),
        dma((SUMS, 4)),
        dma((SUMS,)),
        dma((SUMS,)),
        dma((2, nlon)),
        dma((2, nlon)),
        dma((4,)),
        dma((4,)),
        dma((1,)),
        dma((4,)),
    ]
    shape = jax.ShapeDtypeStruct(split, f32)
    x, p, r, q, size = pl.pallas_call(
        functools.partial(kernel, nlat, nlon),
        out_shape=(shape, shape, shape, shape, jax.ShapeDtypeStruct((8, cols), f32)),
        in_specs=[hbm] * 10,
        out_specs=(hbm, hbm, hbm, hbm, pl.BlockSpec(memory_space=vmem)),
        scratch_shapes=scratch,
        compiler_params=pltpu.CompilerParams(
            collective_id=0, has_side_effects=True, vmem_limit_bytes=62 * 2**20
        ),
    )(
        tile_route.reshape(-1), tile_block, depth, friction, ocean_mask, forcing.reshape(split),
        obs_cell, obs_time, obs_value, obs_weight,
    )
    x, p, r, q = (v.reshape(forcing.shape) for v in (x, p, r, q))
    return x + size[0, 0] * p, r - size[0, 0] * q


def solution(mesh):
    tile = P(("lat", "lon"), None)
    grid = P("lat", "lon")
    in_specs = (grid, grid, grid, P(None, "lat", "lon"), tile, P(("lat", "lon")), tile, tile, tile, tile)
    out_specs = (P(None, "lat", "lon"), P(None, "lat", "lon"))
    body = functools.partial(shards, mesh.shape["lat"], mesh.shape["lon"])
    return jax.shard_map(body, mesh=mesh, in_specs=in_specs, out_specs=out_specs, check_vma=False)
```

```python
import functools
import math

import jax
import jax.numpy as jnp
import numpy as np
from jax import lax
from jax.experimental import pallas as pl
from jax.experimental.pallas import tpu as pltpu
from jax.sharding import PartitionSpec as P

BLOCK = 128
CAP = 2
ITERS = 3
OUTER = 2
SUMS = ITERS * OUTER
MESH = pl.DeviceIdType.MESH
OMEGA_DEGREES = (28.984104, 30.0, 28.43973, 30.082137, 15.041069, 13.943036, 14.958931, 13.398661)
RATES = np.array(OMEGA_DEGREES, np.float32) * np.float32(math.pi / 180.0)
STIFF = np.float32(0.2) * (RATES / RATES[0]) ** 2


def sin_cos(angle):
    turn = jnp.floor(angle * (2.0 / math.pi) + 0.5)
    x = ((angle - turn * 1.5703125) - turn * 4.837512969970703125e-4) - turn * 7.54978995489188216e-8
    z = x * x
    s = ((-1.9515295891e-4 * z + 8.3321608736e-3) * z - 1.6666654611e-1) * z * x + x
    c = ((2.443315711809948e-5 * z - 1.388731625493765e-3) * z + 4.166664568298827e-2) * z * z - 0.5 * z + 1.0
    quarter = turn.astype(jnp.int32)
    odd = (quarter & 1) == 1
    sine = jnp.where(odd, c, s)
    cosine = jnp.where(odd, s, c)
    sine = jnp.where((quarter & 2) == 2, -sine, sine)
    cosine = jnp.where(((quarter + 1) & 2) == 2, -cosine, cosine)
    return sine, cosine


def kernel(
    nlat, nlon,
    route_in, tblk_in, depth_in, fric_in, mask_in, forc_in, ocell_in, otime_in, oval_in, oweight_in,
    x_out, r_out,
    route, tblk, depth, fric, mask, forc, ocell, otime, oval, oweight,
    dw, dwn, dws, dwe, dww, wetfric, coef, diag,
    pay, payi, outf, outi, inf, ini, plan, splan, waves, mats, oslot,
    field, seen, r1, p1, q1, z1, r2, p2, q2, x, turned,
    pk, hq, hq1, hx, hp, sum_a, part_row, ready,
    load, hs, hrv, as_, ar, os_, orv, ds_, dr, loc,
):
    rows, cols = depth.shape
    nblk = cols // BLOCK
    slots = nlon * CAP
    tiles = otime.shape[0]
    me_lat = lax.axis_index("lat")
    me_lon = lax.axis_index("lon")
    north, south = lax.rem(me_lat + 1, nlat), lax.rem(me_lat + nlat - 1, nlat)
    east, west = lax.rem(me_lon + 1, nlon), lax.rem(me_lon + nlon - 1, nlon)
    me = me_lat * nlon + me_lon
    count = nlat * nlon

    barrier = pltpu.get_barrier_semaphore()
    for k in range(1, nlon):
        pl.semaphore_signal(barrier, inc=1, device_id={"lon": lax.rem(me_lon + k, nlon)}, device_id_type=MESH)
    for k in range(1, nlat):
        pl.semaphore_signal(barrier, inc=1, device_id={"lat": lax.rem(me_lat + k, nlat)}, device_id_type=MESH)
    pairs = [
        (route_in, route), (tblk_in, tblk), (ocell_in, ocell), (otime_in, otime), (oval_in, oval),
        (oweight_in, oweight), (depth_in, depth), (mask_in, mask), (fric_in, fric), (forc_in, forc),
    ]
    loads = [pltpu.make_async_copy(src, dst, load.at[k]) for k, (src, dst) in enumerate(pairs)]
    for c in loads:
        c.start()

    def remote(src, dst, send, recv, where):
        return pltpu.make_async_remote_copy(
            src_ref=src, dst_ref=dst, send_sem=send, recv_sem=recv, device_id=where, device_id_type=MESH
        )

    lane = lax.broadcasted_iota(jnp.int32, (1, BLOCK), 1)
    lane8 = lax.broadcasted_iota(jnp.int32, (8, BLOCK), 1)
    sub8 = lax.broadcasted_iota(jnp.int32, (8, BLOCK), 0)
    zero = jnp.zeros((2, 8, BLOCK), jnp.float32)

    for c in loads[:8]:
        c.wait()
    wet = mask[...].astype(jnp.float32)
    dw[...] = depth[...] * wet

    for t in range(tiles):
        pay[t] = jnp.concatenate([otime[t : t + 1], oval[t : t + 1], oweight[t : t + 1], oval[t : t + 1]] * 2, axis=0)
        payi[t] = jnp.broadcast_to(ocell[t : t + 1] + tblk[t] * BLOCK, (8, BLOCK))
    pay[tiles] = jnp.zeros((8, BLOCK), jnp.float32)
    payi[tiles] = jnp.zeros((8, BLOCK), jnp.int32)

    def pick(p, carry):
        first, second = jnp.int32(tiles), jnp.int32(tiles)
        for t in reversed(range(tiles)):
            hit = route[t] == p
            second = jnp.where(hit, first, second)
            first = jnp.where(hit, jnp.int32(t), first)
        outf[p] = jnp.where(sub8 < 4, pay[first], pay[second])
        outi[p] = jnp.where(sub8 == 0, payi[first], payi[second])
        return carry

    lax.fori_loop(0, nlon, pick, 0)
    pl.semaphore_wait(barrier, nlon + nlat - 2)

    def obs_copy(k):
        peer = lax.rem(me_lon + k, nlon)
        return [
            remote(outf.at[peer], inf.at[me_lon], os_.at[0, peer], orv.at[0, me_lon], {"lon": peer}),
            remote(outi.at[peer], ini.at[me_lon], os_.at[1, peer], orv.at[1, me_lon], {"lon": peer}),
        ]

    def obs_wait(k):
        peer = lax.rem(me_lon + k, nlon)
        remote(outf.at[peer], inf.at[peer], os_.at[0, peer], orv.at[0, peer], {"lon": peer}).wait_recv()
        remote(outi.at[peer], ini.at[peer], os_.at[1, peer], orv.at[1, peer], {"lon": peer}).wait_recv()

    obs_sends = [c for k in range(1, nlon) for c in obs_copy(k)]
    for c in obs_sends:
        c.start()
    first_copies = [
        remote(dw.at[:, pl.ds(0, BLOCK)], dwe, ds_.at[2], dr.at[2], {"lon": west}),
        remote(dw.at[:, pl.ds(cols - BLOCK, BLOCK)], dww, ds_.at[3], dr.at[3], {"lon": east}),
        remote(dw, dws, ds_.at[0], dr.at[0], {"lat": north}),
        remote(dw, dwn, ds_.at[1], dr.at[1], {"lat": south}),
    ]
    for c in first_copies:
        c.start()
    for k in range(1, nlat):
        pl.semaphore_signal(ready, inc=1, device_id={"lat": lax.rem(me_lat + k, nlat)}, device_id_type=MESH)
    inf[me_lon] = outf[me_lon]
    ini[me_lon] = outi[me_lon]
    for c in loads[8:]:
        c.wait()

    for cb in range(nblk):
        at = pl.ds(cb * BLOCK, BLOCK)
        for h in range(2):
            wetted = forc[h, :, :, at] * wet[None, :, cb * BLOCK : cb * BLOCK + BLOCK]
            field[0, pl.ds(1, rows), cb, h] = jnp.swapaxes(wetted, 0, 1)
    oslot[slots] = zero
    mats[slots] = jnp.zeros((256, BLOCK), jnp.float32)
    stiff = jnp.zeros((8, 1), jnp.float32)
    rate = jnp.zeros((8, BLOCK), jnp.float32)
    sub1 = lax.broadcasted_iota(jnp.int32, (8, 1), 0)
    for c in range(8):
        stiff = jnp.where(sub1 == c, float(STIFF[c]), stiff)
        rate = jnp.where(sub8 == c, float(RATES[c]), rate)
    cells = lax.broadcasted_iota(jnp.int32, (BLOCK, BLOCK), 0)

    for k in range(1, nlon):
        obs_wait(k)

    def where_is(s):
        return ini[s // CAP, pl.ds(s % CAP, 1), :]

    rep = jnp.full((1, BLOCK), slots, jnp.int32)
    homes = jnp.full((1, BLOCK), -1, jnp.int32)
    for s in reversed(range(slots)):
        home = where_is(s) >> 7
        rep = jnp.where(home == lane, s, rep)
        homes = jnp.where(lane == s, home, homes)
    chain = jnp.full((1, BLOCK), slots, jnp.int32)
    for s in reversed(range(slots)):
        home = where_is(s) >> 7
        chain = jnp.where((home == homes) & (lane < s), s, chain)
    plan[...] = jnp.where(
        sub8 == 0,
        jnp.broadcast_to(homes, (8, BLOCK)),
        jnp.where(sub8 == 1, jnp.broadcast_to(chain, (8, BLOCK)), jnp.broadcast_to(rep, (8, BLOCK))),
    )
    to_scalars = pltpu.make_async_copy(plan, splan, loc.at[0])
    to_scalars.start()

    def onto_cells(o, k, terms):
        cell = ini[o, pl.ds(k, 1), :] & (BLOCK - 1)
        high = terms.astype(jnp.bfloat16)
        low = (terms - high.astype(jnp.float32)).astype(jnp.bfloat16)
        hot = (cells == cell).astype(jnp.float32).astype(jnp.bfloat16)
        return lax.dot_general(
            jnp.concatenate([high, low], axis=1),
            jnp.concatenate([hot, hot], axis=1),
            (((1,), (1,)), ((), ())),
            preferred_element_type=jnp.float32,
        )

    def values(o, carry):
        for k in range(CAP):
            times = inf[o, pl.ds(4 * k, 1), :]
            scaled = inf[o, pl.ds(4 * k + 2, 1), :] * inf[o, pl.ds(4 * k + 1, 1), :]
            sine, cosine = sin_cos(rate * times)
            waves[o * CAP + k, 0] = cosine
            waves[o * CAP + k, 1] = sine
            terms = jnp.concatenate([cosine * scaled, sine * scaled], axis=0)
            oslot[o * CAP + k] = onto_cells(o, k, terms).reshape(2, 8, BLOCK)
        return carry

    lax.fori_loop(0, nlon, values, 0, unroll=4)
    to_scalars.wait()

    def join_values(i, carry):
        s = slots - 1 - i
        oslot[s] = oslot[s] + oslot[splan[1, s]]
        return carry

    lax.fori_loop(0, slots, join_values, 0)

    def pack(row, col, value, packed):
        shift = row if col == 0 else row + 1
        moved = pltpu.roll(value, shift, 2)
        return jnp.where(lane8 == row, moved, packed)

    def pack_ends(row, first, last, carry):
        return pack(row, 0, first, carry[0]), pack(row, 1, last, carry[1])

    def keep_ends(k, ends):
        pk[k, 0] = ends[0]
        pk[k, 1] = ends[1]

    def start_rhs(row, ends):
        v = []
        for cb in range(nblk):
            v.append(field[0, row + 1, cb] + oslot[splan[2, row * nblk + cb]])
            field[0, row + 1, cb] = v[cb]
            seen[row * nblk + cb] = v[cb]
        return pack_ends(row, v[0], v[-1], ends)

    keep_ends(0, lax.fori_loop(0, rows, start_rhs, (zero, zero)))

    def halo(k):
        return [
            remote(pk.at[k, 0], hq.at[k, 1], hs.at[k, 2], hrv.at[k, 2], {"lon": west}),
            remote(pk.at[k, 1], hq.at[k, 0], hs.at[k, 3], hrv.at[k, 3], {"lon": east}),
            remote(field.at[k, 1], field.at[k, rows + 1], hs.at[k, 0], hrv.at[k, 0], {"lat": south}),
            remote(field.at[k, rows], field.at[k, 0], hs.at[k, 1], hrv.at[k, 1], {"lat": north}),
        ]

    def send_halo(k):
        for c in halo(k):
            c.start()

    def wait_halo(k):
        for c in halo(k):
            c.wait_recv()

    send_halo(0)

    for c in first_copies:
        c.wait_recv()
    a = dw[...]
    colid = lax.broadcasted_iota(jnp.int32, (rows, cols), 1)
    rowid = lax.broadcasted_iota(jnp.int32, (rows, cols), 0)
    keep_n = (me_lat < nlat - 1).astype(jnp.float32)
    keep_s = (me_lat > 0).astype(jnp.float32)

    def harmonic(first, second):
        return 2.0 * first * second / jnp.maximum(first + second, 0.5)

    drag = fric[...]
    total = wet * drag + (1.0 - wet)
    around = (
        lambda: jnp.where(colid == cols - 1, dwe[:, 0:1], pltpu.roll(a, cols - 1, 1)),
        lambda: jnp.where(colid == 0, dww[:, BLOCK - 1 : BLOCK], pltpu.roll(a, 1, 1)),
        lambda: jnp.where(rowid == rows - 1, dwn[0:1, :] * keep_n, pltpu.roll(a, rows - 1, 0)),
        lambda: jnp.where(rowid == 0, dws[rows - 1 : rows, :] * keep_s, pltpu.roll(a, 1, 0)),
    )
    for k in range(4):
        side = harmonic(a, around[k]())
        total = total + side
        for row in range(rows):
            coef[k, row] = jnp.broadcast_to(side[row : row + 1], (8, cols))
    dragged = wet * drag
    for row in range(rows):
        wetfric[row] = jnp.broadcast_to(dragged[row : row + 1], (8, cols))
        wide = jnp.broadcast_to(wet[row : row + 1], (8, cols))
        diag[row] = wide * stiff + jnp.broadcast_to(total[row : row + 1], (8, cols))

    def build(o, carry):
        for k in range(CAP):
            weight = inf[o, pl.ds(4 * k + 2, 1), :]
            basis = (waves[o * CAP + k, 0], waves[o * CAP + k, 1])
            parts = []
            for h in range(2):
                for c in range(8):
                    one = weight * basis[h][c : c + 1]
                    parts.append(one * basis[0])
                    parts.append(one * basis[1])
            mats[o * CAP + k] = onto_cells(o, k, jnp.concatenate(parts, axis=0))
        return carry

    lax.fori_loop(0, nlon, build, 0)

    def join_mats(i, carry):
        s = slots - 1 - i
        mats[s] = mats[s] + mats[splan[1, s]]
        return carry

    lax.fori_loop(0, slots, join_mats, 0)

    def observe():
        def slot(s, carry):
            v = seen[splan[0, s]]
            acc = [zero, zero]
            for c in range(16):
                m = mats[s, 16 * c : 16 * c + 16, :].reshape(2, 8, BLOCK)
                acc[c % 2] = acc[c % 2] + m * v[c // 8, c % 8 : c % 8 + 1, :]
            oslot[s] = acc[0] + acc[1]
            return carry

        lax.fori_loop(0, slots, slot, 0, unroll=2)

    def eastward(v, beyond):
        moved = [pltpu.roll(b, BLOCK - 1, 2) for b in v] + [beyond]
        return [jnp.where(lane8 == BLOCK - 1, moved[cb + 1], moved[cb]) for cb in range(nblk)]

    def westward(v, beyond):
        moved = [beyond] + [pltpu.roll(b, 1, 2) for b in v]
        return [jnp.where(lane8 == 0, moved[cb], moved[cb + 1]) for cb in range(nblk)]

    def from_east(halos, row):
        return pltpu.roll(halos[1], BLOCK - 1 - row, 2)

    def from_west(halos, row):
        return pltpu.roll(halos[0], BLOCK - row, 2)

    def image_row(src, dst, row, east_side, west_side):
        v = [src[row + 1, cb] for cb in range(nblk)]
        e = eastward(v, east_side)
        w = westward(v, west_side)
        for cb in range(nblk):
            at = pl.ds(cb * BLOCK, BLOCK)
            dst[row + 1, cb] = (
                diag[row, :, at] * v[cb]
                - coef[0, row, :, at] * e[cb]
                - coef[1, row, :, at] * w[cb]
                - coef[2, row, :, at] * src[row + 2, cb]
                - coef[3, row, :, at] * src[row, cb]
                + oslot[splan[2, row * nblk + cb]]
            )

    def inside(src, dst):
        def line(row, carry):
            image_row(src, dst, row, zero, zero)
            return carry

        lax.fori_loop(1, rows - 1, line, 0)

    def edges(src, halos, dst):
        for row in (0, rows - 1):
            image_row(src, dst, row, from_east(halos, row), from_west(halos, row))

        def mend(row, carry):
            last = pl.ds(cols - BLOCK, BLOCK)
            dst[row + 1, 0] = dst[row + 1, 0] - coef[1, row, :, pl.ds(0, BLOCK)] * jnp.where(
                lane8 == 0, from_west(halos, row), 0.0
            )
            dst[row + 1, nblk - 1] = dst[row + 1, nblk - 1] - coef[0, row, :, last] * jnp.where(
                lane8 == BLOCK - 1, from_east(halos, row), 0.0
            )
            return carry

        lax.fori_loop(1, rows - 1, mend, 0)

    def sum_copy(i, k):
        peer = lax.rem(me + k, count)
        where = {"lat": peer // nlon, "lon": lax.rem(peer, nlon)}
        return remote(part_row.at[i], sum_a.at[i, pl.ds(me, 1)], as_.at[i], ar.at[i], where)

    def sum_wait(i):
        whole = sum_a.at[i, pl.ds(0, count - 1)]
        return remote(whole, whole, as_.at[i], ar.at[i], {"lat": south})

    def send_sums(i, sums):
        part = jnp.zeros((8, BLOCK), jnp.float32)
        for k, s in enumerate(sums):
            part = jnp.where(sub8 == k, jnp.sum(s[0] + s[1], axis=0, keepdims=True), part)
        part = part + pltpu.roll(part, 64, 1)
        part = part + pltpu.roll(part, 32, 1)
        row = jnp.sum(jnp.where(lane8 >> 5 == sub8, part, 0.0), axis=0, keepdims=True)
        part_row[i] = row
        sum_a[i, pl.ds(me, 1)] = row

        def send(k, carry):
            sum_copy(i, k).start()
            return carry

        lax.fori_loop(1, count, send, 0, unroll=True)

    def take_sums(i):
        sum_wait(i).wait_recv()
        total = jnp.sum(sum_a[i], axis=0, keepdims=True)
        whole = jnp.sum(jnp.where(lane8 >> 5 == sub8, total, 0.0), axis=1, keepdims=True)
        return [jnp.broadcast_to(whole[k : k + 1], (8, BLOCK)) for k in range(4)]

    def beta_of(size, rr, rq, qq):
        return (rr - 2.0 * size * rq + size * size * qq) / rr

    def outer(o):
        k0, kq, kz = 3 * o, 3 * o + 1, 3 * o + 2
        r0, q0, z0 = field.at[k0], field.at[kq], field.at[kz]
        observe()
        inside(r0, q0)
        wait_halo(k0)
        edges(r0, hq.at[k0], q0)

        def first_dots(row, carry):
            ends, rr, rq, qq = carry
            for cb in range(nblk):
                res, image = r0[row + 1, cb], q0[row + 1, cb]
                seen[row * nblk + cb] = image
                rr = rr + res * res
                rq = rq + res * image
                qq = qq + image * image
            return pack_ends(row, q0[row + 1, 0], q0[row + 1, nblk - 1], ends), rr, rq, qq

        ends, *sums = lax.fori_loop(0, rows, first_dots, ((zero, zero), zero, zero, zero))
        keep_ends(kq, ends)
        if o == 0:
            pl.semaphore_wait(ready, nlat - 1)
        send_sums(k0, sums)
        send_halo(kq)
        observe()
        inside(q0, z0)
        wait_halo(kq)
        edges(q0, hq.at[kq], z0)

        def pack_z(row, ends):
            return pack_ends(row, z0[row + 1, 0], z0[row + 1, nblk - 1], ends)

        keep_ends(kz, lax.fori_loop(0, rows, pack_z, (zero, zero)))
        send_halo(kz)
        rr, rq, qq, _ = take_sums(k0)
        size0 = rr / rq
        beta0 = beta_of(size0, rr, rq, qq)
        more = 1.0 + beta0

        def second(row, carry):
            rr, rq, dq, qq = carry
            for cb in range(nblk):
                r, q, z = r0[row + 1, cb], q0[row + 1, cb], z0[row + 1, cb]
                res = r - size0 * q
                way = res + beta0 * r
                image = more * q - size0 * z
                r1[row + 1, cb] = res
                p1[row + 1, cb] = way
                q1[row + 1, cb] = image
                seen[row * nblk + cb] = image
                rr = rr + res * res
                rq = rq + res * image
                dq = dq + way * image
                qq = qq + image * image
            return rr, rq, dq, qq

        send_sums(kq, lax.fori_loop(0, rows, second, (zero,) * 4))
        observe()
        inside(q1, z1)
        wait_halo(kz)
        for edge in (0, rows + 1):
            for cb in range(nblk):
                q1[edge, cb] = more * q0[edge, cb] - size0 * z0[edge, cb]
        hq1[...] = more * hq[kq] - size0 * hq[kz]
        edges(q1, hq1, z1)
        rr, rq, dq, qq = take_sums(kq)
        size1 = rr / dq
        beta1 = beta_of(size1, rr, rq, qq)

        def third(row, carry):
            rr, dq = carry
            for cb in range(nblk):
                q = q1[row + 1, cb]
                res = r1[row + 1, cb] - size1 * q
                way = res + beta1 * p1[row + 1, cb]
                image = ((q0[row + 1, cb] - size0 * z0[row + 1, cb]) - size1 * z1[row + 1, cb]) + beta1 * q
                r2[row + 1, cb] = res
                p2[row + 1, cb] = way
                q2[row + 1, cb] = image
                rr = rr + res * res
                dq = dq + way * image
            return rr, dq

        send_sums(kz, lax.fori_loop(0, rows, third, (zero,) * 2))
        return size0, beta0, size1, beta1

    size0, beta0, size1, beta1 = outer(0)
    for c in obs_sends + first_copies:
        c.wait_send()

    def advance(row, carry):
        for cb in range(nblk):
            x[row + 1, cb] = size0 * field[0, row + 1, cb] + size1 * p1[row + 1, cb]
        return carry

    lax.fori_loop(0, rows, advance, 0)

    def beyond(r, q, q_next):
        res = r - size0 * q
        way = res + beta0 * r
        return size0 * r + size1 * way, (res - size1 * q_next) + beta1 * way

    for cb in range(nblk):
        x[rows + 1, cb], p2[rows + 1, cb] = beyond(field[0, rows + 1, cb], field[1, rows + 1, cb], q1[rows + 1, cb])
    hx[...], hp[...] = beyond(hq[0], hq[1], hq1[...])
    rr, dq, _, _ = take_sums(2)
    size2 = rr / dq

    def finish(row, carry):
        for cb in range(nblk):
            x[row + 1, cb] = x[row + 1, cb] + size2 * p2[row + 1, cb]
        return carry

    lax.fori_loop(0, rows + 1, finish, 0)
    hx[...] = hx[...] + size2 * hp[...]

    def friction(row, ends):
        v = [x[row + 1, cb] for cb in range(nblk)]
        e = eastward(v, from_east(hx, row))
        new = []
        for cb in range(nblk):
            at = pl.ds(cb * BLOCK, BLOCK)
            flux_e = coef[0, row, :, at] * (e[cb] - v[cb])
            flux_n = coef[2, row, :, at] * (x[row + 2, cb] - v[cb])
            square = flux_e * flux_e + flux_n * flux_n
            speed = jnp.sum(square[0] + square[1], axis=0, keepdims=True)
            extra = wetfric[row, :, at] * (jnp.sqrt(1.0 + speed / 16.0) - 1.0)
            diag[row, :, at] = diag[row, :, at] + extra
            new.append((r2[row + 1, cb] - size2 * q2[row + 1, cb]) - extra * v[cb])
            field[3, row + 1, cb] = new[cb]
            seen[row * nblk + cb] = new[cb]
        return pack_ends(row, new[0], new[-1], ends)

    keep_ends(3, lax.fori_loop(0, rows, friction, (zero, zero)))
    send_halo(3)
    size0, beta0, size1, beta1 = outer(1)

    def advance_last(row, carry):
        for cb in range(nblk):
            x[row + 1, cb] = (x[row + 1, cb] + size0 * field[3, row + 1, cb]) + size1 * p1[row + 1, cb]
        return carry

    lax.fori_loop(0, rows, advance_last, 0)
    for n, src in enumerate((x, p2, r2, q2)):
        for cb in range(nblk):
            for h in range(2):
                turned[n, h, :, :, pl.ds(cb * BLOCK, BLOCK)] = jnp.swapaxes(src[pl.ds(1, rows), cb, h], 0, 1)
    for k in range(SUMS):
        for c in halo(k):
            c.wait_send()
    rr, dq, _, _ = take_sums(SUMS - 1)
    size2 = rr / dq

    def conclude(c, carry):
        for h in range(2):
            for cb in range(nblk):
                at = pl.ds(cb * BLOCK, BLOCK)
                x_out[h, c, :, at] = turned[0, h, c, :, at] + size2 * turned[1, h, c, :, at]
                r_out[h, c, :, at] = turned[2, h, c, :, at] - size2 * turned[3, h, c, :, at]
        return carry

    lax.fori_loop(0, 8, conclude, 0)
    for i in range(SUMS):
        sum_wait(i).wait_send()


def shards(nlat, nlon, depth, friction, ocean_mask, forcing, tile_route, tile_block, obs_cell, obs_time, obs_value, obs_weight):
    channels, rows, cols = forcing.shape
    slots = nlon * CAP
    nblk, tiles = cols // BLOCK, obs_time.shape[0]
    f32, i32 = jnp.float32, jnp.int32
    vmem, smem = pltpu.VMEM, pltpu.SMEM
    hbm = pl.BlockSpec(memory_space=pltpu.HBM)
    field = (rows + 2, nblk, 2, 8, BLOCK)
    ends = (2, 2, 8, BLOCK)
    split = (2, channels // 2, rows, cols)
    dma = pltpu.SemaphoreType.DMA
    scratch = [
        smem((tiles,), i32),
        smem((tiles,), i32),
        vmem((rows, cols), f32),
        vmem((rows, cols), f32),
        vmem((rows, cols), i32),
        vmem(split, f32),
        vmem((tiles, BLOCK), i32),
        vmem((tiles, BLOCK), f32),
        vmem((tiles, BLOCK), f32),
        vmem((tiles, BLOCK), f32),
        vmem((rows, cols), f32),
        vmem((rows, cols), f32),
        vmem((rows, cols), f32),
        vmem((rows, BLOCK), f32),
        vmem((rows, BLOCK), f32),
        vmem((rows, 8, cols), f32),
        vmem((4, rows, 8, cols), f32),
        vmem((rows, 8, cols), f32),
        vmem((tiles + 1, 8, BLOCK), f32),
        vmem((tiles + 1, 8, BLOCK), i32),
        vmem((nlon, 8, BLOCK), f32),
        vmem((nlon, 8, BLOCK), i32),
        vmem((nlon, 8, BLOCK), f32),
        vmem((nlon, 8, BLOCK), i32),
        vmem((8, BLOCK), i32),
        smem((8, BLOCK), i32),
        vmem((slots, 2, 8, BLOCK), f32),
        vmem((slots + 1, 256, BLOCK), f32),
        vmem((slots + 1, 2, 8, BLOCK), f32),
        vmem((SUMS,) + field, f32),
        vmem((rows * nblk, 2, 8, BLOCK), f32),
        vmem(field, f32),
        vmem(field, f32),
        vmem(field, f32),
        vmem(field, f32),
        vmem(field, f32),
        vmem(field, f32),
        vmem(field, f32),
        vmem(field, f32),
        vmem((4,) + split, f32),
        vmem((SUMS,) + ends, f32),
        vmem((SUMS,) + ends, f32),
        vmem(ends, f32),
        vmem(ends, f32),
        vmem(ends, f32),
        vmem((SUMS, nlat * nlon, BLOCK), f32),
        vmem((SUMS, 1, BLOCK), f32),
        pltpu.SemaphoreType.REGULAR,
        dma((10,)),
        dma((SUMS, 4)),
        dma((SUMS, 4)),
        dma((SUMS,)),
        dma((SUMS,)),
        dma((2, nlon)),
        dma((2, nlon)),
        dma((4,)),
        dma((4,)),
        dma((1,)),
    ]
    shape = vmem(split, f32)
    x, r = pl.pallas_call(
        functools.partial(kernel, nlat, nlon),
        out_shape=(shape, shape),
        in_specs=[hbm] * 10,
        out_specs=(pl.BlockSpec(memory_space=vmem), pl.BlockSpec(memory_space=vmem)),
        scratch_shapes=scratch,
        compiler_params=pltpu.CompilerParams(
            collective_id=0, has_side_effects=True, vmem_limit_bytes=62 * 2**20
        ),
    )(
        tile_route.reshape(-1), tile_block, depth, friction, ocean_mask, forcing.reshape(split),
        obs_cell, obs_time, obs_value, obs_weight,
    )
    return x.reshape(forcing.shape), r.reshape(forcing.shape)


def solution(mesh):
    tile = P(("lat", "lon"), None)
    grid = P("lat", "lon")
    in_specs = (grid, grid, grid, P(None, "lat", "lon"), tile, P(("lat", "lon")), tile, tile, tile, tile)
    out_specs = (P(None, "lat", "lon"), P(None, "lat", "lon"))
    body = functools.partial(shards, mesh.shape["lat"], mesh.shape["lon"])
    return jax.shard_map(body, mesh=mesh, in_specs=in_specs, out_specs=out_specs, check_vma=False)
```

```python
import functools
import math

import jax
import jax.numpy as jnp
import numpy as np
from jax import lax
from jax.experimental import pallas as pl
from jax.experimental.pallas import tpu as pltpu
from jax.sharding import PartitionSpec as P

BLOCK = 128
CAP = 2
ITERS = 3
OUTER = 2
SUMS = ITERS * OUTER
HALOS = 7
MESH = pl.DeviceIdType.MESH
OMEGA_DEGREES = (28.984104, 30.0, 28.43973, 30.082137, 15.041069, 13.943036, 14.958931, 13.398661)
RATES = np.array(OMEGA_DEGREES, np.float32) * np.float32(math.pi / 180.0)
STIFF = np.float32(0.2) * (RATES / RATES[0]) ** 2


def sin_cos(angle):
    turn = jnp.floor(angle * (2.0 / math.pi) + 0.5)
    x = ((angle - turn * 1.5703125) - turn * 4.837512969970703125e-4) - turn * 7.54978995489188216e-8
    z = x * x
    s = ((-1.9515295891e-4 * z + 8.3321608736e-3) * z - 1.6666654611e-1) * z * x + x
    c = ((2.443315711809948e-5 * z - 1.388731625493765e-3) * z + 4.166664568298827e-2) * z * z - 0.5 * z + 1.0
    quarter = turn.astype(jnp.int32)
    odd = (quarter & 1) == 1
    sine = jnp.where(odd, c, s)
    cosine = jnp.where(odd, s, c)
    sine = jnp.where((quarter & 2) == 2, -sine, sine)
    cosine = jnp.where(((quarter + 1) & 2) == 2, -cosine, cosine)
    return sine, cosine


def kernel(
    nlat, nlon,
    route_in, tblk_in, depth_in, fric_in, mask_in, forc_in, ocell_in, otime_in, oval_in, oweight_in,
    x_out, r_out,
    route, tblk, depth, fric, mask, forc, ocell, otime, oval, oweight,
    dw, dwn, dws, dwe, dww, wetfric, coef, diag,
    pay, payi, outf, outi, inf, ini, plan, splan, waves, mats, oslot,
    field, seen, r1, p1, q1, z_last, r2, p2, q2, x, turned,
    pk, hq, hq1, hx, hp, hr, hw, surf, surf_pk, surf_hq, sum_a, part_row, ready,
    load, hs, hrv, ss, sr, as_, ar, os_, orv, ds_, dr, loc,
):
    rows, cols = depth.shape
    nblk = cols // BLOCK
    slots = nlon * CAP
    tiles = otime.shape[0]
    me_lat = lax.axis_index("lat")
    me_lon = lax.axis_index("lon")
    north, south = lax.rem(me_lat + 1, nlat), lax.rem(me_lat + nlat - 1, nlat)
    east, west = lax.rem(me_lon + 1, nlon), lax.rem(me_lon + nlon - 1, nlon)
    me = me_lat * nlon + me_lon
    count = nlat * nlon

    barrier = pltpu.get_barrier_semaphore()
    for k in range(1, nlon):
        pl.semaphore_signal(barrier, inc=1, device_id={"lon": lax.rem(me_lon + k, nlon)}, device_id_type=MESH)
    for k in range(1, nlat):
        pl.semaphore_signal(barrier, inc=1, device_id={"lat": lax.rem(me_lat + k, nlat)}, device_id_type=MESH)
    pairs = [
        (route_in, route), (tblk_in, tblk), (ocell_in, ocell), (otime_in, otime), (oval_in, oval),
        (oweight_in, oweight), (depth_in, depth), (mask_in, mask), (fric_in, fric), (forc_in, forc),
    ]
    loads = [pltpu.make_async_copy(src, dst, load.at[k]) for k, (src, dst) in enumerate(pairs)]
    for c in loads:
        c.start()

    def remote(src, dst, send, recv, where):
        return pltpu.make_async_remote_copy(
            src_ref=src, dst_ref=dst, send_sem=send, recv_sem=recv, device_id=where, device_id_type=MESH
        )

    lane = lax.broadcasted_iota(jnp.int32, (1, BLOCK), 1)
    lane8 = lax.broadcasted_iota(jnp.int32, (8, BLOCK), 1)
    sub8 = lax.broadcasted_iota(jnp.int32, (8, BLOCK), 0)
    zero = jnp.zeros((2, 8, BLOCK), jnp.float32)

    for c in loads[:8]:
        c.wait()
    wet = mask[...].astype(jnp.float32)
    dw[...] = depth[...] * wet

    for t in range(tiles):
        pay[t] = jnp.concatenate([otime[t : t + 1], oval[t : t + 1], oweight[t : t + 1], oval[t : t + 1]] * 2, axis=0)
        payi[t] = jnp.broadcast_to(ocell[t : t + 1] + tblk[t] * BLOCK, (8, BLOCK))
    pay[tiles] = jnp.zeros((8, BLOCK), jnp.float32)
    payi[tiles] = jnp.zeros((8, BLOCK), jnp.int32)

    def pick(p, carry):
        first, second = jnp.int32(tiles), jnp.int32(tiles)
        for t in reversed(range(tiles)):
            hit = route[t] == p
            second = jnp.where(hit, first, second)
            first = jnp.where(hit, jnp.int32(t), first)
        outf[p] = jnp.where(sub8 < 4, pay[first], pay[second])
        outi[p] = jnp.where(sub8 == 0, payi[first], payi[second])
        return carry

    lax.fori_loop(0, nlon, pick, 0)
    pl.semaphore_wait(barrier, nlon + nlat - 2)

    def obs_copy(k):
        peer = lax.rem(me_lon + k, nlon)
        return [
            remote(outf.at[peer], inf.at[me_lon], os_.at[0, peer], orv.at[0, me_lon], {"lon": peer}),
            remote(outi.at[peer], ini.at[me_lon], os_.at[1, peer], orv.at[1, me_lon], {"lon": peer}),
        ]

    def obs_wait(k):
        peer = lax.rem(me_lon + k, nlon)
        remote(outf.at[peer], inf.at[peer], os_.at[0, peer], orv.at[0, peer], {"lon": peer}).wait_recv()
        remote(outi.at[peer], ini.at[peer], os_.at[1, peer], orv.at[1, peer], {"lon": peer}).wait_recv()

    obs_sends = [c for k in range(1, nlon) for c in obs_copy(k)]
    for c in obs_sends:
        c.start()
    first_copies = [
        remote(dw.at[:, pl.ds(0, BLOCK)], dwe, ds_.at[2], dr.at[2], {"lon": west}),
        remote(dw.at[:, pl.ds(cols - BLOCK, BLOCK)], dww, ds_.at[3], dr.at[3], {"lon": east}),
        remote(dw, dws, ds_.at[0], dr.at[0], {"lat": north}),
        remote(dw, dwn, ds_.at[1], dr.at[1], {"lat": south}),
    ]
    for c in first_copies:
        c.start()
    for k in range(1, nlat):
        pl.semaphore_signal(ready, inc=1, device_id={"lat": lax.rem(me_lat + k, nlat)}, device_id_type=MESH)
    inf[me_lon] = outf[me_lon]
    ini[me_lon] = outi[me_lon]
    for c in loads[8:]:
        c.wait()

    for cb in range(nblk):
        at = pl.ds(cb * BLOCK, BLOCK)
        for h in range(2):
            wetted = forc[h, :, :, at] * wet[None, :, cb * BLOCK : cb * BLOCK + BLOCK]
            field[0, pl.ds(1, rows), cb, h] = jnp.swapaxes(wetted, 0, 1)
    oslot[slots] = zero
    mats[slots] = jnp.zeros((256, BLOCK), jnp.float32)
    stiff = jnp.zeros((8, 1), jnp.float32)
    rate = jnp.zeros((8, BLOCK), jnp.float32)
    sub1 = lax.broadcasted_iota(jnp.int32, (8, 1), 0)
    for c in range(8):
        stiff = jnp.where(sub1 == c, float(STIFF[c]), stiff)
        rate = jnp.where(sub8 == c, float(RATES[c]), rate)
    cells = lax.broadcasted_iota(jnp.int32, (BLOCK, BLOCK), 0)

    for k in range(1, nlon):
        obs_wait(k)

    def where_is(s):
        return ini[s // CAP, pl.ds(s % CAP, 1), :]

    rep = jnp.full((1, BLOCK), slots, jnp.int32)
    homes = jnp.full((1, BLOCK), -1, jnp.int32)
    for s in reversed(range(slots)):
        home = where_is(s) >> 7
        rep = jnp.where(home == lane, s, rep)
        homes = jnp.where(lane == s, home, homes)
    chain = jnp.full((1, BLOCK), slots, jnp.int32)
    for s in reversed(range(slots)):
        home = where_is(s) >> 7
        chain = jnp.where((home == homes) & (lane < s), s, chain)
    plan[...] = jnp.where(
        sub8 == 0,
        jnp.broadcast_to(homes, (8, BLOCK)),
        jnp.where(sub8 == 1, jnp.broadcast_to(chain, (8, BLOCK)), jnp.broadcast_to(rep, (8, BLOCK))),
    )
    to_scalars = pltpu.make_async_copy(plan, splan, loc.at[0])
    to_scalars.start()

    def onto_cells(o, k, terms):
        cell = ini[o, pl.ds(k, 1), :] & (BLOCK - 1)
        high = terms.astype(jnp.bfloat16)
        low = (terms - high.astype(jnp.float32)).astype(jnp.bfloat16)
        hot = (cells == cell).astype(jnp.float32).astype(jnp.bfloat16)
        return lax.dot_general(
            jnp.concatenate([high, low], axis=1),
            jnp.concatenate([hot, hot], axis=1),
            (((1,), (1,)), ((), ())),
            preferred_element_type=jnp.float32,
        )

    def values(o, carry):
        for k in range(CAP):
            times = inf[o, pl.ds(4 * k, 1), :]
            scaled = inf[o, pl.ds(4 * k + 2, 1), :] * inf[o, pl.ds(4 * k + 1, 1), :]
            sine, cosine = sin_cos(rate * times)
            waves[o * CAP + k, 0] = cosine
            waves[o * CAP + k, 1] = sine
            terms = jnp.concatenate([cosine * scaled, sine * scaled], axis=0)
            oslot[o * CAP + k] = onto_cells(o, k, terms).reshape(2, 8, BLOCK)
        return carry

    lax.fori_loop(0, nlon, values, 0, unroll=4)
    to_scalars.wait()

    def join_values(i, carry):
        s = slots - 1 - i
        oslot[s] = oslot[s] + oslot[splan[1, s]]
        return carry

    lax.fori_loop(0, slots, join_values, 0)

    def pack(row, col, value, packed):
        shift = row if col == 0 else row + 1
        moved = pltpu.roll(value, shift, 2)
        return jnp.where(lane8 == row, moved, packed)

    def pack_ends(row, first, last, carry):
        return pack(row, 0, first, carry[0]), pack(row, 1, last, carry[1])

    def keep_ends(k, ends):
        pk[k, 0] = ends[0]
        pk[k, 1] = ends[1]

    def start_rhs(row, ends):
        v = []
        for cb in range(nblk):
            v.append(field[0, row + 1, cb] + oslot[splan[2, row * nblk + cb]])
            field[0, row + 1, cb] = v[cb]
            seen[row * nblk + cb] = v[cb]
        return pack_ends(row, v[0], v[-1], ends)

    keep_ends(0, lax.fori_loop(0, rows, start_rhs, (zero, zero)))

    def halo(k):
        return [
            remote(pk.at[k, 0], hq.at[k, 1], hs.at[k, 2], hrv.at[k, 2], {"lon": west}),
            remote(pk.at[k, 1], hq.at[k, 0], hs.at[k, 3], hrv.at[k, 3], {"lon": east}),
            remote(field.at[k, 1], field.at[k, rows + 1], hs.at[k, 0], hrv.at[k, 0], {"lat": south}),
            remote(field.at[k, rows], field.at[k, 0], hs.at[k, 1], hrv.at[k, 1], {"lat": north}),
        ]

    def send_halo(k):
        for c in halo(k):
            c.start()

    def wait_halo(k):
        for c in halo(k):
            c.wait_recv()

    send_halo(0)

    for c in first_copies:
        c.wait_recv()
    a = dw[...]
    colid = lax.broadcasted_iota(jnp.int32, (rows, cols), 1)
    rowid = lax.broadcasted_iota(jnp.int32, (rows, cols), 0)
    keep_n = (me_lat < nlat - 1).astype(jnp.float32)
    keep_s = (me_lat > 0).astype(jnp.float32)

    def harmonic(first, second):
        return 2.0 * first * second / jnp.maximum(first + second, 0.5)

    drag = fric[...]
    total = wet * drag + (1.0 - wet)
    around = (
        lambda: jnp.where(colid == cols - 1, dwe[:, 0:1], pltpu.roll(a, cols - 1, 1)),
        lambda: jnp.where(colid == 0, dww[:, BLOCK - 1 : BLOCK], pltpu.roll(a, 1, 1)),
        lambda: jnp.where(rowid == rows - 1, dwn[0:1, :] * keep_n, pltpu.roll(a, rows - 1, 0)),
        lambda: jnp.where(rowid == 0, dws[rows - 1 : rows, :] * keep_s, pltpu.roll(a, 1, 0)),
    )
    for k in range(4):
        side = harmonic(a, around[k]())
        total = total + side
        for row in range(rows):
            coef[k, row] = jnp.broadcast_to(side[row : row + 1], (8, cols))
    dragged = wet * drag
    for row in range(rows):
        wetfric[row] = jnp.broadcast_to(dragged[row : row + 1], (8, cols))
        wide = jnp.broadcast_to(wet[row : row + 1], (8, cols))
        diag[row] = wide * stiff + jnp.broadcast_to(total[row : row + 1], (8, cols))

    def build(o, carry):
        for k in range(CAP):
            weight = inf[o, pl.ds(4 * k + 2, 1), :]
            basis = (waves[o * CAP + k, 0], waves[o * CAP + k, 1])
            parts = []
            for h in range(2):
                for c in range(8):
                    one = weight * basis[h][c : c + 1]
                    parts.append(one * basis[0])
                    parts.append(one * basis[1])
            mats[o * CAP + k] = onto_cells(o, k, jnp.concatenate(parts, axis=0))
        return carry

    lax.fori_loop(0, nlon, build, 0)

    def join_mats(i, carry):
        s = slots - 1 - i
        mats[s] = mats[s] + mats[splan[1, s]]
        return carry

    lax.fori_loop(0, slots, join_mats, 0)

    def observe():
        def slot(s, carry):
            v = seen[splan[0, s]]
            acc = [zero, zero]
            for c in range(16):
                m = mats[s, 16 * c : 16 * c + 16, :].reshape(2, 8, BLOCK)
                acc[c % 2] = acc[c % 2] + m * v[c // 8, c % 8 : c % 8 + 1, :]
            oslot[s] = acc[0] + acc[1]
            return carry

        lax.fori_loop(0, slots, slot, 0, unroll=2)

    def eastward(v, beyond):
        moved = [pltpu.roll(b, BLOCK - 1, 2) for b in v] + [beyond]
        return [jnp.where(lane8 == BLOCK - 1, moved[cb + 1], moved[cb]) for cb in range(nblk)]

    def westward(v, beyond):
        moved = [beyond] + [pltpu.roll(b, 1, 2) for b in v]
        return [jnp.where(lane8 == 0, moved[cb], moved[cb + 1]) for cb in range(nblk)]

    def from_east(halos, row):
        return pltpu.roll(halos[1], BLOCK - 1 - row, 2)

    def from_west(halos, row):
        return pltpu.roll(halos[0], BLOCK - row, 2)

    def image_row(src, row, east_side, west_side, to_north=True, to_south=True):
        v = [src[row + 1, cb] for cb in range(nblk)]
        e = eastward(v, east_side)
        w = westward(v, west_side)
        images = []
        for cb in range(nblk):
            at = pl.ds(cb * BLOCK, BLOCK)
            image = (
                diag[row, :, at] * v[cb]
                - coef[0, row, :, at] * e[cb]
                - coef[1, row, :, at] * w[cb]
                + oslot[splan[2, row * nblk + cb]]
            )
            if to_north:
                image = image - coef[2, row, :, at] * src[row + 2, cb]
            if to_south:
                image = image - coef[3, row, :, at] * src[row, cb]
            images.append(image)
        return v, images

    def inside(src, dst):
        def put(row, images):
            for cb in range(nblk):
                dst[row + 1, cb] = images[cb]

        def line(row, carry):
            put(row, image_row(src, row, zero, zero)[1])
            return carry

        lax.fori_loop(1, rows - 1, line, 0)
        put(0, image_row(src, 0, zero, zero, to_south=False)[1])
        put(rows - 1, image_row(src, rows - 1, zero, zero, to_north=False)[1])

    def edges(src, halos, dst):
        for cb in range(nblk):
            at = pl.ds(cb * BLOCK, BLOCK)
            dst[1, cb] = dst[1, cb] - coef[3, 0, :, at] * src[0, cb]
            dst[rows, cb] = dst[rows, cb] - coef[2, rows - 1, :, at] * src[rows + 1, cb]

        def mend(row, carry):
            last = pl.ds(cols - BLOCK, BLOCK)
            dst[row + 1, 0] = dst[row + 1, 0] - coef[1, row, :, pl.ds(0, BLOCK)] * jnp.where(
                lane8 == 0, from_west(halos, row), 0.0
            )
            dst[row + 1, nblk - 1] = dst[row + 1, nblk - 1] - coef[0, row, :, last] * jnp.where(
                lane8 == BLOCK - 1, from_east(halos, row), 0.0
            )
            return carry

        lax.fori_loop(0, rows, mend, 0)

    def sum_copy(i, k):
        peer = lax.rem(me + k, count)
        where = {"lat": peer // nlon, "lon": lax.rem(peer, nlon)}
        return remote(part_row.at[i], sum_a.at[i, pl.ds(me, 1)], as_.at[i], ar.at[i], where)

    def sum_wait(i):
        whole = sum_a.at[i, pl.ds(0, count - 1)]
        return remote(whole, whole, as_.at[i], ar.at[i], {"lat": south})

    def send_sums(i, sums):
        part = jnp.zeros((8, BLOCK), jnp.float32)
        for k, s in enumerate(sums):
            part = jnp.where(sub8 == k, jnp.sum(s[0] + s[1], axis=0, keepdims=True), part)
        part = part + pltpu.roll(part, 64, 1)
        part = part + pltpu.roll(part, 32, 1)
        row = jnp.sum(jnp.where(lane8 >> 5 == sub8, part, 0.0), axis=0, keepdims=True)
        part_row[i] = row
        sum_a[i, pl.ds(me, 1)] = row

        def send(k, carry):
            sum_copy(i, k).start()
            return carry

        lax.fori_loop(1, count, send, 0, unroll=True)

    def take_sums(i):
        sum_wait(i).wait_recv()
        total = jnp.sum(sum_a[i], axis=0, keepdims=True)
        whole = jnp.sum(jnp.where(lane8 >> 5 == sub8, total, 0.0), axis=1, keepdims=True)
        return [jnp.broadcast_to(whole[k : k + 1], (8, BLOCK)) for k in range(4)]

    def beta_of(size, rr, rq, qq):
        return (rr - 2.0 * size * rq + size * size * qq) / rr

    def pack_field(src):
        def line(row, ends):
            return pack_ends(row, src[row + 1, 0], src[row + 1, nblk - 1], ends)

        return lax.fori_loop(0, rows, line, (zero, zero))

    def outer(o):
        k0, kq, kz = 4 * o, 4 * o + 1, 4 * o + 2
        i0, i1, i2 = ITERS * o, ITERS * o + 1, ITERS * o + 2
        r0, q0, z0 = field.at[k0], field.at[kq], field.at[kz]
        z1 = field.at[3] if o == 0 else z_last
        observe()
        if o == 0:
            inside(r0, q0)
            wait_halo(k0)
            edges(r0, hq.at[k0], q0)

        def first_dots(row, carry):
            ends, rr, rq, qq = carry
            if o == 0:
                v = [r0[row + 1, cb] for cb in range(nblk)]
                images = [q0[row + 1, cb] for cb in range(nblk)]
            else:
                v, images = image_row(r0, row, from_east(hq.at[k0], row), from_west(hq.at[k0], row))
            for cb in range(nblk):
                res, image = v[cb], images[cb]
                if o > 0:
                    q0[row + 1, cb] = image
                rr = rr + res * res
                rq = rq + res * image
                qq = qq + image * image
            return pack_ends(row, images[0], images[-1], ends), rr, rq, qq

        ends, *sums = lax.fori_loop(0, rows, first_dots, ((zero, zero), zero, zero, zero))
        keep_ends(kq, ends)
        if o == 0:
            pl.semaphore_wait(ready, nlat - 1)
        send_sums(i0, sums)
        send_halo(kq)

        def look(row, carry):
            for cb in range(nblk):
                seen[row * nblk + cb] = q0[row + 1, cb]
            return carry

        lax.fori_loop(0, rows, look, 0)
        observe()
        inside(q0, z0)
        wait_halo(kq)
        edges(q0, hq.at[kq], z0)

        keep_ends(kz, pack_field(z0))
        send_halo(kz)
        rr, rq, qq, _ = take_sums(i0)
        size0 = rr / rq
        beta0 = beta_of(size0, rr, rq, qq)
        more = 1.0 + beta0

        def second(row, carry):
            rr, rq, dq, qq = carry
            for cb in range(nblk):
                r, q, z = r0[row + 1, cb], q0[row + 1, cb], z0[row + 1, cb]
                res = r - size0 * q
                way = res + beta0 * r
                image = more * q - size0 * z
                r1[row + 1, cb] = res
                p1[row + 1, cb] = way
                q1[row + 1, cb] = image
                seen[row * nblk + cb] = image
                rr = rr + res * res
                rq = rq + res * image
                dq = dq + way * image
                qq = qq + image * image
            return rr, rq, dq, qq

        send_sums(i1, lax.fori_loop(0, rows, second, (zero,) * 4))
        observe()
        inside(q1, z1)
        wait_halo(kz)
        for edge in (0, rows + 1):
            for cb in range(nblk):
                q1[edge, cb] = more * q0[edge, cb] - size0 * z0[edge, cb]
        hq1[...] = more * hq[kq] - size0 * hq[kz]
        edges(q1, hq1, z1)
        if o == 0:
            keep_ends(3, pack_field(z1))
            send_halo(3)
        rr, rq, dq, qq = take_sums(i1)
        size1 = rr / dq
        beta1 = beta_of(size1, rr, rq, qq)

        def third(row, carry):
            rr, dq = carry
            for cb in range(nblk):
                q = q1[row + 1, cb]
                res = r1[row + 1, cb] - size1 * q
                way = res + beta1 * p1[row + 1, cb]
                image = ((q0[row + 1, cb] - size0 * z0[row + 1, cb]) - size1 * z1[row + 1, cb]) + beta1 * q
                r2[row + 1, cb] = res
                p2[row + 1, cb] = way
                q2[row + 1, cb] = image
                rr = rr + res * res
                dq = dq + way * image
            return rr, dq

        send_sums(i2, lax.fori_loop(0, rows, third, (zero,) * 2))
        return size0, beta0, size1, beta1

    size0, beta0, size1, beta1 = outer(0)
    for c in obs_sends + first_copies:
        c.wait_send()

    def beyond(r, q, q_next):
        res = r - size0 * q
        way = res + beta0 * r
        res = res - size1 * q_next
        return size0 * r + size1 * way, res + beta1 * way, res

    for edge in (0, rows + 1):
        for cb in range(nblk):
            x[edge, cb], p2[edge, cb], r2[edge, cb] = beyond(field[0, edge, cb], field[1, edge, cb], q1[edge, cb])
    hx[...], hp[...], hr[...] = beyond(hq[0], hq[1], hq1[...])

    def advance(row, carry):
        for cb in range(nblk):
            x[row + 1, cb] = size0 * field[0, row + 1, cb] + size1 * p1[row + 1, cb]
        return carry

    lax.fori_loop(0, rows, advance, 0)

    def add_up(square):
        return jnp.sum(square[0] + square[1], axis=0, keepdims=True)

    def surface(row, cb):
        at = pl.ds(cb * BLOCK, BLOCK)
        flux = []
        for ref, halos in ((x, hx), (p2, hp)):
            v = ref[row + 1, cb]
            after = pltpu.roll(ref[row + 1, cb + 1], BLOCK - 1, 2) if cb < nblk - 1 else from_east(halos, row)
            e = jnp.where(lane8 == BLOCK - 1, after, pltpu.roll(v, BLOCK - 1, 2))
            flux.append((coef[0, row, :, at] * (e - v), coef[2, row, :, at] * (ref[row + 2, cb] - v)))
        (xe, xn), (pe, pn) = flux
        parts = jnp.where(sub8 == 0, add_up(xe * xe + xn * xn), wetfric[row, :, at])
        parts = jnp.where(sub8 == 1, add_up(xe * pe + xn * pn), parts)
        parts = jnp.where(sub8 == 2, add_up(pe * pe + pn * pn), parts)
        surf[row + 1, :, at] = parts
        return parts

    def surface_ends(row, ends):
        first, last = surface(row, 0), surface(row, nblk - 1)
        return (
            jnp.where(lane8 == row, pltpu.roll(first, row, 1), ends[0]),
            jnp.where(lane8 == row, pltpu.roll(last, row + 1, 1), ends[1]),
        )

    blank = jnp.zeros((8, BLOCK), jnp.float32)
    ends = lax.fori_loop(0, rows, surface_ends, (blank, blank))
    surf_pk[0] = ends[0]
    surf_pk[1] = ends[1]
    surf_copies = [
        remote(surf_pk.at[0], surf_hq.at[1], ss.at[2], sr.at[2], {"lon": west}),
        remote(surf_pk.at[1], surf_hq.at[0], ss.at[3], sr.at[3], {"lon": east}),
        remote(surf.at[1], surf.at[rows + 1], ss.at[0], sr.at[0], {"lat": south}),
        remote(surf.at[rows], surf.at[0], ss.at[1], sr.at[1], {"lat": north}),
    ]
    for c in surf_copies[:2]:
        c.start()

    def surface_middle(row, carry):
        for cb in range(1, nblk - 1):
            surface(row, cb)
        return carry

    lax.fori_loop(0, rows, surface_middle, 0)
    for c in surf_copies[2:]:
        c.start()
    wait_halo(3)

    def image_beyond(q, z, z_next, q_next):
        return ((q - size0 * z) - size1 * z_next) + beta1 * q_next

    for edge in (0, rows + 1):
        for cb in range(nblk):
            q2[edge, cb] = image_beyond(field[1, edge, cb], field[2, edge, cb], field[3, edge, cb], q1[edge, cb])
    hw[...] = image_beyond(hq[1], hq[2], hq[3], hq1[...])
    for c in surf_copies:
        c.wait_recv()
    rr, dq, _, _ = take_sums(2)
    size2 = rr / dq
    ramp = jnp.where(sub8 == 0, 1.0, jnp.where(sub8 == 1, 2.0 * size2, jnp.where(sub8 == 2, size2 * size2, 0.0)))

    def extra_of(parts):
        speed = jnp.maximum(jnp.sum(parts * ramp, axis=0, keepdims=True), 0.0)
        return parts[3:4] * (jnp.sqrt(1.0 + speed / 16.0) - 1.0)

    def renew(row, cb):
        extra = extra_of(surf[row, :, pl.ds(cb * BLOCK, BLOCK)])
        place = x[row, cb] + size2 * p2[row, cb]
        new = (r2[row, cb] - size2 * q2[row, cb]) - extra * place
        field[4, row, cb] = new
        return extra, place, new

    def friction(row, carry):
        for cb in range(nblk):
            at = pl.ds(cb * BLOCK, BLOCK)
            extra, place, new = renew(row + 1, cb)
            x[row + 1, cb] = place
            diag[row, :, at] = diag[row, :, at] + extra
            seen[row * nblk + cb] = new
        return carry

    lax.fori_loop(0, rows, friction, 0)
    for edge in (0, rows + 1):
        for cb in range(nblk):
            renew(edge, cb)
    for side in range(2):
        hq[4, side] = (hr[side] - size2 * hw[side]) - extra_of(surf_hq[side]) * (hx[side] + size2 * hp[side])
    size0, beta0, size1, beta1 = outer(1)

    def advance_last(row, carry):
        for cb in range(nblk):
            x[row + 1, cb] = (x[row + 1, cb] + size0 * field[4, row + 1, cb]) + size1 * p1[row + 1, cb]
        return carry

    lax.fori_loop(0, rows, advance_last, 0)
    for n, src in enumerate((x, p2, r2, q2)):
        for cb in range(nblk):
            for h in range(2):
                turned[n, h, :, :, pl.ds(cb * BLOCK, BLOCK)] = jnp.swapaxes(src[pl.ds(1, rows), cb, h], 0, 1)
    for k in (0, 1, 2, 3, 5, 6):
        for c in halo(k):
            c.wait_send()
    for c in surf_copies:
        c.wait_send()
    rr, dq, _, _ = take_sums(SUMS - 1)
    size2 = rr / dq

    def conclude(c, carry):
        for h in range(2):
            for cb in range(nblk):
                at = pl.ds(cb * BLOCK, BLOCK)
                x_out[h, c, :, at] = turned[0, h, c, :, at] + size2 * turned[1, h, c, :, at]
                r_out[h, c, :, at] = turned[2, h, c, :, at] - size2 * turned[3, h, c, :, at]
        return carry

    lax.fori_loop(0, 8, conclude, 0)
    for i in range(SUMS):
        sum_wait(i).wait_send()


def shards(nlat, nlon, depth, friction, ocean_mask, forcing, tile_route, tile_block, obs_cell, obs_time, obs_value, obs_weight):
    channels, rows, cols = forcing.shape
    slots = nlon * CAP
    nblk, tiles = cols // BLOCK, obs_time.shape[0]
    f32, i32 = jnp.float32, jnp.int32
    vmem, smem = pltpu.VMEM, pltpu.SMEM
    hbm = pl.BlockSpec(memory_space=pltpu.HBM)
    field = (rows + 2, nblk, 2, 8, BLOCK)
    ends = (2, 2, 8, BLOCK)
    split = (2, channels // 2, rows, cols)
    dma = pltpu.SemaphoreType.DMA
    scratch = [
        smem((tiles,), i32),
        smem((tiles,), i32),
        vmem((rows, cols), f32),
        vmem((rows, cols), f32),
        vmem((rows, cols), i32),
        vmem(split, f32),
        vmem((tiles, BLOCK), i32),
        vmem((tiles, BLOCK), f32),
        vmem((tiles, BLOCK), f32),
        vmem((tiles, BLOCK), f32),
        vmem((rows, cols), f32),
        vmem((rows, cols), f32),
        vmem((rows, cols), f32),
        vmem((rows, BLOCK), f32),
        vmem((rows, BLOCK), f32),
        vmem((rows, 8, cols), f32),
        vmem((4, rows, 8, cols), f32),
        vmem((rows, 8, cols), f32),
        vmem((tiles + 1, 8, BLOCK), f32),
        vmem((tiles + 1, 8, BLOCK), i32),
        vmem((nlon, 8, BLOCK), f32),
        vmem((nlon, 8, BLOCK), i32),
        vmem((nlon, 8, BLOCK), f32),
        vmem((nlon, 8, BLOCK), i32),
        vmem((8, BLOCK), i32),
        smem((8, BLOCK), i32),
        vmem((slots, 2, 8, BLOCK), f32),
        vmem((slots + 1, 256, BLOCK), f32),
        vmem((slots + 1, 2, 8, BLOCK), f32),
        vmem((HALOS,) + field, f32),
        vmem((rows * nblk, 2, 8, BLOCK), f32),
        vmem(field, f32),
        vmem(field, f32),
        vmem(field, f32),
        vmem(field, f32),
        vmem(field, f32),
        vmem(field, f32),
        vmem(field, f32),
        vmem(field, f32),
        vmem((4,) + split, f32),
        vmem((HALOS,) + ends, f32),
        vmem((HALOS,) + ends, f32),
        vmem(ends, f32),
        vmem(ends, f32),
        vmem(ends, f32),
        vmem(ends, f32),
        vmem(ends, f32),
        vmem((rows + 2, 8, cols), f32),
        vmem((2, 8, BLOCK), f32),
        vmem((2, 8, BLOCK), f32),
        vmem((SUMS, nlat * nlon, BLOCK), f32),
        vmem((SUMS, 1, BLOCK), f32),
        pltpu.SemaphoreType.REGULAR,
        dma((10,)),
        dma((HALOS, 4)),
        dma((HALOS, 4)),
        dma((4,)),
        dma((4,)),
        dma((SUMS,)),
        dma((SUMS,)),
        dma((2, nlon)),
        dma((2, nlon)),
        dma((4,)),
        dma((4,)),
        dma((1,)),
    ]
    shape = vmem(split, f32)
    x, r = pl.pallas_call(
        functools.partial(kernel, nlat, nlon),
        out_shape=(shape, shape),
        in_specs=[hbm] * 10,
        out_specs=(pl.BlockSpec(memory_space=vmem), pl.BlockSpec(memory_space=vmem)),
        scratch_shapes=scratch,
        compiler_params=pltpu.CompilerParams(
            collective_id=0, has_side_effects=True, vmem_limit_bytes=62 * 2**20
        ),
    )(
        tile_route.reshape(-1), tile_block, depth, friction, ocean_mask, forcing.reshape(split),
        obs_cell, obs_time, obs_value, obs_weight,
    )
    return x.reshape(forcing.shape), r.reshape(forcing.shape)


def solution(mesh):
    tile = P(("lat", "lon"), None)
    grid = P("lat", "lon")
    in_specs = (grid, grid, grid, P(None, "lat", "lon"), tile, P(("lat", "lon")), tile, tile, tile, tile)
    out_specs = (P(None, "lat", "lon"), P(None, "lat", "lon"))
    body = functools.partial(shards, mesh.shape["lat"], mesh.shape["lon"])
    return jax.shard_map(body, mesh=mesh, in_specs=in_specs, out_specs=out_specs, check_vma=False)
```

```python
import functools
import math

import jax
import jax.numpy as jnp
import numpy as np
from jax import lax
from jax.experimental import pallas as pl
from jax.experimental.pallas import tpu as pltpu
from jax.sharding import PartitionSpec as P

BLOCK = 128
CAP = 2
ITERS = 3
OUTER = 2
SUMS = ITERS * OUTER
HALOS = 7
MESH = pl.DeviceIdType.MESH
OMEGA_DEGREES = (28.984104, 30.0, 28.43973, 30.082137, 15.041069, 13.943036, 14.958931, 13.398661)
RATES = np.array(OMEGA_DEGREES, np.float32) * np.float32(math.pi / 180.0)
STIFF = np.float32(0.2) * (RATES / RATES[0]) ** 2


def sin_cos(angle):
    turn = jnp.floor(angle * (2.0 / math.pi) + 0.5)
    x = ((angle - turn * 1.5703125) - turn * 4.837512969970703125e-4) - turn * 7.54978995489188216e-8
    z = x * x
    s = ((-1.9515295891e-4 * z + 8.3321608736e-3) * z - 1.6666654611e-1) * z * x + x
    c = ((2.443315711809948e-5 * z - 1.388731625493765e-3) * z + 4.166664568298827e-2) * z * z - 0.5 * z + 1.0
    quarter = turn.astype(jnp.int32)
    odd = (quarter & 1) == 1
    sine = jnp.where(odd, c, s)
    cosine = jnp.where(odd, s, c)
    sine = jnp.where((quarter & 2) == 2, -sine, sine)
    cosine = jnp.where(((quarter + 1) & 2) == 2, -cosine, cosine)
    return sine, cosine


def kernel(
    nlat, nlon,
    route_in, tblk_in, depth_in, fric_in, mask_in, forc_in, ocell_in, otime_in, oval_in, oweight_in,
    x_out, r_out,
    route, tblk, depth, fric, mask, forc, ocell, otime, oval, oweight,
    dw, dwn, dws, dwe, dww, wetfric, coef, diag,
    pay, payi, outf, outi, inf, ini, plan, splan, waves, mats, oslot,
    field, seen, r1, p1, q1, z_last, r2, p2, q2, x, turned,
    pk, hq, hq1, hx, hp, hr, hw, surf, surf_pk, surf_hq, sum_a, part_row, ready,
    load, hs, hrv, ss, sr, as_, ar, os_, orv, ds_, dr, loc,
):
    rows, cols = depth.shape
    nblk = cols // BLOCK
    slots = nlon * CAP
    tiles = otime.shape[0]
    me_lat = lax.axis_index("lat")
    me_lon = lax.axis_index("lon")
    north, south = lax.rem(me_lat + 1, nlat), lax.rem(me_lat + nlat - 1, nlat)
    east, west = lax.rem(me_lon + 1, nlon), lax.rem(me_lon + nlon - 1, nlon)
    me = me_lat * nlon + me_lon
    count = nlat * nlon

    barrier = pltpu.get_barrier_semaphore()
    for k in range(1, nlon):
        pl.semaphore_signal(barrier, inc=1, device_id={"lon": lax.rem(me_lon + k, nlon)}, device_id_type=MESH)
    for k in range(1, nlat):
        pl.semaphore_signal(barrier, inc=1, device_id={"lat": lax.rem(me_lat + k, nlat)}, device_id_type=MESH)
    pairs = [
        (route_in, route), (tblk_in, tblk), (ocell_in, ocell), (otime_in, otime), (oval_in, oval),
        (oweight_in, oweight), (depth_in, depth), (mask_in, mask), (fric_in, fric), (forc_in, forc),
    ]
    loads = [pltpu.make_async_copy(src, dst, load.at[k]) for k, (src, dst) in enumerate(pairs)]
    for c in loads:
        c.start()

    def remote(src, dst, send, recv, where):
        return pltpu.make_async_remote_copy(
            src_ref=src, dst_ref=dst, send_sem=send, recv_sem=recv, device_id=where, device_id_type=MESH
        )

    lane = lax.broadcasted_iota(jnp.int32, (1, BLOCK), 1)
    lane8 = lax.broadcasted_iota(jnp.int32, (8, BLOCK), 1)
    sub8 = lax.broadcasted_iota(jnp.int32, (8, BLOCK), 0)
    zero = jnp.zeros((2, 8, BLOCK), jnp.float32)

    for c in loads[:8]:
        c.wait()
    wet = mask[...].astype(jnp.float32)
    dw[...] = depth[...] * wet

    for t in range(tiles):
        pay[t] = jnp.concatenate([otime[t : t + 1], oval[t : t + 1], oweight[t : t + 1], oval[t : t + 1]] * 2, axis=0)
        payi[t] = jnp.broadcast_to(ocell[t : t + 1] + tblk[t] * BLOCK, (8, BLOCK))
    pay[tiles] = jnp.zeros((8, BLOCK), jnp.float32)
    payi[tiles] = jnp.zeros((8, BLOCK), jnp.int32)

    def pick(p, carry):
        first, second = jnp.int32(tiles), jnp.int32(tiles)
        for t in reversed(range(tiles)):
            hit = route[t] == p
            second = jnp.where(hit, first, second)
            first = jnp.where(hit, jnp.int32(t), first)
        outf[p] = jnp.where(sub8 < 4, pay[first], pay[second])
        outi[p] = jnp.where(sub8 == 0, payi[first], payi[second])
        return carry

    lax.fori_loop(0, nlon, pick, 0)
    pl.semaphore_wait(barrier, nlon + nlat - 2)

    def obs_copy(k):
        peer = lax.rem(me_lon + k, nlon)
        return [
            remote(outf.at[peer], inf.at[me_lon], os_.at[0, peer], orv.at[0, me_lon], {"lon": peer}),
            remote(outi.at[peer], ini.at[me_lon], os_.at[1, peer], orv.at[1, me_lon], {"lon": peer}),
        ]

    def obs_wait(k):
        peer = lax.rem(me_lon + k, nlon)
        remote(outf.at[peer], inf.at[peer], os_.at[0, peer], orv.at[0, peer], {"lon": peer}).wait_recv()
        remote(outi.at[peer], ini.at[peer], os_.at[1, peer], orv.at[1, peer], {"lon": peer}).wait_recv()

    obs_sends = [c for k in range(1, nlon) for c in obs_copy(k)]
    for c in obs_sends:
        c.start()
    first_copies = [
        remote(dw.at[:, pl.ds(0, BLOCK)], dwe, ds_.at[2], dr.at[2], {"lon": west}),
        remote(dw.at[:, pl.ds(cols - BLOCK, BLOCK)], dww, ds_.at[3], dr.at[3], {"lon": east}),
        remote(dw, dws, ds_.at[0], dr.at[0], {"lat": north}),
        remote(dw, dwn, ds_.at[1], dr.at[1], {"lat": south}),
    ]
    for c in first_copies:
        c.start()
    for k in range(1, nlat):
        pl.semaphore_signal(ready, inc=1, device_id={"lat": lax.rem(me_lat + k, nlat)}, device_id_type=MESH)
    inf[me_lon] = outf[me_lon]
    ini[me_lon] = outi[me_lon]
    for c in loads[8:]:
        c.wait()

    for cb in range(nblk):
        at = pl.ds(cb * BLOCK, BLOCK)
        for h in range(2):
            wetted = forc[h, :, :, at] * wet[None, :, cb * BLOCK : cb * BLOCK + BLOCK]
            field[0, pl.ds(1, rows), cb, h] = jnp.swapaxes(wetted, 0, 1)
    oslot[slots] = zero
    mats[slots] = jnp.zeros((256, BLOCK), jnp.float32)
    stiff = jnp.zeros((8, 1), jnp.float32)
    rate = jnp.zeros((8, BLOCK), jnp.float32)
    sub1 = lax.broadcasted_iota(jnp.int32, (8, 1), 0)
    for c in range(8):
        stiff = jnp.where(sub1 == c, float(STIFF[c]), stiff)
        rate = jnp.where(sub8 == c, float(RATES[c]), rate)
    cells = lax.broadcasted_iota(jnp.int32, (BLOCK, BLOCK), 0)

    for k in range(1, nlon):
        obs_wait(k)

    def where_is(s):
        return ini[s // CAP, pl.ds(s % CAP, 1), :]

    rep = jnp.full((1, BLOCK), slots, jnp.int32)
    homes = jnp.full((1, BLOCK), -1, jnp.int32)
    for s in reversed(range(slots)):
        home = where_is(s) >> 7
        rep = jnp.where(home == lane, s, rep)
        homes = jnp.where(lane == s, home, homes)
    chain = jnp.full((1, BLOCK), slots, jnp.int32)
    for s in reversed(range(slots)):
        home = where_is(s) >> 7
        chain = jnp.where((home == homes) & (lane < s), s, chain)
    plan[...] = jnp.where(
        sub8 == 0,
        jnp.broadcast_to(homes, (8, BLOCK)),
        jnp.where(sub8 == 1, jnp.broadcast_to(chain, (8, BLOCK)), jnp.broadcast_to(rep, (8, BLOCK))),
    )
    to_scalars = pltpu.make_async_copy(plan, splan, loc.at[0])
    to_scalars.start()

    def onto_cells(o, k, terms):
        cell = ini[o, pl.ds(k, 1), :] & (BLOCK - 1)
        high = terms.astype(jnp.bfloat16)
        low = (terms - high.astype(jnp.float32)).astype(jnp.bfloat16)
        hot = (cells == cell).astype(jnp.float32).astype(jnp.bfloat16)
        return lax.dot_general(
            jnp.concatenate([high, low], axis=1),
            jnp.concatenate([hot, hot], axis=1),
            (((1,), (1,)), ((), ())),
            preferred_element_type=jnp.float32,
        )

    def values(o, carry):
        for k in range(CAP):
            times = inf[o, pl.ds(4 * k, 1), :]
            scaled = inf[o, pl.ds(4 * k + 2, 1), :] * inf[o, pl.ds(4 * k + 1, 1), :]
            sine, cosine = sin_cos(rate * times)
            waves[o * CAP + k, 0] = cosine
            waves[o * CAP + k, 1] = sine
            terms = jnp.concatenate([cosine * scaled, sine * scaled], axis=0)
            oslot[o * CAP + k] = onto_cells(o, k, terms).reshape(2, 8, BLOCK)
        return carry

    lax.fori_loop(0, nlon, values, 0, unroll=4)
    to_scalars.wait()

    def join_values(i, carry):
        s = slots - 1 - i
        oslot[s] = oslot[s] + oslot[splan[1, s]]
        return carry

    lax.fori_loop(0, slots, join_values, 0)

    def keep_ends(k, src):
        for side, cb in enumerate((0, nblk - 1)):
            packed = zero
            for row in range(rows):
                moved = pltpu.roll(src[row + 1, cb], (row + side) % BLOCK, 2)
                packed = jnp.where(lane8 == row, moved, packed)
            pk[k, side] = packed

    def start_rhs(row, carry):
        for cb in range(nblk):
            v = field[0, row + 1, cb] + oslot[splan[2, row * nblk + cb]]
            field[0, row + 1, cb] = v
            seen[row * nblk + cb] = v
        return carry

    lax.fori_loop(0, rows, start_rhs, 0, unroll=2)
    keep_ends(0, field.at[0])

    def halo(k):
        return [
            remote(pk.at[k, 0], hq.at[k, 1], hs.at[k, 2], hrv.at[k, 2], {"lon": west}),
            remote(pk.at[k, 1], hq.at[k, 0], hs.at[k, 3], hrv.at[k, 3], {"lon": east}),
            remote(field.at[k, 1], field.at[k, rows + 1], hs.at[k, 0], hrv.at[k, 0], {"lat": south}),
            remote(field.at[k, rows], field.at[k, 0], hs.at[k, 1], hrv.at[k, 1], {"lat": north}),
        ]

    def send_halo(k, part=slice(None)):
        for c in halo(k)[part]:
            c.start()

    def wait_halo(k):
        for c in halo(k):
            c.wait_recv()

    send_halo(0)

    for c in first_copies:
        c.wait_recv()
    a = dw[...]
    colid = lax.broadcasted_iota(jnp.int32, (rows, cols), 1)
    rowid = lax.broadcasted_iota(jnp.int32, (rows, cols), 0)
    keep_n = (me_lat < nlat - 1).astype(jnp.float32)
    keep_s = (me_lat > 0).astype(jnp.float32)

    def harmonic(first, second):
        return 2.0 * first * second / jnp.maximum(first + second, 0.5)

    drag = fric[...]
    total = wet * drag + (1.0 - wet)
    around = (
        lambda: jnp.where(colid == cols - 1, dwe[:, 0:1], pltpu.roll(a, cols - 1, 1)),
        lambda: jnp.where(colid == 0, dww[:, BLOCK - 1 : BLOCK], pltpu.roll(a, 1, 1)),
        lambda: jnp.where(rowid == rows - 1, dwn[0:1, :] * keep_n, pltpu.roll(a, rows - 1, 0)),
        lambda: jnp.where(rowid == 0, dws[rows - 1 : rows, :] * keep_s, pltpu.roll(a, 1, 0)),
    )
    for k in range(4):
        side = harmonic(a, around[k]())
        total = total + side
        for row in range(rows):
            coef[k, row] = jnp.broadcast_to(side[row : row + 1], (8, cols))
    dragged = wet * drag
    for row in range(rows):
        wetfric[row] = jnp.broadcast_to(dragged[row : row + 1], (8, cols))
        wide = jnp.broadcast_to(wet[row : row + 1], (8, cols))
        diag[row] = wide * stiff + jnp.broadcast_to(total[row : row + 1], (8, cols))

    def build(o, carry):
        for k in range(CAP):
            weight = inf[o, pl.ds(4 * k + 2, 1), :]
            basis = (waves[o * CAP + k, 0], waves[o * CAP + k, 1])
            parts = []
            for h in range(2):
                for c in range(8):
                    one = weight * basis[h][c : c + 1]
                    parts.append(one * basis[0])
                    parts.append(one * basis[1])
            mats[o * CAP + k] = onto_cells(o, k, jnp.concatenate(parts, axis=0))
        return carry

    lax.fori_loop(0, nlon, build, 0)

    def join_mats(i, carry):
        s = slots - 1 - i
        mats[s] = mats[s] + mats[splan[1, s]]
        return carry

    lax.fori_loop(0, slots, join_mats, 0)

    def observe():
        def slot(s, carry):
            v = seen[splan[0, s]]
            acc = [zero, zero]
            for c in range(16):
                m = mats[s, 16 * c : 16 * c + 16, :].reshape(2, 8, BLOCK)
                acc[c % 2] = acc[c % 2] + m * v[c // 8, c % 8 : c % 8 + 1, :]
            oslot[s] = acc[0] + acc[1]
            return carry

        lax.fori_loop(0, slots, slot, 0, unroll=2)

    def eastward(v, beyond):
        moved = [pltpu.roll(b, BLOCK - 1, 2) for b in v] + [beyond]
        return [jnp.where(lane8 == BLOCK - 1, moved[cb + 1], moved[cb]) for cb in range(nblk)]

    def westward(v, beyond):
        moved = [beyond] + [pltpu.roll(b, 1, 2) for b in v]
        return [jnp.where(lane8 == 0, moved[cb], moved[cb + 1]) for cb in range(nblk)]

    def from_east(halos, row):
        return pltpu.roll(halos[1], BLOCK - 1 - row, 2)

    def from_west(halos, row):
        return pltpu.roll(halos[0], BLOCK - row, 2)

    def image_row(src, row, east_side, west_side, to_north=True, to_south=True):
        v = [src[row + 1, cb] for cb in range(nblk)]
        e = eastward(v, east_side)
        w = westward(v, west_side)
        images = []
        for cb in range(nblk):
            at = pl.ds(cb * BLOCK, BLOCK)
            image = (
                diag[row, :, at] * v[cb]
                - coef[0, row, :, at] * e[cb]
                - coef[1, row, :, at] * w[cb]
                + oslot[splan[2, row * nblk + cb]]
            )
            if to_north:
                image = image - coef[2, row, :, at] * src[row + 2, cb]
            if to_south:
                image = image - coef[3, row, :, at] * src[row, cb]
            images.append(image)
        return v, images

    def inside(src, dst):
        def put(row, images):
            for cb in range(nblk):
                dst[row + 1, cb] = images[cb]

        def line(row, carry):
            put(row, image_row(src, row, zero, zero)[1])
            return carry

        lax.fori_loop(1, rows - 1, line, 0, unroll=2)
        put(0, image_row(src, 0, zero, zero, to_south=False)[1])
        put(rows - 1, image_row(src, rows - 1, zero, zero, to_north=False)[1])

    def edges(src, halos, dst):
        for cb in range(nblk):
            at = pl.ds(cb * BLOCK, BLOCK)
            dst[1, cb] = dst[1, cb] - coef[3, 0, :, at] * src[0, cb]
            dst[rows, cb] = dst[rows, cb] - coef[2, rows - 1, :, at] * src[rows + 1, cb]

        first, last = pl.ds(0, BLOCK), pl.ds(cols - BLOCK, BLOCK)
        for row in range(rows):
            beside = jnp.where(lane8 == 0, from_west(halos, row), 0.0)
            dst[row + 1, 0] = dst[row + 1, 0] - coef[1, row, :, first] * beside
            beside = jnp.where(lane8 == BLOCK - 1, from_east(halos, row), 0.0)
            dst[row + 1, nblk - 1] = dst[row + 1, nblk - 1] - coef[0, row, :, last] * beside

    def sum_copy(i, k):
        peer = lax.rem(me + k, count)
        where = {"lat": peer // nlon, "lon": lax.rem(peer, nlon)}
        return remote(part_row.at[i], sum_a.at[i, pl.ds(me, 1)], as_.at[i], ar.at[i], where)

    def sum_wait(i):
        whole = sum_a.at[i, pl.ds(0, count - 1)]
        return remote(whole, whole, as_.at[i], ar.at[i], {"lat": south})

    def send_sums(i, sums):
        part = jnp.zeros((8, BLOCK), jnp.float32)
        for k, s in enumerate(sums):
            part = jnp.where(sub8 == k, jnp.sum(s[0] + s[1], axis=0, keepdims=True), part)
        part = part + pltpu.roll(part, 64, 1)
        part = part + pltpu.roll(part, 32, 1)
        row = jnp.sum(jnp.where(lane8 >> 5 == sub8, part, 0.0), axis=0, keepdims=True)
        part_row[i] = row
        sum_a[i, pl.ds(me, 1)] = row

        def send(k, carry):
            sum_copy(i, k).start()
            return carry

        lax.fori_loop(1, count, send, 0, unroll=True)

    def take_sums(i):
        sum_wait(i).wait_recv()
        total = jnp.sum(sum_a[i], axis=0, keepdims=True)
        whole = jnp.sum(jnp.where(lane8 >> 5 == sub8, total, 0.0), axis=1, keepdims=True)
        return [jnp.broadcast_to(whole[k : k + 1], (8, BLOCK)) for k in range(4)]

    def beta_of(size, rr, rq, qq):
        return (rr - 2.0 * size * rq + size * size * qq) / rr

    def outer(o):
        k0, kq, kz = 4 * o, 4 * o + 1, 4 * o + 2
        i0, i1, i2 = ITERS * o, ITERS * o + 1, ITERS * o + 2
        r0, q0, z0 = field.at[k0], field.at[kq], field.at[kz]
        z1 = field.at[3] if o == 0 else z_last
        observe()
        if o == 0:
            inside(r0, q0)
            wait_halo(k0)
            edges(r0, hq.at[k0], q0)

        def first_dots(row, carry):
            rr, rq, qq = carry
            if o == 0:
                v = [r0[row + 1, cb] for cb in range(nblk)]
                images = [q0[row + 1, cb] for cb in range(nblk)]
            else:
                v, images = image_row(r0, row, from_east(hq.at[k0], row), from_west(hq.at[k0], row))
            for cb in range(nblk):
                res, image = v[cb], images[cb]
                if o > 0:
                    q0[row + 1, cb] = image
                rr = rr + res * res
                rq = rq + res * image
                qq = qq + image * image
            return rr, rq, qq

        sums = lax.fori_loop(0, rows, first_dots, (zero, zero, zero), unroll=2)
        keep_ends(kq, q0)
        send_halo(kq, slice(0, 2))
        if o == 0:
            pl.semaphore_wait(ready, nlat - 1)
        send_sums(i0, sums)
        send_halo(kq, slice(2, 4))

        def look(row, carry):
            for cb in range(nblk):
                seen[row * nblk + cb] = q0[row + 1, cb]
            return carry

        lax.fori_loop(0, rows, look, 0)
        observe()
        inside(q0, z0)
        wait_halo(kq)
        edges(q0, hq.at[kq], z0)

        keep_ends(kz, z0)
        send_halo(kz)
        rr, rq, qq, _ = take_sums(i0)
        size0 = rr / rq
        beta0 = beta_of(size0, rr, rq, qq)
        more = 1.0 + beta0

        def second(row, carry):
            rr, rq, dq, qq = carry
            for cb in range(nblk):
                r, q, z = r0[row + 1, cb], q0[row + 1, cb], z0[row + 1, cb]
                res = r - size0 * q
                way = res + beta0 * r
                image = more * q - size0 * z
                r1[row + 1, cb] = res
                p1[row + 1, cb] = way
                q1[row + 1, cb] = image
                seen[row * nblk + cb] = image
                rr = rr + res * res
                rq = rq + res * image
                dq = dq + way * image
                qq = qq + image * image
            return rr, rq, dq, qq

        send_sums(i1, lax.fori_loop(0, rows, second, (zero,) * 4, unroll=2))
        observe()
        inside(q1, z1)
        wait_halo(kz)
        for edge in (0, rows + 1):
            for cb in range(nblk):
                q1[edge, cb] = more * q0[edge, cb] - size0 * z0[edge, cb]
        hq1[...] = more * hq[kq] - size0 * hq[kz]
        edges(q1, hq1, z1)
        if o == 0:
            keep_ends(3, z1)
            send_halo(3)
        rr, rq, dq, qq = take_sums(i1)
        size1 = rr / dq
        beta1 = beta_of(size1, rr, rq, qq)

        def third(row, carry):
            rr, dq = carry
            for cb in range(nblk):
                q = q1[row + 1, cb]
                res = r1[row + 1, cb] - size1 * q
                way = res + beta1 * p1[row + 1, cb]
                image = ((q0[row + 1, cb] - size0 * z0[row + 1, cb]) - size1 * z1[row + 1, cb]) + beta1 * q
                r2[row + 1, cb] = res
                p2[row + 1, cb] = way
                q2[row + 1, cb] = image
                rr = rr + res * res
                dq = dq + way * image
            return rr, dq

        send_sums(i2, lax.fori_loop(0, rows, third, (zero,) * 2, unroll=2))
        return size0, beta0, size1, beta1

    size0, beta0, size1, beta1 = outer(0)
    for c in obs_sends + first_copies:
        c.wait_send()

    def beyond(r, q, q_next):
        res = r - size0 * q
        way = res + beta0 * r
        res = res - size1 * q_next
        return size0 * r + size1 * way, res + beta1 * way, res

    for edge in (0, rows + 1):
        for cb in range(nblk):
            x[edge, cb], p2[edge, cb], r2[edge, cb] = beyond(field[0, edge, cb], field[1, edge, cb], q1[edge, cb])
    hx[...], hp[...], hr[...] = beyond(hq[0], hq[1], hq1[...])

    def advance(row, carry):
        for cb in range(nblk):
            x[row + 1, cb] = size0 * field[0, row + 1, cb] + size1 * p1[row + 1, cb]
        return carry

    lax.fori_loop(0, rows, advance, 0)

    def add_up(square):
        return jnp.sum(square[0] + square[1], axis=0, keepdims=True)

    def surface(row, cb):
        at = pl.ds(cb * BLOCK, BLOCK)
        flux = []
        for ref, halos in ((x, hx), (p2, hp)):
            v = ref[row + 1, cb]
            after = pltpu.roll(ref[row + 1, cb + 1], BLOCK - 1, 2) if cb < nblk - 1 else from_east(halos, row)
            e = jnp.where(lane8 == BLOCK - 1, after, pltpu.roll(v, BLOCK - 1, 2))
            flux.append((coef[0, row, :, at] * (e - v), coef[2, row, :, at] * (ref[row + 2, cb] - v)))
        (xe, xn), (pe, pn) = flux
        parts = jnp.where(sub8 == 0, add_up(xe * xe + xn * xn), wetfric[row, :, at])
        parts = jnp.where(sub8 == 1, add_up(xe * pe + xn * pn), parts)
        parts = jnp.where(sub8 == 2, add_up(pe * pe + pn * pn), parts)
        surf[row + 1, :, at] = parts
        return parts

    def surface_ends(row, ends):
        first, last = surface(row, 0), surface(row, nblk - 1)
        return (
            jnp.where(lane8 == row, pltpu.roll(first, row, 1), ends[0]),
            jnp.where(lane8 == row, pltpu.roll(last, row + 1, 1), ends[1]),
        )

    blank = jnp.zeros((8, BLOCK), jnp.float32)
    ends = lax.fori_loop(0, rows, surface_ends, (blank, blank))
    surf_pk[0] = ends[0]
    surf_pk[1] = ends[1]
    surf_copies = [
        remote(surf_pk.at[0], surf_hq.at[1], ss.at[2], sr.at[2], {"lon": west}),
        remote(surf_pk.at[1], surf_hq.at[0], ss.at[3], sr.at[3], {"lon": east}),
        remote(surf.at[1], surf.at[rows + 1], ss.at[0], sr.at[0], {"lat": south}),
        remote(surf.at[rows], surf.at[0], ss.at[1], sr.at[1], {"lat": north}),
    ]
    for c in surf_copies[:2]:
        c.start()

    def surface_middle(row, carry):
        for cb in range(1, nblk - 1):
            surface(row, cb)
        return carry

    lax.fori_loop(0, rows, surface_middle, 0)
    for c in surf_copies[2:]:
        c.start()
    wait_halo(3)

    def image_beyond(q, z, z_next, q_next):
        return ((q - size0 * z) - size1 * z_next) + beta1 * q_next

    for edge in (0, rows + 1):
        for cb in range(nblk):
            q2[edge, cb] = image_beyond(field[1, edge, cb], field[2, edge, cb], field[3, edge, cb], q1[edge, cb])
    hw[...] = image_beyond(hq[1], hq[2], hq[3], hq1[...])
    for c in surf_copies:
        c.wait_recv()
    rr, dq, _, _ = take_sums(2)
    size2 = rr / dq
    ramp = jnp.where(sub8 == 0, 1.0, jnp.where(sub8 == 1, 2.0 * size2, jnp.where(sub8 == 2, size2 * size2, 0.0)))

    def extra_of(parts):
        speed = jnp.maximum(jnp.sum(parts * ramp, axis=0, keepdims=True), 0.0)
        return parts[3:4] * (jnp.sqrt(1.0 + speed / 16.0) - 1.0)

    def renew(row, cb):
        extra = extra_of(surf[row, :, pl.ds(cb * BLOCK, BLOCK)])
        place = x[row, cb] + size2 * p2[row, cb]
        new = (r2[row, cb] - size2 * q2[row, cb]) - extra * place
        field[4, row, cb] = new
        return extra, place, new

    def friction(row, carry):
        for cb in range(nblk):
            at = pl.ds(cb * BLOCK, BLOCK)
            extra, place, new = renew(row + 1, cb)
            x[row + 1, cb] = place
            diag[row, :, at] = diag[row, :, at] + extra
            seen[row * nblk + cb] = new
        return carry

    lax.fori_loop(0, rows, friction, 0, unroll=2)
    for edge in (0, rows + 1):
        for cb in range(nblk):
            renew(edge, cb)
    for side in range(2):
        hq[4, side] = (hr[side] - size2 * hw[side]) - extra_of(surf_hq[side]) * (hx[side] + size2 * hp[side])
    size0, beta0, size1, beta1 = outer(1)

    def advance_last(row, carry):
        for cb in range(nblk):
            x[row + 1, cb] = (x[row + 1, cb] + size0 * field[4, row + 1, cb]) + size1 * p1[row + 1, cb]
        return carry

    lax.fori_loop(0, rows, advance_last, 0)
    for n, src in enumerate((x, p2, r2, q2)):
        for cb in range(nblk):
            for h in range(2):
                turned[n, h, :, :, pl.ds(cb * BLOCK, BLOCK)] = jnp.swapaxes(src[pl.ds(1, rows), cb, h], 0, 1)
    for k in (0, 1, 2, 3, 5, 6):
        for c in halo(k):
            c.wait_send()
    for c in surf_copies:
        c.wait_send()
    rr, dq, _, _ = take_sums(SUMS - 1)
    size2 = rr / dq

    def conclude(c, carry):
        for h in range(2):
            for cb in range(nblk):
                at = pl.ds(cb * BLOCK, BLOCK)
                x_out[h, c, :, at] = turned[0, h, c, :, at] + size2 * turned[1, h, c, :, at]
                r_out[h, c, :, at] = turned[2, h, c, :, at] - size2 * turned[3, h, c, :, at]
        return carry

    lax.fori_loop(0, 8, conclude, 0)
    for i in range(SUMS):
        sum_wait(i).wait_send()


def shards(nlat, nlon, depth, friction, ocean_mask, forcing, tile_route, tile_block, obs_cell, obs_time, obs_value, obs_weight):
    channels, rows, cols = forcing.shape
    slots = nlon * CAP
    nblk, tiles = cols // BLOCK, obs_time.shape[0]
    f32, i32 = jnp.float32, jnp.int32
    vmem, smem = pltpu.VMEM, pltpu.SMEM
    hbm = pl.BlockSpec(memory_space=pltpu.HBM)
    field = (rows + 2, nblk, 2, 8, BLOCK)
    ends = (2, 2, 8, BLOCK)
    split = (2, channels // 2, rows, cols)
    dma = pltpu.SemaphoreType.DMA
    scratch = [
        smem((tiles,), i32),
        smem((tiles,), i32),
        vmem((rows, cols), f32),
        vmem((rows, cols), f32),
        vmem((rows, cols), i32),
        vmem(split, f32),
        vmem((tiles, BLOCK), i32),
        vmem((tiles, BLOCK), f32),
        vmem((tiles, BLOCK), f32),
        vmem((tiles, BLOCK), f32),
        vmem((rows, cols), f32),
        vmem((rows, cols), f32),
        vmem((rows, cols), f32),
        vmem((rows, BLOCK), f32),
        vmem((rows, BLOCK), f32),
        vmem((rows, 8, cols), f32),
        vmem((4, rows, 8, cols), f32),
        vmem((rows, 8, cols), f32),
        vmem((tiles + 1, 8, BLOCK), f32),
        vmem((tiles + 1, 8, BLOCK), i32),
        vmem((nlon, 8, BLOCK), f32),
        vmem((nlon, 8, BLOCK), i32),
        vmem((nlon, 8, BLOCK), f32),
        vmem((nlon, 8, BLOCK), i32),
        vmem((8, BLOCK), i32),
        smem((8, BLOCK), i32),
        vmem((slots, 2, 8, BLOCK), f32),
        vmem((slots + 1, 256, BLOCK), f32),
        vmem((slots + 1, 2, 8, BLOCK), f32),
        vmem((HALOS,) + field, f32),
        vmem((rows * nblk, 2, 8, BLOCK), f32),
        vmem(field, f32),
        vmem(field, f32),
        vmem(field, f32),
        vmem(field, f32),
        vmem(field, f32),
        vmem(field, f32),
        vmem(field, f32),
        vmem(field, f32),
        vmem((4,) + split, f32),
        vmem((HALOS,) + ends, f32),
        vmem((HALOS,) + ends, f32),
        vmem(ends, f32),
        vmem(ends, f32),
        vmem(ends, f32),
        vmem(ends, f32),
        vmem(ends, f32),
        vmem((rows + 2, 8, cols), f32),
        vmem((2, 8, BLOCK), f32),
        vmem((2, 8, BLOCK), f32),
        vmem((SUMS, nlat * nlon, BLOCK), f32),
        vmem((SUMS, 1, BLOCK), f32),
        pltpu.SemaphoreType.REGULAR,
        dma((10,)),
        dma((HALOS, 4)),
        dma((HALOS, 4)),
        dma((4,)),
        dma((4,)),
        dma((SUMS,)),
        dma((SUMS,)),
        dma((2, nlon)),
        dma((2, nlon)),
        dma((4,)),
        dma((4,)),
        dma((1,)),
    ]
    shape = vmem(split, f32)
    x, r = pl.pallas_call(
        functools.partial(kernel, nlat, nlon),
        out_shape=(shape, shape),
        in_specs=[hbm] * 10,
        out_specs=(pl.BlockSpec(memory_space=vmem), pl.BlockSpec(memory_space=vmem)),
        scratch_shapes=scratch,
        compiler_params=pltpu.CompilerParams(
            collective_id=0, has_side_effects=True, vmem_limit_bytes=62 * 2**20
        ),
    )(
        tile_route.reshape(-1), tile_block, depth, friction, ocean_mask, forcing.reshape(split),
        obs_cell, obs_time, obs_value, obs_weight,
    )
    return x.reshape(forcing.shape), r.reshape(forcing.shape)


def solution(mesh):
    tile = P(("lat", "lon"), None)
    grid = P("lat", "lon")
    in_specs = (grid, grid, grid, P(None, "lat", "lon"), tile, P(("lat", "lon")), tile, tile, tile, tile)
    out_specs = (P(None, "lat", "lon"), P(None, "lat", "lon"))
    body = functools.partial(shards, mesh.shape["lat"], mesh.shape["lon"])
    return jax.shard_map(body, mesh=mesh, in_specs=in_specs, out_specs=out_specs, check_vma=False)
```

```python
import functools
import math

import jax
import jax.numpy as jnp
import numpy as np
from jax import lax
from jax.experimental import pallas as pl
from jax.experimental.pallas import tpu as pltpu
from jax.sharding import PartitionSpec as P

BLOCK = 128
CAP = 2
ITERS = 3
OUTER = 2
SUMS = ITERS * OUTER
HALOS = 7
MESH = pl.DeviceIdType.MESH
OMEGA_DEGREES = (28.984104, 30.0, 28.43973, 30.082137, 15.041069, 13.943036, 14.958931, 13.398661)
RATES = np.array(OMEGA_DEGREES, np.float32) * np.float32(math.pi / 180.0)
STIFF = np.float32(0.2) * (RATES / RATES[0]) ** 2


def sin_cos(angle):
    turn = jnp.floor(angle * (2.0 / math.pi) + 0.5)
    x = ((angle - turn * 1.5703125) - turn * 4.837512969970703125e-4) - turn * 7.54978995489188216e-8
    z = x * x
    s = ((-1.9515295891e-4 * z + 8.3321608736e-3) * z - 1.6666654611e-1) * z * x + x
    c = ((2.443315711809948e-5 * z - 1.388731625493765e-3) * z + 4.166664568298827e-2) * z * z - 0.5 * z + 1.0
    quarter = turn.astype(jnp.int32)
    odd = (quarter & 1) == 1
    sine = jnp.where(odd, c, s)
    cosine = jnp.where(odd, s, c)
    sine = jnp.where((quarter & 2) == 2, -sine, sine)
    cosine = jnp.where(((quarter + 1) & 2) == 2, -cosine, cosine)
    return sine, cosine


def kernel(
    nlat, nlon,
    route_in, tblk_in, depth_in, fric_in, mask_in, forc_in, ocell_in, otime_in, oval_in, oweight_in,
    x_out, p_out, r_out, q_out, size_out,
    route, tblk, depth, fric, mask, forc, ocell, otime, oval, oweight,
    dw, dwn, dws, dwe, dww, wetfric, coef, diag,
    pay, payi, outf, outi, inf, ini, plan, splan, waves, mats, oslot,
    field, seen, r1, p1, q1, z_last, r2, p2, q2, x,
    pk, hq, hq1, hx, hp, hr, hw, surf, surf_pk, surf_hq, sum_a, part_row, ready,
    load, hs, hrv, ss, sr, as_, ar, os_, orv, ds_, dr, loc,
):
    rows, cols = depth.shape
    nblk = cols // BLOCK
    slots = nlon * CAP
    tiles = otime.shape[0]
    me_lat = lax.axis_index("lat")
    me_lon = lax.axis_index("lon")
    north, south = lax.rem(me_lat + 1, nlat), lax.rem(me_lat + nlat - 1, nlat)
    east, west = lax.rem(me_lon + 1, nlon), lax.rem(me_lon + nlon - 1, nlon)
    me = me_lat * nlon + me_lon
    count = nlat * nlon

    barrier = pltpu.get_barrier_semaphore()
    for k in range(1, nlon):
        pl.semaphore_signal(barrier, inc=1, device_id={"lon": lax.rem(me_lon + k, nlon)}, device_id_type=MESH)
    for k in range(1, nlat):
        pl.semaphore_signal(barrier, inc=1, device_id={"lat": lax.rem(me_lat + k, nlat)}, device_id_type=MESH)
    pairs = [
        (route_in, route), (tblk_in, tblk), (ocell_in, ocell), (otime_in, otime), (oval_in, oval),
        (oweight_in, oweight), (depth_in, depth), (mask_in, mask), (fric_in, fric), (forc_in, forc),
    ]
    loads = [pltpu.make_async_copy(src, dst, load.at[k]) for k, (src, dst) in enumerate(pairs)]
    for c in loads:
        c.start()

    def remote(src, dst, send, recv, where):
        return pltpu.make_async_remote_copy(
            src_ref=src, dst_ref=dst, send_sem=send, recv_sem=recv, device_id=where, device_id_type=MESH
        )

    lane = lax.broadcasted_iota(jnp.int32, (1, BLOCK), 1)
    lane8 = lax.broadcasted_iota(jnp.int32, (8, BLOCK), 1)
    sub8 = lax.broadcasted_iota(jnp.int32, (8, BLOCK), 0)
    zero = jnp.zeros((2, 8, BLOCK), jnp.float32)

    for c in loads[:8]:
        c.wait()
    wet = mask[...].astype(jnp.float32)
    dw[...] = depth[...] * wet

    for t in range(tiles):
        pay[t] = jnp.concatenate([otime[t : t + 1], oval[t : t + 1], oweight[t : t + 1], oval[t : t + 1]] * 2, axis=0)
        payi[t] = jnp.broadcast_to(ocell[t : t + 1] + tblk[t] * BLOCK, (8, BLOCK))
    pay[tiles] = jnp.zeros((8, BLOCK), jnp.float32)
    payi[tiles] = jnp.zeros((8, BLOCK), jnp.int32)

    def pick(p, carry):
        first, second = jnp.int32(tiles), jnp.int32(tiles)
        for t in reversed(range(tiles)):
            hit = route[t] == p
            second = jnp.where(hit, first, second)
            first = jnp.where(hit, jnp.int32(t), first)
        outf[p] = jnp.where(sub8 < 4, pay[first], pay[second])
        outi[p] = jnp.where(sub8 == 0, payi[first], payi[second])
        return carry

    lax.fori_loop(0, nlon, pick, 0)
    pl.semaphore_wait(barrier, nlon + nlat - 2)

    def obs_copy(k):
        peer = lax.rem(me_lon + k, nlon)
        return [
            remote(outf.at[peer], inf.at[me_lon], os_.at[0, peer], orv.at[0, me_lon], {"lon": peer}),
            remote(outi.at[peer], ini.at[me_lon], os_.at[1, peer], orv.at[1, me_lon], {"lon": peer}),
        ]

    def obs_wait(k):
        peer = lax.rem(me_lon + k, nlon)
        remote(outf.at[peer], inf.at[peer], os_.at[0, peer], orv.at[0, peer], {"lon": peer}).wait_recv()
        remote(outi.at[peer], ini.at[peer], os_.at[1, peer], orv.at[1, peer], {"lon": peer}).wait_recv()

    obs_sends = [c for k in range(1, nlon) for c in obs_copy(k)]
    for c in obs_sends:
        c.start()
    first_copies = [
        remote(dw.at[:, pl.ds(0, BLOCK)], dwe, ds_.at[2], dr.at[2], {"lon": west}),
        remote(dw.at[:, pl.ds(cols - BLOCK, BLOCK)], dww, ds_.at[3], dr.at[3], {"lon": east}),
        remote(dw, dws, ds_.at[0], dr.at[0], {"lat": north}),
        remote(dw, dwn, ds_.at[1], dr.at[1], {"lat": south}),
    ]
    for c in first_copies:
        c.start()
    for k in range(1, nlat):
        pl.semaphore_signal(ready, inc=1, device_id={"lat": lax.rem(me_lat + k, nlat)}, device_id_type=MESH)
    inf[me_lon] = outf[me_lon]
    ini[me_lon] = outi[me_lon]
    for c in loads[8:]:
        c.wait()

    for cb in range(nblk):
        at = pl.ds(cb * BLOCK, BLOCK)
        for h in range(2):
            wetted = forc[h, :, :, at] * wet[None, :, cb * BLOCK : cb * BLOCK + BLOCK]
            field[0, pl.ds(1, rows), cb, h] = jnp.swapaxes(wetted, 0, 1)
    oslot[slots] = zero
    mats[slots] = jnp.zeros((256, BLOCK), jnp.float32)
    stiff = jnp.zeros((8, 1), jnp.float32)
    rate = jnp.zeros((8, BLOCK), jnp.float32)
    sub1 = lax.broadcasted_iota(jnp.int32, (8, 1), 0)
    for c in range(8):
        stiff = jnp.where(sub1 == c, float(STIFF[c]), stiff)
        rate = jnp.where(sub8 == c, float(RATES[c]), rate)
    cells = lax.broadcasted_iota(jnp.int32, (BLOCK, BLOCK), 0)

    for k in range(1, nlon):
        obs_wait(k)

    def where_is(s):
        return ini[s // CAP, pl.ds(s % CAP, 1), :]

    rep = jnp.full((1, BLOCK), slots, jnp.int32)
    homes = jnp.full((1, BLOCK), -1, jnp.int32)
    for s in reversed(range(slots)):
        home = where_is(s) >> 7
        rep = jnp.where(home == lane, s, rep)
        homes = jnp.where(lane == s, home, homes)
    chain = jnp.full((1, BLOCK), slots, jnp.int32)
    for s in reversed(range(slots)):
        home = where_is(s) >> 7
        chain = jnp.where((home == homes) & (lane < s), s, chain)
    plan[...] = jnp.where(
        sub8 == 0,
        jnp.broadcast_to(homes, (8, BLOCK)),
        jnp.where(sub8 == 1, jnp.broadcast_to(chain, (8, BLOCK)), jnp.broadcast_to(rep, (8, BLOCK))),
    )
    to_scalars = pltpu.make_async_copy(plan, splan, loc.at[0])
    to_scalars.start()

    def onto_cells(o, k, terms):
        cell = ini[o, pl.ds(k, 1), :] & (BLOCK - 1)
        high = terms.astype(jnp.bfloat16)
        low = (terms - high.astype(jnp.float32)).astype(jnp.bfloat16)
        hot = (cells == cell).astype(jnp.float32).astype(jnp.bfloat16)
        return lax.dot_general(
            jnp.concatenate([high, low], axis=1),
            jnp.concatenate([hot, hot], axis=1),
            (((1,), (1,)), ((), ())),
            preferred_element_type=jnp.float32,
        )

    def values(o, carry):
        for k in range(CAP):
            times = inf[o, pl.ds(4 * k, 1), :]
            scaled = inf[o, pl.ds(4 * k + 2, 1), :] * inf[o, pl.ds(4 * k + 1, 1), :]
            sine, cosine = sin_cos(rate * times)
            waves[o * CAP + k, 0] = cosine
            waves[o * CAP + k, 1] = sine
            terms = jnp.concatenate([cosine * scaled, sine * scaled], axis=0)
            oslot[o * CAP + k] = onto_cells(o, k, terms).reshape(2, 8, BLOCK)
        return carry

    lax.fori_loop(0, nlon, values, 0, unroll=4)
    to_scalars.wait()

    def join_values(i, carry):
        s = slots - 1 - i
        oslot[s] = oslot[s] + oslot[splan[1, s]]
        return carry

    lax.fori_loop(0, slots, join_values, 0)

    def keep_ends(k, src):
        for side, cb in enumerate((0, nblk - 1)):
            packed = zero
            for row in range(rows):
                moved = pltpu.roll(src[row + 1, cb], (row + side) % BLOCK, 2)
                packed = jnp.where(lane8 == row, moved, packed)
            pk[k, side] = packed

    def start_rhs(blocks):
        def line(row, carry):
            for cb in blocks:
                v = field[0, row + 1, cb] + oslot[splan[2, row * nblk + cb]]
                field[0, row + 1, cb] = v
                seen[row * nblk + cb] = v
            return carry

        lax.fori_loop(0, rows, line, 0, unroll=rows if len(blocks) == 2 else 2)

    start_rhs((0, nblk - 1))
    keep_ends(0, field.at[0])

    def halo(k):
        return [
            remote(pk.at[k, 0], hq.at[k, 1], hs.at[k, 2], hrv.at[k, 2], {"lon": west}),
            remote(pk.at[k, 1], hq.at[k, 0], hs.at[k, 3], hrv.at[k, 3], {"lon": east}),
            remote(field.at[k, 1], field.at[k, rows + 1], hs.at[k, 0], hrv.at[k, 0], {"lat": south}),
            remote(field.at[k, rows], field.at[k, 0], hs.at[k, 1], hrv.at[k, 1], {"lat": north}),
        ]

    def send_halo(k, part=slice(None)):
        for c in halo(k)[part]:
            c.start()

    def wait_halo(k):
        for c in halo(k):
            c.wait_recv()

    send_halo(0, slice(0, 2))
    start_rhs(range(1, nblk - 1))
    send_halo(0, slice(2, 4))

    for c in first_copies:
        c.wait_recv()
    a = dw[...]
    colid = lax.broadcasted_iota(jnp.int32, (rows, cols), 1)
    rowid = lax.broadcasted_iota(jnp.int32, (rows, cols), 0)
    keep_n = (me_lat < nlat - 1).astype(jnp.float32)
    keep_s = (me_lat > 0).astype(jnp.float32)

    def harmonic(first, second):
        return 2.0 * first * second / jnp.maximum(first + second, 0.5)

    drag = fric[...]
    total = wet * drag + (1.0 - wet)
    around = (
        lambda: jnp.where(colid == cols - 1, dwe[:, 0:1], pltpu.roll(a, cols - 1, 1)),
        lambda: jnp.where(colid == 0, dww[:, BLOCK - 1 : BLOCK], pltpu.roll(a, 1, 1)),
        lambda: jnp.where(rowid == rows - 1, dwn[0:1, :] * keep_n, pltpu.roll(a, rows - 1, 0)),
        lambda: jnp.where(rowid == 0, dws[rows - 1 : rows, :] * keep_s, pltpu.roll(a, 1, 0)),
    )
    for k in range(4):
        side = harmonic(a, around[k]())
        total = total + side
        for row in range(rows):
            coef[k, row] = jnp.broadcast_to(side[row : row + 1], (8, cols))
    dragged = wet * drag
    for row in range(rows):
        wetfric[row] = jnp.broadcast_to(dragged[row : row + 1], (8, cols))
        wide = jnp.broadcast_to(wet[row : row + 1], (8, cols))
        diag[row] = wide * stiff + jnp.broadcast_to(total[row : row + 1], (8, cols))

    def build(o, carry):
        for k in range(CAP):
            weight = inf[o, pl.ds(4 * k + 2, 1), :]
            basis = (waves[o * CAP + k, 0], waves[o * CAP + k, 1])
            parts = []
            for h in range(2):
                for c in range(8):
                    one = weight * basis[h][c : c + 1]
                    parts.append(one * basis[0])
                    parts.append(one * basis[1])
            mats[o * CAP + k] = onto_cells(o, k, jnp.concatenate(parts, axis=0))
        return carry

    lax.fori_loop(0, nlon, build, 0)

    def join_mats(i, carry):
        s = slots - 1 - i
        mats[s] = mats[s] + mats[splan[1, s]]
        return carry

    lax.fori_loop(0, slots, join_mats, 0)

    def observe():
        def slot(s, carry):
            v = seen[splan[0, s]]
            acc = [zero, zero]
            for c in range(16):
                m = mats[s, 16 * c : 16 * c + 16, :].reshape(2, 8, BLOCK)
                acc[c % 2] = acc[c % 2] + m * v[c // 8, c % 8 : c % 8 + 1, :]
            oslot[s] = acc[0] + acc[1]
            return carry

        lax.fori_loop(0, slots, slot, 0, unroll=2)

    def eastward(v, beyond):
        moved = [pltpu.roll(b, BLOCK - 1, 2) for b in v] + [beyond]
        return [jnp.where(lane8 == BLOCK - 1, moved[cb + 1], moved[cb]) for cb in range(nblk)]

    def westward(v, beyond):
        moved = [beyond] + [pltpu.roll(b, 1, 2) for b in v]
        return [jnp.where(lane8 == 0, moved[cb], moved[cb + 1]) for cb in range(nblk)]

    def from_east(halos, row):
        return pltpu.roll(halos[1], BLOCK - 1 - row, 2)

    def from_west(halos, row):
        return pltpu.roll(halos[0], BLOCK - row, 2)

    def image_row(src, row, east_side, west_side, to_north=True, to_south=True):
        v = [src[row + 1, cb] for cb in range(nblk)]
        e = eastward(v, east_side)
        w = westward(v, west_side)
        images = []
        for cb in range(nblk):
            at = pl.ds(cb * BLOCK, BLOCK)
            image = (
                diag[row, :, at] * v[cb]
                - coef[0, row, :, at] * e[cb]
                - coef[1, row, :, at] * w[cb]
                + oslot[splan[2, row * nblk + cb]]
            )
            if to_north:
                image = image - coef[2, row, :, at] * src[row + 2, cb]
            if to_south:
                image = image - coef[3, row, :, at] * src[row, cb]
            images.append(image)
        return v, images

    def inside(src, dst):
        def put(row, images):
            for cb in range(nblk):
                dst[row + 1, cb] = images[cb]

        def line(row, carry):
            put(row, image_row(src, row, zero, zero)[1])
            return carry

        lax.fori_loop(1, rows - 1, line, 0, unroll=2)
        put(0, image_row(src, 0, zero, zero, to_south=False)[1])
        put(rows - 1, image_row(src, rows - 1, zero, zero, to_north=False)[1])

    def edges(src, halos, dst):
        for cb in range(nblk):
            at = pl.ds(cb * BLOCK, BLOCK)
            dst[1, cb] = dst[1, cb] - coef[3, 0, :, at] * src[0, cb]
            dst[rows, cb] = dst[rows, cb] - coef[2, rows - 1, :, at] * src[rows + 1, cb]

        first, last = pl.ds(0, BLOCK), pl.ds(cols - BLOCK, BLOCK)
        for row in range(rows):
            beside = jnp.where(lane8 == 0, from_west(halos, row), 0.0)
            dst[row + 1, 0] = dst[row + 1, 0] - coef[1, row, :, first] * beside
            beside = jnp.where(lane8 == BLOCK - 1, from_east(halos, row), 0.0)
            dst[row + 1, nblk - 1] = dst[row + 1, nblk - 1] - coef[0, row, :, last] * beside

    lat_order = sorted(range(nlat), key=lambda k: (k == 0, abs(k - nlat // 2)))
    lon_order = sorted(range(nlon), key=lambda k: (k == 0, k % 2 == 0, -abs(k - nlon // 2)))
    lat_peers = {k: lax.rem(me_lat + k, nlat) for k in lat_order}
    lon_peers = {k: lax.rem(me_lon + k, nlon) for k in lon_order}

    def sum_wait(i):
        whole = sum_a.at[i, pl.ds(0, count - 1)]
        return remote(whole, whole, as_.at[i], ar.at[i], {"lat": south})

    def send_sums(i, sums):
        part = jnp.zeros((8, BLOCK), jnp.float32)
        for k, s in enumerate(sums):
            both = s[0] + s[1]
            both = both + pltpu.roll(both, 64, 1)
            both = both + pltpu.roll(both, 32, 1)
            part = jnp.where(lane8 >> 5 == k, both, part)
        row = jnp.sum(part, axis=0, keepdims=True)
        part_row[i] = row
        sum_a[i, pl.ds(me, 1)] = row
        for a in lat_order:
            for b in lon_order:
                if a or b:
                    where = {"lat": lat_peers[a], "lon": lon_peers[b]}
                    remote(part_row.at[i], sum_a.at[i, pl.ds(me, 1)], as_.at[i], ar.at[i], where).start()

    def take_sums(i):
        sum_wait(i).wait_recv()
        total = jnp.sum(sum_a[i], axis=0, keepdims=True)
        whole = jnp.sum(jnp.where(lane8 >> 5 == sub8, total, 0.0), axis=1, keepdims=True)
        return [jnp.broadcast_to(whole[k : k + 1], (8, BLOCK)) for k in range(4)]

    def beta_of(size, rr, rq, qq):
        return (rr - 2.0 * size * rq + size * size * qq) / rr

    def outer(o):
        k0, kq, kz = 4 * o, 4 * o + 1, 4 * o + 2
        i0, i1, i2 = ITERS * o, ITERS * o + 1, ITERS * o + 2
        r0, q0, z0 = field.at[k0], field.at[kq], field.at[kz]
        z1 = field.at[3] if o == 0 else z_last
        observe()
        if o == 0:
            inside(r0, q0)
            wait_halo(k0)
            edges(r0, hq.at[k0], q0)

        def first_dots(row, carry):
            rr, rq, qq = carry
            if o == 0:
                v = [r0[row + 1, cb] for cb in range(nblk)]
                images = [q0[row + 1, cb] for cb in range(nblk)]
            else:
                v, images = image_row(r0, row, from_east(hq.at[k0], row), from_west(hq.at[k0], row))
            for cb in range(nblk):
                res, image = v[cb], images[cb]
                if o > 0:
                    q0[row + 1, cb] = image
                rr = rr + res * res
                rq = rq + res * image
                qq = qq + image * image
            return rr, rq, qq

        sums = lax.fori_loop(0, rows, first_dots, (zero, zero, zero), unroll=2)
        keep_ends(kq, q0)
        send_halo(kq, slice(0, 2))
        if o == 0:
            pl.semaphore_wait(ready, nlat - 1)
        send_sums(i0, sums)
        send_halo(kq, slice(2, 4))

        def look(row, carry):
            for cb in range(nblk):
                seen[row * nblk + cb] = q0[row + 1, cb]
            return carry

        lax.fori_loop(0, rows, look, 0)
        observe()
        inside(q0, z0)
        wait_halo(kq)
        edges(q0, hq.at[kq], z0)

        keep_ends(kz, z0)
        send_halo(kz)
        rr, rq, qq, _ = take_sums(i0)
        size0 = rr / rq
        beta0 = beta_of(size0, rr, rq, qq)
        more = 1.0 + beta0

        def second(row, carry):
            rr, rq, dq, qq = carry
            for cb in range(nblk):
                r, q, z = r0[row + 1, cb], q0[row + 1, cb], z0[row + 1, cb]
                res = r - size0 * q
                way = res + beta0 * r
                image = more * q - size0 * z
                r1[row + 1, cb] = res
                p1[row + 1, cb] = way
                q1[row + 1, cb] = image
                seen[row * nblk + cb] = image
                rr = rr + res * res
                rq = rq + res * image
                dq = dq + way * image
                qq = qq + image * image
            return rr, rq, dq, qq

        send_sums(i1, lax.fori_loop(0, rows, second, (zero,) * 4, unroll=2))
        observe()
        inside(q1, z1)
        wait_halo(kz)
        for edge in (0, rows + 1):
            for cb in range(nblk):
                q1[edge, cb] = more * q0[edge, cb] - size0 * z0[edge, cb]
        hq1[...] = more * hq[kq] - size0 * hq[kz]
        edges(q1, hq1, z1)
        if o == 0:
            keep_ends(3, z1)
            send_halo(3)
        rr, rq, dq, qq = take_sums(i1)
        size1 = rr / dq
        beta1 = beta_of(size1, rr, rq, qq)

        def third(row, carry):
            rr, dq = carry
            for cb in range(nblk):
                q = q1[row + 1, cb]
                res = r1[row + 1, cb] - size1 * q
                way = res + beta1 * p1[row + 1, cb]
                image = ((q0[row + 1, cb] - size0 * z0[row + 1, cb]) - size1 * z1[row + 1, cb]) + beta1 * q
                r2[row + 1, cb] = res
                p2[row + 1, cb] = way
                q2[row + 1, cb] = image
                rr = rr + res * res
                dq = dq + way * image
            return rr, dq

        send_sums(i2, lax.fori_loop(0, rows, third, (zero,) * 2, unroll=2))
        return size0, beta0, size1, beta1

    size0, beta0, size1, beta1 = outer(0)
    for c in obs_sends + first_copies:
        c.wait_send()

    def beyond(r, q, q_next):
        res = r - size0 * q
        way = res + beta0 * r
        res = res - size1 * q_next
        return size0 * r + size1 * way, res + beta1 * way, res

    for edge in (0, rows + 1):
        for cb in range(nblk):
            x[edge, cb], p2[edge, cb], r2[edge, cb] = beyond(field[0, edge, cb], field[1, edge, cb], q1[edge, cb])
    hx[...], hp[...], hr[...] = beyond(hq[0], hq[1], hq1[...])

    def advance(row, carry):
        for cb in range(nblk):
            x[row + 1, cb] = size0 * field[0, row + 1, cb] + size1 * p1[row + 1, cb]
        return carry

    lax.fori_loop(0, rows, advance, 0)

    def add_up(square):
        return jnp.sum(square[0] + square[1], axis=0, keepdims=True)

    def surface(row, cb):
        at = pl.ds(cb * BLOCK, BLOCK)
        flux = []
        for ref, halos in ((x, hx), (p2, hp)):
            v = ref[row + 1, cb]
            after = pltpu.roll(ref[row + 1, cb + 1], BLOCK - 1, 2) if cb < nblk - 1 else from_east(halos, row)
            e = jnp.where(lane8 == BLOCK - 1, after, pltpu.roll(v, BLOCK - 1, 2))
            flux.append((coef[0, row, :, at] * (e - v), coef[2, row, :, at] * (ref[row + 2, cb] - v)))
        (xe, xn), (pe, pn) = flux
        parts = jnp.where(sub8 == 0, add_up(xe * xe + xn * xn), wetfric[row, :, at])
        parts = jnp.where(sub8 == 1, add_up(xe * pe + xn * pn), parts)
        parts = jnp.where(sub8 == 2, add_up(pe * pe + pn * pn), parts)
        surf[row + 1, :, at] = parts
        return parts

    def surface_ends(row, ends):
        first, last = surface(row, 0), surface(row, nblk - 1)
        return (
            jnp.where(lane8 == row, pltpu.roll(first, row, 1), ends[0]),
            jnp.where(lane8 == row, pltpu.roll(last, row + 1, 1), ends[1]),
        )

    blank = jnp.zeros((8, BLOCK), jnp.float32)
    ends = lax.fori_loop(0, rows, surface_ends, (blank, blank))
    surf_pk[0] = ends[0]
    surf_pk[1] = ends[1]
    surf_copies = [
        remote(surf_pk.at[0], surf_hq.at[1], ss.at[2], sr.at[2], {"lon": west}),
        remote(surf_pk.at[1], surf_hq.at[0], ss.at[3], sr.at[3], {"lon": east}),
        remote(surf.at[1], surf.at[rows + 1], ss.at[0], sr.at[0], {"lat": south}),
        remote(surf.at[rows], surf.at[0], ss.at[1], sr.at[1], {"lat": north}),
    ]
    for c in surf_copies[:2]:
        c.start()

    def surface_middle(row, carry):
        for cb in range(1, nblk - 1):
            surface(row, cb)
        return carry

    lax.fori_loop(0, rows, surface_middle, 0)
    for c in surf_copies[2:]:
        c.start()
    wait_halo(3)

    def image_beyond(q, z, z_next, q_next):
        return ((q - size0 * z) - size1 * z_next) + beta1 * q_next

    for edge in (0, rows + 1):
        for cb in range(nblk):
            q2[edge, cb] = image_beyond(field[1, edge, cb], field[2, edge, cb], field[3, edge, cb], q1[edge, cb])
    hw[...] = image_beyond(hq[1], hq[2], hq[3], hq1[...])
    for c in surf_copies:
        c.wait_recv()
    rr, dq, _, _ = take_sums(2)
    size2 = rr / dq
    ramp = jnp.where(sub8 == 0, 1.0, jnp.where(sub8 == 1, 2.0 * size2, jnp.where(sub8 == 2, size2 * size2, 0.0)))

    def extra_of(parts):
        speed = jnp.maximum(jnp.sum(parts * ramp, axis=0, keepdims=True), 0.0)
        return parts[3:4] * (jnp.sqrt(1.0 + speed / 16.0) - 1.0)

    def renew(row, cb):
        extra = extra_of(surf[row, :, pl.ds(cb * BLOCK, BLOCK)])
        place = x[row, cb] + size2 * p2[row, cb]
        new = (r2[row, cb] - size2 * q2[row, cb]) - extra * place
        field[4, row, cb] = new
        return extra, place, new

    def friction(row, carry):
        for cb in range(nblk):
            at = pl.ds(cb * BLOCK, BLOCK)
            extra, place, new = renew(row + 1, cb)
            x[row + 1, cb] = place
            diag[row, :, at] = diag[row, :, at] + extra
            seen[row * nblk + cb] = new
        return carry

    lax.fori_loop(0, rows, friction, 0, unroll=2)
    for edge in (0, rows + 1):
        for cb in range(nblk):
            renew(edge, cb)
    for side in range(2):
        hq[4, side] = (hr[side] - size2 * hw[side]) - extra_of(surf_hq[side]) * (hx[side] + size2 * hp[side])
    size0, beta0, size1, beta1 = outer(1)

    def advance_last(row, carry):
        for cb in range(nblk):
            x[row + 1, cb] = (x[row + 1, cb] + size0 * field[4, row + 1, cb]) + size1 * p1[row + 1, cb]
        return carry

    lax.fori_loop(0, rows, advance_last, 0)
    for src, dst in ((x, x_out), (p2, p_out), (r2, r_out), (q2, q_out)):
        for cb in range(nblk):
            for h in range(2):
                dst[h, :, :, pl.ds(cb * BLOCK, BLOCK)] = jnp.swapaxes(src[pl.ds(1, rows), cb, h], 0, 1)
    for k in (0, 1, 2, 3, 5, 6):
        for c in halo(k):
            c.wait_send()
    for c in surf_copies:
        c.wait_send()
    rr, dq, _, _ = take_sums(SUMS - 1)
    size_out[...] = jnp.broadcast_to((rr / dq)[:, 0:1], (8, cols))
    for i in range(SUMS):
        sum_wait(i).wait_send()


def shards(nlat, nlon, depth, friction, ocean_mask, forcing, tile_route, tile_block, obs_cell, obs_time, obs_value, obs_weight):
    channels, rows, cols = forcing.shape
    slots = nlon * CAP
    nblk, tiles = cols // BLOCK, obs_time.shape[0]
    f32, i32 = jnp.float32, jnp.int32
    vmem, smem = pltpu.VMEM, pltpu.SMEM
    hbm = pl.BlockSpec(memory_space=pltpu.HBM)
    field = (rows + 2, nblk, 2, 8, BLOCK)
    ends = (2, 2, 8, BLOCK)
    split = (2, channels // 2, rows, cols)
    dma = pltpu.SemaphoreType.DMA
    scratch = [
        smem((tiles,), i32),
        smem((tiles,), i32),
        vmem((rows, cols), f32),
        vmem((rows, cols), f32),
        vmem((rows, cols), i32),
        vmem(split, f32),
        vmem((tiles, BLOCK), i32),
        vmem((tiles, BLOCK), f32),
        vmem((tiles, BLOCK), f32),
        vmem((tiles, BLOCK), f32),
        vmem((rows, cols), f32),
        vmem((rows, cols), f32),
        vmem((rows, cols), f32),
        vmem((rows, BLOCK), f32),
        vmem((rows, BLOCK), f32),
        vmem((rows, 8, cols), f32),
        vmem((4, rows, 8, cols), f32),
        vmem((rows, 8, cols), f32),
        vmem((tiles + 1, 8, BLOCK), f32),
        vmem((tiles + 1, 8, BLOCK), i32),
        vmem((nlon, 8, BLOCK), f32),
        vmem((nlon, 8, BLOCK), i32),
        vmem((nlon, 8, BLOCK), f32),
        vmem((nlon, 8, BLOCK), i32),
        vmem((8, BLOCK), i32),
        smem((8, BLOCK), i32),
        vmem((slots, 2, 8, BLOCK), f32),
        vmem((slots + 1, 256, BLOCK), f32),
        vmem((slots + 1, 2, 8, BLOCK), f32),
        vmem((HALOS,) + field, f32),
        vmem((rows * nblk, 2, 8, BLOCK), f32),
        vmem(field, f32),
        vmem(field, f32),
        vmem(field, f32),
        vmem(field, f32),
        vmem(field, f32),
        vmem(field, f32),
        vmem(field, f32),
        vmem(field, f32),
        vmem((HALOS,) + ends, f32),
        vmem((HALOS,) + ends, f32),
        vmem(ends, f32),
        vmem(ends, f32),
        vmem(ends, f32),
        vmem(ends, f32),
        vmem(ends, f32),
        vmem((rows + 2, 8, cols), f32),
        vmem((2, 8, BLOCK), f32),
        vmem((2, 8, BLOCK), f32),
        vmem((SUMS, nlat * nlon, BLOCK), f32),
        vmem((SUMS, 1, BLOCK), f32),
        pltpu.SemaphoreType.REGULAR,
        dma((10,)),
        dma((HALOS, 4)),
        dma((HALOS, 4)),
        dma((4,)),
        dma((4,)),
        dma((SUMS,)),
        dma((SUMS,)),
        dma((2, nlon)),
        dma((2, nlon)),
        dma((4,)),
        dma((4,)),
        dma((1,)),
    ]
    shape = vmem(split, f32)
    x, p, r, q, size = pl.pallas_call(
        functools.partial(kernel, nlat, nlon),
        out_shape=(shape,) * 4 + (vmem((rows, cols), f32),),
        in_specs=[hbm] * 10,
        out_specs=(pl.BlockSpec(memory_space=vmem),) * 5,
        scratch_shapes=scratch,
        compiler_params=pltpu.CompilerParams(
            collective_id=0, has_side_effects=True, vmem_limit_bytes=61 * 2**20
        ),
    )(
        tile_route.reshape(-1), tile_block, depth, friction, ocean_mask, forcing.reshape(split),
        obs_cell, obs_time, obs_value, obs_weight,
    )
    return (x + size * p).reshape(forcing.shape), (r - size * q).reshape(forcing.shape)


def solution(mesh):
    tile = P(("lat", "lon"), None)
    grid = P("lat", "lon")
    in_specs = (grid, grid, grid, P(None, "lat", "lon"), tile, P(("lat", "lon")), tile, tile, tile, tile)
    out_specs = (P(None, "lat", "lon"), P(None, "lat", "lon"))
    body = functools.partial(shards, mesh.shape["lat"], mesh.shape["lon"])
    return jax.shard_map(body, mesh=mesh, in_specs=in_specs, out_specs=out_specs, check_vma=False)
```

```python
import functools
import math

import jax
import jax.numpy as jnp
import numpy as np
from jax import lax
from jax.experimental import pallas as pl
from jax.experimental.pallas import tpu as pltpu
from jax.sharding import PartitionSpec as P

BLOCK = 128
CAP = 2
ITERS = 3
OUTER = 2
SUMS = ITERS * OUTER
HALOS = 7
MESH = pl.DeviceIdType.MESH
OMEGA_DEGREES = (28.984104, 30.0, 28.43973, 30.082137, 15.041069, 13.943036, 14.958931, 13.398661)
RATES = np.array(OMEGA_DEGREES, np.float32) * np.float32(math.pi / 180.0)
STIFF = np.float32(0.2) * (RATES / RATES[0]) ** 2


def sin_cos(angle):
    turn = jnp.floor(angle * (2.0 / math.pi) + 0.5)
    x = ((angle - turn * 1.5703125) - turn * 4.837512969970703125e-4) - turn * 7.54978995489188216e-8
    z = x * x
    s = ((-1.9515295891e-4 * z + 8.3321608736e-3) * z - 1.6666654611e-1) * z * x + x
    c = ((2.443315711809948e-5 * z - 1.388731625493765e-3) * z + 4.166664568298827e-2) * z * z - 0.5 * z + 1.0
    quarter = turn.astype(jnp.int32)
    odd = (quarter & 1) == 1
    sine = jnp.where(odd, c, s)
    cosine = jnp.where(odd, s, c)
    sine = jnp.where((quarter & 2) == 2, -sine, sine)
    cosine = jnp.where(((quarter + 1) & 2) == 2, -cosine, cosine)
    return sine, cosine


def kernel(
    nlat, nlon,
    route_in, tblk_in, depth_in, fric_in, mask_in, forc_in, ocell_in, otime_in, oval_in, oweight_in,
    x_out, p_out, r_out, q_out, size_out,
    route, tblk, depth, fric, mask, forc, ocell, otime, oval, oweight,
    dw, dwn, dws, dwe, dww, wetfric, coef, diag,
    pay, payi, outf, outi, inf, ini, plan, splan, waves, mats, oslot,
    field, seen, r1, p1, q1, z_last, r2, p2, q2, x,
    pk, hq, hq1, hx, hp, hr, hw, surf, surf_pk, surf_hq, sum_a, part_row, ready,
    load, hs, hrv, ss, sr, as_, ar, os_, orv, ds_, dr, loc,
):
    rows, cols = depth.shape
    nblk = cols // BLOCK
    slots = nlon * CAP
    tiles = otime.shape[0]
    me_lat = lax.axis_index("lat")
    me_lon = lax.axis_index("lon")
    north, south = lax.rem(me_lat + 1, nlat), lax.rem(me_lat + nlat - 1, nlat)
    east, west = lax.rem(me_lon + 1, nlon), lax.rem(me_lon + nlon - 1, nlon)
    me = me_lat * nlon + me_lon
    count = nlat * nlon

    barrier = pltpu.get_barrier_semaphore()
    for k in range(1, nlon):
        pl.semaphore_signal(barrier, inc=1, device_id={"lon": lax.rem(me_lon + k, nlon)}, device_id_type=MESH)
    for k in range(1, nlat):
        pl.semaphore_signal(barrier, inc=1, device_id={"lat": lax.rem(me_lat + k, nlat)}, device_id_type=MESH)
    pairs = [
        (route_in, route), (tblk_in, tblk), (ocell_in, ocell), (otime_in, otime), (oval_in, oval),
        (oweight_in, oweight), (depth_in, depth), (mask_in, mask), (fric_in, fric), (forc_in, forc),
    ]
    loads = [pltpu.make_async_copy(src, dst, load.at[k]) for k, (src, dst) in enumerate(pairs)]
    for c in loads:
        c.start()

    def remote(src, dst, send, recv, where):
        return pltpu.make_async_remote_copy(
            src_ref=src, dst_ref=dst, send_sem=send, recv_sem=recv, device_id=where, device_id_type=MESH
        )

    lane = lax.broadcasted_iota(jnp.int32, (1, BLOCK), 1)
    lane8 = lax.broadcasted_iota(jnp.int32, (8, BLOCK), 1)
    sub8 = lax.broadcasted_iota(jnp.int32, (8, BLOCK), 0)
    zero = jnp.zeros((2, 8, BLOCK), jnp.float32)

    for c in loads[:8]:
        c.wait()
    wet = mask[...].astype(jnp.float32)
    dw[...] = depth[...] * wet

    for t in range(tiles):
        pay[t] = jnp.concatenate([otime[t : t + 1], oval[t : t + 1], oweight[t : t + 1], oval[t : t + 1]] * 2, axis=0)
        payi[t] = jnp.broadcast_to(ocell[t : t + 1] + tblk[t] * BLOCK, (8, BLOCK))
    pay[tiles] = jnp.zeros((8, BLOCK), jnp.float32)
    payi[tiles] = jnp.zeros((8, BLOCK), jnp.int32)

    def pick(p, carry):
        first, second = jnp.int32(tiles), jnp.int32(tiles)
        for t in reversed(range(tiles)):
            hit = route[t] == p
            second = jnp.where(hit, first, second)
            first = jnp.where(hit, jnp.int32(t), first)
        outf[p] = jnp.where(sub8 < 4, pay[first], pay[second])
        outi[p] = jnp.where(sub8 == 0, payi[first], payi[second])
        return carry

    lax.fori_loop(0, nlon, pick, 0)
    pl.semaphore_wait(barrier, nlon + nlat - 2)

    def obs_copy(k):
        peer = lax.rem(me_lon + k, nlon)
        return [
            remote(outf.at[peer], inf.at[me_lon], os_.at[0, peer], orv.at[0, me_lon], {"lon": peer}),
            remote(outi.at[peer], ini.at[me_lon], os_.at[1, peer], orv.at[1, me_lon], {"lon": peer}),
        ]

    def obs_wait(k):
        peer = lax.rem(me_lon + k, nlon)
        remote(outf.at[peer], inf.at[peer], os_.at[0, peer], orv.at[0, peer], {"lon": peer}).wait_recv()
        remote(outi.at[peer], ini.at[peer], os_.at[1, peer], orv.at[1, peer], {"lon": peer}).wait_recv()

    obs_sends = [c for k in range(1, nlon) for c in obs_copy(k)]
    for c in obs_sends:
        c.start()
    first_copies = [
        remote(dw.at[:, pl.ds(0, BLOCK)], dwe, ds_.at[2], dr.at[2], {"lon": west}),
        remote(dw.at[:, pl.ds(cols - BLOCK, BLOCK)], dww, ds_.at[3], dr.at[3], {"lon": east}),
        remote(dw, dws, ds_.at[0], dr.at[0], {"lat": north}),
        remote(dw, dwn, ds_.at[1], dr.at[1], {"lat": south}),
    ]
    for c in first_copies:
        c.start()
    for k in range(1, nlat):
        pl.semaphore_signal(ready, inc=1, device_id={"lat": lax.rem(me_lat + k, nlat)}, device_id_type=MESH)
    inf[me_lon] = outf[me_lon]
    ini[me_lon] = outi[me_lon]
    for c in loads[8:]:
        c.wait()

    for cb in range(nblk):
        at = pl.ds(cb * BLOCK, BLOCK)
        for h in range(2):
            wetted = forc[h, :, :, at] * wet[None, :, cb * BLOCK : cb * BLOCK + BLOCK]
            field[0, pl.ds(1, rows), cb, h] = jnp.swapaxes(wetted, 0, 1)
    oslot[slots] = zero
    mats[slots] = jnp.zeros((256, BLOCK), jnp.float32)
    stiff = jnp.zeros((8, 1), jnp.float32)
    rate = jnp.zeros((8, BLOCK), jnp.float32)
    sub1 = lax.broadcasted_iota(jnp.int32, (8, 1), 0)
    for c in range(8):
        stiff = jnp.where(sub1 == c, float(STIFF[c]), stiff)
        rate = jnp.where(sub8 == c, float(RATES[c]), rate)
    cells = lax.broadcasted_iota(jnp.int32, (BLOCK, BLOCK), 0)

    for k in range(1, nlon):
        obs_wait(k)

    def where_is(s):
        return ini[s // CAP, pl.ds(s % CAP, 1), :]

    rep = jnp.full((1, BLOCK), slots, jnp.int32)
    homes = jnp.full((1, BLOCK), -1, jnp.int32)
    for s in reversed(range(slots)):
        home = where_is(s) >> 7
        rep = jnp.where(home == lane, s, rep)
        homes = jnp.where(lane == s, home, homes)
    chain = jnp.full((1, BLOCK), slots, jnp.int32)
    for s in reversed(range(slots)):
        home = where_is(s) >> 7
        chain = jnp.where((home == homes) & (lane < s), s, chain)
    plan[...] = jnp.where(
        sub8 == 0,
        jnp.broadcast_to(homes, (8, BLOCK)),
        jnp.where(sub8 == 1, jnp.broadcast_to(chain, (8, BLOCK)), jnp.broadcast_to(rep, (8, BLOCK))),
    )
    to_scalars = pltpu.make_async_copy(plan, splan, loc.at[0])
    to_scalars.start()

    def onto_cells(o, k, terms):
        cell = ini[o, pl.ds(k, 1), :] & (BLOCK - 1)
        high = terms.astype(jnp.bfloat16)
        low = (terms - high.astype(jnp.float32)).astype(jnp.bfloat16)
        hot = (cells == cell).astype(jnp.float32).astype(jnp.bfloat16)
        return lax.dot_general(
            jnp.concatenate([high, low], axis=1),
            jnp.concatenate([hot, hot], axis=1),
            (((1,), (1,)), ((), ())),
            preferred_element_type=jnp.float32,
        )

    def values(o, carry):
        for k in range(CAP):
            times = inf[o, pl.ds(4 * k, 1), :]
            scaled = inf[o, pl.ds(4 * k + 2, 1), :] * inf[o, pl.ds(4 * k + 1, 1), :]
            sine, cosine = sin_cos(rate * times)
            waves[o * CAP + k, 0] = cosine
            waves[o * CAP + k, 1] = sine
            terms = jnp.concatenate([cosine * scaled, sine * scaled], axis=0)
            oslot[o * CAP + k] = onto_cells(o, k, terms).reshape(2, 8, BLOCK)
        return carry

    lax.fori_loop(0, nlon, values, 0, unroll=4)
    to_scalars.wait()

    def join_values(i, carry):
        s = slots - 1 - i
        oslot[s] = oslot[s] + oslot[splan[1, s]]
        return carry

    lax.fori_loop(0, slots, join_values, 0)

    def keep_ends(k, src):
        for side, cb in enumerate((0, nblk - 1)):
            packed = zero
            for row in range(rows):
                moved = pltpu.roll(src[row + 1, cb], (row + side) % BLOCK, 2)
                packed = jnp.where(lane8 == row, moved, packed)
            pk[k, side] = packed

    def start_rhs(blocks):
        def line(row, carry):
            for cb in blocks:
                v = field[0, row + 1, cb] + oslot[splan[2, row * nblk + cb]]
                field[0, row + 1, cb] = v
                seen[row * nblk + cb] = v
            return carry

        lax.fori_loop(0, rows, line, 0, unroll=rows if len(blocks) == 2 else 2)

    start_rhs((0, nblk - 1))
    keep_ends(0, field.at[0])

    def halo(k):
        return [
            remote(pk.at[k, 0], hq.at[k, 1], hs.at[k, 2], hrv.at[k, 2], {"lon": west}),
            remote(pk.at[k, 1], hq.at[k, 0], hs.at[k, 3], hrv.at[k, 3], {"lon": east}),
            remote(field.at[k, 1], field.at[k, rows + 1], hs.at[k, 0], hrv.at[k, 0], {"lat": south}),
            remote(field.at[k, rows], field.at[k, 0], hs.at[k, 1], hrv.at[k, 1], {"lat": north}),
        ]

    def send_halo(k, part=slice(None)):
        for c in halo(k)[part]:
            c.start()

    def wait_halo(k):
        for c in halo(k):
            c.wait_recv()

    send_halo(0, slice(0, 2))
    start_rhs(range(1, nblk - 1))
    send_halo(0, slice(2, 4))

    for c in first_copies:
        c.wait_recv()
    a = dw[...]
    colid = lax.broadcasted_iota(jnp.int32, (rows, cols), 1)
    rowid = lax.broadcasted_iota(jnp.int32, (rows, cols), 0)
    keep_n = (me_lat < nlat - 1).astype(jnp.float32)
    keep_s = (me_lat > 0).astype(jnp.float32)

    def harmonic(first, second):
        return 2.0 * first * second / jnp.maximum(first + second, 0.5)

    drag = fric[...]
    total = wet * drag + (1.0 - wet)
    around = (
        lambda: jnp.where(colid == cols - 1, dwe[:, 0:1], pltpu.roll(a, cols - 1, 1)),
        lambda: jnp.where(colid == 0, dww[:, BLOCK - 1 : BLOCK], pltpu.roll(a, 1, 1)),
        lambda: jnp.where(rowid == rows - 1, dwn[0:1, :] * keep_n, pltpu.roll(a, rows - 1, 0)),
        lambda: jnp.where(rowid == 0, dws[rows - 1 : rows, :] * keep_s, pltpu.roll(a, 1, 0)),
    )
    for k in range(4):
        side = harmonic(a, around[k]())
        total = total + side
        for row in range(rows):
            coef[k, row] = jnp.broadcast_to(side[row : row + 1], (8, cols))
    dragged = wet * drag
    for row in range(rows):
        wetfric[row] = jnp.broadcast_to(dragged[row : row + 1], (8, cols))
        wide = jnp.broadcast_to(wet[row : row + 1], (8, cols))
        diag[row] = wide * stiff + jnp.broadcast_to(total[row : row + 1], (8, cols))

    def build(o, carry):
        for k in range(CAP):
            weight = inf[o, pl.ds(4 * k + 2, 1), :]
            basis = (waves[o * CAP + k, 0], waves[o * CAP + k, 1])
            parts = []
            for h in range(2):
                for c in range(8):
                    one = weight * basis[h][c : c + 1]
                    parts.append(one * basis[0])
                    parts.append(one * basis[1])
            mats[o * CAP + k] = onto_cells(o, k, jnp.concatenate(parts, axis=0))
        return carry

    lax.fori_loop(0, nlon, build, 0)

    def join_mats(i, carry):
        s = slots - 1 - i
        mats[s] = mats[s] + mats[splan[1, s]]
        return carry

    lax.fori_loop(0, slots, join_mats, 0)

    def observe():
        def slot(s, carry):
            v = seen[splan[0, s]]
            acc = [zero, zero]
            for c in range(16):
                m = mats[s, 16 * c : 16 * c + 16, :].reshape(2, 8, BLOCK)
                acc[c % 2] = acc[c % 2] + m * v[c // 8, c % 8 : c % 8 + 1, :]
            oslot[s] = acc[0] + acc[1]
            return carry

        lax.fori_loop(0, slots, slot, 0, unroll=2)

    def eastward(v, beyond):
        moved = [pltpu.roll(b, BLOCK - 1, 2) for b in v] + [beyond]
        return [jnp.where(lane8 == BLOCK - 1, moved[cb + 1], moved[cb]) for cb in range(nblk)]

    def westward(v, beyond):
        moved = [beyond] + [pltpu.roll(b, 1, 2) for b in v]
        return [jnp.where(lane8 == 0, moved[cb], moved[cb + 1]) for cb in range(nblk)]

    def from_east(halos, row):
        return pltpu.roll(halos[1], BLOCK - 1 - row, 2)

    def from_west(halos, row):
        return pltpu.roll(halos[0], BLOCK - row, 2)

    def image_row(src, row, east_side, west_side, to_north=True, to_south=True):
        v = [src[row + 1, cb] for cb in range(nblk)]
        e = eastward(v, east_side)
        w = westward(v, west_side)
        images = []
        for cb in range(nblk):
            at = pl.ds(cb * BLOCK, BLOCK)
            image = (
                diag[row, :, at] * v[cb]
                - coef[0, row, :, at] * e[cb]
                - coef[1, row, :, at] * w[cb]
                + oslot[splan[2, row * nblk + cb]]
            )
            if to_north:
                image = image - coef[2, row, :, at] * src[row + 2, cb]
            if to_south:
                image = image - coef[3, row, :, at] * src[row, cb]
            images.append(image)
        return v, images

    def inside(src, dst):
        def put(row, images):
            for cb in range(nblk):
                dst[row + 1, cb] = images[cb]

        def line(row, carry):
            put(row, image_row(src, row, zero, zero)[1])
            return carry

        lax.fori_loop(1, rows - 1, line, 0, unroll=2)
        put(0, image_row(src, 0, zero, zero, to_south=False)[1])
        put(rows - 1, image_row(src, rows - 1, zero, zero, to_north=False)[1])

    def edges(src, halos, dst):
        for cb in range(nblk):
            at = pl.ds(cb * BLOCK, BLOCK)
            dst[1, cb] = dst[1, cb] - coef[3, 0, :, at] * src[0, cb]
            dst[rows, cb] = dst[rows, cb] - coef[2, rows - 1, :, at] * src[rows + 1, cb]

        first, last = pl.ds(0, BLOCK), pl.ds(cols - BLOCK, BLOCK)
        for row in range(rows):
            beside = jnp.where(lane8 == 0, from_west(halos, row), 0.0)
            dst[row + 1, 0] = dst[row + 1, 0] - coef[1, row, :, first] * beside
            beside = jnp.where(lane8 == BLOCK - 1, from_east(halos, row), 0.0)
            dst[row + 1, nblk - 1] = dst[row + 1, nblk - 1] - coef[0, row, :, last] * beside

    lat_order = sorted(range(nlat), key=lambda k: (k == 0, abs(k - nlat // 2)))
    lon_order = sorted(range(nlon), key=lambda k: (k == 0, k % 2 == 0, -abs(k - nlon // 2)))
    lat_peers = {k: lax.rem(me_lat + k, nlat) for k in lat_order}
    lon_peers = {k: lax.rem(me_lon + k, nlon) for k in lon_order}

    def sum_wait(i):
        whole = sum_a.at[i, pl.ds(0, count - 1)]
        return remote(whole, whole, as_.at[i], ar.at[i], {"lat": south})

    def send_sums(i, sums):
        part = jnp.zeros((8, BLOCK), jnp.float32)
        for k, s in enumerate(sums):
            both = s + pltpu.roll(s, 64, 1)
            both = both + pltpu.roll(both, 32, 1)
            part = jnp.where(lane8 >> 5 == k, both, part)
        row = jnp.sum(part, axis=0, keepdims=True)
        part_row[i] = row
        sum_a[i, pl.ds(me, 1)] = row
        for a in lat_order:
            for b in lon_order:
                if a or b:
                    where = {"lat": lat_peers[a], "lon": lon_peers[b]}
                    remote(part_row.at[i], sum_a.at[i, pl.ds(me, 1)], as_.at[i], ar.at[i], where).start()

    def take_sums(i):
        sum_wait(i).wait_recv()
        total = jnp.sum(sum_a[i], axis=0, keepdims=True)
        whole = jnp.sum(jnp.where(lane8 >> 5 == sub8, total, 0.0), axis=1, keepdims=True)
        return [jnp.broadcast_to(whole[k : k + 1], (8, BLOCK)) for k in range(4)]

    def beta_of(size, rr, rq, qq):
        return (rr - 2.0 * size * rq + size * size * qq) / rr

    def halves(sums):
        return [v[0] + v[1] for v in sums]

    def outer(o):
        k0, kq, kz = 4 * o, 4 * o + 1, 4 * o + 2
        i0, i1, i2 = ITERS * o, ITERS * o + 1, ITERS * o + 2
        r0, q0, z0 = field.at[k0], field.at[kq], field.at[kz]
        z1 = field.at[3] if o == 0 else z_last
        observe()
        if o == 0:
            inside(r0, q0)
            wait_halo(k0)
            edges(r0, hq.at[k0], q0)

        def first_dots(row, carry):
            rr, rq, qq = carry
            if o == 0:
                v = [r0[row + 1, cb] for cb in range(nblk)]
                images = [q0[row + 1, cb] for cb in range(nblk)]
            else:
                v, images = image_row(r0, row, from_east(hq.at[k0], row), from_west(hq.at[k0], row))
            for cb in range(nblk):
                res, image = v[cb], images[cb]
                if o > 0:
                    q0[row + 1, cb] = image
                rr = rr + res * res
                rq = rq + res * image
                qq = qq + image * image
            return rr, rq, qq

        sums = halves(lax.fori_loop(0, rows, first_dots, (zero, zero, zero), unroll=2))
        keep_ends(kq, q0)
        send_halo(kq, slice(0, 2))
        if o == 0:
            pl.semaphore_wait(ready, nlat - 1)
        send_sums(i0, sums)
        send_halo(kq, slice(2, 4))

        def look(row, carry):
            for cb in range(nblk):
                seen[row * nblk + cb] = q0[row + 1, cb]
            return carry

        lax.fori_loop(0, rows, look, 0)
        observe()
        inside(q0, z0)
        wait_halo(kq)
        edges(q0, hq.at[kq], z0)

        keep_ends(kz, z0)
        send_halo(kz)
        rr, rq, qq, _ = take_sums(i0)
        size0 = rr / rq
        beta0 = beta_of(size0, rr, rq, qq)
        more = 1.0 + beta0

        def second_vectors(row, cb):
            r, q, z = r0[row + 1, cb], q0[row + 1, cb], z0[row + 1, cb]
            res = r - size0 * q
            return res, res + beta0 * r, more * q - size0 * z

        def second(row, carry):
            rr, rq, dq, qq = carry
            for cb in range(nblk):
                res, way, image = second_vectors(row, cb)
                rr = rr + res * res
                rq = rq + res * image
                dq = dq + way * image
                qq = qq + image * image
            return rr, rq, dq, qq

        part_rr, part_rq, part_dq, part_qq = sums = halves(lax.fori_loop(0, rows, second, (zero,) * 4, unroll=2))
        send_sums(i1, sums)

        def keep_second(row, carry):
            for cb in range(nblk):
                r1[row + 1, cb], p1[row + 1, cb], image = second_vectors(row, cb)
                q1[row + 1, cb] = image
                seen[row * nblk + cb] = image
            return carry

        lax.fori_loop(0, rows, keep_second, 0, unroll=2)
        observe()
        inside(q1, z1)
        wait_halo(kz)
        for edge in (0, rows + 1):
            for cb in range(nblk):
                q1[edge, cb] = more * q0[edge, cb] - size0 * z0[edge, cb]
        hq1[...] = more * hq[kq] - size0 * hq[kz]
        edges(q1, hq1, z1)
        if o == 0:
            keep_ends(3, z1)
            send_halo(3)

        def third(row, carry):
            rw, rz, qw, qz, pw, pz = carry
            for cb in range(nblk):
                r, q, p, z = r1[row + 1, cb], q1[row + 1, cb], p1[row + 1, cb], z1[row + 1, cb]
                w = q0[row + 1, cb] - size0 * z0[row + 1, cb]
                rw = rw + r * w
                rz = rz + r * z
                qw = qw + q * w
                qz = qz + q * z
                pw = pw + p * w
                pz = pz + p * z
            return rw, rz, qw, qz, pw, pz

        rw, rz, qw, qz, pw, pz = halves(lax.fori_loop(0, rows, third, (zero,) * 6, unroll=2))
        rr, rq, dq, qq = take_sums(i1)
        size1 = rr / dq
        beta1 = beta_of(size1, rr, rq, qq)
        with_r = rw - size1 * rz + beta1 * part_rq
        with_q = qw - size1 * qz + beta1 * part_qq
        with_p = pw - size1 * pz + beta1 * part_dq
        send_sums(
            i2,
            [
                part_rr - 2.0 * size1 * part_rq + size1 * size1 * part_qq,
                with_r - size1 * with_q + beta1 * with_p,
            ],
        )

        def settle(blocks):
            def line(row, carry):
                for cb in blocks:
                    q, p = q1[row + 1, cb], p1[row + 1, cb]
                    res = r1[row + 1, cb] - size1 * q
                    r2[row + 1, cb] = res
                    p2[row + 1, cb] = res + beta1 * p
                    w = q0[row + 1, cb] - size0 * z0[row + 1, cb]
                    q2[row + 1, cb] = (w - size1 * z1[row + 1, cb]) + beta1 * q
                    moved = size0 * r0[row + 1, cb]
                    x[row + 1, cb] = (moved if o == 0 else x[row + 1, cb] + moved) + size1 * p
                return carry

            lax.fori_loop(0, rows, line, 0, unroll=2)

        return size0, beta0, size1, beta1, settle

    size0, beta0, size1, beta1, settle = outer(0)
    end_blocks = sorted({0, 1, nblk - 1})
    settle(end_blocks)

    def beyond(r, q, q_next):
        res = r - size0 * q
        way = res + beta0 * r
        res = res - size1 * q_next
        return size0 * r + size1 * way, res + beta1 * way, res

    for edge in (0, rows + 1):
        for cb in range(nblk):
            x[edge, cb], p2[edge, cb], r2[edge, cb] = beyond(field[0, edge, cb], field[1, edge, cb], q1[edge, cb])
    hx[...], hp[...], hr[...] = beyond(hq[0], hq[1], hq1[...])

    def add_up(square):
        return jnp.sum(square[0] + square[1], axis=0, keepdims=True)

    def surface(row, cb):
        at = pl.ds(cb * BLOCK, BLOCK)
        flux = []
        for ref, halos in ((x, hx), (p2, hp)):
            v = ref[row + 1, cb]
            after = pltpu.roll(ref[row + 1, cb + 1], BLOCK - 1, 2) if cb < nblk - 1 else from_east(halos, row)
            e = jnp.where(lane8 == BLOCK - 1, after, pltpu.roll(v, BLOCK - 1, 2))
            flux.append((coef[0, row, :, at] * (e - v), coef[2, row, :, at] * (ref[row + 2, cb] - v)))
        (xe, xn), (pe, pn) = flux
        parts = jnp.where(sub8 == 0, add_up(xe * xe + xn * xn), wetfric[row, :, at])
        parts = jnp.where(sub8 == 1, add_up(xe * pe + xn * pn), parts)
        parts = jnp.where(sub8 == 2, add_up(pe * pe + pn * pn), parts)
        surf[row + 1, :, at] = parts
        return parts

    def surface_ends(row, ends):
        first, last = surface(row, 0), surface(row, nblk - 1)
        return (
            jnp.where(lane8 == row, pltpu.roll(first, row, 1), ends[0]),
            jnp.where(lane8 == row, pltpu.roll(last, row + 1, 1), ends[1]),
        )

    blank = jnp.zeros((8, BLOCK), jnp.float32)
    ends = lax.fori_loop(0, rows, surface_ends, (blank, blank), unroll=4)
    surf_pk[0] = ends[0]
    surf_pk[1] = ends[1]
    surf_copies = [
        remote(surf_pk.at[0], surf_hq.at[1], ss.at[2], sr.at[2], {"lon": west}),
        remote(surf_pk.at[1], surf_hq.at[0], ss.at[3], sr.at[3], {"lon": east}),
        remote(surf.at[1], surf.at[rows + 1], ss.at[0], sr.at[0], {"lat": south}),
        remote(surf.at[rows], surf.at[0], ss.at[1], sr.at[1], {"lat": north}),
    ]
    for c in surf_copies[:2]:
        c.start()
    settle([cb for cb in range(nblk) if cb not in end_blocks])

    def surface_middle(row, carry):
        for cb in range(1, nblk - 1):
            surface(row, cb)
        return carry

    lax.fori_loop(0, rows, surface_middle, 0)
    for c in surf_copies[2:]:
        c.start()
    wait_halo(3)

    def image_beyond(q, z, z_next, q_next):
        return ((q - size0 * z) - size1 * z_next) + beta1 * q_next

    for edge in (0, rows + 1):
        for cb in range(nblk):
            q2[edge, cb] = image_beyond(field[1, edge, cb], field[2, edge, cb], field[3, edge, cb], q1[edge, cb])
    hw[...] = image_beyond(hq[1], hq[2], hq[3], hq1[...])
    for c in surf_copies:
        c.wait_recv()
    rr, dq, _, _ = take_sums(2)
    size2 = rr / dq
    ramp = jnp.where(sub8 == 0, 1.0, jnp.where(sub8 == 1, 2.0 * size2, jnp.where(sub8 == 2, size2 * size2, 0.0)))

    def extra_of(parts):
        speed = jnp.maximum(jnp.sum(parts * ramp, axis=0, keepdims=True), 0.0)
        return parts[3:4] * (jnp.sqrt(1.0 + speed / 16.0) - 1.0)

    def renew(row, cb):
        extra = extra_of(surf[row, :, pl.ds(cb * BLOCK, BLOCK)])
        place = x[row, cb] + size2 * p2[row, cb]
        new = (r2[row, cb] - size2 * q2[row, cb]) - extra * place
        field[4, row, cb] = new
        return extra, place, new

    def friction(row, carry):
        for cb in range(nblk):
            at = pl.ds(cb * BLOCK, BLOCK)
            extra, place, new = renew(row + 1, cb)
            x[row + 1, cb] = place
            diag[row, :, at] = diag[row, :, at] + extra
            seen[row * nblk + cb] = new
        return carry

    lax.fori_loop(0, rows, friction, 0, unroll=2)
    for edge in (0, rows + 1):
        for cb in range(nblk):
            renew(edge, cb)
    for side in range(2):
        hq[4, side] = (hr[side] - size2 * hw[side]) - extra_of(surf_hq[side]) * (hx[side] + size2 * hp[side])
    size0, beta0, size1, beta1, settle = outer(1)
    settle(range(nblk))
    for c in obs_sends + first_copies:
        c.wait_send()
    for src, dst in ((x, x_out), (p2, p_out), (r2, r_out), (q2, q_out)):
        for cb in range(nblk):
            for h in range(2):
                dst[h, :, :, pl.ds(cb * BLOCK, BLOCK)] = jnp.swapaxes(src[pl.ds(1, rows), cb, h], 0, 1)
    for k in (0, 1, 2, 3, 5, 6):
        for c in halo(k):
            c.wait_send()
    for c in surf_copies:
        c.wait_send()
    rr, dq, _, _ = take_sums(SUMS - 1)
    size_out[...] = jnp.broadcast_to((rr / dq)[:, 0:1], (8, cols))
    for i in range(SUMS):
        sum_wait(i).wait_send()


def shards(nlat, nlon, depth, friction, ocean_mask, forcing, tile_route, tile_block, obs_cell, obs_time, obs_value, obs_weight):
    channels, rows, cols = forcing.shape
    slots = nlon * CAP
    nblk, tiles = cols // BLOCK, obs_time.shape[0]
    f32, i32 = jnp.float32, jnp.int32
    vmem, smem = pltpu.VMEM, pltpu.SMEM
    hbm = pl.BlockSpec(memory_space=pltpu.HBM)
    field = (rows + 2, nblk, 2, 8, BLOCK)
    ends = (2, 2, 8, BLOCK)
    split = (2, channels // 2, rows, cols)
    dma = pltpu.SemaphoreType.DMA
    scratch = [
        smem((tiles,), i32),
        smem((tiles,), i32),
        vmem((rows, cols), f32),
        vmem((rows, cols), f32),
        vmem((rows, cols), i32),
        vmem(split, f32),
        vmem((tiles, BLOCK), i32),
        vmem((tiles, BLOCK), f32),
        vmem((tiles, BLOCK), f32),
        vmem((tiles, BLOCK), f32),
        vmem((rows, cols), f32),
        vmem((rows, cols), f32),
        vmem((rows, cols), f32),
        vmem((rows, BLOCK), f32),
        vmem((rows, BLOCK), f32),
        vmem((rows, 8, cols), f32),
        vmem((4, rows, 8, cols), f32),
        vmem((rows, 8, cols), f32),
        vmem((tiles + 1, 8, BLOCK), f32),
        vmem((tiles + 1, 8, BLOCK), i32),
        vmem((nlon, 8, BLOCK), f32),
        vmem((nlon, 8, BLOCK), i32),
        vmem((nlon, 8, BLOCK), f32),
        vmem((nlon, 8, BLOCK), i32),
        vmem((8, BLOCK), i32),
        smem((8, BLOCK), i32),
        vmem((slots, 2, 8, BLOCK), f32),
        vmem((slots + 1, 256, BLOCK), f32),
        vmem((slots + 1, 2, 8, BLOCK), f32),
        vmem((HALOS,) + field, f32),
        vmem((rows * nblk, 2, 8, BLOCK), f32),
        vmem(field, f32),
        vmem(field, f32),
        vmem(field, f32),
        vmem(field, f32),
        vmem(field, f32),
        vmem(field, f32),
        vmem(field, f32),
        vmem(field, f32),
        vmem((HALOS,) + ends, f32),
        vmem((HALOS,) + ends, f32),
        vmem(ends, f32),
        vmem(ends, f32),
        vmem(ends, f32),
        vmem(ends, f32),
        vmem(ends, f32),
        vmem((rows + 2, 8, cols), f32),
        vmem((2, 8, BLOCK), f32),
        vmem((2, 8, BLOCK), f32),
        vmem((SUMS, nlat * nlon, BLOCK), f32),
        vmem((SUMS, 1, BLOCK), f32),
        pltpu.SemaphoreType.REGULAR,
        dma((10,)),
        dma((HALOS, 4)),
        dma((HALOS, 4)),
        dma((4,)),
        dma((4,)),
        dma((SUMS,)),
        dma((SUMS,)),
        dma((2, nlon)),
        dma((2, nlon)),
        dma((4,)),
        dma((4,)),
        dma((1,)),
    ]
    shape = vmem(split, f32)
    x, p, r, q, size = pl.pallas_call(
        functools.partial(kernel, nlat, nlon),
        out_shape=(shape,) * 4 + (vmem((rows, cols), f32),),
        in_specs=[hbm] * 10,
        out_specs=(pl.BlockSpec(memory_space=vmem),) * 5,
        scratch_shapes=scratch,
        compiler_params=pltpu.CompilerParams(
            collective_id=0, has_side_effects=True, vmem_limit_bytes=61 * 2**20
        ),
    )(
        tile_route.reshape(-1), tile_block, depth, friction, ocean_mask, forcing.reshape(split),
        obs_cell, obs_time, obs_value, obs_weight,
    )
    return (x + size * p).reshape(forcing.shape), (r - size * q).reshape(forcing.shape)


def solution(mesh):
    tile = P(("lat", "lon"), None)
    grid = P("lat", "lon")
    in_specs = (grid, grid, grid, P(None, "lat", "lon"), tile, P(("lat", "lon")), tile, tile, tile, tile)
    out_specs = (P(None, "lat", "lon"), P(None, "lat", "lon"))
    body = functools.partial(shards, mesh.shape["lat"], mesh.shape["lon"])
    return jax.shard_map(body, mesh=mesh, in_specs=in_specs, out_specs=out_specs, check_vma=False)
```

```python
import functools
import math

import jax
import jax.numpy as jnp
import numpy as np
from jax import lax
from jax.experimental import pallas as pl
from jax.experimental.pallas import tpu as pltpu
from jax.sharding import PartitionSpec as P

BLOCK = 128
CAP = 2
ITERS = 3
OUTER = 2
SUMS = ITERS * OUTER
HALOS = 7
MESH = pl.DeviceIdType.MESH
OMEGA_DEGREES = (28.984104, 30.0, 28.43973, 30.082137, 15.041069, 13.943036, 14.958931, 13.398661)
RATES = np.array(OMEGA_DEGREES, np.float32) * np.float32(math.pi / 180.0)
STIFF = np.float32(0.2) * (RATES / RATES[0]) ** 2


def sin_cos(angle):
    turn = jnp.floor(angle * (2.0 / math.pi) + 0.5)
    x = ((angle - turn * 1.5703125) - turn * 4.837512969970703125e-4) - turn * 7.54978995489188216e-8
    z = x * x
    s = ((-1.9515295891e-4 * z + 8.3321608736e-3) * z - 1.6666654611e-1) * z * x + x
    c = ((2.443315711809948e-5 * z - 1.388731625493765e-3) * z + 4.166664568298827e-2) * z * z - 0.5 * z + 1.0
    quarter = turn.astype(jnp.int32)
    odd = (quarter & 1) == 1
    sine = jnp.where(odd, c, s)
    cosine = jnp.where(odd, s, c)
    sine = jnp.where((quarter & 2) == 2, -sine, sine)
    cosine = jnp.where(((quarter + 1) & 2) == 2, -cosine, cosine)
    return sine, cosine


def kernel(
    nlat, nlon,
    route_in, tblk_in, depth_in, fric_in, mask_in, forc_in, ocell_in, otime_in, oval_in, oweight_in,
    x_out, p_out, r_out, q_out, size_out,
    route, tblk, depth, fric, mask, forc, ocell, otime, oval, oweight,
    dw, dwn, dws, dwe, dww, wetfric, coef, diag,
    pay, payi, outf, outi, inf, ini, plan, splan, waves, mats, oslot,
    field, seen, r1, p1, q1, z_last, r2, p2, q2, x,
    pk, hq, hq1, hx, hp, hr, hw, surf, surf_pk, surf_hq, near, end_coef, sum_a, part_row, ready,
    load, hs, hrv, ss, sr, as_, ar, os_, orv, ds_, dr, loc,
):
    rows, cols = depth.shape
    nblk = cols // BLOCK
    slots = nlon * CAP
    tiles = otime.shape[0]
    me_lat = lax.axis_index("lat")
    me_lon = lax.axis_index("lon")
    north, south = lax.rem(me_lat + 1, nlat), lax.rem(me_lat + nlat - 1, nlat)
    east, west = lax.rem(me_lon + 1, nlon), lax.rem(me_lon + nlon - 1, nlon)
    me = me_lat * nlon + me_lon
    count = nlat * nlon

    barrier = pltpu.get_barrier_semaphore()
    for k in range(1, nlon):
        pl.semaphore_signal(barrier, inc=1, device_id={"lon": lax.rem(me_lon + k, nlon)}, device_id_type=MESH)
    for k in range(1, nlat):
        pl.semaphore_signal(barrier, inc=1, device_id={"lat": lax.rem(me_lat + k, nlat)}, device_id_type=MESH)
    pairs = [
        (route_in, route), (tblk_in, tblk), (ocell_in, ocell), (otime_in, otime), (oval_in, oval),
        (oweight_in, oweight), (depth_in, depth), (mask_in, mask), (fric_in, fric), (forc_in, forc),
    ]
    loads = [pltpu.make_async_copy(src, dst, load.at[k]) for k, (src, dst) in enumerate(pairs)]
    for c in loads:
        c.start()

    def remote(src, dst, send, recv, where):
        return pltpu.make_async_remote_copy(
            src_ref=src, dst_ref=dst, send_sem=send, recv_sem=recv, device_id=where, device_id_type=MESH
        )

    lane = lax.broadcasted_iota(jnp.int32, (1, BLOCK), 1)
    lane8 = lax.broadcasted_iota(jnp.int32, (8, BLOCK), 1)
    sub8 = lax.broadcasted_iota(jnp.int32, (8, BLOCK), 0)
    zero = jnp.zeros((2, 8, BLOCK), jnp.float32)

    for c in loads[:8]:
        c.wait()
    wet = mask[...].astype(jnp.float32)
    dw[...] = depth[...] * wet

    for t in range(tiles):
        pay[t] = jnp.concatenate([otime[t : t + 1], oval[t : t + 1], oweight[t : t + 1], oval[t : t + 1]] * 2, axis=0)
        payi[t] = jnp.broadcast_to(ocell[t : t + 1] + tblk[t] * BLOCK, (8, BLOCK))
    pay[tiles] = jnp.zeros((8, BLOCK), jnp.float32)
    payi[tiles] = jnp.zeros((8, BLOCK), jnp.int32)

    def pick(p, carry):
        first, second = jnp.int32(tiles), jnp.int32(tiles)
        for t in reversed(range(tiles)):
            hit = route[t] == p
            second = jnp.where(hit, first, second)
            first = jnp.where(hit, jnp.int32(t), first)
        outf[p] = jnp.where(sub8 < 4, pay[first], pay[second])
        outi[p] = jnp.where(sub8 == 0, payi[first], payi[second])
        return carry

    lax.fori_loop(0, nlon, pick, 0)
    pl.semaphore_wait(barrier, nlon + nlat - 2)

    def obs_copy(k):
        peer = lax.rem(me_lon + k, nlon)
        return [
            remote(outf.at[peer], inf.at[me_lon], os_.at[0, peer], orv.at[0, me_lon], {"lon": peer}),
            remote(outi.at[peer], ini.at[me_lon], os_.at[1, peer], orv.at[1, me_lon], {"lon": peer}),
        ]

    def obs_wait(k):
        peer = lax.rem(me_lon + k, nlon)
        remote(outf.at[peer], inf.at[peer], os_.at[0, peer], orv.at[0, peer], {"lon": peer}).wait_recv()
        remote(outi.at[peer], ini.at[peer], os_.at[1, peer], orv.at[1, peer], {"lon": peer}).wait_recv()

    obs_sends = [c for k in range(1, nlon) for c in obs_copy(k)]
    for c in obs_sends:
        c.start()
    first_copies = [
        remote(dw.at[:, pl.ds(0, BLOCK)], dwe, ds_.at[2], dr.at[2], {"lon": west}),
        remote(dw.at[:, pl.ds(cols - BLOCK, BLOCK)], dww, ds_.at[3], dr.at[3], {"lon": east}),
        remote(dw, dws, ds_.at[0], dr.at[0], {"lat": north}),
        remote(dw, dwn, ds_.at[1], dr.at[1], {"lat": south}),
    ]
    for c in first_copies:
        c.start()
    for k in range(1, nlat):
        pl.semaphore_signal(ready, inc=1, device_id={"lat": lax.rem(me_lat + k, nlat)}, device_id_type=MESH)
    inf[me_lon] = outf[me_lon]
    ini[me_lon] = outi[me_lon]
    for c in loads[8:]:
        c.wait()

    for cb in range(nblk):
        at = pl.ds(cb * BLOCK, BLOCK)
        for h in range(2):
            wetted = forc[h, :, :, at] * wet[None, :, cb * BLOCK : cb * BLOCK + BLOCK]
            field[0, pl.ds(1, rows), cb, h] = jnp.swapaxes(wetted, 0, 1)
    oslot[slots] = zero
    mats[slots] = jnp.zeros((256, BLOCK), jnp.float32)
    stiff = jnp.zeros((8, 1), jnp.float32)
    rate = jnp.zeros((8, BLOCK), jnp.float32)
    sub1 = lax.broadcasted_iota(jnp.int32, (8, 1), 0)
    for c in range(8):
        stiff = jnp.where(sub1 == c, float(STIFF[c]), stiff)
        rate = jnp.where(sub8 == c, float(RATES[c]), rate)
    cells = lax.broadcasted_iota(jnp.int32, (BLOCK, BLOCK), 0)

    for k in range(1, nlon):
        obs_wait(k)

    def where_is(s):
        return ini[s // CAP, pl.ds(s % CAP, 1), :]

    rep = jnp.full((1, BLOCK), slots, jnp.int32)
    homes = jnp.full((1, BLOCK), -1, jnp.int32)
    for s in reversed(range(slots)):
        home = where_is(s) >> 7
        rep = jnp.where(home == lane, s, rep)
        homes = jnp.where(lane == s, home, homes)
    chain = jnp.full((1, BLOCK), slots, jnp.int32)
    for s in reversed(range(slots)):
        home = where_is(s) >> 7
        chain = jnp.where((home == homes) & (lane < s), s, chain)
    plan[...] = jnp.where(
        sub8 == 0,
        jnp.broadcast_to(homes, (8, BLOCK)),
        jnp.where(sub8 == 1, jnp.broadcast_to(chain, (8, BLOCK)), jnp.broadcast_to(rep, (8, BLOCK))),
    )
    to_scalars = pltpu.make_async_copy(plan, splan, loc.at[0])
    to_scalars.start()

    def onto_cells(o, k, terms):
        cell = ini[o, pl.ds(k, 1), :] & (BLOCK - 1)
        high = terms.astype(jnp.bfloat16)
        low = (terms - high.astype(jnp.float32)).astype(jnp.bfloat16)
        hot = (cells == cell).astype(jnp.float32).astype(jnp.bfloat16)
        return lax.dot_general(
            jnp.concatenate([high, low], axis=1),
            jnp.concatenate([hot, hot], axis=1),
            (((1,), (1,)), ((), ())),
            preferred_element_type=jnp.float32,
        )

    def values(o, carry):
        for k in range(CAP):
            times = inf[o, pl.ds(4 * k, 1), :]
            scaled = inf[o, pl.ds(4 * k + 2, 1), :] * inf[o, pl.ds(4 * k + 1, 1), :]
            sine, cosine = sin_cos(rate * times)
            waves[o * CAP + k, 0] = cosine
            waves[o * CAP + k, 1] = sine
            terms = jnp.concatenate([cosine * scaled, sine * scaled], axis=0)
            oslot[o * CAP + k] = onto_cells(o, k, terms).reshape(2, 8, BLOCK)
        return carry

    lax.fori_loop(0, nlon, values, 0, unroll=4)
    to_scalars.wait()

    def join_values(i, carry):
        s = slots - 1 - i
        oslot[s] = oslot[s] + oslot[splan[1, s]]
        return carry

    lax.fori_loop(0, slots, join_values, 0)

    def keep_ends(k, src):
        for side, cb in enumerate((0, nblk - 1)):
            packed = zero
            for row in range(rows):
                moved = pltpu.roll(src[row + 1, cb], (row + side) % BLOCK, 2)
                packed = jnp.where(lane8 == row, moved, packed)
            pk[k, side] = packed

    def keep_near(k):
        packed = zero
        for row in range(rows):
            packed = jnp.where(lane8 == row, pltpu.roll(field[k, row + 1, 0], (row + BLOCK - 1) % BLOCK, 2), packed)
        near[k] = packed

    def start_rhs(blocks):
        def line(row, carry):
            for cb in blocks:
                v = field[0, row + 1, cb] + oslot[splan[2, row * nblk + cb]]
                field[0, row + 1, cb] = v
                seen[row * nblk + cb] = v
            return carry

        lax.fori_loop(0, rows, line, 0, unroll=rows if len(blocks) == 2 else 2)

    start_rhs((0, nblk - 1))
    keep_ends(0, field.at[0])

    def halo(k):
        return [
            remote(pk.at[k, 0], hq.at[k, 1], hs.at[k, 2], hrv.at[k, 2], {"lon": west}),
            remote(pk.at[k, 1], hq.at[k, 0], hs.at[k, 3], hrv.at[k, 3], {"lon": east}),
            remote(field.at[k, 1], field.at[k, rows + 1], hs.at[k, 0], hrv.at[k, 0], {"lat": south}),
            remote(field.at[k, rows], field.at[k, 0], hs.at[k, 1], hrv.at[k, 1], {"lat": north}),
        ]

    def send_halo(k, part=slice(None)):
        for c in halo(k)[part]:
            c.start()

    def wait_halo(k):
        for c in halo(k):
            c.wait_recv()

    send_halo(0, slice(0, 2))
    start_rhs(range(1, nblk - 1))
    send_halo(0, slice(2, 4))

    for c in first_copies:
        c.wait_recv()
    a = dw[...]
    colid = lax.broadcasted_iota(jnp.int32, (rows, cols), 1)
    rowid = lax.broadcasted_iota(jnp.int32, (rows, cols), 0)
    keep_n = (me_lat < nlat - 1).astype(jnp.float32)
    keep_s = (me_lat > 0).astype(jnp.float32)

    def harmonic(first, second):
        return 2.0 * first * second / jnp.maximum(first + second, 0.5)

    drag = fric[...]
    total = wet * drag + (1.0 - wet)
    around = (
        lambda: jnp.where(colid == cols - 1, dwe[:, 0:1], pltpu.roll(a, cols - 1, 1)),
        lambda: jnp.where(colid == 0, dww[:, BLOCK - 1 : BLOCK], pltpu.roll(a, 1, 1)),
        lambda: jnp.where(rowid == rows - 1, dwn[0:1, :] * keep_n, pltpu.roll(a, rows - 1, 0)),
        lambda: jnp.where(rowid == 0, dws[rows - 1 : rows, :] * keep_s, pltpu.roll(a, 1, 0)),
    )
    for k in range(4):
        side = harmonic(a, around[k]())
        total = total + side
        for row in range(rows):
            coef[k, row] = jnp.broadcast_to(side[row : row + 1], (8, cols))
    dragged = wet * drag
    for row in range(rows):
        wetfric[row] = jnp.broadcast_to(dragged[row : row + 1], (8, cols))
        wide = jnp.broadcast_to(wet[row : row + 1], (8, cols))
        diag[row] = wide * stiff + jnp.broadcast_to(total[row : row + 1], (8, cols))

    def pack_rows(ref, lead, side):
        packed = jnp.zeros((8, BLOCK), jnp.float32)
        at = pl.ds(side * (cols - BLOCK), BLOCK)
        for row in range(rows):
            value = ref[lead + (row, slice(None), at)]
            packed = jnp.where(lane8 == row, pltpu.roll(value, (row + side) % BLOCK, 1), packed)
        return packed

    def build(o, carry):
        for k in range(CAP):
            weight = inf[o, pl.ds(4 * k + 2, 1), :]
            basis = (waves[o * CAP + k, 0], waves[o * CAP + k, 1])
            parts = []
            for h in range(2):
                for c in range(8):
                    one = weight * basis[h][c : c + 1]
                    parts.append(one * basis[0])
                    parts.append(one * basis[1])
            mats[o * CAP + k] = onto_cells(o, k, jnp.concatenate(parts, axis=0))
        return carry

    lax.fori_loop(0, nlon, build, 0)

    def join_mats(i, carry):
        s = slots - 1 - i
        mats[s] = mats[s] + mats[splan[1, s]]
        return carry

    lax.fori_loop(0, slots, join_mats, 0)
    for side in range(2):
        end_coef[side, 0] = pack_rows(coef, (0,), side)
        end_coef[side, 1] = pack_rows(coef, (2,), side)
        end_coef[side, 2] = pack_rows(wetfric, (), side)

    def observe():
        def slot(s, carry):
            v = seen[splan[0, s]]
            acc = [zero, zero]
            for c in range(16):
                m = mats[s, 16 * c : 16 * c + 16, :].reshape(2, 8, BLOCK)
                acc[c % 2] = acc[c % 2] + m * v[c // 8, c % 8 : c % 8 + 1, :]
            oslot[s] = acc[0] + acc[1]
            return carry

        lax.fori_loop(0, slots, slot, 0, unroll=2)

    def eastward(v, beyond):
        moved = [pltpu.roll(b, BLOCK - 1, 2) for b in v] + [beyond]
        return [jnp.where(lane8 == BLOCK - 1, moved[cb + 1], moved[cb]) for cb in range(nblk)]

    def westward(v, beyond):
        moved = [beyond] + [pltpu.roll(b, 1, 2) for b in v]
        return [jnp.where(lane8 == 0, moved[cb], moved[cb + 1]) for cb in range(nblk)]

    def from_east(halos, row):
        return pltpu.roll(halos[1], BLOCK - 1 - row, 2)

    def from_west(halos, row):
        return pltpu.roll(halos[0], BLOCK - row, 2)

    def image_row(src, row, east_side, west_side, to_north=True, to_south=True):
        v = [src[row + 1, cb] for cb in range(nblk)]
        e = eastward(v, east_side)
        w = westward(v, west_side)
        images = []
        for cb in range(nblk):
            at = pl.ds(cb * BLOCK, BLOCK)
            image = (
                diag[row, :, at] * v[cb]
                - coef[0, row, :, at] * e[cb]
                - coef[1, row, :, at] * w[cb]
                + oslot[splan[2, row * nblk + cb]]
            )
            if to_north:
                image = image - coef[2, row, :, at] * src[row + 2, cb]
            if to_south:
                image = image - coef[3, row, :, at] * src[row, cb]
            images.append(image)
        return v, images

    def inside(src, dst):
        def put(row, images):
            for cb in range(nblk):
                dst[row + 1, cb] = images[cb]

        def line(row, carry):
            put(row, image_row(src, row, zero, zero)[1])
            return carry

        lax.fori_loop(1, rows - 1, line, 0, unroll=2)
        put(0, image_row(src, 0, zero, zero, to_south=False)[1])
        put(rows - 1, image_row(src, rows - 1, zero, zero, to_north=False)[1])

    def edges(src, halos, dst):
        for cb in range(nblk):
            at = pl.ds(cb * BLOCK, BLOCK)
            dst[1, cb] = dst[1, cb] - coef[3, 0, :, at] * src[0, cb]
            dst[rows, cb] = dst[rows, cb] - coef[2, rows - 1, :, at] * src[rows + 1, cb]

        first, last = pl.ds(0, BLOCK), pl.ds(cols - BLOCK, BLOCK)
        for row in range(rows):
            beside = jnp.where(lane8 == 0, from_west(halos, row), 0.0)
            dst[row + 1, 0] = dst[row + 1, 0] - coef[1, row, :, first] * beside
            beside = jnp.where(lane8 == BLOCK - 1, from_east(halos, row), 0.0)
            dst[row + 1, nblk - 1] = dst[row + 1, nblk - 1] - coef[0, row, :, last] * beside

    lat_order = sorted(range(nlat), key=lambda k: (k == 0, abs(k - nlat // 2)))
    lon_order = sorted(range(nlon), key=lambda k: (k == 0, k % 2 == 0, -abs(k - nlon // 2)))
    lat_peers = {k: lax.rem(me_lat + k, nlat) for k in lat_order}
    lon_peers = {k: lax.rem(me_lon + k, nlon) for k in lon_order}

    def sum_wait(i):
        whole = sum_a.at[i, pl.ds(0, count - 1)]
        return remote(whole, whole, as_.at[i], ar.at[i], {"lat": south})

    def send_sums(i, sums):
        part = jnp.zeros((8, BLOCK), jnp.float32)
        for k, s in enumerate(sums):
            both = s + pltpu.roll(s, 64, 1)
            both = both + pltpu.roll(both, 32, 1)
            part = jnp.where(lane8 >> 5 == k, both, part)
        row = jnp.sum(part, axis=0, keepdims=True)
        part_row[i] = row
        sum_a[i, pl.ds(me, 1)] = row
        for a in lat_order:
            for b in lon_order:
                if a or b:
                    where = {"lat": lat_peers[a], "lon": lon_peers[b]}
                    remote(part_row.at[i], sum_a.at[i, pl.ds(me, 1)], as_.at[i], ar.at[i], where).start()

    def take_sums(i):
        sum_wait(i).wait_recv()
        total = jnp.sum(sum_a[i], axis=0, keepdims=True)
        whole = jnp.sum(jnp.where(lane8 >> 5 == sub8, total, 0.0), axis=1, keepdims=True)
        return [jnp.broadcast_to(whole[k : k + 1], (8, BLOCK)) for k in range(4)]

    def beta_of(size, rr, rq, qq):
        return (rr - 2.0 * size * rq + size * size * qq) / rr

    def halves(sums):
        return [v[0] + v[1] for v in sums]

    def outer(o):
        k0, kq, kz = 4 * o, 4 * o + 1, 4 * o + 2
        i0, i1, i2 = ITERS * o, ITERS * o + 1, ITERS * o + 2
        r0, q0, z0 = field.at[k0], field.at[kq], field.at[kz]
        z1 = field.at[3] if o == 0 else z_last
        observe()
        if o == 0:
            inside(r0, q0)
            wait_halo(k0)
            edges(r0, hq.at[k0], q0)

        def first_dots(row, carry):
            rr, rq, qq = carry
            if o == 0:
                v = [r0[row + 1, cb] for cb in range(nblk)]
                images = [q0[row + 1, cb] for cb in range(nblk)]
            else:
                v, images = image_row(r0, row, from_east(hq.at[k0], row), from_west(hq.at[k0], row))
            for cb in range(nblk):
                res, image = v[cb], images[cb]
                if o > 0:
                    q0[row + 1, cb] = image
                rr = rr + res * res
                rq = rq + res * image
                qq = qq + image * image
            return rr, rq, qq

        sums = halves(lax.fori_loop(0, rows, first_dots, (zero, zero, zero), unroll=2))
        keep_ends(kq, q0)
        send_halo(kq, slice(0, 2))
        if o == 0:
            pl.semaphore_wait(ready, nlat - 1)
        send_sums(i0, sums)
        send_halo(kq, slice(2, 4))
        if o == 0:
            keep_near(0)
            keep_near(1)

        def look(row, carry):
            for cb in range(nblk):
                seen[row * nblk + cb] = q0[row + 1, cb]
            return carry

        lax.fori_loop(0, rows, look, 0)
        observe()
        inside(q0, z0)
        wait_halo(kq)
        edges(q0, hq.at[kq], z0)

        keep_ends(kz, z0)
        send_halo(kz)
        if o == 0:
            keep_near(2)
        rr, rq, qq, _ = take_sums(i0)
        size0 = rr / rq
        beta0 = beta_of(size0, rr, rq, qq)
        more = 1.0 + beta0

        def second_vectors(row, cb):
            r, q, z = r0[row + 1, cb], q0[row + 1, cb], z0[row + 1, cb]
            res = r - size0 * q
            return res, res + beta0 * r, more * q - size0 * z

        def second(row, carry):
            ri, qi, ii = carry
            for cb in range(nblk):
                q = q0[row + 1, cb]
                image = more * q - size0 * z0[row + 1, cb]
                ri = ri + r0[row + 1, cb] * image
                qi = qi + q * image
                ii = ii + image * image
            return ri, qi, ii

        part_ri, part_qi, part_qq = halves(lax.fori_loop(0, rows, second, (zero,) * 3, unroll=2))
        part_rr = sums[0] - 2.0 * size0 * sums[1] + size0 * size0 * sums[2]
        part_rq = part_ri - size0 * part_qi
        part_dq = part_rq + beta0 * part_ri
        sums = (part_rr, part_rq, part_dq, part_qq)
        send_sums(i1, sums)

        def keep_second(row, carry):
            for cb in range(nblk):
                r1[row + 1, cb], p1[row + 1, cb], image = second_vectors(row, cb)
                q1[row + 1, cb] = image
                seen[row * nblk + cb] = image
            return carry

        lax.fori_loop(0, rows, keep_second, 0, unroll=2)
        observe()
        inside(q1, z1)
        wait_halo(kz)
        for edge in (0, rows + 1):
            for cb in range(nblk):
                q1[edge, cb] = more * q0[edge, cb] - size0 * z0[edge, cb]
        hq1[...] = more * hq[kq] - size0 * hq[kz]
        edges(q1, hq1, z1)
        if o == 0:
            keep_ends(3, z1)
            send_halo(3)

        def third(row, carry):
            rw, rz, qw, qz, pw, pz = carry
            for cb in range(nblk):
                r, q, p, z = r1[row + 1, cb], q1[row + 1, cb], p1[row + 1, cb], z1[row + 1, cb]
                w = q0[row + 1, cb] - size0 * z0[row + 1, cb]
                rw = rw + r * w
                rz = rz + r * z
                qw = qw + q * w
                qz = qz + q * z
                pw = pw + p * w
                pz = pz + p * z
            return rw, rz, qw, qz, pw, pz

        rw, rz, qw, qz, pw, pz = halves(lax.fori_loop(0, rows, third, (zero,) * 6, unroll=2))
        rr, rq, dq, qq = take_sums(i1)
        size1 = rr / dq
        beta1 = beta_of(size1, rr, rq, qq)
        with_r = rw - size1 * rz + beta1 * part_rq
        with_q = qw - size1 * qz + beta1 * part_qq
        with_p = pw - size1 * pz + beta1 * part_dq
        send_sums(
            i2,
            [
                part_rr - 2.0 * size1 * part_rq + size1 * size1 * part_qq,
                with_r - size1 * with_q + beta1 * with_p,
            ],
        )

        def settle(blocks):
            def line(row, carry):
                for cb in blocks:
                    q, p = q1[row + 1, cb], p1[row + 1, cb]
                    res = r1[row + 1, cb] - size1 * q
                    r2[row + 1, cb] = res
                    p2[row + 1, cb] = res + beta1 * p
                    w = q0[row + 1, cb] - size0 * z0[row + 1, cb]
                    q2[row + 1, cb] = (w - size1 * z1[row + 1, cb]) + beta1 * q
                    moved = size0 * r0[row + 1, cb]
                    x[row + 1, cb] = (moved if o == 0 else x[row + 1, cb] + moved) + size1 * p
                return carry

            lax.fori_loop(0, rows, line, 0, unroll=2)

        return size0, beta0, size1, beta1, settle

    size0, beta0, size1, beta1, settle = outer(0)

    def beyond(r, q, q_next):
        res = r - size0 * q
        way = res + beta0 * r
        res = res - size1 * q_next
        return size0 * r + size1 * way, res + beta1 * way, res

    hx[...], hp[...], hr[...] = beyond(hq[0], hq[1], hq1[...])

    def add_up(square):
        return jnp.sum(square[0] + square[1], axis=0, keepdims=True)

    def parts_of(flux, dragged):
        (xe, xn), (pe, pn) = flux
        parts = jnp.where(sub8 == 0, add_up(xe * xe + xn * xn), dragged)
        parts = jnp.where(sub8 == 1, add_up(xe * pe + xn * pn), parts)
        return jnp.where(sub8 == 2, add_up(pe * pe + pn * pn), parts)

    def extended(k, side):
        corner = field[k, rows + 1, side * (nblk - 1)]
        return jnp.where(lane8 == rows, pltpu.roll(corner, (rows + side) % BLOCK, 2), pk[k, side])

    def state(r, q, z):
        return beyond(r, q, (1.0 + beta0) * q - size0 * z)[:2]

    for side in range(2):
        own = state(*(extended(k, side) for k in range(3)))
        after = (hx[1], hp[1]) if side else state(near[0], near[1], near[2])
        flux = [
            (end_coef[side, 0] * (e - v), end_coef[side, 1] * (pltpu.roll(v, BLOCK - 1, 2) - v))
            for v, e in zip(own, after)
        ]
        surf_pk[side] = parts_of(flux, end_coef[side, 2])
    surf_copies = [
        remote(surf_pk.at[0], surf_hq.at[1], ss.at[2], sr.at[2], {"lon": west}),
        remote(surf_pk.at[1], surf_hq.at[0], ss.at[3], sr.at[3], {"lon": east}),
        remote(surf.at[1], surf.at[rows + 1], ss.at[0], sr.at[0], {"lat": south}),
        remote(surf.at[rows], surf.at[0], ss.at[1], sr.at[1], {"lat": north}),
    ]
    for c in surf_copies[:2]:
        c.start()
    settle(range(nblk))
    for edge in (0, rows + 1):
        for cb in range(nblk):
            x[edge, cb], p2[edge, cb], r2[edge, cb] = beyond(field[0, edge, cb], field[1, edge, cb], q1[edge, cb])

    def surface(row, carry):
        for cb in range(nblk):
            at = pl.ds(cb * BLOCK, BLOCK)
            flux = []
            for ref, halos in ((x, hx), (p2, hp)):
                v = ref[row + 1, cb]
                after = pltpu.roll(ref[row + 1, cb + 1], BLOCK - 1, 2) if cb < nblk - 1 else from_east(halos, row)
                e = jnp.where(lane8 == BLOCK - 1, after, pltpu.roll(v, BLOCK - 1, 2))
                flux.append((coef[0, row, :, at] * (e - v), coef[2, row, :, at] * (ref[row + 2, cb] - v)))
            surf[row + 1, :, at] = parts_of(flux, wetfric[row, :, at])
        return carry

    lax.fori_loop(0, rows, surface, 0)
    for c in surf_copies[2:]:
        c.start()
    wait_halo(3)

    def image_beyond(q, z, z_next, q_next):
        return ((q - size0 * z) - size1 * z_next) + beta1 * q_next

    for edge in (0, rows + 1):
        for cb in range(nblk):
            q2[edge, cb] = image_beyond(field[1, edge, cb], field[2, edge, cb], field[3, edge, cb], q1[edge, cb])
    hw[...] = image_beyond(hq[1], hq[2], hq[3], hq1[...])
    for c in surf_copies:
        c.wait_recv()
    rr, dq, _, _ = take_sums(2)
    size2 = rr / dq
    ramp = jnp.where(sub8 == 0, 1.0, jnp.where(sub8 == 1, 2.0 * size2, jnp.where(sub8 == 2, size2 * size2, 0.0)))

    def extra_of(parts):
        speed = jnp.maximum(jnp.sum(parts * ramp, axis=0, keepdims=True), 0.0)
        return parts[3:4] * (jnp.sqrt(1.0 + speed / 16.0) - 1.0)

    def renew(row, cb):
        extra = extra_of(surf[row, :, pl.ds(cb * BLOCK, BLOCK)])
        place = x[row, cb] + size2 * p2[row, cb]
        new = (r2[row, cb] - size2 * q2[row, cb]) - extra * place
        field[4, row, cb] = new
        return extra, place, new

    def friction(row, carry):
        for cb in range(nblk):
            at = pl.ds(cb * BLOCK, BLOCK)
            extra, place, new = renew(row + 1, cb)
            x[row + 1, cb] = place
            diag[row, :, at] = diag[row, :, at] + extra
            seen[row * nblk + cb] = new
        return carry

    lax.fori_loop(0, rows, friction, 0, unroll=2)
    for edge in (0, rows + 1):
        for cb in range(nblk):
            renew(edge, cb)
    for side in range(2):
        hq[4, side] = (hr[side] - size2 * hw[side]) - extra_of(surf_hq[side]) * (hx[side] + size2 * hp[side])
    size0, beta0, size1, beta1, settle = outer(1)
    settle(range(nblk))
    for c in obs_sends + first_copies:
        c.wait_send()
    for src, dst in ((x, x_out), (p2, p_out), (r2, r_out), (q2, q_out)):
        for cb in range(nblk):
            for h in range(2):
                dst[h, :, :, pl.ds(cb * BLOCK, BLOCK)] = jnp.swapaxes(src[pl.ds(1, rows), cb, h], 0, 1)
    for k in (0, 1, 2, 3, 5, 6):
        for c in halo(k):
            c.wait_send()
    for c in surf_copies:
        c.wait_send()
    rr, dq, _, _ = take_sums(SUMS - 1)
    size_out[...] = jnp.broadcast_to((rr / dq)[:, 0:1], (8, cols))
    for i in range(SUMS):
        sum_wait(i).wait_send()


def shards(nlat, nlon, depth, friction, ocean_mask, forcing, tile_route, tile_block, obs_cell, obs_time, obs_value, obs_weight):
    channels, rows, cols = forcing.shape
    slots = nlon * CAP
    nblk, tiles = cols // BLOCK, obs_time.shape[0]
    f32, i32 = jnp.float32, jnp.int32
    vmem, smem = pltpu.VMEM, pltpu.SMEM
    hbm = pl.BlockSpec(memory_space=pltpu.HBM)
    field = (rows + 2, nblk, 2, 8, BLOCK)
    ends = (2, 2, 8, BLOCK)
    split = (2, channels // 2, rows, cols)
    dma = pltpu.SemaphoreType.DMA
    scratch = [
        smem((tiles,), i32),
        smem((tiles,), i32),
        vmem((rows, cols), f32),
        vmem((rows, cols), f32),
        vmem((rows, cols), i32),
        vmem(split, f32),
        vmem((tiles, BLOCK), i32),
        vmem((tiles, BLOCK), f32),
        vmem((tiles, BLOCK), f32),
        vmem((tiles, BLOCK), f32),
        vmem((rows, cols), f32),
        vmem((rows, cols), f32),
        vmem((rows, cols), f32),
        vmem((rows, BLOCK), f32),
        vmem((rows, BLOCK), f32),
        vmem((rows, 8, cols), f32),
        vmem((4, rows, 8, cols), f32),
        vmem((rows, 8, cols), f32),
        vmem((tiles + 1, 8, BLOCK), f32),
        vmem((tiles + 1, 8, BLOCK), i32),
        vmem((nlon, 8, BLOCK), f32),
        vmem((nlon, 8, BLOCK), i32),
        vmem((nlon, 8, BLOCK), f32),
        vmem((nlon, 8, BLOCK), i32),
        vmem((8, BLOCK), i32),
        smem((8, BLOCK), i32),
        vmem((slots, 2, 8, BLOCK), f32),
        vmem((slots + 1, 256, BLOCK), f32),
        vmem((slots + 1, 2, 8, BLOCK), f32),
        vmem((HALOS,) + field, f32),
        vmem((rows * nblk, 2, 8, BLOCK), f32),
        vmem(field, f32),
        vmem(field, f32),
        vmem(field, f32),
        vmem(field, f32),
        vmem(field, f32),
        vmem(field, f32),
        vmem(field, f32),
        vmem(field, f32),
        vmem((HALOS,) + ends, f32),
        vmem((HALOS,) + ends, f32),
        vmem(ends, f32),
        vmem(ends, f32),
        vmem(ends, f32),
        vmem(ends, f32),
        vmem(ends, f32),
        vmem((rows + 2, 8, cols), f32),
        vmem((2, 8, BLOCK), f32),
        vmem((2, 8, BLOCK), f32),
        vmem((3, 2, 8, BLOCK), f32),
        vmem((2, 3, 8, BLOCK), f32),
        vmem((SUMS, nlat * nlon, BLOCK), f32),
        vmem((SUMS, 1, BLOCK), f32),
        pltpu.SemaphoreType.REGULAR,
        dma((10,)),
        dma((HALOS, 4)),
        dma((HALOS, 4)),
        dma((4,)),
        dma((4,)),
        dma((SUMS,)),
        dma((SUMS,)),
        dma((2, nlon)),
        dma((2, nlon)),
        dma((4,)),
        dma((4,)),
        dma((1,)),
    ]
    shape = vmem(split, f32)
    x, p, r, q, size = pl.pallas_call(
        functools.partial(kernel, nlat, nlon),
        out_shape=(shape,) * 4 + (vmem((rows, cols), f32),),
        in_specs=[hbm] * 10,
        out_specs=(pl.BlockSpec(memory_space=vmem),) * 5,
        scratch_shapes=scratch,
        compiler_params=pltpu.CompilerParams(
            collective_id=0, has_side_effects=True, vmem_limit_bytes=61 * 2**20
        ),
    )(
        tile_route.reshape(-1), tile_block, depth, friction, ocean_mask, forcing.reshape(split),
        obs_cell, obs_time, obs_value, obs_weight,
    )
    return (x + size * p).reshape(forcing.shape), (r - size * q).reshape(forcing.shape)


def solution(mesh):
    tile = P(("lat", "lon"), None)
    grid = P("lat", "lon")
    in_specs = (grid, grid, grid, P(None, "lat", "lon"), tile, P(("lat", "lon")), tile, tile, tile, tile)
    out_specs = (P(None, "lat", "lon"), P(None, "lat", "lon"))
    body = functools.partial(shards, mesh.shape["lat"], mesh.shape["lon"])
    return jax.shard_map(body, mesh=mesh, in_specs=in_specs, out_specs=out_specs, check_vma=False)
```

```python
import functools
import math

import jax
import jax.numpy as jnp
import numpy as np
from jax import lax
from jax.experimental import pallas as pl
from jax.experimental.pallas import tpu as pltpu
from jax.sharding import PartitionSpec as P

BLOCK = 128
CAP = 2
ITERS = 3
OUTER = 2
SUMS = ITERS * OUTER
HALOS = 7
MESH = pl.DeviceIdType.MESH
OMEGA_DEGREES = (28.984104, 30.0, 28.43973, 30.082137, 15.041069, 13.943036, 14.958931, 13.398661)
RATES = np.array(OMEGA_DEGREES, np.float32) * np.float32(math.pi / 180.0)
STIFF = np.float32(0.2) * (RATES / RATES[0]) ** 2


def sin_cos(angle):
    turn = jnp.floor(angle * (2.0 / math.pi) + 0.5)
    x = ((angle - turn * 1.5703125) - turn * 4.837512969970703125e-4) - turn * 7.54978995489188216e-8
    z = x * x
    s = ((-1.9515295891e-4 * z + 8.3321608736e-3) * z - 1.6666654611e-1) * z * x + x
    c = ((2.443315711809948e-5 * z - 1.388731625493765e-3) * z + 4.166664568298827e-2) * z * z - 0.5 * z + 1.0
    quarter = turn.astype(jnp.int32)
    odd = (quarter & 1) == 1
    sine = jnp.where(odd, c, s)
    cosine = jnp.where(odd, s, c)
    sine = jnp.where((quarter & 2) == 2, -sine, sine)
    cosine = jnp.where(((quarter + 1) & 2) == 2, -cosine, cosine)
    return sine, cosine


def kernel(
    nlat, nlon,
    route_in, tblk_in, depth_in, fric_in, mask_in, forc_in, ocell_in, otime_in, oval_in, oweight_in,
    x_out, p_out, r_out, q_out, size_out,
    route, tblk, depth, fric, mask, forc, ocell, otime, oval, oweight,
    dw, dwn, dws, dwe, dww, wetfric, coef, diag,
    pay, payi, outf, outi, inf, ini, plan, splan, waves, mats, oslot,
    field, seen, r1, p1, q1, z_last, r2, p2, q2, x,
    pk, hq, hq1, hx, hp, hr, hw, surf, surf_pk, surf_hq, near, end_coef, sum_a, part_row, ready,
    load, hs, hrv, ss, sr, as_, ar, os_, orv, ds_, dr, loc,
):
    rows, cols = depth.shape
    nblk = cols // BLOCK
    slots = nlon * CAP
    tiles = otime.shape[0]
    me_lat = lax.axis_index("lat")
    me_lon = lax.axis_index("lon")
    north, south = lax.rem(me_lat + 1, nlat), lax.rem(me_lat + nlat - 1, nlat)
    east, west = lax.rem(me_lon + 1, nlon), lax.rem(me_lon + nlon - 1, nlon)
    me = me_lat * nlon + me_lon
    count = nlat * nlon

    barrier = pltpu.get_barrier_semaphore()
    for k in range(1, nlon):
        pl.semaphore_signal(barrier, inc=1, device_id={"lon": lax.rem(me_lon + k, nlon)}, device_id_type=MESH)
    for k in range(1, nlat):
        pl.semaphore_signal(barrier, inc=1, device_id={"lat": lax.rem(me_lat + k, nlat)}, device_id_type=MESH)
    pairs = [
        (route_in, route), (tblk_in, tblk), (ocell_in, ocell), (otime_in, otime), (oval_in, oval),
        (oweight_in, oweight), (depth_in, depth), (mask_in, mask), (fric_in, fric), (forc_in, forc),
    ]
    loads = [pltpu.make_async_copy(src, dst, load.at[k]) for k, (src, dst) in enumerate(pairs)]
    for c in loads:
        c.start()

    def remote(src, dst, send, recv, where):
        return pltpu.make_async_remote_copy(
            src_ref=src, dst_ref=dst, send_sem=send, recv_sem=recv, device_id=where, device_id_type=MESH
        )

    lane = lax.broadcasted_iota(jnp.int32, (1, BLOCK), 1)
    lane8 = lax.broadcasted_iota(jnp.int32, (8, BLOCK), 1)
    sub8 = lax.broadcasted_iota(jnp.int32, (8, BLOCK), 0)
    zero = jnp.zeros((2, 8, BLOCK), jnp.float32)

    for c in loads[:8]:
        c.wait()
    wet = mask[...].astype(jnp.float32)
    dw[...] = depth[...] * wet

    for t in range(tiles):
        pay[t] = jnp.concatenate([otime[t : t + 1], oval[t : t + 1], oweight[t : t + 1], oval[t : t + 1]] * 2, axis=0)
        payi[t] = jnp.broadcast_to(ocell[t : t + 1] + tblk[t] * BLOCK, (8, BLOCK))
    pay[tiles] = jnp.zeros((8, BLOCK), jnp.float32)
    payi[tiles] = jnp.zeros((8, BLOCK), jnp.int32)

    def pick(p, carry):
        first, second = jnp.int32(tiles), jnp.int32(tiles)
        for t in reversed(range(tiles)):
            hit = route[t] == p
            second = jnp.where(hit, first, second)
            first = jnp.where(hit, jnp.int32(t), first)
        outf[p] = jnp.where(sub8 < 4, pay[first], pay[second])
        outi[p] = jnp.where(sub8 == 0, payi[first], payi[second])
        return carry

    lax.fori_loop(0, nlon, pick, 0)
    pl.semaphore_wait(barrier, nlon + nlat - 2)

    def obs_copy(n, k):
        src, dst = ((outi, ini), (outf, inf))[n]
        peer = lax.rem(me_lon + k, nlon)
        return remote(src.at[peer], dst.at[me_lon], os_.at[n, peer], orv.at[n, me_lon], {"lon": peer})

    def obs_wait(n):
        src, dst = ((outi, ini), (outf, inf))[n]
        for k in range(1, nlon):
            peer = lax.rem(me_lon + k, nlon)
            remote(src.at[peer], dst.at[peer], os_.at[n, peer], orv.at[n, peer], {"lon": peer}).wait_recv()

    obs_sends = [obs_copy(n, k) for n in range(2) for k in range(1, nlon)]
    for c in obs_sends:
        c.start()
    first_copies = [
        remote(dw.at[:, pl.ds(0, BLOCK)], dwe, ds_.at[2], dr.at[2], {"lon": west}),
        remote(dw.at[:, pl.ds(cols - BLOCK, BLOCK)], dww, ds_.at[3], dr.at[3], {"lon": east}),
        remote(dw, dws, ds_.at[0], dr.at[0], {"lat": north}),
        remote(dw, dwn, ds_.at[1], dr.at[1], {"lat": south}),
    ]
    for c in first_copies:
        c.start()
    for k in range(1, nlat):
        pl.semaphore_signal(ready, inc=1, device_id={"lat": lax.rem(me_lat + k, nlat)}, device_id_type=MESH)
    inf[me_lon] = outf[me_lon]
    ini[me_lon] = outi[me_lon]
    for c in loads[8:]:
        c.wait()

    for cb in range(nblk):
        at = pl.ds(cb * BLOCK, BLOCK)
        for h in range(2):
            wetted = forc[h, :, :, at] * wet[None, :, cb * BLOCK : cb * BLOCK + BLOCK]
            field[0, pl.ds(1, rows), cb, h] = jnp.swapaxes(wetted, 0, 1)
    oslot[slots] = zero
    mats[slots] = jnp.zeros((256, BLOCK), jnp.float32)
    stiff = jnp.zeros((8, 1), jnp.float32)
    rate = jnp.zeros((8, BLOCK), jnp.float32)
    sub1 = lax.broadcasted_iota(jnp.int32, (8, 1), 0)
    for c in range(8):
        stiff = jnp.where(sub1 == c, float(STIFF[c]), stiff)
        rate = jnp.where(sub8 == c, float(RATES[c]), rate)
    cells = lax.broadcasted_iota(jnp.int32, (BLOCK, BLOCK), 0)

    obs_wait(0)
    places = [ini[s // CAP, pl.ds(s % CAP, 1), :] >> 7 for s in range(slots)]
    rep = jnp.full((1, BLOCK), slots, jnp.int32)
    homes = jnp.full((1, BLOCK), -1, jnp.int32)
    for s in reversed(range(slots)):
        home = places[s]
        rep = jnp.where(home == lane, s, rep)
        homes = jnp.where(lane == s, home, homes)
    chain = jnp.full((1, BLOCK), slots, jnp.int32)
    for s in reversed(range(slots)):
        home = places[s]
        chain = jnp.where((home == homes) & (lane < s), s, chain)
    plan[...] = jnp.where(
        sub8 == 0,
        jnp.broadcast_to(homes, (8, BLOCK)),
        jnp.where(sub8 == 1, jnp.broadcast_to(chain, (8, BLOCK)), jnp.broadcast_to(rep, (8, BLOCK))),
    )
    to_scalars = pltpu.make_async_copy(plan, splan, loc.at[0])
    to_scalars.start()
    obs_wait(1)

    def onto_cells(o, k, terms):
        cell = ini[o, pl.ds(k, 1), :] & (BLOCK - 1)
        high = terms.astype(jnp.bfloat16)
        low = (terms - high.astype(jnp.float32)).astype(jnp.bfloat16)
        hot = (cells == cell).astype(jnp.float32).astype(jnp.bfloat16)
        return lax.dot_general(
            jnp.concatenate([high, low], axis=1),
            jnp.concatenate([hot, hot], axis=1),
            (((1,), (1,)), ((), ())),
            preferred_element_type=jnp.float32,
        )

    def values(o, carry):
        for k in range(CAP):
            times = inf[o, pl.ds(4 * k, 1), :]
            scaled = inf[o, pl.ds(4 * k + 2, 1), :] * inf[o, pl.ds(4 * k + 1, 1), :]
            sine, cosine = sin_cos(rate * times)
            waves[o * CAP + k, 0] = cosine
            waves[o * CAP + k, 1] = sine
            terms = jnp.concatenate([cosine * scaled, sine * scaled], axis=0)
            oslot[o * CAP + k] = onto_cells(o, k, terms).reshape(2, 8, BLOCK)
        return carry

    lax.fori_loop(0, nlon, values, 0, unroll=4)
    to_scalars.wait()

    def join_values(i, carry):
        s = slots - 1 - i
        oslot[s] = oslot[s] + oslot[splan[1, s]]
        return carry

    lax.fori_loop(0, slots, join_values, 0)

    def keep_ends(k, src):
        for side, cb in enumerate((0, nblk - 1)):
            packed = zero
            for row in range(rows):
                moved = pltpu.roll(src[row + 1, cb], (row + side) % BLOCK, 2)
                packed = jnp.where(lane8 == row, moved, packed)
            pk[k, side] = packed

    def keep_near(k):
        packed = zero
        for row in range(rows):
            packed = jnp.where(lane8 == row, pltpu.roll(field[k, row + 1, 0], (row + BLOCK - 1) % BLOCK, 2), packed)
        near[k] = packed

    def start_rhs(blocks):
        def line(row, carry):
            for cb in blocks:
                v = field[0, row + 1, cb] + oslot[splan[2, row * nblk + cb]]
                field[0, row + 1, cb] = v
                seen[row * nblk + cb] = v
            return carry

        lax.fori_loop(0, rows, line, 0, unroll=rows if len(blocks) == 2 else 2)

    start_rhs((0, nblk - 1))
    keep_ends(0, field.at[0])

    def halo(k):
        return [
            remote(pk.at[k, 0], hq.at[k, 1], hs.at[k, 2], hrv.at[k, 2], {"lon": west}),
            remote(pk.at[k, 1], hq.at[k, 0], hs.at[k, 3], hrv.at[k, 3], {"lon": east}),
            remote(field.at[k, 1], field.at[k, rows + 1], hs.at[k, 0], hrv.at[k, 0], {"lat": south}),
            remote(field.at[k, rows], field.at[k, 0], hs.at[k, 1], hrv.at[k, 1], {"lat": north}),
        ]

    def send_halo(k, part=slice(None)):
        for c in halo(k)[part]:
            c.start()

    def wait_halo(k, part=slice(None)):
        for c in halo(k)[part]:
            c.wait_recv()

    send_halo(0, slice(0, 2))
    start_rhs(range(1, nblk - 1))
    send_halo(0, slice(2, 4))

    for c in first_copies:
        c.wait_recv()
    a = dw[...]
    colid = lax.broadcasted_iota(jnp.int32, (rows, cols), 1)
    rowid = lax.broadcasted_iota(jnp.int32, (rows, cols), 0)
    keep_n = (me_lat < nlat - 1).astype(jnp.float32)
    keep_s = (me_lat > 0).astype(jnp.float32)

    def harmonic(first, second):
        return 2.0 * first * second / jnp.maximum(first + second, 0.5)

    drag = fric[...]
    total = wet * drag + (1.0 - wet)
    around = (
        lambda: jnp.where(colid == cols - 1, dwe[:, 0:1], pltpu.roll(a, cols - 1, 1)),
        lambda: jnp.where(colid == 0, dww[:, BLOCK - 1 : BLOCK], pltpu.roll(a, 1, 1)),
        lambda: jnp.where(rowid == rows - 1, dwn[0:1, :] * keep_n, pltpu.roll(a, rows - 1, 0)),
        lambda: jnp.where(rowid == 0, dws[rows - 1 : rows, :] * keep_s, pltpu.roll(a, 1, 0)),
    )
    for k in range(4):
        side = harmonic(a, around[k]())
        total = total + side
        for row in range(rows):
            coef[k, row] = jnp.broadcast_to(side[row : row + 1], (8, cols))
    dragged = wet * drag
    for row in range(rows):
        wetfric[row] = jnp.broadcast_to(dragged[row : row + 1], (8, cols))
        wide = jnp.broadcast_to(wet[row : row + 1], (8, cols))
        diag[row] = wide * stiff + jnp.broadcast_to(total[row : row + 1], (8, cols))

    def pack_rows(ref, lead, side):
        packed = jnp.zeros((8, BLOCK), jnp.float32)
        at = pl.ds(side * (cols - BLOCK), BLOCK)
        for row in range(rows):
            value = ref[lead + (row, slice(None), at)]
            packed = jnp.where(lane8 == row, pltpu.roll(value, (row + side) % BLOCK, 1), packed)
        return packed

    def build(o, carry):
        for k in range(CAP):
            weight = inf[o, pl.ds(4 * k + 2, 1), :]
            basis = (waves[o * CAP + k, 0], waves[o * CAP + k, 1])
            parts = []
            for h in range(2):
                for c in range(8):
                    one = weight * basis[h][c : c + 1]
                    parts.append(one * basis[0])
                    parts.append(one * basis[1])
            mats[o * CAP + k] = onto_cells(o, k, jnp.concatenate(parts, axis=0))
        return carry

    lax.fori_loop(0, nlon, build, 0)

    def join_mats(i, carry):
        s = slots - 1 - i
        mats[s] = mats[s] + mats[splan[1, s]]
        return carry

    lax.fori_loop(0, slots, join_mats, 0)
    for side in range(2):
        end_coef[side, 0] = pack_rows(coef, (0,), side)
        end_coef[side, 1] = pack_rows(coef, (2,), side)
        end_coef[side, 2] = pack_rows(wetfric, (), side)

    def observe():
        def slot(s, carry):
            v = seen[splan[0, s]]
            acc = [zero, zero]
            for c in range(16):
                m = mats[s, 16 * c : 16 * c + 16, :].reshape(2, 8, BLOCK)
                acc[c % 2] = acc[c % 2] + m * v[c // 8, c % 8 : c % 8 + 1, :]
            oslot[s] = acc[0] + acc[1]
            return carry

        lax.fori_loop(0, slots, slot, 0, unroll=4)

    def eastward(v, beyond):
        moved = [pltpu.roll(b, BLOCK - 1, 2) for b in v] + [beyond]
        return [jnp.where(lane8 == BLOCK - 1, moved[cb + 1], moved[cb]) for cb in range(nblk)]

    def westward(v, beyond):
        moved = [beyond] + [pltpu.roll(b, 1, 2) for b in v]
        return [jnp.where(lane8 == 0, moved[cb], moved[cb + 1]) for cb in range(nblk)]

    def from_east(halos, row):
        return pltpu.roll(halos[1], BLOCK - 1 - row, 2)

    def from_west(halos, row):
        return pltpu.roll(halos[0], BLOCK - row, 2)

    def image_row(src, row, east_side, west_side, to_north=True, to_south=True):
        v = [src[row + 1, cb] for cb in range(nblk)]
        e = eastward(v, east_side)
        w = westward(v, west_side)
        images = []
        for cb in range(nblk):
            at = pl.ds(cb * BLOCK, BLOCK)
            image = (
                diag[row, :, at] * v[cb]
                - coef[0, row, :, at] * e[cb]
                - coef[1, row, :, at] * w[cb]
                + oslot[splan[2, row * nblk + cb]]
            )
            if to_north:
                image = image - coef[2, row, :, at] * src[row + 2, cb]
            if to_south:
                image = image - coef[3, row, :, at] * src[row, cb]
            images.append(image)
        return v, images

    def inside(src, dst):
        def put(row, images):
            for cb in range(nblk):
                dst[row + 1, cb] = images[cb]

        def line(row, carry):
            put(row, image_row(src, row, zero, zero)[1])
            return carry

        lax.fori_loop(1, rows - 1, line, 0, unroll=2)
        put(0, image_row(src, 0, zero, zero, to_south=False)[1])
        put(rows - 1, image_row(src, rows - 1, zero, zero, to_north=False)[1])

    def lat_edges(src, dst):
        for cb in range(nblk):
            at = pl.ds(cb * BLOCK, BLOCK)
            dst[1, cb] = dst[1, cb] - coef[3, 0, :, at] * src[0, cb]
            dst[rows, cb] = dst[rows, cb] - coef[2, rows - 1, :, at] * src[rows + 1, cb]

    def lon_edges(src, halos, dst):
        rq, qq = zero, zero
        for row in range(rows):
            for side in range(2):
                cb = side * (nblk - 1)
                beyond = from_east(halos, row) if side else from_west(halos, row)
                at = pl.ds(cb * BLOCK, BLOCK)
                change = coef[1 - side, row, :, at] * jnp.where(lane8 == side * (BLOCK - 1), -beyond, 0.0)
                old = dst[row + 1, cb]
                dst[row + 1, cb] = old + change
                rq = rq + src[row + 1, cb] * change
                qq = qq + change * (old + old + change)
        return rq, qq

    def edges(src, halos, dst):
        lat_edges(src, dst)
        lon_edges(src, halos, dst)

    lat_order = sorted(range(nlat), key=lambda k: (k == 0, abs(k - nlat // 2)))
    lon_order = sorted(range(nlon), key=lambda k: (k == 0, k % 2 == 0, -abs(k - nlon // 2)))
    lat_peers = {k: lax.rem(me_lat + k, nlat) for k in lat_order}
    lon_peers = {k: lax.rem(me_lon + k, nlon) for k in lon_order}

    def sum_wait(i):
        whole = sum_a.at[i, pl.ds(0, count - 1)]
        return remote(whole, whole, as_.at[i], ar.at[i], {"lat": south})

    def send_sums(i, sums):
        part = jnp.zeros((8, BLOCK), jnp.float32)
        for k, s in enumerate(sums):
            both = s + pltpu.roll(s, 64, 1)
            both = both + pltpu.roll(both, 32, 1)
            part = jnp.where(lane8 >> 5 == k, both, part)
        row = jnp.sum(part, axis=0, keepdims=True)
        part_row[i] = row
        sum_a[i, pl.ds(me, 1)] = row
        for a in lat_order:
            for b in lon_order:
                if a or b:
                    where = {"lat": lat_peers[a], "lon": lon_peers[b]}
                    remote(part_row.at[i], sum_a.at[i, pl.ds(me, 1)], as_.at[i], ar.at[i], where).start()

    def take_sums(i):
        sum_wait(i).wait_recv()
        total = jnp.sum(sum_a[i], axis=0, keepdims=True)
        whole = jnp.sum(jnp.where(lane8 >> 5 == sub8, total, 0.0), axis=1, keepdims=True)
        return [jnp.broadcast_to(whole[k : k + 1], (8, BLOCK)) for k in range(4)]

    def beta_of(size, rr, rq, qq):
        return (rr - 2.0 * size * rq + size * size * qq) / rr

    def halves(sums):
        return [v[0] + v[1] for v in sums]

    def outer(o):
        k0, kq, kz = 4 * o, 4 * o + 1, 4 * o + 2
        i0, i1, i2 = ITERS * o, ITERS * o + 1, ITERS * o + 2
        r0, q0, z0 = field.at[k0], field.at[kq], field.at[kz]
        z1 = field.at[3] if o == 0 else z_last
        observe()
        if o == 0:
            inside(r0, q0)
            wait_halo(k0, slice(2, 4))
            lat_edges(r0, q0)

        def first_dots(row, carry):
            rr, rq, qq = carry
            if o == 0:
                v = [r0[row + 1, cb] for cb in range(nblk)]
                images = [q0[row + 1, cb] for cb in range(nblk)]
            else:
                v, images = image_row(r0, row, from_east(hq.at[k0], row), from_west(hq.at[k0], row))
            for cb in range(nblk):
                res, image = v[cb], images[cb]
                if o > 0:
                    q0[row + 1, cb] = image
                rr = rr + res * res
                rq = rq + res * image
                qq = qq + image * image
            return rr, rq, qq

        sums = halves(lax.fori_loop(0, rows, first_dots, (zero, zero, zero), unroll=rows))
        if o == 0:
            wait_halo(k0, slice(0, 2))
            more_rq, more_qq = halves(lon_edges(r0, hq.at[k0], q0))
            sums = [sums[0], sums[1] + more_rq, sums[2] + more_qq]
        keep_ends(kq, q0)
        send_halo(kq, slice(0, 2))
        if o == 0:
            pl.semaphore_wait(ready, nlat - 1)
        send_sums(i0, sums)
        send_halo(kq, slice(2, 4))
        if o == 0:
            keep_near(0)
            keep_near(1)

        def look(row, carry):
            for cb in range(nblk):
                seen[row * nblk + cb] = q0[row + 1, cb]
            return carry

        lax.fori_loop(0, rows, look, 0)
        observe()
        inside(q0, z0)
        wait_halo(kq)
        edges(q0, hq.at[kq], z0)

        keep_ends(kz, z0)
        send_halo(kz)
        if o == 0:
            keep_near(2)
        rr, rq, qq, _ = take_sums(i0)
        size0 = rr / rq
        beta0 = beta_of(size0, rr, rq, qq)
        more = 1.0 + beta0

        def second_vectors(row, cb):
            r, q, z = r0[row + 1, cb], q0[row + 1, cb], z0[row + 1, cb]
            res = r - size0 * q
            return res, res + beta0 * r, more * q - size0 * z

        def second(row, carry):
            ri, qi, ii = carry
            for cb in range(nblk):
                q = q0[row + 1, cb]
                image = more * q - size0 * z0[row + 1, cb]
                ri = ri + r0[row + 1, cb] * image
                qi = qi + q * image
                ii = ii + image * image
            return ri, qi, ii

        part_ri, part_qi, part_qq = halves(lax.fori_loop(0, rows, second, (zero,) * 3, unroll=4))
        part_rr = sums[0] - 2.0 * size0 * sums[1] + size0 * size0 * sums[2]
        part_rq = part_ri - size0 * part_qi
        part_dq = part_rq + beta0 * part_ri
        sums = (part_rr, part_rq, part_dq, part_qq)
        send_sums(i1, sums)

        def keep_second(row, carry):
            for cb in range(nblk):
                r1[row + 1, cb], p1[row + 1, cb], image = second_vectors(row, cb)
                q1[row + 1, cb] = image
                seen[row * nblk + cb] = image
            return carry

        lax.fori_loop(0, rows, keep_second, 0, unroll=2)
        observe()
        inside(q1, z1)
        wait_halo(kz)
        for edge in (0, rows + 1):
            for cb in range(nblk):
                q1[edge, cb] = more * q0[edge, cb] - size0 * z0[edge, cb]
        hq1[...] = more * hq[kq] - size0 * hq[kz]
        edges(q1, hq1, z1)
        if o == 0:
            keep_ends(3, z1)
            send_halo(3)

        def third(row, carry):
            rw, rz, qw, qz, pw, pz = carry
            for cb in range(nblk):
                r, q, p, z = r1[row + 1, cb], q1[row + 1, cb], p1[row + 1, cb], z1[row + 1, cb]
                w = q0[row + 1, cb] - size0 * z0[row + 1, cb]
                rw = rw + r * w
                rz = rz + r * z
                qw = qw + q * w
                qz = qz + q * z
                pw = pw + p * w
                pz = pz + p * z
            return rw, rz, qw, qz, pw, pz

        rw, rz, qw, qz, pw, pz = halves(lax.fori_loop(0, rows, third, (zero,) * 6, unroll=2))
        rr, rq, dq, qq = take_sums(i1)
        size1 = rr / dq
        beta1 = beta_of(size1, rr, rq, qq)
        with_r = rw - size1 * rz + beta1 * part_rq
        with_q = qw - size1 * qz + beta1 * part_qq
        with_p = pw - size1 * pz + beta1 * part_dq
        send_sums(
            i2,
            [
                part_rr - 2.0 * size1 * part_rq + size1 * size1 * part_qq,
                with_r - size1 * with_q + beta1 * with_p,
            ],
        )

        def settle(blocks):
            def line(row, carry):
                for cb in blocks:
                    q, p = q1[row + 1, cb], p1[row + 1, cb]
                    res = r1[row + 1, cb] - size1 * q
                    r2[row + 1, cb] = res
                    p2[row + 1, cb] = res + beta1 * p
                    w = q0[row + 1, cb] - size0 * z0[row + 1, cb]
                    q2[row + 1, cb] = (w - size1 * z1[row + 1, cb]) + beta1 * q
                    moved = size0 * r0[row + 1, cb]
                    x[row + 1, cb] = (moved if o == 0 else x[row + 1, cb] + moved) + size1 * p
                return carry

            lax.fori_loop(0, rows, line, 0, unroll=2)

        return size0, beta0, size1, beta1, settle

    size0, beta0, size1, beta1, settle = outer(0)

    def beyond(r, q, q_next):
        res = r - size0 * q
        way = res + beta0 * r
        res = res - size1 * q_next
        return size0 * r + size1 * way, res + beta1 * way, res

    hx[...], hp[...], hr[...] = beyond(hq[0], hq[1], hq1[...])

    def add_up(square):
        return jnp.sum(square[0] + square[1], axis=0, keepdims=True)

    def parts_of(flux, dragged):
        (xe, xn), (pe, pn) = flux
        parts = jnp.where(sub8 == 0, add_up(xe * xe + xn * xn), dragged)
        parts = jnp.where(sub8 == 1, add_up(xe * pe + xn * pn), parts)
        return jnp.where(sub8 == 2, add_up(pe * pe + pn * pn), parts)

    def extended(k, side):
        corner = field[k, rows + 1, side * (nblk - 1)]
        return jnp.where(lane8 == rows, pltpu.roll(corner, (rows + side) % BLOCK, 2), pk[k, side])

    def state(r, q, z):
        return beyond(r, q, (1.0 + beta0) * q - size0 * z)[:2]

    for side in range(2):
        own = state(*(extended(k, side) for k in range(3)))
        after = (hx[1], hp[1]) if side else state(near[0], near[1], near[2])
        flux = [
            (end_coef[side, 0] * (e - v), end_coef[side, 1] * (pltpu.roll(v, BLOCK - 1, 2) - v))
            for v, e in zip(own, after)
        ]
        surf_pk[side] = parts_of(flux, end_coef[side, 2])
    surf_copies = [
        remote(surf_pk.at[0], surf_hq.at[1], ss.at[2], sr.at[2], {"lon": west}),
        remote(surf_pk.at[1], surf_hq.at[0], ss.at[3], sr.at[3], {"lon": east}),
        remote(surf.at[1], surf.at[rows + 1], ss.at[0], sr.at[0], {"lat": south}),
        remote(surf.at[rows], surf.at[0], ss.at[1], sr.at[1], {"lat": north}),
    ]
    for c in surf_copies[:2]:
        c.start()
    settle(range(nblk))
    for edge in (0, rows + 1):
        for cb in range(nblk):
            x[edge, cb], p2[edge, cb], r2[edge, cb] = beyond(field[0, edge, cb], field[1, edge, cb], q1[edge, cb])

    def surface(row, carry):
        for cb in range(nblk):
            at = pl.ds(cb * BLOCK, BLOCK)
            flux = []
            for ref, halos in ((x, hx), (p2, hp)):
                v = ref[row + 1, cb]
                after = pltpu.roll(ref[row + 1, cb + 1], BLOCK - 1, 2) if cb < nblk - 1 else from_east(halos, row)
                e = jnp.where(lane8 == BLOCK - 1, after, pltpu.roll(v, BLOCK - 1, 2))
                flux.append((coef[0, row, :, at] * (e - v), coef[2, row, :, at] * (ref[row + 2, cb] - v)))
            surf[row + 1, :, at] = parts_of(flux, wetfric[row, :, at])
        return carry

    lax.fori_loop(0, rows, surface, 0)
    for c in surf_copies[2:]:
        c.start()
    wait_halo(3)

    def image_beyond(q, z, z_next, q_next):
        return ((q - size0 * z) - size1 * z_next) + beta1 * q_next

    for edge in (0, rows + 1):
        for cb in range(nblk):
            q2[edge, cb] = image_beyond(field[1, edge, cb], field[2, edge, cb], field[3, edge, cb], q1[edge, cb])
    hw[...] = image_beyond(hq[1], hq[2], hq[3], hq1[...])
    for c in surf_copies:
        c.wait_recv()
    rr, dq, _, _ = take_sums(2)
    size2 = rr / dq
    ramp = jnp.where(sub8 == 0, 1.0, jnp.where(sub8 == 1, 2.0 * size2, jnp.where(sub8 == 2, size2 * size2, 0.0)))

    def extra_of(parts):
        speed = jnp.maximum(jnp.sum(parts * ramp, axis=0, keepdims=True), 0.0)
        return parts[3:4] * (jnp.sqrt(1.0 + speed / 16.0) - 1.0)

    def renew(row, cb):
        extra = extra_of(surf[row, :, pl.ds(cb * BLOCK, BLOCK)])
        place = x[row, cb] + size2 * p2[row, cb]
        new = (r2[row, cb] - size2 * q2[row, cb]) - extra * place
        field[4, row, cb] = new
        return extra, place, new

    def friction(row, carry):
        for cb in range(nblk):
            at = pl.ds(cb * BLOCK, BLOCK)
            extra, place, new = renew(row + 1, cb)
            x[row + 1, cb] = place
            diag[row, :, at] = diag[row, :, at] + extra
            seen[row * nblk + cb] = new
        return carry

    lax.fori_loop(0, rows, friction, 0, unroll=4)
    for edge in (0, rows + 1):
        for cb in range(nblk):
            renew(edge, cb)
    for side in range(2):
        hq[4, side] = (hr[side] - size2 * hw[side]) - extra_of(surf_hq[side]) * (hx[side] + size2 * hp[side])
    size0, beta0, size1, beta1, settle = outer(1)
    settle(range(nblk))
    for c in obs_sends + first_copies:
        c.wait_send()
    for src, dst in ((x, x_out), (p2, p_out), (r2, r_out), (q2, q_out)):
        for cb in range(nblk):
            for h in range(2):
                dst[h, :, :, pl.ds(cb * BLOCK, BLOCK)] = jnp.swapaxes(src[pl.ds(1, rows), cb, h], 0, 1)
    for k in (0, 1, 2, 3, 5, 6):
        for c in halo(k):
            c.wait_send()
    for c in surf_copies:
        c.wait_send()
    rr, dq, _, _ = take_sums(SUMS - 1)
    size_out[...] = jnp.broadcast_to((rr / dq)[:, 0:1], (8, cols))
    for i in range(SUMS):
        sum_wait(i).wait_send()


def shards(nlat, nlon, depth, friction, ocean_mask, forcing, tile_route, tile_block, obs_cell, obs_time, obs_value, obs_weight):
    channels, rows, cols = forcing.shape
    slots = nlon * CAP
    nblk, tiles = cols // BLOCK, obs_time.shape[0]
    f32, i32 = jnp.float32, jnp.int32
    vmem, smem = pltpu.VMEM, pltpu.SMEM
    hbm = pl.BlockSpec(memory_space=pltpu.HBM)
    field = (rows + 2, nblk, 2, 8, BLOCK)
    ends = (2, 2, 8, BLOCK)
    split = (2, channels // 2, rows, cols)
    dma = pltpu.SemaphoreType.DMA
    scratch = [
        smem((tiles,), i32),
        smem((tiles,), i32),
        vmem((rows, cols), f32),
        vmem((rows, cols), f32),
        vmem((rows, cols), i32),
        vmem(split, f32),
        vmem((tiles, BLOCK), i32),
        vmem((tiles, BLOCK), f32),
        vmem((tiles, BLOCK), f32),
        vmem((tiles, BLOCK), f32),
        vmem((rows, cols), f32),
        vmem((rows, cols), f32),
        vmem((rows, cols), f32),
        vmem((rows, BLOCK), f32),
        vmem((rows, BLOCK), f32),
        vmem((rows, 8, cols), f32),
        vmem((4, rows, 8, cols), f32),
        vmem((rows, 8, cols), f32),
        vmem((tiles + 1, 8, BLOCK), f32),
        vmem((tiles + 1, 8, BLOCK), i32),
        vmem((nlon, 8, BLOCK), f32),
        vmem((nlon, 8, BLOCK), i32),
        vmem((nlon, 8, BLOCK), f32),
        vmem((nlon, 8, BLOCK), i32),
        vmem((8, BLOCK), i32),
        smem((8, BLOCK), i32),
        vmem((slots, 2, 8, BLOCK), f32),
        vmem((slots + 1, 256, BLOCK), f32),
        vmem((slots + 1, 2, 8, BLOCK), f32),
        vmem((HALOS,) + field, f32),
        vmem((rows * nblk, 2, 8, BLOCK), f32),
        vmem(field, f32),
        vmem(field, f32),
        vmem(field, f32),
        vmem(field, f32),
        vmem(field, f32),
        vmem(field, f32),
        vmem(field, f32),
        vmem(field, f32),
        vmem((HALOS,) + ends, f32),
        vmem((HALOS,) + ends, f32),
        vmem(ends, f32),
        vmem(ends, f32),
        vmem(ends, f32),
        vmem(ends, f32),
        vmem(ends, f32),
        vmem((rows + 2, 8, cols), f32),
        vmem((2, 8, BLOCK), f32),
        vmem((2, 8, BLOCK), f32),
        vmem((3, 2, 8, BLOCK), f32),
        vmem((2, 3, 8, BLOCK), f32),
        vmem((SUMS, nlat * nlon, BLOCK), f32),
        vmem((SUMS, 1, BLOCK), f32),
        pltpu.SemaphoreType.REGULAR,
        dma((10,)),
        dma((HALOS, 4)),
        dma((HALOS, 4)),
        dma((4,)),
        dma((4,)),
        dma((SUMS,)),
        dma((SUMS,)),
        dma((2, nlon)),
        dma((2, nlon)),
        dma((4,)),
        dma((4,)),
        dma((1,)),
    ]
    shape = vmem(split, f32)
    x, p, r, q, size = pl.pallas_call(
        functools.partial(kernel, nlat, nlon),
        out_shape=(shape,) * 4 + (vmem((rows, cols), f32),),
        in_specs=[hbm] * 10,
        out_specs=(pl.BlockSpec(memory_space=vmem),) * 5,
        scratch_shapes=scratch,
        compiler_params=pltpu.CompilerParams(
            collective_id=0, has_side_effects=True, vmem_limit_bytes=61 * 2**20
        ),
    )(
        tile_route.reshape(-1), tile_block, depth, friction, ocean_mask, forcing.reshape(split),
        obs_cell, obs_time, obs_value, obs_weight,
    )
    return (x + size * p).reshape(forcing.shape), (r - size * q).reshape(forcing.shape)


def solution(mesh):
    tile = P(("lat", "lon"), None)
    grid = P("lat", "lon")
    in_specs = (grid, grid, grid, P(None, "lat", "lon"), tile, P(("lat", "lon")), tile, tile, tile, tile)
    out_specs = (P(None, "lat", "lon"), P(None, "lat", "lon"))
    body = functools.partial(shards, mesh.shape["lat"], mesh.shape["lon"])
    return jax.shard_map(body, mesh=mesh, in_specs=in_specs, out_specs=out_specs, check_vma=False)
```

```python
import functools
import math

import jax
import jax.numpy as jnp
import numpy as np
from jax import lax
from jax.experimental import pallas as pl
from jax.experimental.pallas import tpu as pltpu
from jax.sharding import PartitionSpec as P

BLOCK = 128
CAP = 2
ITERS = 3
OUTER = 2
SUMS = ITERS * OUTER
HALOS = 7
MESH = pl.DeviceIdType.MESH
OMEGA_DEGREES = (28.984104, 30.0, 28.43973, 30.082137, 15.041069, 13.943036, 14.958931, 13.398661)
RATES = np.array(OMEGA_DEGREES, np.float32) * np.float32(math.pi / 180.0)
STIFF = np.float32(0.2) * (RATES / RATES[0]) ** 2


def sin_cos(angle):
    turn = jnp.floor(angle * (2.0 / math.pi) + 0.5)
    x = ((angle - turn * 1.5703125) - turn * 4.837512969970703125e-4) - turn * 7.54978995489188216e-8
    z = x * x
    s = ((-1.9515295891e-4 * z + 8.3321608736e-3) * z - 1.6666654611e-1) * z * x + x
    c = ((2.443315711809948e-5 * z - 1.388731625493765e-3) * z + 4.166664568298827e-2) * z * z - 0.5 * z + 1.0
    quarter = turn.astype(jnp.int32)
    odd = (quarter & 1) == 1
    sine = jnp.where(odd, c, s)
    cosine = jnp.where(odd, s, c)
    sine = jnp.where((quarter & 2) == 2, -sine, sine)
    cosine = jnp.where(((quarter + 1) & 2) == 2, -cosine, cosine)
    return sine, cosine


def kernel(
    nlat, nlon,
    route_in, tblk_in, depth_in, fric_in, mask_in, forc_in, ocell_in, otime_in, oval_in, oweight_in,
    x_out, p_out, r_out, q_out, w_out, z_out, first_out, second_out, third_out,
    route, tblk, depth, fric, mask, forc, ocell, otime, oval, oweight,
    dw, dwn, dws, dwe, dww, wetfric, coef, diag,
    pay, payi, outf, outi, inf, ini, plan, splan, waves, mats, oslot,
    field, seen, r1, p1, q1, z_last, r2, p2, q2, x,
    pk, hq, hq1, hx, hp, hr, hw, surf, surf_pk, surf_hq, near, end_coef, sum_a, part_row, ready,
    load, hs, hrv, ss, sr, as_, ar, os_, orv, ds_, dr, loc,
):
    rows, cols = depth.shape
    nblk = cols // BLOCK
    slots = nlon * CAP
    tiles = otime.shape[0]
    me_lat = lax.axis_index("lat")
    me_lon = lax.axis_index("lon")
    north, south = lax.rem(me_lat + 1, nlat), lax.rem(me_lat + nlat - 1, nlat)
    east, west = lax.rem(me_lon + 1, nlon), lax.rem(me_lon + nlon - 1, nlon)
    me = me_lat * nlon + me_lon
    count = nlat * nlon

    barrier = pltpu.get_barrier_semaphore()
    for k in range(1, nlon):
        pl.semaphore_signal(barrier, inc=1, device_id={"lon": lax.rem(me_lon + k, nlon)}, device_id_type=MESH)
    for k in range(1, nlat):
        pl.semaphore_signal(barrier, inc=1, device_id={"lat": lax.rem(me_lat + k, nlat)}, device_id_type=MESH)
    pairs = [
        (route_in, route), (tblk_in, tblk), (ocell_in, ocell), (otime_in, otime), (oval_in, oval),
        (oweight_in, oweight), (depth_in, depth), (mask_in, mask), (fric_in, fric), (forc_in, forc),
    ]
    loads = [pltpu.make_async_copy(src, dst, load.at[k]) for k, (src, dst) in enumerate(pairs)]
    for c in loads:
        c.start()

    def remote(src, dst, send, recv, where):
        return pltpu.make_async_remote_copy(
            src_ref=src, dst_ref=dst, send_sem=send, recv_sem=recv, device_id=where, device_id_type=MESH
        )

    lane = lax.broadcasted_iota(jnp.int32, (1, BLOCK), 1)
    lane8 = lax.broadcasted_iota(jnp.int32, (8, BLOCK), 1)
    sub8 = lax.broadcasted_iota(jnp.int32, (8, BLOCK), 0)
    zero = jnp.zeros((2, 8, BLOCK), jnp.float32)

    for c in loads[:8]:
        c.wait()
    wet = mask[...].astype(jnp.float32)
    dw[...] = depth[...] * wet

    for t in range(tiles):
        pay[t] = jnp.concatenate([otime[t : t + 1], oval[t : t + 1], oweight[t : t + 1], oval[t : t + 1]] * 2, axis=0)
        payi[t] = jnp.broadcast_to(ocell[t : t + 1] + tblk[t] * BLOCK, (8, BLOCK))
    pay[tiles] = jnp.zeros((8, BLOCK), jnp.float32)
    payi[tiles] = jnp.zeros((8, BLOCK), jnp.int32)

    def pick(p, carry):
        first, second = jnp.int32(tiles), jnp.int32(tiles)
        for t in reversed(range(tiles)):
            hit = route[t] == p
            second = jnp.where(hit, first, second)
            first = jnp.where(hit, jnp.int32(t), first)
        outf[p] = jnp.where(sub8 < 4, pay[first], pay[second])
        outi[p] = jnp.where(sub8 == 0, payi[first], payi[second])
        return carry

    lax.fori_loop(0, nlon, pick, 0)
    pl.semaphore_wait(barrier, nlon + nlat - 2)

    def obs_copy(n, k):
        src, dst = ((outi, ini), (outf, inf))[n]
        peer = lax.rem(me_lon + k, nlon)
        return remote(src.at[peer], dst.at[me_lon], os_.at[n, peer], orv.at[n, me_lon], {"lon": peer})

    def obs_wait(n):
        src, dst = ((outi, ini), (outf, inf))[n]
        for k in range(1, nlon):
            peer = lax.rem(me_lon + k, nlon)
            remote(src.at[peer], dst.at[peer], os_.at[n, peer], orv.at[n, peer], {"lon": peer}).wait_recv()

    obs_sends = [obs_copy(n, k) for n in range(2) for k in range(1, nlon)]
    for c in obs_sends:
        c.start()
    first_copies = [
        remote(dw.at[:, pl.ds(0, BLOCK)], dwe, ds_.at[2], dr.at[2], {"lon": west}),
        remote(dw.at[:, pl.ds(cols - BLOCK, BLOCK)], dww, ds_.at[3], dr.at[3], {"lon": east}),
        remote(dw, dws, ds_.at[0], dr.at[0], {"lat": north}),
        remote(dw, dwn, ds_.at[1], dr.at[1], {"lat": south}),
    ]
    for c in first_copies:
        c.start()
    for k in range(1, nlat):
        pl.semaphore_signal(ready, inc=1, device_id={"lat": lax.rem(me_lat + k, nlat)}, device_id_type=MESH)
    inf[me_lon] = outf[me_lon]
    ini[me_lon] = outi[me_lon]
    for c in loads[8:]:
        c.wait()

    for cb in range(nblk):
        at = pl.ds(cb * BLOCK, BLOCK)
        for h in range(2):
            wetted = forc[h, :, :, at] * wet[None, :, cb * BLOCK : cb * BLOCK + BLOCK]
            field[0, pl.ds(1, rows), cb, h] = jnp.swapaxes(wetted, 0, 1)
    oslot[slots] = zero
    mats[slots] = jnp.zeros((256, BLOCK), jnp.float32)
    stiff = jnp.zeros((8, 1), jnp.float32)
    rate = jnp.zeros((8, BLOCK), jnp.float32)
    sub1 = lax.broadcasted_iota(jnp.int32, (8, 1), 0)
    for c in range(8):
        stiff = jnp.where(sub1 == c, float(STIFF[c]), stiff)
        rate = jnp.where(sub8 == c, float(RATES[c]), rate)
    cells = lax.broadcasted_iota(jnp.int32, (BLOCK, BLOCK), 0)

    obs_wait(0)
    places = [ini[s // CAP, pl.ds(s % CAP, 1), :] >> 7 for s in range(slots)]
    rep = jnp.full((1, BLOCK), slots, jnp.int32)
    homes = jnp.full((1, BLOCK), -1, jnp.int32)
    for s in reversed(range(slots)):
        home = places[s]
        rep = jnp.where(home == lane, s, rep)
        homes = jnp.where(lane == s, home, homes)
    chain = jnp.full((1, BLOCK), slots, jnp.int32)
    for s in reversed(range(slots)):
        home = places[s]
        chain = jnp.where((home == homes) & (lane < s), s, chain)
    plan[...] = jnp.where(
        sub8 == 0,
        jnp.broadcast_to(homes, (8, BLOCK)),
        jnp.where(sub8 == 1, jnp.broadcast_to(chain, (8, BLOCK)), jnp.broadcast_to(rep, (8, BLOCK))),
    )
    to_scalars = pltpu.make_async_copy(plan, splan, loc.at[0])
    to_scalars.start()
    obs_wait(1)

    def onto_cells(o, k, terms):
        cell = ini[o, pl.ds(k, 1), :] & (BLOCK - 1)
        high = terms.astype(jnp.bfloat16)
        low = (terms - high.astype(jnp.float32)).astype(jnp.bfloat16)
        hot = (cells == cell).astype(jnp.float32).astype(jnp.bfloat16)
        return lax.dot_general(
            jnp.concatenate([high, low], axis=1),
            jnp.concatenate([hot, hot], axis=1),
            (((1,), (1,)), ((), ())),
            preferred_element_type=jnp.float32,
        )

    def values(o, carry):
        for k in range(CAP):
            times = inf[o, pl.ds(4 * k, 1), :]
            scaled = inf[o, pl.ds(4 * k + 2, 1), :] * inf[o, pl.ds(4 * k + 1, 1), :]
            sine, cosine = sin_cos(rate * times)
            waves[o * CAP + k, 0] = cosine
            waves[o * CAP + k, 1] = sine
            terms = jnp.concatenate([cosine * scaled, sine * scaled], axis=0)
            oslot[o * CAP + k] = onto_cells(o, k, terms).reshape(2, 8, BLOCK)
        return carry

    lax.fori_loop(0, nlon, values, 0, unroll=4)
    to_scalars.wait()

    def join_values(i, carry):
        s = slots - 1 - i
        oslot[s] = oslot[s] + oslot[splan[1, s]]
        return carry

    lax.fori_loop(0, slots, join_values, 0)

    def keep_ends(k, src):
        for side, cb in enumerate((0, nblk - 1)):
            packed = zero
            for row in range(rows):
                moved = pltpu.roll(src[row + 1, cb], (row + side) % BLOCK, 2)
                packed = jnp.where(lane8 == row, moved, packed)
            pk[k, side] = packed

    def keep_near(k):
        packed = zero
        for row in range(rows):
            packed = jnp.where(lane8 == row, pltpu.roll(field[k, row + 1, 0], (row + BLOCK - 1) % BLOCK, 2), packed)
        near[k] = packed

    def start_rhs(blocks):
        def line(row, carry):
            for cb in blocks:
                v = field[0, row + 1, cb] + oslot[splan[2, row * nblk + cb]]
                field[0, row + 1, cb] = v
                seen[row * nblk + cb] = v
            return carry

        lax.fori_loop(0, rows, line, 0, unroll=rows if len(blocks) == 2 else 2)

    start_rhs((0, nblk - 1))
    keep_ends(0, field.at[0])

    def halo(k):
        return [
            remote(pk.at[k, 0], hq.at[k, 1], hs.at[k, 2], hrv.at[k, 2], {"lon": west}),
            remote(pk.at[k, 1], hq.at[k, 0], hs.at[k, 3], hrv.at[k, 3], {"lon": east}),
            remote(field.at[k, 1], field.at[k, rows + 1], hs.at[k, 0], hrv.at[k, 0], {"lat": south}),
            remote(field.at[k, rows], field.at[k, 0], hs.at[k, 1], hrv.at[k, 1], {"lat": north}),
        ]

    def send_halo(k, part=slice(None)):
        for c in halo(k)[part]:
            c.start()

    def wait_halo(k, part=slice(None)):
        for c in halo(k)[part]:
            c.wait_recv()

    send_halo(0, slice(0, 2))
    start_rhs(range(1, nblk - 1))
    send_halo(0, slice(2, 4))

    for c in first_copies:
        c.wait_recv()
    a = dw[...]
    colid = lax.broadcasted_iota(jnp.int32, (rows, cols), 1)
    rowid = lax.broadcasted_iota(jnp.int32, (rows, cols), 0)
    keep_n = (me_lat < nlat - 1).astype(jnp.float32)
    keep_s = (me_lat > 0).astype(jnp.float32)

    def harmonic(first, second):
        return 2.0 * first * second / jnp.maximum(first + second, 0.5)

    drag = fric[...]
    total = wet * drag + (1.0 - wet)
    around = (
        lambda: jnp.where(colid == cols - 1, dwe[:, 0:1], pltpu.roll(a, cols - 1, 1)),
        lambda: jnp.where(colid == 0, dww[:, BLOCK - 1 : BLOCK], pltpu.roll(a, 1, 1)),
        lambda: jnp.where(rowid == rows - 1, dwn[0:1, :] * keep_n, pltpu.roll(a, rows - 1, 0)),
        lambda: jnp.where(rowid == 0, dws[rows - 1 : rows, :] * keep_s, pltpu.roll(a, 1, 0)),
    )
    for k in range(4):
        side = harmonic(a, around[k]())
        total = total + side
        for row in range(rows):
            coef[k, row] = jnp.broadcast_to(side[row : row + 1], (8, cols))
    dragged = wet * drag
    for row in range(rows):
        wetfric[row] = jnp.broadcast_to(dragged[row : row + 1], (8, cols))
        wide = jnp.broadcast_to(wet[row : row + 1], (8, cols))
        diag[row] = wide * stiff + jnp.broadcast_to(total[row : row + 1], (8, cols))

    def pack_rows(ref, lead, side):
        packed = jnp.zeros((8, BLOCK), jnp.float32)
        at = pl.ds(side * (cols - BLOCK), BLOCK)
        for row in range(rows):
            value = ref[lead + (row, slice(None), at)]
            packed = jnp.where(lane8 == row, pltpu.roll(value, (row + side) % BLOCK, 1), packed)
        return packed

    def build(o, carry):
        for k in range(CAP):
            weight = inf[o, pl.ds(4 * k + 2, 1), :]
            basis = (waves[o * CAP + k, 0], waves[o * CAP + k, 1])
            parts = []
            for h in range(2):
                for c in range(8):
                    one = weight * basis[h][c : c + 1]
                    parts.append(one * basis[0])
                    parts.append(one * basis[1])
            mats[o * CAP + k] = onto_cells(o, k, jnp.concatenate(parts, axis=0))
        return carry

    lax.fori_loop(0, nlon, build, 0)

    def join_mats(i, carry):
        s = slots - 1 - i
        mats[s] = mats[s] + mats[splan[1, s]]
        return carry

    lax.fori_loop(0, slots, join_mats, 0)
    for side in range(2):
        end_coef[side, 0] = pack_rows(coef, (0,), side)
        end_coef[side, 1] = pack_rows(coef, (2,), side)
        end_coef[side, 2] = pack_rows(wetfric, (), side)

    def observe():
        def slot(s, carry):
            v = seen[splan[0, s]]
            acc = [zero, zero]
            for c in range(16):
                m = mats[s, 16 * c : 16 * c + 16, :].reshape(2, 8, BLOCK)
                acc[c % 2] = acc[c % 2] + m * v[c // 8, c % 8 : c % 8 + 1, :]
            oslot[s] = acc[0] + acc[1]
            return carry

        lax.fori_loop(0, slots, slot, 0, unroll=4)

    def eastward(v, beyond):
        moved = [pltpu.roll(b, BLOCK - 1, 2) for b in v] + [beyond]
        return [jnp.where(lane8 == BLOCK - 1, moved[cb + 1], moved[cb]) for cb in range(nblk)]

    def westward(v, beyond):
        moved = [beyond] + [pltpu.roll(b, 1, 2) for b in v]
        return [jnp.where(lane8 == 0, moved[cb], moved[cb + 1]) for cb in range(nblk)]

    def from_east(halos, row):
        return pltpu.roll(halos[1], BLOCK - 1 - row, 2)

    def from_west(halos, row):
        return pltpu.roll(halos[0], BLOCK - row, 2)

    def image_row(src, row, east_side, west_side, to_north=True, to_south=True):
        v = [src[row + 1, cb] for cb in range(nblk)]
        e = eastward(v, east_side)
        w = westward(v, west_side)
        images = []
        for cb in range(nblk):
            at = pl.ds(cb * BLOCK, BLOCK)
            image = (
                diag[row, :, at] * v[cb]
                - coef[0, row, :, at] * e[cb]
                - coef[1, row, :, at] * w[cb]
                + oslot[splan[2, row * nblk + cb]]
            )
            if to_north:
                image = image - coef[2, row, :, at] * src[row + 2, cb]
            if to_south:
                image = image - coef[3, row, :, at] * src[row, cb]
            images.append(image)
        return v, images

    def inside(src, dst):
        def put(row, images):
            for cb in range(nblk):
                dst[row + 1, cb] = images[cb]

        def line(row, carry):
            put(row, image_row(src, row, zero, zero)[1])
            return carry

        lax.fori_loop(1, rows - 1, line, 0, unroll=2)
        put(0, image_row(src, 0, zero, zero, to_south=False)[1])
        put(rows - 1, image_row(src, rows - 1, zero, zero, to_north=False)[1])

    def lat_edges(src, dst):
        for cb in range(nblk):
            at = pl.ds(cb * BLOCK, BLOCK)
            dst[1, cb] = dst[1, cb] - coef[3, 0, :, at] * src[0, cb]
            dst[rows, cb] = dst[rows, cb] - coef[2, rows - 1, :, at] * src[rows + 1, cb]

    def lon_edges(halos, dst, refs=()):
        dots, square = [zero] * len(refs), zero
        for row in range(rows):
            for side in range(2):
                cb = side * (nblk - 1)
                beyond = from_east(halos, row) if side else from_west(halos, row)
                at = pl.ds(cb * BLOCK, BLOCK)
                change = coef[1 - side, row, :, at] * jnp.where(lane8 == side * (BLOCK - 1), -beyond, 0.0)
                old = dst[row + 1, cb]
                dst[row + 1, cb] = old + change
                dots = [dot + ref[row + 1, cb] * change for dot, ref in zip(dots, refs)]
                square = square + change * (old + old + change)
        return [v[0] + v[1] for v in dots + [square]]

    lat_order = sorted(range(nlat), key=lambda k: (k == 0, abs(k - nlat // 2)))
    lon_order = sorted(range(nlon), key=lambda k: (k == 0, k % 2 == 0, -abs(k - nlon // 2)))
    lat_peers = {k: lax.rem(me_lat + k, nlat) for k in lat_order}
    lon_peers = {k: lax.rem(me_lon + k, nlon) for k in lon_order}

    def sum_wait(i):
        whole = sum_a.at[i, pl.ds(0, count - 1)]
        return remote(whole, whole, as_.at[i], ar.at[i], {"lat": south})

    def send_sums(i, sums):
        part = jnp.zeros((8, BLOCK), jnp.float32)
        groups = 4 if len(sums) <= 4 else 16
        for k, s in enumerate(sums):
            both, wide = s, BLOCK
            while wide * groups > BLOCK:
                wide = wide // 2
                both = both + pltpu.roll(both, wide, 1)
            part = jnp.where(lane8 // (BLOCK // groups) == k, both, part)
        row = jnp.sum(part, axis=0, keepdims=True)
        part_row[i] = row
        sum_a[i, pl.ds(me, 1)] = row
        for a in lat_order:
            for b in lon_order:
                if a or b:
                    where = {"lat": lat_peers[a], "lon": lon_peers[b]}
                    remote(part_row.at[i], sum_a.at[i, pl.ds(me, 1)], as_.at[i], ar.at[i], where).start()

    def take_sums(i, number=4):
        sum_wait(i).wait_recv()
        groups, tall = (4, 8) if number <= 4 else (16, 16)
        total = jnp.sum(sum_a[i], axis=0, keepdims=True)
        lanes = lax.broadcasted_iota(jnp.int32, (tall, BLOCK), 1) // (BLOCK // groups)
        own = lanes == lax.broadcasted_iota(jnp.int32, (tall, BLOCK), 0)
        whole = jnp.sum(jnp.where(own, total, 0.0), axis=1, keepdims=True)
        return [jnp.broadcast_to(whole[k : k + 1], (8, BLOCK)) for k in range(number)]

    def beta_of(size, rr, rq, qq):
        return (rr - 2.0 * size * rq + size * size * qq) / rr

    def halves(sums):
        return [v[0] + v[1] for v in sums]

    def last_sums(size, beta, rr, rq, dq, qq, rw, rz, qw, qz, pw, pz):
        with_r = rw - size * rz + beta * rq
        with_q = qw - size * qz + beta * qq
        with_p = pw - size * pz + beta * dq
        return [rr - 2.0 * size * rq + size * size * qq, with_r - size * with_q + beta * with_p]

    def outer(o):
        k0, kq, kz = 4 * o, 4 * o + 1, 4 * o + 2
        i0, i1, i2 = ITERS * o, ITERS * o + 1, ITERS * o + 2
        r0, q0, z0 = field.at[k0], field.at[kq], field.at[kz]
        z1 = field.at[3] if o == 0 else z_last
        observe()
        if o == 0:
            inside(r0, q0)
            wait_halo(k0, slice(2, 4))
            lat_edges(r0, q0)

        def first_dots(row, carry):
            rr, rq, qq = carry
            if o == 0:
                v = [r0[row + 1, cb] for cb in range(nblk)]
                images = [q0[row + 1, cb] for cb in range(nblk)]
            else:
                v, images = image_row(r0, row, from_east(hq.at[k0], row), from_west(hq.at[k0], row))
            for cb in range(nblk):
                res, image = v[cb], images[cb]
                if o > 0:
                    q0[row + 1, cb] = image
                rr = rr + res * res
                rq = rq + res * image
                qq = qq + image * image
            return rr, rq, qq

        sums = halves(lax.fori_loop(0, rows, first_dots, (zero, zero, zero), unroll=rows))
        if o == 0:
            wait_halo(k0, slice(0, 2))
            more_rq, more_qq = lon_edges(hq.at[k0], q0, (r0,))
            sums = [sums[0], sums[1] + more_rq, sums[2] + more_qq]
        keep_ends(kq, q0)
        send_halo(kq, slice(0, 2))
        if o == 0:
            pl.semaphore_wait(ready, nlat - 1)
        send_sums(i0, sums)
        send_halo(kq, slice(2, 4))
        if o == 0:
            keep_near(0)
            keep_near(1)

        def look(row, carry):
            for cb in range(nblk):
                seen[row * nblk + cb] = q0[row + 1, cb]
            return carry

        lax.fori_loop(0, rows, look, 0)
        observe()
        inside(q0, z0)
        wait_halo(kq, slice(2, 4))
        lat_edges(q0, z0)
        wait_halo(kq, slice(0, 2))
        lon_edges(hq.at[kq], z0)

        keep_ends(kz, z0)
        send_halo(kz)
        if o == 0:
            keep_near(2)
        rr, rq, qq, _ = take_sums(i0)
        size0 = rr / rq
        beta0 = beta_of(size0, rr, rq, qq)
        more = 1.0 + beta0

        def second_vectors(row, cb):
            r, q, z = r0[row + 1, cb], q0[row + 1, cb], z0[row + 1, cb]
            res = r - size0 * q
            return res, res + beta0 * r, more * q - size0 * z

        def second(row, carry):
            ri, qi, ii = carry
            for cb in range(nblk):
                q = q0[row + 1, cb]
                image = more * q - size0 * z0[row + 1, cb]
                ri = ri + r0[row + 1, cb] * image
                qi = qi + q * image
                ii = ii + image * image
            return ri, qi, ii

        part_ri, part_qi, part_qq = halves(lax.fori_loop(0, rows, second, (zero,) * 3, unroll=4))
        part_rr = sums[0] - 2.0 * size0 * sums[1] + size0 * size0 * sums[2]
        part_rq = part_ri - size0 * part_qi
        part_dq = part_rq + beta0 * part_ri
        sums = (part_rr, part_rq, part_dq, part_qq)
        if o == 0:
            send_sums(i1, sums)

        def keep_second(row, carry):
            for cb in range(nblk):
                r1[row + 1, cb], p1[row + 1, cb], image = second_vectors(row, cb)
                q1[row + 1, cb] = image
                seen[row * nblk + cb] = image
            return carry

        lax.fori_loop(0, rows, keep_second, 0, unroll=2)
        observe()
        inside(q1, z1)
        wait_halo(kz, slice(2, 4))
        for edge in (0, rows + 1):
            for cb in range(nblk):
                q1[edge, cb] = more * q0[edge, cb] - size0 * z0[edge, cb]
        lat_edges(q1, z1)

        def third(row, carry):
            rw, rz, qw, qz, pw, pz = carry
            for cb in range(nblk):
                r, q, p, z = r1[row + 1, cb], q1[row + 1, cb], p1[row + 1, cb], z1[row + 1, cb]
                w = q0[row + 1, cb] - size0 * z0[row + 1, cb]
                rw = rw + r * w
                rz = rz + r * z
                qw = qw + q * w
                qz = qz + q * z
                pw = pw + p * w
                pz = pz + p * z
            return rw, rz, qw, qz, pw, pz

        rw, rz, qw, qz, pw, pz = halves(lax.fori_loop(0, rows, third, (zero,) * 6, unroll=2))
        wait_halo(kz, slice(0, 2))
        hq1[...] = more * hq[kq] - size0 * hq[kz]
        more_rz, more_qz, more_pz, _ = lon_edges(hq1, z1, (r1, q1, p1))
        rz, qz, pz = rz + more_rz, qz + more_qz, pz + more_pz
        if o == 0:
            keep_ends(3, z1)
            send_halo(3)
        if o > 0:
            send_sums(i1, list(sums) + [rw, rz, qw, qz, pw, pz])
            return size0
        rr, rq, dq, qq = take_sums(i1)
        size1 = rr / dq
        beta1 = beta_of(size1, rr, rq, qq)
        send_sums(i2, last_sums(size1, beta1, *sums, rw, rz, qw, qz, pw, pz))

        def settle(blocks):
            def line(row, carry):
                for cb in blocks:
                    q, p = q1[row + 1, cb], p1[row + 1, cb]
                    res = r1[row + 1, cb] - size1 * q
                    r2[row + 1, cb] = res
                    p2[row + 1, cb] = res + beta1 * p
                    w = q0[row + 1, cb] - size0 * z0[row + 1, cb]
                    q2[row + 1, cb] = (w - size1 * z1[row + 1, cb]) + beta1 * q
                    x[row + 1, cb] = size0 * r0[row + 1, cb] + size1 * p
                return carry

            lax.fori_loop(0, rows, line, 0, unroll=2)

        return size0, beta0, size1, beta1, settle

    size0, beta0, size1, beta1, settle = outer(0)

    def beyond(r, q, q_next):
        res = r - size0 * q
        way = res + beta0 * r
        res = res - size1 * q_next
        return size0 * r + size1 * way, res + beta1 * way, res

    hx[...], hp[...], hr[...] = beyond(hq[0], hq[1], hq1[...])

    def add_up(square):
        return jnp.sum(square[0] + square[1], axis=0, keepdims=True)

    def parts_of(flux, dragged):
        (xe, xn), (pe, pn) = flux
        parts = jnp.where(sub8 == 0, add_up(xe * xe + xn * xn), dragged)
        parts = jnp.where(sub8 == 1, add_up(xe * pe + xn * pn), parts)
        return jnp.where(sub8 == 2, add_up(pe * pe + pn * pn), parts)

    def extended(k, side):
        corner = field[k, rows + 1, side * (nblk - 1)]
        return jnp.where(lane8 == rows, pltpu.roll(corner, (rows + side) % BLOCK, 2), pk[k, side])

    def state(r, q, z):
        return beyond(r, q, (1.0 + beta0) * q - size0 * z)[:2]

    for side in range(2):
        own = state(*(extended(k, side) for k in range(3)))
        after = (hx[1], hp[1]) if side else state(near[0], near[1], near[2])
        flux = [
            (end_coef[side, 0] * (e - v), end_coef[side, 1] * (pltpu.roll(v, BLOCK - 1, 2) - v))
            for v, e in zip(own, after)
        ]
        surf_pk[side] = parts_of(flux, end_coef[side, 2])
    surf_copies = [
        remote(surf_pk.at[0], surf_hq.at[1], ss.at[2], sr.at[2], {"lon": west}),
        remote(surf_pk.at[1], surf_hq.at[0], ss.at[3], sr.at[3], {"lon": east}),
        remote(surf.at[1], surf.at[rows + 1], ss.at[0], sr.at[0], {"lat": south}),
        remote(surf.at[rows], surf.at[0], ss.at[1], sr.at[1], {"lat": north}),
    ]
    for c in surf_copies[:2]:
        c.start()
    settle(range(nblk))
    for edge in (0, rows + 1):
        for cb in range(nblk):
            x[edge, cb], p2[edge, cb], r2[edge, cb] = beyond(field[0, edge, cb], field[1, edge, cb], q1[edge, cb])

    def surface(row, carry):
        for cb in range(nblk):
            at = pl.ds(cb * BLOCK, BLOCK)
            flux = []
            for ref, halos in ((x, hx), (p2, hp)):
                v = ref[row + 1, cb]
                after = pltpu.roll(ref[row + 1, cb + 1], BLOCK - 1, 2) if cb < nblk - 1 else from_east(halos, row)
                e = jnp.where(lane8 == BLOCK - 1, after, pltpu.roll(v, BLOCK - 1, 2))
                flux.append((coef[0, row, :, at] * (e - v), coef[2, row, :, at] * (ref[row + 2, cb] - v)))
            surf[row + 1, :, at] = parts_of(flux, wetfric[row, :, at])
        return carry

    lax.fori_loop(0, rows, surface, 0)
    for c in surf_copies[2:]:
        c.start()
    wait_halo(3)

    def image_beyond(q, z, z_next, q_next):
        return ((q - size0 * z) - size1 * z_next) + beta1 * q_next

    for edge in (0, rows + 1):
        for cb in range(nblk):
            q2[edge, cb] = image_beyond(field[1, edge, cb], field[2, edge, cb], field[3, edge, cb], q1[edge, cb])
    hw[...] = image_beyond(hq[1], hq[2], hq[3], hq1[...])
    for c in surf_copies:
        c.wait_recv()
    rr, dq, _, _ = take_sums(2)
    size2 = rr / dq
    ramp = jnp.where(sub8 == 0, 1.0, jnp.where(sub8 == 1, 2.0 * size2, jnp.where(sub8 == 2, size2 * size2, 0.0)))

    def extra_of(parts):
        speed = jnp.maximum(jnp.sum(parts * ramp, axis=0, keepdims=True), 0.0)
        return parts[3:4] * (jnp.sqrt(1.0 + speed / 16.0) - 1.0)

    def renew(row, cb):
        extra = extra_of(surf[row, :, pl.ds(cb * BLOCK, BLOCK)])
        place = x[row, cb] + size2 * p2[row, cb]
        new = (r2[row, cb] - size2 * q2[row, cb]) - extra * place
        field[4, row, cb] = new
        return extra, place, new

    def friction(row, carry):
        for cb in range(nblk):
            at = pl.ds(cb * BLOCK, BLOCK)
            extra, place, new = renew(row + 1, cb)
            x[row + 1, cb] = place
            diag[row, :, at] = diag[row, :, at] + extra
            seen[row * nblk + cb] = new
        return carry

    lax.fori_loop(0, rows, friction, 0, unroll=4)
    for edge in (0, rows + 1):
        for cb in range(nblk):
            renew(edge, cb)
    for side in range(2):
        hq[4, side] = (hr[side] - size2 * hw[side]) - extra_of(surf_hq[side]) * (hx[side] + size2 * hp[side])
    size0 = outer(1)
    for cb in range(nblk):
        at = pl.ds(cb * BLOCK, BLOCK)
        for h in range(2):
            own = (pl.ds(1, rows), cb, h)
            x_out[h, :, :, at] = jnp.swapaxes(x[own] + size0 * field[(4,) + own], 0, 1)
            w_out[h, :, :, at] = jnp.swapaxes(field[(5,) + own] - size0 * field[(6,) + own], 0, 1)
            for src, dst in ((p1, p_out), (r1, r_out), (q1, q_out), (z_last, z_out)):
                dst[h, :, :, at] = jnp.swapaxes(src[own], 0, 1)
    for c in obs_sends + first_copies:
        c.wait_send()
    for k in (0, 1, 2, 3, 5, 6):
        for c in halo(k):
            c.wait_send()
    for c in surf_copies:
        c.wait_send()
    rr, rq, dq, qq, *others = take_sums(SUMS - 2, 10)
    size1 = rr / dq
    beta1 = beta_of(size1, rr, rq, qq)
    rr, dq = last_sums(size1, beta1, rr, rq, dq, qq, *others)
    size2 = rr / dq
    for dst, value in ((first_out, size1 + size2 * beta1), (second_out, size2), (third_out, size1 * size2)):
        dst[...] = jnp.broadcast_to(value[:, 0:1], (8, cols))
    for i in range(SUMS - 1):
        sum_wait(i).wait_send()


def shards(nlat, nlon, depth, friction, ocean_mask, forcing, tile_route, tile_block, obs_cell, obs_time, obs_value, obs_weight):
    channels, rows, cols = forcing.shape
    slots = nlon * CAP
    nblk, tiles = cols // BLOCK, obs_time.shape[0]
    f32, i32 = jnp.float32, jnp.int32
    vmem, smem = pltpu.VMEM, pltpu.SMEM
    hbm = pl.BlockSpec(memory_space=pltpu.HBM)
    field = (rows + 2, nblk, 2, 8, BLOCK)
    ends = (2, 2, 8, BLOCK)
    split = (2, channels // 2, rows, cols)
    dma = pltpu.SemaphoreType.DMA
    scratch = [
        smem((tiles,), i32),
        smem((tiles,), i32),
        vmem((rows, cols), f32),
        vmem((rows, cols), f32),
        vmem((rows, cols), i32),
        vmem(split, f32),
        vmem((tiles, BLOCK), i32),
        vmem((tiles, BLOCK), f32),
        vmem((tiles, BLOCK), f32),
        vmem((tiles, BLOCK), f32),
        vmem((rows, cols), f32),
        vmem((rows, cols), f32),
        vmem((rows, cols), f32),
        vmem((rows, BLOCK), f32),
        vmem((rows, BLOCK), f32),
        vmem((rows, 8, cols), f32),
        vmem((4, rows, 8, cols), f32),
        vmem((rows, 8, cols), f32),
        vmem((tiles + 1, 8, BLOCK), f32),
        vmem((tiles + 1, 8, BLOCK), i32),
        vmem((nlon, 8, BLOCK), f32),
        vmem((nlon, 8, BLOCK), i32),
        vmem((nlon, 8, BLOCK), f32),
        vmem((nlon, 8, BLOCK), i32),
        vmem((8, BLOCK), i32),
        smem((8, BLOCK), i32),
        vmem((slots, 2, 8, BLOCK), f32),
        vmem((slots + 1, 256, BLOCK), f32),
        vmem((slots + 1, 2, 8, BLOCK), f32),
        vmem((HALOS,) + field, f32),
        vmem((rows * nblk, 2, 8, BLOCK), f32),
        vmem(field, f32),
        vmem(field, f32),
        vmem(field, f32),
        vmem(field, f32),
        vmem(field, f32),
        vmem(field, f32),
        vmem(field, f32),
        vmem(field, f32),
        vmem((HALOS,) + ends, f32),
        vmem((HALOS,) + ends, f32),
        vmem(ends, f32),
        vmem(ends, f32),
        vmem(ends, f32),
        vmem(ends, f32),
        vmem(ends, f32),
        vmem((rows + 2, 8, cols), f32),
        vmem((2, 8, BLOCK), f32),
        vmem((2, 8, BLOCK), f32),
        vmem((3, 2, 8, BLOCK), f32),
        vmem((2, 3, 8, BLOCK), f32),
        vmem((SUMS, nlat * nlon, BLOCK), f32),
        vmem((SUMS, 1, BLOCK), f32),
        pltpu.SemaphoreType.REGULAR,
        dma((10,)),
        dma((HALOS, 4)),
        dma((HALOS, 4)),
        dma((4,)),
        dma((4,)),
        dma((SUMS,)),
        dma((SUMS,)),
        dma((2, nlon)),
        dma((2, nlon)),
        dma((4,)),
        dma((4,)),
        dma((1,)),
    ]
    shape = vmem(split, f32)
    x, p, r, q, w, z, first, second, third = pl.pallas_call(
        functools.partial(kernel, nlat, nlon),
        out_shape=(shape,) * 6 + (vmem((8, cols), f32),) * 3,
        in_specs=[hbm] * 10,
        out_specs=(pl.BlockSpec(memory_space=vmem),) * 9,
        scratch_shapes=scratch,
        compiler_params=pltpu.CompilerParams(
            collective_id=0, has_side_effects=True, vmem_limit_bytes=60 * 2**20
        ),
    )(
        tile_route.reshape(-1), tile_block, depth, friction, ocean_mask, forcing.reshape(split),
        obs_cell, obs_time, obs_value, obs_weight,
    )
    x = x + first * p + second * r - third * q
    r = r - first * q - second * w + third * z
    return x.reshape(forcing.shape), r.reshape(forcing.shape)


def solution(mesh):
    tile = P(("lat", "lon"), None)
    grid = P("lat", "lon")
    in_specs = (grid, grid, grid, P(None, "lat", "lon"), tile, P(("lat", "lon")), tile, tile, tile, tile)
    out_specs = (P(None, "lat", "lon"), P(None, "lat", "lon"))
    body = functools.partial(shards, mesh.shape["lat"], mesh.shape["lon"])
    return jax.shard_map(body, mesh=mesh, in_specs=in_specs, out_specs=out_specs, check_vma=False)
```

```python
import functools
import math

import jax
import jax.numpy as jnp
import numpy as np
from jax import lax
from jax.experimental import pallas as pl
from jax.experimental.pallas import tpu as pltpu
from jax.sharding import PartitionSpec as P

BLOCK = 128
CAP = 2
ITERS = 3
OUTER = 2
SUMS = ITERS * OUTER
HALOS = 7
MESH = pl.DeviceIdType.MESH
OMEGA_DEGREES = (28.984104, 30.0, 28.43973, 30.082137, 15.041069, 13.943036, 14.958931, 13.398661)
RATES = np.array(OMEGA_DEGREES, np.float32) * np.float32(math.pi / 180.0)
STIFF = np.float32(0.2) * (RATES / RATES[0]) ** 2


def sin_cos(angle):
    turn = jnp.floor(angle * (2.0 / math.pi) + 0.5)
    x = ((angle - turn * 1.5703125) - turn * 4.837512969970703125e-4) - turn * 7.54978995489188216e-8
    z = x * x
    s = ((-1.9515295891e-4 * z + 8.3321608736e-3) * z - 1.6666654611e-1) * z * x + x
    c = ((2.443315711809948e-5 * z - 1.388731625493765e-3) * z + 4.166664568298827e-2) * z * z - 0.5 * z + 1.0
    quarter = turn.astype(jnp.int32)
    odd = (quarter & 1) == 1
    sine = jnp.where(odd, c, s)
    cosine = jnp.where(odd, s, c)
    sine = jnp.where((quarter & 2) == 2, -sine, sine)
    cosine = jnp.where(((quarter + 1) & 2) == 2, -cosine, cosine)
    return sine, cosine


def kernel(
    nlat, nlon,
    route_in, tblk_in, depth_in, fric_in, mask_in, forc_in, ocell_in, otime_in, oval_in, oweight_in,
    x_out, p_out, r_out, q_out, w_out, z_out, first_out, second_out, third_out,
    route, tblk, depth, fric, mask, forc, ocell, otime, oval, oweight,
    dw, dwn, dws, dwe, dww, wetfric, coef, diag,
    pay, payi, outf, outi, inf, ini, plan, splan, waves, mats, oslot,
    field, seen, r1, p1, q1, z_last, r2, p2, q2, x,
    pk, hq, hq1, hx, hp, hr, hw, surf, surf_pk, surf_hq, near, end_coef, sum_a, part_row, ready,
    load, hs, hrv, ss, sr, as_, ar, os_, orv, ds_, dr, loc,
):
    rows, cols = depth.shape
    nblk = cols // BLOCK
    slots = nlon * CAP
    tiles = otime.shape[0]
    me_lat = lax.axis_index("lat")
    me_lon = lax.axis_index("lon")
    north, south = lax.rem(me_lat + 1, nlat), lax.rem(me_lat + nlat - 1, nlat)
    east, west = lax.rem(me_lon + 1, nlon), lax.rem(me_lon + nlon - 1, nlon)
    me = me_lat * nlon + me_lon
    count = nlat * nlon

    barrier = pltpu.get_barrier_semaphore()
    lon_order = sorted(range(nlon), key=lambda k: (k == 0, k % 2 == 0, -abs(k - nlon // 2)))
    for k in lon_order[:-1]:
        pl.semaphore_signal(barrier, inc=1, device_id={"lon": lax.rem(me_lon + k, nlon)}, device_id_type=MESH)
    for k in range(1, nlat):
        pl.semaphore_signal(barrier, inc=1, device_id={"lat": lax.rem(me_lat + k, nlat)}, device_id_type=MESH)
    pairs = [
        (route_in, route), (tblk_in, tblk), (ocell_in, ocell), (otime_in, otime), (oval_in, oval),
        (oweight_in, oweight), (depth_in, depth), (mask_in, mask), (fric_in, fric), (forc_in, forc),
    ]
    loads = [pltpu.make_async_copy(src, dst, load.at[k]) for k, (src, dst) in enumerate(pairs)]
    for c in loads:
        c.start()

    def remote(src, dst, send, recv, where):
        return pltpu.make_async_remote_copy(
            src_ref=src, dst_ref=dst, send_sem=send, recv_sem=recv, device_id=where, device_id_type=MESH
        )

    lane = lax.broadcasted_iota(jnp.int32, (1, BLOCK), 1)
    lane8 = lax.broadcasted_iota(jnp.int32, (8, BLOCK), 1)
    sub8 = lax.broadcasted_iota(jnp.int32, (8, BLOCK), 0)
    zero = jnp.zeros((2, 8, BLOCK), jnp.float32)

    for c in loads[:8]:
        c.wait()
    wet = mask[...].astype(jnp.float32)
    dw[...] = depth[...] * wet

    for t in range(tiles):
        pay[t] = jnp.concatenate([otime[t : t + 1], oval[t : t + 1], oweight[t : t + 1], oval[t : t + 1]] * 2, axis=0)
        payi[t] = jnp.broadcast_to(ocell[t : t + 1] + tblk[t] * BLOCK, (8, BLOCK))
    pay[tiles] = jnp.zeros((8, BLOCK), jnp.float32)
    payi[tiles] = jnp.zeros((8, BLOCK), jnp.int32)

    def pick(p, carry):
        first, second = jnp.int32(tiles), jnp.int32(tiles)
        for t in reversed(range(tiles)):
            hit = route[t] == p
            second = jnp.where(hit, first, second)
            first = jnp.where(hit, jnp.int32(t), first)
        outf[p] = jnp.where(sub8 < 4, pay[first], pay[second])
        outi[p] = jnp.where(sub8 == 0, payi[first], payi[second])
        return carry

    lax.fori_loop(0, nlon, pick, 0)
    pl.semaphore_wait(barrier, nlon + nlat - 2)

    def obs_copy(n, k):
        src, dst = ((outi, ini), (outf, inf))[n]
        peer = lax.rem(me_lon + k, nlon)
        return remote(src.at[peer], dst.at[me_lon], os_.at[n, peer], orv.at[n, me_lon], {"lon": peer})

    def obs_wait(n):
        src, dst = ((outi, ini), (outf, inf))[n]
        for k in range(1, nlon):
            peer = lax.rem(me_lon + k, nlon)
            remote(src.at[peer], dst.at[peer], os_.at[n, peer], orv.at[n, peer], {"lon": peer}).wait_recv()

    obs_sends = [obs_copy(n, k) for n in range(2) for k in lon_order[:-1]]
    for c in obs_sends:
        c.start()
    first_copies = [
        remote(dw.at[:, pl.ds(0, BLOCK)], dwe, ds_.at[2], dr.at[2], {"lon": west}),
        remote(dw.at[:, pl.ds(cols - BLOCK, BLOCK)], dww, ds_.at[3], dr.at[3], {"lon": east}),
        remote(dw, dws, ds_.at[0], dr.at[0], {"lat": north}),
        remote(dw, dwn, ds_.at[1], dr.at[1], {"lat": south}),
    ]
    for c in first_copies:
        c.start()
    for k in range(1, nlat):
        pl.semaphore_signal(ready, inc=1, device_id={"lat": lax.rem(me_lat + k, nlat)}, device_id_type=MESH)
    inf[me_lon] = outf[me_lon]
    ini[me_lon] = outi[me_lon]
    for c in loads[8:]:
        c.wait()

    for cb in range(nblk):
        at = pl.ds(cb * BLOCK, BLOCK)
        for h in range(2):
            wetted = forc[h, :, :, at] * wet[None, :, cb * BLOCK : cb * BLOCK + BLOCK]
            field[0, pl.ds(1, rows), cb, h] = jnp.swapaxes(wetted, 0, 1)
    oslot[slots] = zero
    mats[slots] = jnp.zeros((256, BLOCK), jnp.float32)
    stiff = jnp.zeros((8, 1), jnp.float32)
    rate = jnp.zeros((8, BLOCK), jnp.float32)
    sub1 = lax.broadcasted_iota(jnp.int32, (8, 1), 0)
    for c in range(8):
        stiff = jnp.where(sub1 == c, float(STIFF[c]), stiff)
        rate = jnp.where(sub8 == c, float(RATES[c]), rate)
    cells = lax.broadcasted_iota(jnp.int32, (BLOCK, BLOCK), 0)

    obs_wait(0)
    places = [ini[s // CAP, pl.ds(s % CAP, 1), :] >> 7 for s in range(slots)]
    rep = jnp.full((1, BLOCK), slots, jnp.int32)
    homes = jnp.full((1, BLOCK), -1, jnp.int32)
    for s in reversed(range(slots)):
        home = places[s]
        rep = jnp.where(home == lane, s, rep)
        homes = jnp.where(lane == s, home, homes)
    chain = jnp.full((1, BLOCK), slots, jnp.int32)
    for s in reversed(range(slots)):
        home = places[s]
        chain = jnp.where((home == homes) & (lane < s), s, chain)
    plan[...] = jnp.where(
        sub8 == 0,
        jnp.broadcast_to(homes, (8, BLOCK)),
        jnp.where(sub8 == 1, jnp.broadcast_to(chain, (8, BLOCK)), jnp.broadcast_to(rep, (8, BLOCK))),
    )
    to_scalars = pltpu.make_async_copy(plan, splan, loc.at[0])
    to_scalars.start()
    obs_wait(1)

    def onto_cells(o, k, terms):
        cell = ini[o, pl.ds(k, 1), :] & (BLOCK - 1)
        high = terms.astype(jnp.bfloat16)
        low = (terms - high.astype(jnp.float32)).astype(jnp.bfloat16)
        hot = (cells == cell).astype(jnp.float32).astype(jnp.bfloat16)
        return lax.dot_general(
            jnp.concatenate([high, low], axis=1),
            jnp.concatenate([hot, hot], axis=1),
            (((1,), (1,)), ((), ())),
            preferred_element_type=jnp.float32,
        )

    def values(o, carry):
        for k in range(CAP):
            times = inf[o, pl.ds(4 * k, 1), :]
            scaled = inf[o, pl.ds(4 * k + 2, 1), :] * inf[o, pl.ds(4 * k + 1, 1), :]
            sine, cosine = sin_cos(rate * times)
            waves[o * CAP + k, 0] = cosine
            waves[o * CAP + k, 1] = sine
            terms = jnp.concatenate([cosine * scaled, sine * scaled], axis=0)
            oslot[o * CAP + k] = onto_cells(o, k, terms).reshape(2, 8, BLOCK)
        return carry

    lax.fori_loop(0, nlon, values, 0, unroll=4)
    to_scalars.wait()

    def join_values(i, carry):
        s = slots - 1 - i
        oslot[s] = oslot[s] + oslot[splan[1, s]]
        return carry

    lax.fori_loop(0, slots, join_values, 0)

    def keep_ends(k, src):
        for side, cb in enumerate((0, nblk - 1)):
            packed = zero
            for row in range(rows):
                moved = pltpu.roll(src[row + 1, cb], (row + side) % BLOCK, 2)
                packed = jnp.where(lane8 == row, moved, packed)
            pk[k, side] = packed

    def keep_near(k):
        packed = zero
        for row in range(rows):
            packed = jnp.where(lane8 == row, pltpu.roll(field[k, row + 1, 0], (row + BLOCK - 1) % BLOCK, 2), packed)
        near[k] = packed

    def start_rhs(blocks):
        def line(row, carry):
            for cb in blocks:
                v = field[0, row + 1, cb] + oslot[splan[2, row * nblk + cb]]
                field[0, row + 1, cb] = v
                seen[row * nblk + cb] = v
            return carry

        lax.fori_loop(0, rows, line, 0, unroll=rows if len(blocks) == 2 else 2)

    start_rhs((0, nblk - 1))
    keep_ends(0, field.at[0])

    def halo(k):
        return [
            remote(pk.at[k, 0], hq.at[k, 1], hs.at[k, 2], hrv.at[k, 2], {"lon": west}),
            remote(pk.at[k, 1], hq.at[k, 0], hs.at[k, 3], hrv.at[k, 3], {"lon": east}),
            remote(field.at[k, 1], field.at[k, rows + 1], hs.at[k, 0], hrv.at[k, 0], {"lat": south}),
            remote(field.at[k, rows], field.at[k, 0], hs.at[k, 1], hrv.at[k, 1], {"lat": north}),
        ]

    def send_halo(k, part=slice(None)):
        for c in halo(k)[part]:
            c.start()

    def wait_halo(k, part=slice(None)):
        for c in halo(k)[part]:
            c.wait_recv()

    send_halo(0, slice(0, 2))
    start_rhs(range(1, nblk - 1))
    send_halo(0, slice(2, 4))

    for c in first_copies:
        c.wait_recv()
    a = dw[...]
    colid = lax.broadcasted_iota(jnp.int32, (rows, cols), 1)
    rowid = lax.broadcasted_iota(jnp.int32, (rows, cols), 0)
    keep_n = (me_lat < nlat - 1).astype(jnp.float32)
    keep_s = (me_lat > 0).astype(jnp.float32)

    def harmonic(first, second):
        return 2.0 * first * second / jnp.maximum(first + second, 0.5)

    drag = fric[...]
    total = wet * drag + (1.0 - wet)
    around = (
        lambda: jnp.where(colid == cols - 1, dwe[:, 0:1], pltpu.roll(a, cols - 1, 1)),
        lambda: jnp.where(colid == 0, dww[:, BLOCK - 1 : BLOCK], pltpu.roll(a, 1, 1)),
        lambda: jnp.where(rowid == rows - 1, dwn[0:1, :] * keep_n, pltpu.roll(a, rows - 1, 0)),
        lambda: jnp.where(rowid == 0, dws[rows - 1 : rows, :] * keep_s, pltpu.roll(a, 1, 0)),
    )
    for k in range(4):
        side = harmonic(a, around[k]())
        total = total + side
        for row in range(rows):
            coef[k, row] = jnp.broadcast_to(side[row : row + 1], (8, cols))
    dragged = wet * drag
    for row in range(rows):
        wetfric[row] = jnp.broadcast_to(dragged[row : row + 1], (8, cols))
        wide = jnp.broadcast_to(wet[row : row + 1], (8, cols))
        diag[row] = wide * stiff + jnp.broadcast_to(total[row : row + 1], (8, cols))

    def pack_rows(ref, lead, side):
        packed = jnp.zeros((8, BLOCK), jnp.float32)
        at = pl.ds(side * (cols - BLOCK), BLOCK)
        for row in range(rows):
            value = ref[lead + (row, slice(None), at)]
            packed = jnp.where(lane8 == row, pltpu.roll(value, (row + side) % BLOCK, 1), packed)
        return packed

    def build(o, carry):
        for k in range(CAP):
            weight = inf[o, pl.ds(4 * k + 2, 1), :]
            basis = (waves[o * CAP + k, 0], waves[o * CAP + k, 1])
            parts = []
            for h in range(2):
                for c in range(8):
                    one = weight * basis[h][c : c + 1]
                    parts.append(one * basis[0])
                    parts.append(one * basis[1])
            mats[o * CAP + k] = onto_cells(o, k, jnp.concatenate(parts, axis=0))
        return carry

    lax.fori_loop(0, nlon, build, 0)

    def join_mats(i, carry):
        s = slots - 1 - i
        mats[s] = mats[s] + mats[splan[1, s]]
        return carry

    lax.fori_loop(0, slots, join_mats, 0)
    for side in range(2):
        end_coef[side, 0] = pack_rows(coef, (0,), side)
        end_coef[side, 1] = pack_rows(coef, (2,), side)
        end_coef[side, 2] = pack_rows(wetfric, (), side)

    def observe():
        def slot(s, carry):
            v = seen[splan[0, s]]
            acc = [zero, zero]
            for c in range(16):
                m = mats[s, 16 * c : 16 * c + 16, :].reshape(2, 8, BLOCK)
                acc[c % 2] = acc[c % 2] + m * v[c // 8, c % 8 : c % 8 + 1, :]
            oslot[s] = acc[0] + acc[1]
            return carry

        lax.fori_loop(0, slots, slot, 0, unroll=4)

    def eastward(v, beyond):
        moved = [pltpu.roll(b, BLOCK - 1, 2) for b in v] + [beyond]
        return [jnp.where(lane8 == BLOCK - 1, moved[cb + 1], moved[cb]) for cb in range(nblk)]

    def westward(v, beyond):
        moved = [beyond] + [pltpu.roll(b, 1, 2) for b in v]
        return [jnp.where(lane8 == 0, moved[cb], moved[cb + 1]) for cb in range(nblk)]

    def from_east(halos, row):
        return pltpu.roll(halos[1], BLOCK - 1 - row, 2)

    def from_west(halos, row):
        return pltpu.roll(halos[0], BLOCK - row, 2)

    def image_row(src, row, east_side, west_side, to_north=True, to_south=True):
        v = [src[row + 1, cb] for cb in range(nblk)]
        e = eastward(v, east_side)
        w = westward(v, west_side)
        images = []
        for cb in range(nblk):
            at = pl.ds(cb * BLOCK, BLOCK)
            image = (
                diag[row, :, at] * v[cb]
                - coef[0, row, :, at] * e[cb]
                - coef[1, row, :, at] * w[cb]
                + oslot[splan[2, row * nblk + cb]]
            )
            if to_north:
                image = image - coef[2, row, :, at] * src[row + 2, cb]
            if to_south:
                image = image - coef[3, row, :, at] * src[row, cb]
            images.append(image)
        return v, images

    def inside(src, dst):
        def put(row, images):
            for cb in range(nblk):
                dst[row + 1, cb] = images[cb]

        def line(row, carry):
            put(row, image_row(src, row, zero, zero)[1])
            return carry

        lax.fori_loop(1, rows - 1, line, 0, unroll=3 if (rows - 2) % 3 == 0 else 2)
        put(0, image_row(src, 0, zero, zero, to_south=False)[1])
        put(rows - 1, image_row(src, rows - 1, zero, zero, to_north=False)[1])

    def lat_edges(src, dst):
        for cb in range(nblk):
            at = pl.ds(cb * BLOCK, BLOCK)
            dst[1, cb] = dst[1, cb] - coef[3, 0, :, at] * src[0, cb]
            dst[rows, cb] = dst[rows, cb] - coef[2, rows - 1, :, at] * src[rows + 1, cb]

    def lon_edges(halos, dst, refs=()):
        dots, square = [zero] * len(refs), zero
        for row in range(rows):
            for side in range(2):
                cb = side * (nblk - 1)
                beyond = from_east(halos, row) if side else from_west(halos, row)
                at = pl.ds(cb * BLOCK, BLOCK)
                change = coef[1 - side, row, :, at] * jnp.where(lane8 == side * (BLOCK - 1), -beyond, 0.0)
                old = dst[row + 1, cb]
                dst[row + 1, cb] = old + change
                dots = [dot + ref[row + 1, cb] * change for dot, ref in zip(dots, refs)]
                square = square + change * (old + old + change)
        return [v[0] + v[1] for v in dots + [square]]

    lat_order = sorted(range(nlat), key=lambda k: (k == 0, abs(k - nlat // 2)))
    lat_peers = {k: lax.rem(me_lat + k, nlat) for k in lat_order}
    lon_peers = {k: lax.rem(me_lon + k, nlon) for k in lon_order}

    def sum_wait(i):
        whole = sum_a.at[i, pl.ds(0, count - 1)]
        return remote(whole, whole, as_.at[i], ar.at[i], {"lat": south})

    def send_sums(i, sums):
        part = jnp.zeros((8, BLOCK), jnp.float32)
        groups = 4 if len(sums) <= 4 else 16
        for k, s in enumerate(sums):
            both, wide = s, BLOCK
            while wide * groups > BLOCK:
                wide = wide // 2
                both = both + pltpu.roll(both, wide, 1)
            part = jnp.where(lane8 // (BLOCK // groups) == k, both, part)
        row = jnp.sum(part, axis=0, keepdims=True)
        part_row[i] = row
        sum_a[i, pl.ds(me, 1)] = row
        for a in lat_order:
            for b in lon_order:
                if a or b:
                    where = {"lat": lat_peers[a], "lon": lon_peers[b]}
                    remote(part_row.at[i], sum_a.at[i, pl.ds(me, 1)], as_.at[i], ar.at[i], where).start()

    def take_sums(i, number=4):
        sum_wait(i).wait_recv()
        groups, tall = (4, 8) if number <= 4 else (16, 16)
        total = jnp.sum(sum_a[i], axis=0, keepdims=True)
        lanes = lax.broadcasted_iota(jnp.int32, (tall, BLOCK), 1) // (BLOCK // groups)
        own = lanes == lax.broadcasted_iota(jnp.int32, (tall, BLOCK), 0)
        whole = jnp.sum(jnp.where(own, total, 0.0), axis=1, keepdims=True)
        return [jnp.broadcast_to(whole[k : k + 1], (8, BLOCK)) for k in range(number)]

    def beta_of(size, rr, rq, qq):
        return (rr - 2.0 * size * rq + size * size * qq) / rr

    def halves(sums):
        return [v[0] + v[1] for v in sums]

    def last_sums(size, beta, rr, rq, dq, qq, rw, rz, qw, qz, pw, pz):
        with_r = rw - size * rz + beta * rq
        with_q = qw - size * qz + beta * qq
        with_p = pw - size * pz + beta * dq
        return [rr - 2.0 * size * rq + size * size * qq, with_r - size * with_q + beta * with_p]

    def outer(o):
        k0, kq, kz = 4 * o, 4 * o + 1, 4 * o + 2
        i0, i1, i2 = ITERS * o, ITERS * o + 1, ITERS * o + 2
        r0, q0, z0 = field.at[k0], field.at[kq], field.at[kz]
        z1 = field.at[3] if o == 0 else z_last
        observe()
        if o == 0:
            inside(r0, q0)
            wait_halo(k0, slice(2, 4))
            lat_edges(r0, q0)

        def first_dots(row, carry):
            rr, rq, qq = carry
            if o == 0:
                v = [r0[row + 1, cb] for cb in range(nblk)]
                images = [q0[row + 1, cb] for cb in range(nblk)]
            else:
                v, images = image_row(r0, row, from_east(hq.at[k0], row), from_west(hq.at[k0], row))
            for cb in range(nblk):
                res, image = v[cb], images[cb]
                if o > 0:
                    q0[row + 1, cb] = image
                rr = rr + res * res
                rq = rq + res * image
                qq = qq + image * image
            return rr, rq, qq

        sums = halves(lax.fori_loop(0, rows, first_dots, (zero, zero, zero), unroll=rows))
        if o == 0:
            wait_halo(k0, slice(0, 2))
            more_rq, more_qq = lon_edges(hq.at[k0], q0, (r0,))
            sums = [sums[0], sums[1] + more_rq, sums[2] + more_qq]
        keep_ends(kq, q0)
        send_halo(kq, slice(0, 2) if o == 0 else slice(None))
        if o == 0:
            pl.semaphore_wait(ready, nlat - 1)
        send_sums(i0, sums)
        if o == 0:
            send_halo(kq, slice(2, 4))
        if o == 0:
            keep_near(0)
            keep_near(1)

        def look(row, carry):
            for cb in range(nblk):
                seen[row * nblk + cb] = q0[row + 1, cb]
            return carry

        lax.fori_loop(0, rows, look, 0)
        observe()
        inside(q0, z0)
        wait_halo(kq, slice(2, 4))
        lat_edges(q0, z0)
        wait_halo(kq, slice(0, 2))
        lon_edges(hq.at[kq], z0)

        keep_ends(kz, z0)
        send_halo(kz)
        if o == 0:
            keep_near(2)
        rr, rq, qq, _ = take_sums(i0)
        size0 = rr / rq
        beta0 = beta_of(size0, rr, rq, qq)
        more = 1.0 + beta0

        def second_vectors(row, cb):
            r, q, z = r0[row + 1, cb], q0[row + 1, cb], z0[row + 1, cb]
            res = r - size0 * q
            return res, res + beta0 * r, more * q - size0 * z

        def second(row, carry):
            ri, qi, ii = carry
            for cb in range(nblk):
                q = q0[row + 1, cb]
                image = more * q - size0 * z0[row + 1, cb]
                ri = ri + r0[row + 1, cb] * image
                qi = qi + q * image
                ii = ii + image * image
            return ri, qi, ii

        part_ri, part_qi, part_qq = halves(lax.fori_loop(0, rows, second, (zero,) * 3, unroll=4))
        part_rr = sums[0] - 2.0 * size0 * sums[1] + size0 * size0 * sums[2]
        part_rq = part_ri - size0 * part_qi
        part_dq = part_rq + beta0 * part_ri
        sums = (part_rr, part_rq, part_dq, part_qq)
        if o == 0:
            send_sums(i1, sums)

        def keep_second(row, carry):
            for cb in range(nblk):
                r1[row + 1, cb], p1[row + 1, cb], image = second_vectors(row, cb)
                q1[row + 1, cb] = image
                seen[row * nblk + cb] = image
            return carry

        lax.fori_loop(0, rows, keep_second, 0, unroll=4)
        observe()
        inside(q1, z1)
        wait_halo(kz, slice(2, 4))
        for edge in (0, rows + 1):
            for cb in range(nblk):
                q1[edge, cb] = more * q0[edge, cb] - size0 * z0[edge, cb]
        lat_edges(q1, z1)

        def third(row, carry):
            rw, rz, qw, qz, pw, pz = carry
            for cb in range(nblk):
                r, q, p, z = r1[row + 1, cb], q1[row + 1, cb], p1[row + 1, cb], z1[row + 1, cb]
                w = q0[row + 1, cb] - size0 * z0[row + 1, cb]
                rw = rw + r * w
                rz = rz + r * z
                qw = qw + q * w
                qz = qz + q * z
                pw = pw + p * w
                pz = pz + p * z
            return rw, rz, qw, qz, pw, pz

        rw, rz, qw, qz, pw, pz = halves(lax.fori_loop(0, rows, third, (zero,) * 6, unroll=4))
        wait_halo(kz, slice(0, 2))
        hq1[...] = more * hq[kq] - size0 * hq[kz]
        more_rz, more_qz, more_pz, _ = lon_edges(hq1, z1, (r1, q1, p1))
        rz, qz, pz = rz + more_rz, qz + more_qz, pz + more_pz
        if o == 0:
            keep_ends(3, z1)
            send_halo(3)
        if o > 0:
            send_sums(i1, list(sums) + [rw, rz, qw, qz, pw, pz])
            return size0
        rr, rq, dq, qq = take_sums(i1)
        size1 = rr / dq
        beta1 = beta_of(size1, rr, rq, qq)
        send_sums(i2, last_sums(size1, beta1, *sums, rw, rz, qw, qz, pw, pz))

        def settle(blocks):
            def line(row, carry):
                for cb in blocks:
                    q, p = q1[row + 1, cb], p1[row + 1, cb]
                    res = r1[row + 1, cb] - size1 * q
                    r2[row + 1, cb] = res
                    p2[row + 1, cb] = res + beta1 * p
                    w = q0[row + 1, cb] - size0 * z0[row + 1, cb]
                    q2[row + 1, cb] = (w - size1 * z1[row + 1, cb]) + beta1 * q
                    x[row + 1, cb] = size0 * r0[row + 1, cb] + size1 * p
                return carry

            lax.fori_loop(0, rows, line, 0, unroll=2)

        return size0, beta0, size1, beta1, settle

    size0, beta0, size1, beta1, settle = outer(0)

    def beyond(r, q, q_next):
        res = r - size0 * q
        way = res + beta0 * r
        res = res - size1 * q_next
        return size0 * r + size1 * way, res + beta1 * way, res

    hx[...], hp[...], hr[...] = beyond(hq[0], hq[1], hq1[...])

    def add_up(square):
        return jnp.sum(square[0] + square[1], axis=0, keepdims=True)

    def parts_of(flux, dragged):
        (xe, xn), (pe, pn) = flux
        parts = jnp.where(sub8 == 0, add_up(xe * xe + xn * xn), dragged)
        parts = jnp.where(sub8 == 1, add_up(xe * pe + xn * pn), parts)
        return jnp.where(sub8 == 2, add_up(pe * pe + pn * pn), parts)

    def extended(k, side):
        corner = field[k, rows + 1, side * (nblk - 1)]
        return jnp.where(lane8 == rows, pltpu.roll(corner, (rows + side) % BLOCK, 2), pk[k, side])

    def state(r, q, z):
        return beyond(r, q, (1.0 + beta0) * q - size0 * z)[:2]

    for side in range(2):
        own = state(*(extended(k, side) for k in range(3)))
        after = (hx[1], hp[1]) if side else state(near[0], near[1], near[2])
        flux = [
            (end_coef[side, 0] * (e - v), end_coef[side, 1] * (pltpu.roll(v, BLOCK - 1, 2) - v))
            for v, e in zip(own, after)
        ]
        surf_pk[side] = parts_of(flux, end_coef[side, 2])
    surf_copies = [
        remote(surf_pk.at[0], surf_hq.at[1], ss.at[2], sr.at[2], {"lon": west}),
        remote(surf_pk.at[1], surf_hq.at[0], ss.at[3], sr.at[3], {"lon": east}),
        remote(surf.at[1], surf.at[rows + 1], ss.at[0], sr.at[0], {"lat": south}),
        remote(surf.at[rows], surf.at[0], ss.at[1], sr.at[1], {"lat": north}),
    ]
    for c in surf_copies[:2]:
        c.start()
    settle(range(nblk))
    for edge in (0, rows + 1):
        for cb in range(nblk):
            x[edge, cb], p2[edge, cb], r2[edge, cb] = beyond(field[0, edge, cb], field[1, edge, cb], q1[edge, cb])

    def surface(row, carry):
        for cb in range(nblk):
            at = pl.ds(cb * BLOCK, BLOCK)
            flux = []
            for ref, halos in ((x, hx), (p2, hp)):
                v = ref[row + 1, cb]
                after = pltpu.roll(ref[row + 1, cb + 1], BLOCK - 1, 2) if cb < nblk - 1 else from_east(halos, row)
                e = jnp.where(lane8 == BLOCK - 1, after, pltpu.roll(v, BLOCK - 1, 2))
                flux.append((coef[0, row, :, at] * (e - v), coef[2, row, :, at] * (ref[row + 2, cb] - v)))
            surf[row + 1, :, at] = parts_of(flux, wetfric[row, :, at])
        return carry

    lax.fori_loop(0, rows, surface, 0)
    for c in surf_copies[2:]:
        c.start()
    wait_halo(3)

    def image_beyond(q, z, z_next, q_next):
        return ((q - size0 * z) - size1 * z_next) + beta1 * q_next

    for edge in (0, rows + 1):
        for cb in range(nblk):
            q2[edge, cb] = image_beyond(field[1, edge, cb], field[2, edge, cb], field[3, edge, cb], q1[edge, cb])
    hw[...] = image_beyond(hq[1], hq[2], hq[3], hq1[...])
    for c in surf_copies:
        c.wait_recv()
    rr, dq, _, _ = take_sums(2)
    size2 = rr / dq
    ramp = jnp.where(sub8 == 0, 1.0, jnp.where(sub8 == 1, 2.0 * size2, jnp.where(sub8 == 2, size2 * size2, 0.0)))

    def extra_of(parts):
        speed = jnp.maximum(jnp.sum(parts * ramp, axis=0, keepdims=True), 0.0)
        return parts[3:4] * (jnp.sqrt(1.0 + speed / 16.0) - 1.0)

    def renew(row, cb):
        extra = extra_of(surf[row, :, pl.ds(cb * BLOCK, BLOCK)])
        place = x[row, cb] + size2 * p2[row, cb]
        new = (r2[row, cb] - size2 * q2[row, cb]) - extra * place
        field[4, row, cb] = new
        return extra, place, new

    def friction(row, carry):
        for cb in range(nblk):
            at = pl.ds(cb * BLOCK, BLOCK)
            extra, place, new = renew(row + 1, cb)
            x[row + 1, cb] = place
            diag[row, :, at] = diag[row, :, at] + extra
            seen[row * nblk + cb] = new
        return carry

    lax.fori_loop(0, rows, friction, 0, unroll=4)
    for edge in (0, rows + 1):
        for cb in range(nblk):
            renew(edge, cb)
    for side in range(2):
        hq[4, side] = (hr[side] - size2 * hw[side]) - extra_of(surf_hq[side]) * (hx[side] + size2 * hp[side])
    size0 = outer(1)
    for cb in range(nblk):
        at = pl.ds(cb * BLOCK, BLOCK)
        for h in range(2):
            own = (pl.ds(1, rows), cb, h)
            x_out[h, :, :, at] = jnp.swapaxes(x[own] + size0 * field[(4,) + own], 0, 1)
            w_out[h, :, :, at] = jnp.swapaxes(field[(5,) + own] - size0 * field[(6,) + own], 0, 1)
            for src, dst in ((p1, p_out), (r1, r_out), (q1, q_out), (z_last, z_out)):
                dst[h, :, :, at] = jnp.swapaxes(src[own], 0, 1)
    for c in obs_sends + first_copies:
        c.wait_send()
    for k in (0, 1, 2, 3, 5, 6):
        for c in halo(k):
            c.wait_send()
    for c in surf_copies:
        c.wait_send()
    rr, rq, dq, qq, *others = take_sums(SUMS - 2, 10)
    size1 = rr / dq
    beta1 = beta_of(size1, rr, rq, qq)
    rr, dq = last_sums(size1, beta1, rr, rq, dq, qq, *others)
    size2 = rr / dq
    for dst, value in ((first_out, size1 + size2 * beta1), (second_out, size2), (third_out, size1 * size2)):
        dst[...] = jnp.broadcast_to(value[:, 0:1], (8, cols))
    for i in range(SUMS - 1):
        sum_wait(i).wait_send()


def shards(nlat, nlon, depth, friction, ocean_mask, forcing, tile_route, tile_block, obs_cell, obs_time, obs_value, obs_weight):
    channels, rows, cols = forcing.shape
    slots = nlon * CAP
    nblk, tiles = cols // BLOCK, obs_time.shape[0]
    f32, i32 = jnp.float32, jnp.int32
    vmem, smem = pltpu.VMEM, pltpu.SMEM
    hbm = pl.BlockSpec(memory_space=pltpu.HBM)
    field = (rows + 2, nblk, 2, 8, BLOCK)
    ends = (2, 2, 8, BLOCK)
    split = (2, channels // 2, rows, cols)
    dma = pltpu.SemaphoreType.DMA
    scratch = [
        smem((tiles,), i32),
        smem((tiles,), i32),
        vmem((rows, cols), f32),
        vmem((rows, cols), f32),
        vmem((rows, cols), i32),
        vmem(split, f32),
        vmem((tiles, BLOCK), i32),
        vmem((tiles, BLOCK), f32),
        vmem((tiles, BLOCK), f32),
        vmem((tiles, BLOCK), f32),
        vmem((rows, cols), f32),
        vmem((rows, cols), f32),
        vmem((rows, cols), f32),
        vmem((rows, BLOCK), f32),
        vmem((rows, BLOCK), f32),
        vmem((rows, 8, cols), f32),
        vmem((4, rows, 8, cols), f32),
        vmem((rows, 8, cols), f32),
        vmem((tiles + 1, 8, BLOCK), f32),
        vmem((tiles + 1, 8, BLOCK), i32),
        vmem((nlon, 8, BLOCK), f32),
        vmem((nlon, 8, BLOCK), i32),
        vmem((nlon, 8, BLOCK), f32),
        vmem((nlon, 8, BLOCK), i32),
        vmem((8, BLOCK), i32),
        smem((8, BLOCK), i32),
        vmem((slots, 2, 8, BLOCK), f32),
        vmem((slots + 1, 256, BLOCK), f32),
        vmem((slots + 1, 2, 8, BLOCK), f32),
        vmem((HALOS,) + field, f32),
        vmem((rows * nblk, 2, 8, BLOCK), f32),
        vmem(field, f32),
        vmem(field, f32),
        vmem(field, f32),
        vmem(field, f32),
        vmem(field, f32),
        vmem(field, f32),
        vmem(field, f32),
        vmem(field, f32),
        vmem((HALOS,) + ends, f32),
        vmem((HALOS,) + ends, f32),
        vmem(ends, f32),
        vmem(ends, f32),
        vmem(ends, f32),
        vmem(ends, f32),
        vmem(ends, f32),
        vmem((rows + 2, 8, cols), f32),
        vmem((2, 8, BLOCK), f32),
        vmem((2, 8, BLOCK), f32),
        vmem((3, 2, 8, BLOCK), f32),
        vmem((2, 3, 8, BLOCK), f32),
        vmem((SUMS, nlat * nlon, BLOCK), f32),
        vmem((SUMS, 1, BLOCK), f32),
        pltpu.SemaphoreType.REGULAR,
        dma((10,)),
        dma((HALOS, 4)),
        dma((HALOS, 4)),
        dma((4,)),
        dma((4,)),
        dma((SUMS,)),
        dma((SUMS,)),
        dma((2, nlon)),
        dma((2, nlon)),
        dma((4,)),
        dma((4,)),
        dma((1,)),
    ]
    shape = vmem(split, f32)
    x, p, r, q, w, z, first, second, third = pl.pallas_call(
        functools.partial(kernel, nlat, nlon),
        out_shape=(shape,) * 6 + (vmem((8, cols), f32),) * 3,
        in_specs=[hbm] * 10,
        out_specs=(pl.BlockSpec(memory_space=vmem),) * 9,
        scratch_shapes=scratch,
        compiler_params=pltpu.CompilerParams(
            collective_id=0, has_side_effects=True, vmem_limit_bytes=60 * 2**20
        ),
    )(
        tile_route.reshape(-1), tile_block, depth, friction, ocean_mask, forcing.reshape(split),
        obs_cell, obs_time, obs_value, obs_weight,
    )
    x = x + first * p + second * r - third * q
    r = r - first * q - second * w + third * z
    return x.reshape(forcing.shape), r.reshape(forcing.shape)


def solution(mesh):
    tile = P(("lat", "lon"), None)
    grid = P("lat", "lon")
    in_specs = (grid, grid, grid, P(None, "lat", "lon"), tile, P(("lat", "lon")), tile, tile, tile, tile)
    out_specs = (P(None, "lat", "lon"), P(None, "lat", "lon"))
    body = functools.partial(shards, mesh.shape["lat"], mesh.shape["lon"])
    return jax.shard_map(body, mesh=mesh, in_specs=in_specs, out_specs=out_specs, check_vma=False)
```

```python
import functools
import math

import jax
import jax.numpy as jnp
import numpy as np
from jax import lax
from jax.experimental import pallas as pl
from jax.experimental.pallas import tpu as pltpu
from jax.sharding import PartitionSpec as P

BLOCK = 128
CAP = 2
ITERS = 3
OUTER = 2
SUMS = ITERS * OUTER
HALOS = 7
MESH = pl.DeviceIdType.MESH
OMEGA_DEGREES = (28.984104, 30.0, 28.43973, 30.082137, 15.041069, 13.943036, 14.958931, 13.398661)
RATES = np.array(OMEGA_DEGREES, np.float32) * np.float32(math.pi / 180.0)
STIFF = np.float32(0.2) * (RATES / RATES[0]) ** 2


def sin_cos(angle):
    turn = jnp.floor(angle * (2.0 / math.pi) + 0.5)
    x = ((angle - turn * 1.5703125) - turn * 4.837512969970703125e-4) - turn * 7.54978995489188216e-8
    z = x * x
    s = ((-1.9515295891e-4 * z + 8.3321608736e-3) * z - 1.6666654611e-1) * z * x + x
    c = ((2.443315711809948e-5 * z - 1.388731625493765e-3) * z + 4.166664568298827e-2) * z * z - 0.5 * z + 1.0
    quarter = turn.astype(jnp.int32)
    odd = (quarter & 1) == 1
    sine = jnp.where(odd, c, s)
    cosine = jnp.where(odd, s, c)
    sine = jnp.where((quarter & 2) == 2, -sine, sine)
    cosine = jnp.where(((quarter + 1) & 2) == 2, -cosine, cosine)
    return sine, cosine


def kernel(
    nlat, nlon,
    route_in, tblk_in, depth_in, fric_in, mask_in, forc_in, ocell_in, otime_in, oval_in, oweight_in,
    x_out, p_out, r_out, q_out, w_out, z_out, first_out, second_out, third_out,
    route, tblk, depth, fric, mask, forc, ocell, otime, oval, oweight,
    dw, dwn, dws, dwe, dww, wetfric, coef, diag,
    pay, payi, outf, outi, inf, ini, plan, splan, waves, mats, oslot,
    field, seen, r1, p1, q1, z_last, r2, p2, q2, x,
    pk, hq, hq1, hx, hp, hr, hw, surf, surf_pk, surf_hq, near, end_coef, sum_a, part_row, ready,
    load, hs, hrv, ss, sr, as_, ar, os_, orv, ds_, dr, loc,
):
    rows, cols = depth.shape
    nblk = cols // BLOCK
    slots = nlon * CAP
    tiles = otime.shape[0]
    me_lat = lax.axis_index("lat")
    me_lon = lax.axis_index("lon")
    north, south = lax.rem(me_lat + 1, nlat), lax.rem(me_lat + nlat - 1, nlat)
    east, west = lax.rem(me_lon + 1, nlon), lax.rem(me_lon + nlon - 1, nlon)
    me = me_lat * nlon + me_lon
    count = nlat * nlon

    barrier = pltpu.get_barrier_semaphore()
    lon_order = sorted(range(nlon), key=lambda k: (k == 0, k % 2 == 0, -abs(k - nlon // 2)))
    for k in lon_order[:-1]:
        pl.semaphore_signal(barrier, inc=1, device_id={"lon": lax.rem(me_lon + k, nlon)}, device_id_type=MESH)
    for k in range(1, nlat):
        pl.semaphore_signal(barrier, inc=1, device_id={"lat": lax.rem(me_lat + k, nlat)}, device_id_type=MESH)
    pairs = [
        (route_in, route), (tblk_in, tblk), (ocell_in, ocell), (otime_in, otime), (oval_in, oval),
        (oweight_in, oweight), (depth_in, depth), (mask_in, mask), (fric_in, fric), (forc_in, forc),
    ]
    loads = [pltpu.make_async_copy(src, dst, load.at[k]) for k, (src, dst) in enumerate(pairs)]
    for c in loads:
        c.start()

    def remote(src, dst, send, recv, where):
        return pltpu.make_async_remote_copy(
            src_ref=src, dst_ref=dst, send_sem=send, recv_sem=recv, device_id=where, device_id_type=MESH
        )

    lane = lax.broadcasted_iota(jnp.int32, (1, BLOCK), 1)
    lane8 = lax.broadcasted_iota(jnp.int32, (8, BLOCK), 1)
    sub8 = lax.broadcasted_iota(jnp.int32, (8, BLOCK), 0)
    zero = jnp.zeros((2, 8, BLOCK), jnp.float32)

    for c in loads[:8]:
        c.wait()
    wet = mask[...].astype(jnp.float32)
    dw[...] = depth[...] * wet

    for t in range(tiles):
        pay[t] = jnp.concatenate([otime[t : t + 1], oval[t : t + 1], oweight[t : t + 1], oval[t : t + 1]] * 2, axis=0)
        payi[t] = jnp.broadcast_to(ocell[t : t + 1] + tblk[t] * BLOCK, (8, BLOCK))
    pay[tiles] = jnp.zeros((8, BLOCK), jnp.float32)
    payi[tiles] = jnp.zeros((8, BLOCK), jnp.int32)

    def pick(p, carry):
        first, second = jnp.int32(tiles), jnp.int32(tiles)
        for t in reversed(range(tiles)):
            hit = route[t] == p
            second = jnp.where(hit, first, second)
            first = jnp.where(hit, jnp.int32(t), first)
        outf[p] = jnp.where(sub8 < 4, pay[first], pay[second])
        outi[p] = jnp.where(sub8 == 0, payi[first], payi[second])
        return carry

    lax.fori_loop(0, nlon, pick, 0)
    pl.semaphore_wait(barrier, nlon + nlat - 2)

    def obs_copy(n, k):
        src, dst = ((outi, ini), (outf, inf))[n]
        peer = lax.rem(me_lon + k, nlon)
        return remote(src.at[peer], dst.at[me_lon], os_.at[n, peer], orv.at[n, me_lon], {"lon": peer})

    def obs_wait(n):
        src, dst = ((outi, ini), (outf, inf))[n]
        for k in range(1, nlon):
            peer = lax.rem(me_lon + k, nlon)
            remote(src.at[peer], dst.at[peer], os_.at[n, peer], orv.at[n, peer], {"lon": peer}).wait_recv()

    obs_sends = [obs_copy(n, k) for n in range(2) for k in lon_order[:-1]]
    for c in obs_sends:
        c.start()
    first_copies = [
        remote(dw.at[:, pl.ds(0, BLOCK)], dwe, ds_.at[2], dr.at[2], {"lon": west}),
        remote(dw.at[:, pl.ds(cols - BLOCK, BLOCK)], dww, ds_.at[3], dr.at[3], {"lon": east}),
        remote(dw, dws, ds_.at[0], dr.at[0], {"lat": north}),
        remote(dw, dwn, ds_.at[1], dr.at[1], {"lat": south}),
    ]
    for c in first_copies:
        c.start()
    for k in range(1, nlat):
        pl.semaphore_signal(ready, inc=1, device_id={"lat": lax.rem(me_lat + k, nlat)}, device_id_type=MESH)
    inf[me_lon] = outf[me_lon]
    ini[me_lon] = outi[me_lon]
    for c in loads[8:]:
        c.wait()

    for cb in range(nblk):
        at = pl.ds(cb * BLOCK, BLOCK)
        for h in range(2):
            wetted = forc[h, :, :, at] * wet[None, :, cb * BLOCK : cb * BLOCK + BLOCK]
            field[0, pl.ds(1, rows), cb, h] = jnp.swapaxes(wetted, 0, 1)
    oslot[slots] = zero
    mats[slots] = jnp.zeros((256, BLOCK), jnp.float32)
    stiff = jnp.zeros((8, 1), jnp.float32)
    rate = jnp.zeros((8, BLOCK), jnp.float32)
    sub1 = lax.broadcasted_iota(jnp.int32, (8, 1), 0)
    for c in range(8):
        stiff = jnp.where(sub1 == c, float(STIFF[c]), stiff)
        rate = jnp.where(sub8 == c, float(RATES[c]), rate)
    cells = lax.broadcasted_iota(jnp.int32, (BLOCK, BLOCK), 0)

    for c in first_copies[2:]:
        c.wait_recv()
    a = dw[...]
    colid = lax.broadcasted_iota(jnp.int32, (rows, cols), 1)
    rowid = lax.broadcasted_iota(jnp.int32, (rows, cols), 0)
    keep_n = (me_lat < nlat - 1).astype(jnp.float32)
    keep_s = (me_lat > 0).astype(jnp.float32)

    def harmonic(first, second):
        return 2.0 * first * second / jnp.maximum(first + second, 0.5)

    drag = fric[...]
    total = wet * drag + (1.0 - wet)
    around = (
        lambda: jnp.where(colid == cols - 1, dwe[:, 0:1], pltpu.roll(a, cols - 1, 1)),
        lambda: jnp.where(colid == 0, dww[:, BLOCK - 1 : BLOCK], pltpu.roll(a, 1, 1)),
        lambda: jnp.where(rowid == rows - 1, dwn[0:1, :] * keep_n, pltpu.roll(a, rows - 1, 0)),
        lambda: jnp.where(rowid == 0, dws[rows - 1 : rows, :] * keep_s, pltpu.roll(a, 1, 0)),
    )
    for k in (2, 3):
        side = harmonic(a, around[k]())
        total = total + side
        for row in range(rows):
            coef[k, row] = jnp.broadcast_to(side[row : row + 1], (8, cols))
    obs_wait(0)
    places = [ini[s // CAP, pl.ds(s % CAP, 1), :] >> 7 for s in range(slots)]
    rep = jnp.full((1, BLOCK), slots, jnp.int32)
    homes = jnp.full((1, BLOCK), -1, jnp.int32)
    for s in reversed(range(slots)):
        home = places[s]
        rep = jnp.where(home == lane, s, rep)
        homes = jnp.where(lane == s, home, homes)
    chain = jnp.full((1, BLOCK), slots, jnp.int32)
    for s in reversed(range(slots)):
        home = places[s]
        chain = jnp.where((home == homes) & (lane < s), s, chain)
    plan[...] = jnp.where(
        sub8 == 0,
        jnp.broadcast_to(homes, (8, BLOCK)),
        jnp.where(sub8 == 1, jnp.broadcast_to(chain, (8, BLOCK)), jnp.broadcast_to(rep, (8, BLOCK))),
    )
    to_scalars = pltpu.make_async_copy(plan, splan, loc.at[0])
    to_scalars.start()
    obs_wait(1)

    def onto_cells(o, k, terms):
        cell = ini[o, pl.ds(k, 1), :] & (BLOCK - 1)
        high = terms.astype(jnp.bfloat16)
        low = (terms - high.astype(jnp.float32)).astype(jnp.bfloat16)
        hot = (cells == cell).astype(jnp.float32).astype(jnp.bfloat16)
        return lax.dot_general(
            jnp.concatenate([high, low], axis=1),
            jnp.concatenate([hot, hot], axis=1),
            (((1,), (1,)), ((), ())),
            preferred_element_type=jnp.float32,
        )

    def values(o, carry):
        for k in range(CAP):
            times = inf[o, pl.ds(4 * k, 1), :]
            scaled = inf[o, pl.ds(4 * k + 2, 1), :] * inf[o, pl.ds(4 * k + 1, 1), :]
            sine, cosine = sin_cos(rate * times)
            waves[o * CAP + k, 0] = cosine
            waves[o * CAP + k, 1] = sine
            terms = jnp.concatenate([cosine * scaled, sine * scaled], axis=0)
            oslot[o * CAP + k] = onto_cells(o, k, terms).reshape(2, 8, BLOCK)
        return carry

    lax.fori_loop(0, nlon, values, 0, unroll=4)
    to_scalars.wait()

    def join_values(i, carry):
        s = slots - 1 - i
        oslot[s] = oslot[s] + oslot[splan[1, s]]
        return carry

    lax.fori_loop(0, slots, join_values, 0)

    def keep_ends(k, src):
        for side, cb in enumerate((0, nblk - 1)):
            packed = zero
            for row in range(rows):
                moved = pltpu.roll(src[row + 1, cb], (row + side) % BLOCK, 2)
                packed = jnp.where(lane8 == row, moved, packed)
            pk[k, side] = packed

    def keep_near(k):
        packed = zero
        for row in range(rows):
            packed = jnp.where(lane8 == row, pltpu.roll(field[k, row + 1, 0], (row + BLOCK - 1) % BLOCK, 2), packed)
        near[k] = packed

    def start_rhs(blocks):
        def line(row, carry):
            for cb in blocks:
                v = field[0, row + 1, cb] + oslot[splan[2, row * nblk + cb]]
                field[0, row + 1, cb] = v
                seen[row * nblk + cb] = v
            return carry

        lax.fori_loop(0, rows, line, 0, unroll=rows if len(blocks) == 2 else 2)

    start_rhs((0, nblk - 1))
    keep_ends(0, field.at[0])

    def halo(k):
        return [
            remote(pk.at[k, 0], hq.at[k, 1], hs.at[k, 2], hrv.at[k, 2], {"lon": west}),
            remote(pk.at[k, 1], hq.at[k, 0], hs.at[k, 3], hrv.at[k, 3], {"lon": east}),
            remote(field.at[k, 1], field.at[k, rows + 1], hs.at[k, 0], hrv.at[k, 0], {"lat": south}),
            remote(field.at[k, rows], field.at[k, 0], hs.at[k, 1], hrv.at[k, 1], {"lat": north}),
        ]

    def send_halo(k, part=slice(None)):
        for c in halo(k)[part]:
            c.start()

    def wait_halo(k, part=slice(None)):
        for c in halo(k)[part]:
            c.wait_recv()

    send_halo(0, slice(0, 2))
    start_rhs(range(1, nblk - 1))
    send_halo(0, slice(2, 4))

    for c in first_copies[:2]:
        c.wait_recv()
    for k in (0, 1):
        side = harmonic(a, around[k]())
        total = total + side
        for row in range(rows):
            coef[k, row] = jnp.broadcast_to(side[row : row + 1], (8, cols))
    dragged = wet * drag
    for row in range(rows):
        wetfric[row] = jnp.broadcast_to(dragged[row : row + 1], (8, cols))
        wide = jnp.broadcast_to(wet[row : row + 1], (8, cols))
        diag[row] = wide * stiff + jnp.broadcast_to(total[row : row + 1], (8, cols))

    def pack_rows(ref, lead, side):
        packed = jnp.zeros((8, BLOCK), jnp.float32)
        at = pl.ds(side * (cols - BLOCK), BLOCK)
        for row in range(rows):
            value = ref[lead + (row, slice(None), at)]
            packed = jnp.where(lane8 == row, pltpu.roll(value, (row + side) % BLOCK, 1), packed)
        return packed

    def build(o, carry):
        for k in range(CAP):
            weight = inf[o, pl.ds(4 * k + 2, 1), :]
            basis = (waves[o * CAP + k, 0], waves[o * CAP + k, 1])
            parts = []
            for h in range(2):
                for c in range(8):
                    one = weight * basis[h][c : c + 1]
                    parts.append(one * basis[0])
                    parts.append(one * basis[1])
            mats[o * CAP + k] = onto_cells(o, k, jnp.concatenate(parts, axis=0))
        return carry

    lax.fori_loop(0, nlon, build, 0)

    def join_mats(i, carry):
        s = slots - 1 - i
        mats[s] = mats[s] + mats[splan[1, s]]
        return carry

    lax.fori_loop(0, slots, join_mats, 0)
    for side in range(2):
        end_coef[side, 0] = pack_rows(coef, (0,), side)
        end_coef[side, 1] = pack_rows(coef, (2,), side)
        end_coef[side, 2] = pack_rows(wetfric, (), side)

    def observe():
        def slot(s, carry):
            v = seen[splan[0, s]]
            acc = [zero, zero]
            for c in range(16):
                m = mats[s, 16 * c : 16 * c + 16, :].reshape(2, 8, BLOCK)
                acc[c % 2] = acc[c % 2] + m * v[c // 8, c % 8 : c % 8 + 1, :]
            oslot[s] = acc[0] + acc[1]
            return carry

        lax.fori_loop(0, slots, slot, 0, unroll=4)

    def eastward(v, beyond):
        moved = [pltpu.roll(b, BLOCK - 1, 2) for b in v] + [beyond]
        return [jnp.where(lane8 == BLOCK - 1, moved[cb + 1], moved[cb]) for cb in range(nblk)]

    def westward(v, beyond):
        moved = [beyond] + [pltpu.roll(b, 1, 2) for b in v]
        return [jnp.where(lane8 == 0, moved[cb], moved[cb + 1]) for cb in range(nblk)]

    def from_east(halos, row):
        return pltpu.roll(halos[1], BLOCK - 1 - row, 2)

    def from_west(halos, row):
        return pltpu.roll(halos[0], BLOCK - row, 2)

    def image_row(src, row, east_side, west_side, to_north=True, to_south=True):
        v = [src[row + 1, cb] for cb in range(nblk)]
        e = eastward(v, east_side)
        w = westward(v, west_side)
        images = []
        for cb in range(nblk):
            at = pl.ds(cb * BLOCK, BLOCK)
            image = (
                diag[row, :, at] * v[cb]
                - coef[0, row, :, at] * e[cb]
                - coef[1, row, :, at] * w[cb]
                + oslot[splan[2, row * nblk + cb]]
            )
            if to_north:
                image = image - coef[2, row, :, at] * src[row + 2, cb]
            if to_south:
                image = image - coef[3, row, :, at] * src[row, cb]
            images.append(image)
        return v, images

    def inside(src, dst):
        def put(row, images):
            for cb in range(nblk):
                dst[row + 1, cb] = images[cb]

        def line(row, carry):
            put(row, image_row(src, row, zero, zero)[1])
            return carry

        lax.fori_loop(1, rows - 1, line, 0, unroll=3 if (rows - 2) % 3 == 0 else 2)
        put(0, image_row(src, 0, zero, zero, to_south=False)[1])
        put(rows - 1, image_row(src, rows - 1, zero, zero, to_north=False)[1])

    def lat_edges(src, dst):
        for cb in range(nblk):
            at = pl.ds(cb * BLOCK, BLOCK)
            dst[1, cb] = dst[1, cb] - coef[3, 0, :, at] * src[0, cb]
            dst[rows, cb] = dst[rows, cb] - coef[2, rows - 1, :, at] * src[rows + 1, cb]

    def lon_edges(halos, dst, refs=()):
        dots, square = [zero] * len(refs), zero
        for row in range(rows):
            for side in range(2):
                cb = side * (nblk - 1)
                beyond = from_east(halos, row) if side else from_west(halos, row)
                at = pl.ds(cb * BLOCK, BLOCK)
                change = coef[1 - side, row, :, at] * jnp.where(lane8 == side * (BLOCK - 1), -beyond, 0.0)
                old = dst[row + 1, cb]
                dst[row + 1, cb] = old + change
                dots = [dot + ref[row + 1, cb] * change for dot, ref in zip(dots, refs)]
                square = square + change * (old + old + change)
        return [v[0] + v[1] for v in dots + [square]]

    lat_order = sorted(range(nlat), key=lambda k: (k == 0, abs(k - nlat // 2)))
    lat_peers = {k: lax.rem(me_lat + k, nlat) for k in lat_order}
    lon_peers = {k: lax.rem(me_lon + k, nlon) for k in lon_order}

    def sum_wait(i):
        whole = sum_a.at[i, pl.ds(0, count - 1)]
        return remote(whole, whole, as_.at[i], ar.at[i], {"lat": south})

    def send_sums(i, sums):
        part = jnp.zeros((8, BLOCK), jnp.float32)
        groups = 4 if len(sums) <= 4 else 16
        for k, s in enumerate(sums):
            both, wide = s, BLOCK
            while wide * groups > BLOCK:
                wide = wide // 2
                both = both + pltpu.roll(both, wide, 1)
            part = jnp.where(lane8 // (BLOCK // groups) == k, both, part)
        row = jnp.sum(part, axis=0, keepdims=True)
        part_row[i] = row
        sum_a[i, pl.ds(me, 1)] = row
        for a in lat_order:
            for b in lon_order:
                if a or b:
                    where = {"lat": lat_peers[a], "lon": lon_peers[b]}
                    remote(part_row.at[i], sum_a.at[i, pl.ds(me, 1)], as_.at[i], ar.at[i], where).start()

    def take_sums(i, number=4):
        sum_wait(i).wait_recv()
        groups, tall = (4, 8) if number <= 4 else (16, 16)
        total = jnp.sum(sum_a[i], axis=0, keepdims=True)
        lanes = lax.broadcasted_iota(jnp.int32, (tall, BLOCK), 1) // (BLOCK // groups)
        own = lanes == lax.broadcasted_iota(jnp.int32, (tall, BLOCK), 0)
        whole = jnp.sum(jnp.where(own, total, 0.0), axis=1, keepdims=True)
        return [jnp.broadcast_to(whole[k : k + 1], (8, BLOCK)) for k in range(number)]

    def beta_of(size, rr, rq, qq):
        return (rr - 2.0 * size * rq + size * size * qq) / rr

    def halves(sums):
        return [v[0] + v[1] for v in sums]

    def last_sums(size, beta, rr, rq, dq, qq, rw, rz, qw, qz, pw, pz):
        with_r = rw - size * rz + beta * rq
        with_q = qw - size * qz + beta * qq
        with_p = pw - size * pz + beta * dq
        return [rr - 2.0 * size * rq + size * size * qq, with_r - size * with_q + beta * with_p]

    def outer(o):
        k0, kq, kz = 4 * o, 4 * o + 1, 4 * o + 2
        i0, i1, i2 = ITERS * o, ITERS * o + 1, ITERS * o + 2
        r0, q0, z0 = field.at[k0], field.at[kq], field.at[kz]
        z1 = field.at[3] if o == 0 else z_last
        observe()
        if o == 0:
            inside(r0, q0)
            wait_halo(k0, slice(2, 4))
            lat_edges(r0, q0)

        def first_dots(row, carry):
            rr, rq, qq = carry
            if o == 0:
                v = [r0[row + 1, cb] for cb in range(nblk)]
                images = [q0[row + 1, cb] for cb in range(nblk)]
            else:
                v, images = image_row(r0, row, from_east(hq.at[k0], row), from_west(hq.at[k0], row))
            for cb in range(nblk):
                res, image = v[cb], images[cb]
                if o > 0:
                    q0[row + 1, cb] = image
                rr = rr + res * res
                rq = rq + res * image
                qq = qq + image * image
            return rr, rq, qq

        sums = halves(lax.fori_loop(0, rows, first_dots, (zero, zero, zero), unroll=rows))
        if o == 0:
            wait_halo(k0, slice(0, 2))
            more_rq, more_qq = lon_edges(hq.at[k0], q0, (r0,))
            sums = [sums[0], sums[1] + more_rq, sums[2] + more_qq]
        keep_ends(kq, q0)
        send_halo(kq, slice(0, 2) if o == 0 else slice(None))
        if o == 0:
            pl.semaphore_wait(ready, nlat - 1)
        send_sums(i0, sums)
        if o == 0:
            send_halo(kq, slice(2, 4))
        if o == 0:
            keep_near(0)
            keep_near(1)

        def look(row, carry):
            for cb in range(nblk):
                seen[row * nblk + cb] = q0[row + 1, cb]
            return carry

        lax.fori_loop(0, rows, look, 0)
        observe()
        inside(q0, z0)
        wait_halo(kq, slice(2, 4))
        lat_edges(q0, z0)
        wait_halo(kq, slice(0, 2))
        lon_edges(hq.at[kq], z0)

        keep_ends(kz, z0)
        send_halo(kz)
        if o == 0:
            keep_near(2)
        rr, rq, qq, _ = take_sums(i0)
        size0 = rr / rq
        beta0 = beta_of(size0, rr, rq, qq)
        more = 1.0 + beta0

        def second_vectors(row, cb):
            r, q, z = r0[row + 1, cb], q0[row + 1, cb], z0[row + 1, cb]
            res = r - size0 * q
            return res, res + beta0 * r, more * q - size0 * z

        def second(row, carry):
            ri, qi, ii = carry
            for cb in range(nblk):
                q = q0[row + 1, cb]
                image = more * q - size0 * z0[row + 1, cb]
                ri = ri + r0[row + 1, cb] * image
                qi = qi + q * image
                ii = ii + image * image
            return ri, qi, ii

        part_ri, part_qi, part_qq = halves(lax.fori_loop(0, rows, second, (zero,) * 3, unroll=4))
        part_rr = sums[0] - 2.0 * size0 * sums[1] + size0 * size0 * sums[2]
        part_rq = part_ri - size0 * part_qi
        part_dq = part_rq + beta0 * part_ri
        sums = (part_rr, part_rq, part_dq, part_qq)
        if o == 0:
            send_sums(i1, sums)

        def keep_second(row, carry):
            for cb in range(nblk):
                r1[row + 1, cb], p1[row + 1, cb], image = second_vectors(row, cb)
                q1[row + 1, cb] = image
                seen[row * nblk + cb] = image
            return carry

        lax.fori_loop(0, rows, keep_second, 0, unroll=4)
        observe()
        inside(q1, z1)
        wait_halo(kz, slice(2, 4))
        for edge in (0, rows + 1):
            for cb in range(nblk):
                q1[edge, cb] = more * q0[edge, cb] - size0 * z0[edge, cb]
        lat_edges(q1, z1)

        def third(row, carry):
            rw, rz, qw, qz, pw, pz = carry
            for cb in range(nblk):
                r, q, p, z = r1[row + 1, cb], q1[row + 1, cb], p1[row + 1, cb], z1[row + 1, cb]
                w = q0[row + 1, cb] - size0 * z0[row + 1, cb]
                rw = rw + r * w
                rz = rz + r * z
                qw = qw + q * w
                qz = qz + q * z
                pw = pw + p * w
                pz = pz + p * z
            return rw, rz, qw, qz, pw, pz

        rw, rz, qw, qz, pw, pz = halves(lax.fori_loop(0, rows, third, (zero,) * 6, unroll=4))
        wait_halo(kz, slice(0, 2))
        hq1[...] = more * hq[kq] - size0 * hq[kz]
        more_rz, more_qz, more_pz, _ = lon_edges(hq1, z1, (r1, q1, p1))
        rz, qz, pz = rz + more_rz, qz + more_qz, pz + more_pz
        if o == 0:
            keep_ends(3, z1)
            send_halo(3)
        if o > 0:
            send_sums(i1, list(sums) + [rw, rz, qw, qz, pw, pz])
            return size0
        rr, rq, dq, qq = take_sums(i1)
        size1 = rr / dq
        beta1 = beta_of(size1, rr, rq, qq)
        send_sums(i2, last_sums(size1, beta1, *sums, rw, rz, qw, qz, pw, pz))

        def settle(blocks):
            def line(row, carry):
                for cb in blocks:
                    q, p = q1[row + 1, cb], p1[row + 1, cb]
                    res = r1[row + 1, cb] - size1 * q
                    r2[row + 1, cb] = res
                    p2[row + 1, cb] = res + beta1 * p
                    w = q0[row + 1, cb] - size0 * z0[row + 1, cb]
                    q2[row + 1, cb] = (w - size1 * z1[row + 1, cb]) + beta1 * q
                    x[row + 1, cb] = size0 * r0[row + 1, cb] + size1 * p
                return carry

            lax.fori_loop(0, rows, line, 0, unroll=2)

        return size0, beta0, size1, beta1, settle

    size0, beta0, size1, beta1, settle = outer(0)

    def beyond(r, q, q_next):
        res = r - size0 * q
        way = res + beta0 * r
        res = res - size1 * q_next
        return size0 * r + size1 * way, res + beta1 * way, res

    hx[...], hp[...], hr[...] = beyond(hq[0], hq[1], hq1[...])

    def add_up(square):
        return jnp.sum(square[0] + square[1], axis=0, keepdims=True)

    def parts_of(flux, dragged):
        (xe, xn), (pe, pn) = flux
        parts = jnp.where(sub8 == 0, add_up(xe * xe + xn * xn), dragged)
        parts = jnp.where(sub8 == 1, add_up(xe * pe + xn * pn), parts)
        return jnp.where(sub8 == 2, add_up(pe * pe + pn * pn), parts)

    def extended(k, side):
        corner = field[k, rows + 1, side * (nblk - 1)]
        return jnp.where(lane8 == rows, pltpu.roll(corner, (rows + side) % BLOCK, 2), pk[k, side])

    def state(r, q, z):
        return beyond(r, q, (1.0 + beta0) * q - size0 * z)[:2]

    for side in range(2):
        own = state(*(extended(k, side) for k in range(3)))
        after = (hx[1], hp[1]) if side else state(near[0], near[1], near[2])
        flux = [
            (end_coef[side, 0] * (e - v), end_coef[side, 1] * (pltpu.roll(v, BLOCK - 1, 2) - v))
            for v, e in zip(own, after)
        ]
        surf_pk[side] = parts_of(flux, end_coef[side, 2])
    surf_copies = [
        remote(surf_pk.at[0], surf_hq.at[1], ss.at[2], sr.at[2], {"lon": west}),
        remote(surf_pk.at[1], surf_hq.at[0], ss.at[3], sr.at[3], {"lon": east}),
        remote(surf.at[1], surf.at[rows + 1], ss.at[0], sr.at[0], {"lat": south}),
        remote(surf.at[rows], surf.at[0], ss.at[1], sr.at[1], {"lat": north}),
    ]
    for c in surf_copies[:2]:
        c.start()
    settle(range(nblk))
    for edge in (0, rows + 1):
        for cb in range(nblk):
            x[edge, cb], p2[edge, cb], r2[edge, cb] = beyond(field[0, edge, cb], field[1, edge, cb], q1[edge, cb])

    def surface(row, carry):
        for cb in range(nblk):
            at = pl.ds(cb * BLOCK, BLOCK)
            flux = []
            for ref, halos in ((x, hx), (p2, hp)):
                v = ref[row + 1, cb]
                after = pltpu.roll(ref[row + 1, cb + 1], BLOCK - 1, 2) if cb < nblk - 1 else from_east(halos, row)
                e = jnp.where(lane8 == BLOCK - 1, after, pltpu.roll(v, BLOCK - 1, 2))
                flux.append((coef[0, row, :, at] * (e - v), coef[2, row, :, at] * (ref[row + 2, cb] - v)))
            surf[row + 1, :, at] = parts_of(flux, wetfric[row, :, at])
        return carry

    lax.fori_loop(0, rows, surface, 0)
    for c in surf_copies[2:]:
        c.start()
    wait_halo(3)

    def image_beyond(q, z, z_next, q_next):
        return ((q - size0 * z) - size1 * z_next) + beta1 * q_next

    for edge in (0, rows + 1):
        for cb in range(nblk):
            q2[edge, cb] = image_beyond(field[1, edge, cb], field[2, edge, cb], field[3, edge, cb], q1[edge, cb])
    hw[...] = image_beyond(hq[1], hq[2], hq[3], hq1[...])
    for c in surf_copies:
        c.wait_recv()
    rr, dq, _, _ = take_sums(2)
    size2 = rr / dq
    ramp = jnp.where(sub8 == 0, 1.0, jnp.where(sub8 == 1, 2.0 * size2, jnp.where(sub8 == 2, size2 * size2, 0.0)))

    def extra_of(parts):
        speed = jnp.maximum(jnp.sum(parts * ramp, axis=0, keepdims=True), 0.0)
        return parts[3:4] * (jnp.sqrt(1.0 + speed / 16.0) - 1.0)

    def renew(row, cb):
        extra = extra_of(surf[row, :, pl.ds(cb * BLOCK, BLOCK)])
        place = x[row, cb] + size2 * p2[row, cb]
        new = (r2[row, cb] - size2 * q2[row, cb]) - extra * place
        field[4, row, cb] = new
        return extra, place, new

    def friction(row, carry):
        for cb in range(nblk):
            at = pl.ds(cb * BLOCK, BLOCK)
            extra, place, new = renew(row + 1, cb)
            x[row + 1, cb] = place
            diag[row, :, at] = diag[row, :, at] + extra
            seen[row * nblk + cb] = new
        return carry

    lax.fori_loop(0, rows, friction, 0, unroll=4)
    for edge in (0, rows + 1):
        for cb in range(nblk):
            renew(edge, cb)
    for side in range(2):
        hq[4, side] = (hr[side] - size2 * hw[side]) - extra_of(surf_hq[side]) * (hx[side] + size2 * hp[side])
    size0 = outer(1)
    for cb in range(nblk):
        at = pl.ds(cb * BLOCK, BLOCK)
        for h in range(2):
            own = (pl.ds(1, rows), cb, h)
            x_out[h, :, :, at] = jnp.swapaxes(x[own] + size0 * field[(4,) + own], 0, 1)
            w_out[h, :, :, at] = jnp.swapaxes(field[(5,) + own] - size0 * field[(6,) + own], 0, 1)
            for src, dst in ((p1, p_out), (r1, r_out), (q1, q_out), (z_last, z_out)):
                dst[h, :, :, at] = jnp.swapaxes(src[own], 0, 1)
    for c in obs_sends + first_copies:
        c.wait_send()
    for k in (0, 1, 2, 3, 5, 6):
        for c in halo(k):
            c.wait_send()
    for c in surf_copies:
        c.wait_send()
    rr, rq, dq, qq, *others = take_sums(SUMS - 2, 10)
    size1 = rr / dq
    beta1 = beta_of(size1, rr, rq, qq)
    rr, dq = last_sums(size1, beta1, rr, rq, dq, qq, *others)
    size2 = rr / dq
    for dst, value in ((first_out, size1 + size2 * beta1), (second_out, size2), (third_out, size1 * size2)):
        dst[...] = jnp.broadcast_to(value[:, 0:1], (8, cols))
    for i in range(SUMS - 1):
        sum_wait(i).wait_send()


def shards(nlat, nlon, depth, friction, ocean_mask, forcing, tile_route, tile_block, obs_cell, obs_time, obs_value, obs_weight):
    channels, rows, cols = forcing.shape
    slots = nlon * CAP
    nblk, tiles = cols // BLOCK, obs_time.shape[0]
    f32, i32 = jnp.float32, jnp.int32
    vmem, smem = pltpu.VMEM, pltpu.SMEM
    hbm = pl.BlockSpec(memory_space=pltpu.HBM)
    field = (rows + 2, nblk, 2, 8, BLOCK)
    ends = (2, 2, 8, BLOCK)
    split = (2, channels // 2, rows, cols)
    dma = pltpu.SemaphoreType.DMA
    scratch = [
        smem((tiles,), i32),
        smem((tiles,), i32),
        vmem((rows, cols), f32),
        vmem((rows, cols), f32),
        vmem((rows, cols), i32),
        vmem(split, f32),
        vmem((tiles, BLOCK), i32),
        vmem((tiles, BLOCK), f32),
        vmem((tiles, BLOCK), f32),
        vmem((tiles, BLOCK), f32),
        vmem((rows, cols), f32),
        vmem((rows, cols), f32),
        vmem((rows, cols), f32),
        vmem((rows, BLOCK), f32),
        vmem((rows, BLOCK), f32),
        vmem((rows, 8, cols), f32),
        vmem((4, rows, 8, cols), f32),
        vmem((rows, 8, cols), f32),
        vmem((tiles + 1, 8, BLOCK), f32),
        vmem((tiles + 1, 8, BLOCK), i32),
        vmem((nlon, 8, BLOCK), f32),
        vmem((nlon, 8, BLOCK), i32),
        vmem((nlon, 8, BLOCK), f32),
        vmem((nlon, 8, BLOCK), i32),
        vmem((8, BLOCK), i32),
        smem((8, BLOCK), i32),
        vmem((slots, 2, 8, BLOCK), f32),
        vmem((slots + 1, 256, BLOCK), f32),
        vmem((slots + 1, 2, 8, BLOCK), f32),
        vmem((HALOS,) + field, f32),
        vmem((rows * nblk, 2, 8, BLOCK), f32),
        vmem(field, f32),
        vmem(field, f32),
        vmem(field, f32),
        vmem(field, f32),
        vmem(field, f32),
        vmem(field, f32),
        vmem(field, f32),
        vmem(field, f32),
        vmem((HALOS,) + ends, f32),
        vmem((HALOS,) + ends, f32),
        vmem(ends, f32),
        vmem(ends, f32),
        vmem(ends, f32),
        vmem(ends, f32),
        vmem(ends, f32),
        vmem((rows + 2, 8, cols), f32),
        vmem((2, 8, BLOCK), f32),
        vmem((2, 8, BLOCK), f32),
        vmem((3, 2, 8, BLOCK), f32),
        vmem((2, 3, 8, BLOCK), f32),
        vmem((SUMS, nlat * nlon, BLOCK), f32),
        vmem((SUMS, 1, BLOCK), f32),
        pltpu.SemaphoreType.REGULAR,
        dma((10,)),
        dma((HALOS, 4)),
        dma((HALOS, 4)),
        dma((4,)),
        dma((4,)),
        dma((SUMS,)),
        dma((SUMS,)),
        dma((2, nlon)),
        dma((2, nlon)),
        dma((4,)),
        dma((4,)),
        dma((1,)),
    ]
    shape = vmem(split, f32)
    x, p, r, q, w, z, first, second, third = pl.pallas_call(
        functools.partial(kernel, nlat, nlon),
        out_shape=(shape,) * 6 + (vmem((8, cols), f32),) * 3,
        in_specs=[hbm] * 10,
        out_specs=(pl.BlockSpec(memory_space=vmem),) * 9,
        scratch_shapes=scratch,
        compiler_params=pltpu.CompilerParams(
            collective_id=0, has_side_effects=True, vmem_limit_bytes=60 * 2**20
        ),
    )(
        tile_route.reshape(-1), tile_block, depth, friction, ocean_mask, forcing.reshape(split),
        obs_cell, obs_time, obs_value, obs_weight,
    )
    x = x + first * p + second * r - third * q
    r = r - first * q - second * w + third * z
    return x.reshape(forcing.shape), r.reshape(forcing.shape)


def solution(mesh):
    tile = P(("lat", "lon"), None)
    grid = P("lat", "lon")
    in_specs = (grid, grid, grid, P(None, "lat", "lon"), tile, P(("lat", "lon")), tile, tile, tile, tile)
    out_specs = (P(None, "lat", "lon"), P(None, "lat", "lon"))
    body = functools.partial(shards, mesh.shape["lat"], mesh.shape["lon"])
    return jax.shard_map(body, mesh=mesh, in_specs=in_specs, out_specs=out_specs, check_vma=False)
```
